32 devices in a mesh: pipe: 2 (over x), dp: 4 (over y, core), tensor: 4 (over z).
Axes of the slice: x: 2, y: 2, z: 4, core: 2. Of those that a mesh axis runs over, the one named last changes fastest.
Arguments:
- boundary: bfloat16 [2, 8, 1024, 2048], P('pipe', 'dp'), may hold values from -6 to 6
- segments: int32 [8, 1024], P('dp'), may hold values from 0 to 7, never falling along the last dimension, each value on 1 to 256 neighbouring positions
- ln1_gain: bfloat16 [2, 2048], P('pipe', 'dp'), may hold values from 0.5 to 1.5
- ln1_bias: bfloat16 [2, 2048], P('pipe', 'dp'), may hold values from -1.75 to 1.75
- ln2_gain: bfloat16 [2, 2048], P('pipe', 'dp'), may hold values from 0.5 to 1.5
- ln2_bias: bfloat16 [2, 2048], P('pipe', 'dp'), may hold values from -1.75 to 1.75
- qkv_weight: bfloat16 [2, 2048, 8, 768], P('pipe', 'dp', 'tensor'), may hold values from -0.125 to 0.125
- qkv_bias: bfloat16 [2, 8, 768], P('pipe', 'tensor', 'dp'), may hold values from -1.75 to 1.75
- dense_weight: bfloat16 [2, 2048, 2048], P('pipe', 'tensor', 'dp'), may hold values from -0.5 to 0.5
- dense_bias: bfloat16 [2, 2048], P('pipe', 'dp'), may hold values from -1.75 to 1.75
- fc1_weight: bfloat16 [2, 2048, 8192], P('pipe', 'dp', 'tensor'), may hold values from -0.125 to 0.125
- fc1_bias: bfloat16 [2, 8192], P('pipe', ('tensor', 'dp')), may hold values from -1.75 to 1.75
- fc2_weight: bfloat16 [2, 8192, 2048], P('pipe', 'tensor', 'dp'), may hold values from -0.0625 to 0.0625
- fc2_bias: bfloat16 [2, 2048], P('pipe', 'dp'), may hold values from -1.75 to 1.75
Outputs:
- boundary_out: float32 [2, 8, 1024, 2048], P('pipe', 'dp', 'tensor')
- ln1_gain_grad: float32 [2, 2048], P('pipe', ('dp', 'tensor'))
- ln1_bias_grad: float32 [2, 2048], P('pipe', ('dp', 'tensor'))
- ln2_gain_grad: float32 [2, 2048], P('pipe', ('dp', 'tensor'))
- ln2_bias_grad: float32 [2, 2048], P('pipe', ('dp', 'tensor'))
- qkv_weight_grad: float32 [2, 2048, 8, 768], P('pipe', 'dp', 'tensor')
- qkv_bias_grad: float32 [2, 8, 768], P('pipe', 'tensor', 'dp')
- dense_weight_grad: float32 [2, 2048, 2048], P('pipe', 'tensor', 'dp')
- dense_bias_grad: float32 [2, 2048], P('pipe', 'dp')
- fc1_weight_grad: float32 [2, 2048, 8192], P('pipe', 'dp', 'tensor')
- fc1_bias_grad: float32 [2, 8192], P('pipe', ('tensor', 'dp'))
- fc2_weight_grad: float32 [2, 8192, 2048], P('pipe', 'tensor', 'dp')
- fc2_bias_grad: float32 [2, 2048], P('pipe', 'dp')
The draws below stay inside these ranges and needn't reach their ends.
Inputs may be any that keep to these rules, and one draw needn't show every extreme that they name: `segments`: along each sequence the document number never falls; every sequence holds all 8 documents, each of 1 to 256 tokens, one of exactly 256.
All inputs are finite; a program needn't handle non-finite values.
Results may differ from the reference program's by a relative error of at most 0.015.
Values may be sent and summed in bfloat16 or wider, within the bound.
A program may use at most 320 MiB of HBM per device.

```python
import math
import jax
import jax.numpy as jnp
import numpy as np
from jax import lax

D = 2048
H = 8
HD = 256
FF = 8192
LEN = 1024
DOCS = 8
SEQS = 8


def level_of(key, dims, pieces, smallest, high):
    gain, own = 1.0, jax.random.fold_in(key, 6)
    for position, parts in pieces:
        draws = jnp.exp(jax.random.uniform(jax.random.fold_in(own, position), (parts,), jnp.float32, smallest / len(pieces), high / len(pieces)))
        gain = gain * jnp.repeat(draws, dims[position] // parts).reshape([-1 if axis == position else 1 for axis in range(len(dims))])
    return gain


def split_up(number_of, total, bound, lean):
    loads = [(1 << 20) // math.isqrt(grade ** lean) + 1 for grade in range(2, number_of + 1)]
    rest, given = total - bound - (number_of - 1), [1] * (number_of - 1)
    while rest > 0:
        free = [i for i in range(number_of - 1) if given[i] < bound]
        mass, left = sum([loads[i] for i in free]), rest
        for i in free:
            addition = min(bound - given[i], max(1, left * loads[i] // mass), rest)
            given[i] = given[i] + addition
            rest = rest - addition
    return np.array([bound] + given)


def uneven_parts(own_key, amount, total, most, slope):
    if amount == 2:
        one = jax.random.randint(own_key, (), max(1, total - most), min(most, total - 1) + 1)
        return jnp.stack([one, total - one])
    tallies = jnp.asarray(split_up(amount, total, most, slope), jnp.int32)
    pairs = (amount - 1) // 2
    source_of, taker = tallies[1:1 + 2 * pairs:2], tallies[2:2 + 2 * pairs:2]
    slack = jnp.minimum(source_of - 1, most - taker)
    passed = jax.random.randint(jax.random.fold_in(own_key, 1), (pairs,), 0, 1 << 20) % (slack + 1)
    tallies = tallies.at[1:1 + 2 * pairs:2].set(source_of - passed).at[2:2 + 2 * pairs:2].set(taker + passed)
    return tallies[jax.random.permutation(jax.random.fold_in(own_key, 2), amount)]


def noise(own_key, shape, width, bound, cuts=(), held_as=jnp.bfloat16):
    array = width * jax.random.normal(own_key, shape, jnp.float32)
    if cuts:
        array = array * level_of(own_key, shape, cuts, -0.22, 0.18)
    return jnp.clip(array, -bound, bound).astype(held_as)


def setup_inputs(seed: int = 0) -> dict:
    keys = jax.random.split(jax.random.key(seed), 15)
    return {
        "boundary": noise(keys[0], (2, SEQS, LEN, D), 1.0, 6.0, ((0, 2), (1, 4))),
        "segments": jax.vmap(lambda own: jnp.searchsorted(jnp.cumsum(uneven_parts(own, DOCS, LEN, LEN // 4, 0)), jnp.arange(LEN), side="right"))(jax.random.split(keys[1], SEQS)).reshape((SEQS, LEN)).astype(jnp.int32),
        "ln1_gain": jnp.clip(1.0 + 0.1 * jax.random.normal(keys[2], (2, D), jnp.float32), 0.5, 1.5).astype(jnp.bfloat16),
        "ln1_bias": noise(keys[3], (2, D), 0.3, 1.75, ((0, 2), (1, 4))),
        "ln2_gain": jnp.clip(1.0 + 0.1 * jax.random.normal(keys[4], (2, D), jnp.float32), 0.5, 1.5).astype(jnp.bfloat16),
        "ln2_bias": noise(keys[5], (2, D), 0.3, 1.75, ((0, 2), (1, 4))),
        "qkv_weight": noise(keys[6], (2, D, H, 3 * HD), D ** -0.5, 0.125, ((0, 2), (1, 4), (2, 4))),
        "qkv_bias": noise(keys[7], (2, H, 3 * HD), 0.3, 1.75, ((0, 2), (1, 4), (2, 4))),
        "dense_weight": noise(keys[8], (2, D, D), (D // 16) ** -0.5, 0.5, ((0, 2), (1, 4), (2, 4))),
        "dense_bias": noise(keys[9], (2, D), 0.3, 1.75, ((0, 2), (1, 4))),
        "fc1_weight": noise(keys[10], (2, D, FF), D ** -0.5, 0.125, ((0, 2), (1, 4), (2, 4))),
        "fc1_bias": noise(keys[11], (2, FF), 0.3, 1.75, ((0, 2), (1, 16))),
        "fc2_weight": noise(keys[12], (2, FF, D), FF ** -0.5, 0.0625, ((0, 2), (1, 4), (2, 4))),
        "fc2_bias": noise(keys[13], (2, D), 0.3, 1.75, ((0, 2), (1, 4))),
    }


@jax.custom_vjp
def low(v):
    return lax.optimization_barrier(v.astype(jnp.bfloat16)).astype(jnp.float32)

@jax.custom_vjp
def low_back(v):
    return v

def low_keep(v):
    return (low(v), None)

def low_pass(kept, grad):
    return (grad,)

def back_keep(v):
    return (v, None)

def back_low(kept, grad):
    return (low(grad),)
low.defvjp(low_keep, low_pass)
low_back.defvjp(back_keep, back_low)
norm_epsilon = 1e-05
mask_fill = -1e+30
highest = lax.Precision.HIGHEST

def normalize(values, norm_gain, norm_shift):
    average = lax.optimization_barrier(jnp.mean(values, axis=-1, keepdims=True))
    centred = values - average
    spread = lax.optimization_barrier(jnp.mean(centred * centred, axis=-1, keepdims=True))
    return centred * lax.rsqrt(spread + norm_epsilon) * norm_gain + norm_shift

def rotate(values, cos_table, sin_table):
    half_rot = cos_table.shape[-1]
    lower_half = values[..., :half_rot]
    upper_half = values[..., half_rot:2 * half_rot]
    return jnp.concatenate([lower_half * cos_table - upper_half * sin_table, upper_half * cos_table + lower_half * sin_table, values[..., 2 * half_rot:]], axis=-1)

def one_section(inputs, params, cos_table, sin_table, allowed):
    gain_first, bias_first, gain_second, bias_second, weight_qkv, bias_qkv, weight_dense, bias_dense, weight_up, bias_up, weight_down, bias_down = params
    first_in = low(normalize(inputs, gain_first, bias_first))
    second_in = low(normalize(inputs, gain_second, bias_second))
    packed = low_back(jnp.einsum('td,dhe->the', first_in, weight_qkv, precision=highest) + bias_qkv)
    queries = low(rotate(packed[..., :HD], cos_table, sin_table))
    key_rows = low(rotate(packed[..., HD:2 * HD], cos_table, sin_table))
    values = low(packed[..., 2 * HD:])
    scores = jnp.einsum('qhe,khe->hqk', queries, key_rows, precision=highest) * (1.0 / math.sqrt(HD))
    scores = low_back(jnp.where(allowed[None], scores, mask_fill))
    weights = low(jax.nn.softmax(scores, axis=-1))
    attended = jnp.einsum('hqk,khe->qhe', weights, values, precision=highest)
    mixed_heads = low(low_back(attended.reshape(attended.shape[0], H * HD)))
    hidden = low_back(jnp.dot(second_in, weight_up, precision=highest) + bias_up)
    activated = low(jax.nn.gelu(hidden, approximate=False))
    attn_branch = jnp.dot(mixed_heads, weight_dense, precision=highest) + bias_dense
    mlp_branch = jnp.dot(activated, weight_down, precision=highest) + bias_down
    return inputs + attn_branch + mlp_branch

def reference(boundary, segments, ln1_gain, ln1_bias, ln2_gain, ln2_bias, qkv_weight, qkv_bias, dense_weight, dense_bias, fc1_weight, fc1_bias, fc2_weight, fc2_bias):
    stacked = tuple((element.astype(jnp.float32) for element in (ln1_gain, ln1_bias, ln2_gain, ln2_bias, qkv_weight, qkv_bias, dense_weight, dense_bias, fc1_weight, fc1_bias, fc2_weight, fc2_bias)))
    first_params = tuple((element[0] for element in stacked))
    second_params = tuple((element[1] for element in stacked))
    inputs = boundary[0].astype(jnp.float32)
    cotangent = boundary[1].astype(jnp.float32)
    places = jnp.arange(LEN, dtype=jnp.int32)
    frequency = jnp.exp(-math.log(10000.0) * 2.0 * jnp.arange(HD // 8, dtype=jnp.float32) / (HD // 4))

    def one_sequence(totals, element):
        source, grad_out, segment_row = element
        change = jnp.concatenate([jnp.ones((1,), dtype=jnp.int32) > 0, segment_row[1:] != segment_row[:-1]])
        starts = lax.cummax(jnp.where(change, places, 0), axis=0)
        angles = (places - starts).astype(jnp.float32)[:, None, None] * frequency
        cos_table = jnp.cos(angles)
        sin_table = jnp.sin(angles)
        allowed = (places[:, None] >= places[None, :]) & (segment_row[:, None] == segment_row[None, :])

        def two_sections(params_one, params_two, source_in):
            middle = low(low_back(one_section(source_in, params_one, cos_table, sin_table, allowed)))
            return one_section(middle, params_two, cos_table, sin_table, allowed)
        result, pullback = jax.vjp(two_sections, first_params, second_params, source)
        grads_one, grads_two, grad_source = pullback(grad_out)
        totals = jax.tree.map(lambda running, former, latter: running + jnp.stack([former, latter]), totals, grads_one, grads_two)
        return (totals, (grad_source, result))
    empty_totals = tuple((jnp.zeros_like(element) for element in stacked))
    totals, (grad_inputs, outputs) = lax.scan(one_sequence, empty_totals, (inputs, cotangent, segments))
    boundary_out = jnp.stack([grad_inputs, outputs])
    return (boundary_out, totals[0], totals[1], totals[2], totals[3], totals[4], totals[5], totals[6], totals[7], totals[8], totals[9], totals[10], totals[11])
```

```python
import functools
import math

import jax
import jax.numpy as jnp
from jax import lax
from jax.experimental import pallas as pl
from jax.experimental.pallas import tpu as pltpu
from jax.sharding import PartitionSpec as P

norm_epsilon = 1e-05
mask_fill = -1e30
BAND = 256
ROT = 128
f32, bf16 = jnp.float32, jnp.bfloat16


def dot(a, b, contract=((1,), (0,))):
    return lax.dot_general(a, b, (contract, ((), ())), preferred_element_type=f32)


def allowed(seg_col, seg_row, block):
    low = max(block - 1, 0) * BAND
    size = (block + 1) * BAND - low
    own = lax.broadcasted_iota(jnp.int32, (BAND, size), 0) + (block * BAND - low)
    key = lax.broadcasted_iota(jnp.int32, (BAND, size), 1)
    rows = pl.ds(block * BAND, BAND)
    return (own >= key) & (seg_col[0, rows, :] == seg_row[0, :, pl.ds(low, size)])


def turn(values, cos, forward, backward):
    head = values[:, :ROT]
    head = (
        head * cos
        + pltpu.roll(head, ROT - 32, 1) * forward
        + pltpu.roll(head, 32, 1) * backward
    )
    return jnp.concatenate([head, values[:, ROT:]], axis=1)


def attend_kernel(scale, qkv, bias, cos, sin_a, sin_b, seg_col, seg_row, out, qr, kr, vr):
    size = out.shape[1]
    for block in range(out.shape[0] // BAND):
        rows = pl.ds(block * BAND, BAND)
        c, a, b = cos[rows, :], sin_a[rows, :], sin_b[rows, :]
        q = turn(qkv[rows, :size] + bias[:, :size], c, a, b).astype(bf16)
        k = turn(qkv[rows, size : 2 * size] + bias[:, size : 2 * size], c, a, b).astype(bf16)
        qr[rows, :] = q
        kr[rows, :] = k
        vr[rows, :] = (qkv[rows, 2 * size :] + bias[:, 2 * size :]).astype(bf16)
        low = max(block - 1, 0) * BAND
        keys = pl.ds(low, (block + 1) * BAND - low)
        scores = dot(q, kr[keys, :], ((1,), (1,))) * scale
        scores = jnp.where(allowed(seg_col, seg_row, block), scores, mask_fill)
        weights = jnp.exp(scores - jnp.max(scores, axis=1, keepdims=True))
        weights = weights * (1.0 / jnp.sum(weights, axis=1, keepdims=True))
        out[rows, :] = dot(weights.astype(bf16), vr[keys, :]).astype(bf16)


def attend(qkv, bias, tables, seg, heads, length):
    size = qkv.shape[1] // heads // 3
    seqs = qkv.shape[0] // length
    block = pl.BlockSpec((length, size), lambda b, h: (b, h))
    table = pl.BlockSpec((length, ROT), lambda b, h: (b, 0))
    return pl.pallas_call(
        functools.partial(attend_kernel, 1.0 / math.sqrt(size)),
        grid=(seqs, heads),
        in_specs=[
            pl.BlockSpec((length, 3 * size), lambda b, h: (b, h)),
            pl.BlockSpec((1, 3 * size), lambda b, h: (0, h)),
            table,
            table,
            table,
            pl.BlockSpec((1, length, 1), lambda b, h: (b, 0, 0)),
            pl.BlockSpec((1, 1, length), lambda b, h: (b, 0, 0)),
        ],
        out_specs=[block] * 4,
        out_shape=[jax.ShapeDtypeStruct((qkv.shape[0], heads * size), bf16)] * 4,
        compiler_params=pltpu.CompilerParams(vmem_limit_bytes=48 << 20),
        cost_estimate=pl.CostEstimate(
            flops=2 * 2 * qkv.shape[0] * 2 * BAND * heads * size,
            bytes_accessed=qkv.size * 4 + qkv.shape[0] * heads * size * 8,
            transcendentals=qkv.shape[0] * heads * 2 * BAND,
        ),
        name="attend",
    )(qkv, bias, *tables, seg[:, :, None], seg[:, None, :])


def attend_back_kernel(
    scale, qr, kr, vr, grad, cos, sin_a, sin_b, seg_col, seg_row, out, out_sum, dk_acc, dv_acc
):
    size = grad.shape[1]
    blocks = grad.shape[0] // BAND
    sums = [jnp.zeros((1, size), f32)] * 3

    def emit(place, part, values):
        rows = pl.ds(place * BAND, BAND)
        if part < 2:
            values = turn(values, cos[rows, :], -sin_a[rows, :], -sin_b[rows, :])
        values = values.astype(bf16)
        out[rows, part * size : (part + 1) * size] = values
        sums[part] = sums[part] + jnp.sum(values.astype(f32), axis=0, keepdims=True)

    for block in range(blocks):
        rows = pl.ds(block * BAND, BAND)
        low = max(block - 1, 0) * BAND
        keys = pl.ds(low, (block + 1) * BAND - low)
        q, k, v, g = qr[rows, :], kr[keys, :], vr[keys, :], grad[rows, :]
        scores = dot(q, k, ((1,), (1,))) * scale
        scores = jnp.where(allowed(seg_col, seg_row, block), scores, mask_fill)
        weights = jnp.exp(scores - jnp.max(scores, axis=1, keepdims=True))
        weights = weights * (1.0 / jnp.sum(weights, axis=1, keepdims=True))
        grad_weights = dot(g, v, ((1,), (1,)))
        row_dot = jnp.sum(weights * grad_weights, axis=1, keepdims=True)
        grad_scores = (weights * (grad_weights - row_dot)).astype(bf16)
        emit(block, 0, dot(grad_scores, k) * scale)
        dk = dot(grad_scores, q, ((0,), (0,))) * scale
        dv = dot(weights.astype(bf16), g, ((0,), (0,)))
        if block > 0:
            emit(block - 1, 1, dk_acc[...] + dk[:BAND])
            emit(block - 1, 2, dv_acc[...] + dv[:BAND])
            dk, dv = dk[BAND:], dv[BAND:]
        if block == blocks - 1:
            emit(block, 1, dk)
            emit(block, 2, dv)
        else:
            dk_acc[...] = dk
            dv_acc[...] = dv
    out_sum[0] = jnp.concatenate(sums, axis=1)


def attend_back(qr, kr, vr, grad, tables, seg, heads, length):
    size = qr.shape[1] // heads
    tokens = qr.shape[0]
    seqs = tokens // length
    block = pl.BlockSpec((length, size), lambda b, h: (b, h))
    table = pl.BlockSpec((length, ROT), lambda b, h: (b, 0))
    out, sums = pl.pallas_call(
        functools.partial(attend_back_kernel, 1.0 / math.sqrt(size)),
        grid=(seqs, heads),
        in_specs=[block] * 4
        + [table] * 3
        + [
            pl.BlockSpec((1, length, 1), lambda b, h: (b, 0, 0)),
            pl.BlockSpec((1, 1, length), lambda b, h: (b, 0, 0)),
        ],
        out_specs=[
            pl.BlockSpec((length, 3 * size), lambda b, h: (b, h)),
            pl.BlockSpec((1, 1, 3 * size), lambda b, h: (b, 0, h)),
        ],
        out_shape=[
            jax.ShapeDtypeStruct((tokens, heads * 3 * size), bf16),
            jax.ShapeDtypeStruct((seqs, 1, heads * 3 * size), f32),
        ],
        scratch_shapes=[pltpu.VMEM((BAND, size), f32)] * 2,
        compiler_params=pltpu.CompilerParams(vmem_limit_bytes=48 << 20),
        cost_estimate=pl.CostEstimate(
            flops=2 * 5 * tokens * 2 * BAND * heads * size,
            bytes_accessed=tokens * heads * size * 14,
            transcendentals=tokens * heads * 2 * BAND,
        ),
        name="attend_back",
    )(qr, kr, vr, grad, *tables, seg[:, :, None], seg[:, None, :])
    return out, jnp.sum(sums, axis=(0, 1))


def gelu_kernel(x, w, bias, act, slope):
    for row in range(0, x.shape[0], BAND):
        rows = pl.ds(row, BAND)
        h = dot(x[rows, :], w[...]) + bias[...]
        t = 1.0 / (1.0 + (0.3275911 * math.sqrt(0.5)) * jnp.abs(h))
        poly = 1.061405429 * t - 1.453152027
        poly = poly * t + 1.421413741
        poly = poly * t - 0.284496736
        poly = poly * t + 0.254829592
        bell = jnp.exp(-0.5 * h * h)
        tail = 0.5 * poly * t * bell
        cdf = jnp.where(h >= 0.0, 1.0 - tail, tail)
        act[rows, :] = (h * cdf).astype(bf16)
        slope[rows, :] = (cdf + h * bell * (1.0 / math.sqrt(2.0 * math.pi))).astype(bf16)


def gelu_matmul(x, w, bias):
    tokens, depth = x.shape
    width = w.shape[1]
    cols = min(512, width)
    block = pl.BlockSpec((tokens, cols), lambda j: (0, j))
    return pl.pallas_call(
        gelu_kernel,
        grid=(width // cols,),
        in_specs=[
            pl.BlockSpec((tokens, depth), lambda j: (0, 0)),
            pl.BlockSpec((depth, cols), lambda j: (0, j)),
            pl.BlockSpec((1, cols), lambda j: (0, j)),
        ],
        out_specs=[block, block],
        out_shape=[jax.ShapeDtypeStruct((tokens, width), bf16)] * 2,
        compiler_params=pltpu.CompilerParams(vmem_limit_bytes=48 << 20),
        cost_estimate=pl.CostEstimate(
            flops=2 * tokens * depth * width,
            bytes_accessed=2 * (tokens * depth + depth * width + 2 * tokens * width),
            transcendentals=2 * tokens * width,
        ),
        name="gelu_matmul",
    )(x, w, bias)


def to(source, target, send, recv, place):
    return pltpu.make_async_remote_copy(
        src_ref=source,
        dst_ref=target,
        send_sem=send,
        recv_sem=recv,
        device_id=place,
        device_id_type=pl.DeviceIdType.MESH,
    )


def greet(places):
    barrier = pltpu.get_barrier_semaphore()
    for place in places:
        pl.semaphore_signal(
            barrier, inc=1, device_id=place, device_id_type=pl.DeviceIdType.MESH
        )
    pl.semaphore_wait(barrier, len(places))


def chunks_of(shapes, axes, part):
    return [
        (m, row, col)
        for m, (shape, axis) in enumerate(zip(shapes, axes))
        for row in range(0, shape[0], part)
        for col in range(0, shape[1], part)
    ]


def chunk_at(ref, axis, shape, chunk, slot, part):
    _, row, col = chunk
    row, col = (row + slot * shape[0], col) if axis == 0 else (row, col + slot * shape[1])
    return ref.at[pl.ds(row, part), pl.ds(col, part)]


class Spread:
    def __init__(self, full, shapes, axes, ways, sems):
        self.full, self.shapes, self.axes = full, shapes, axes
        self.ring = ways // 2
        self.y_send, self.y_recv, self.c_send, self.c_recv = sems
        self.part = shapes[3][1]
        self.chunks = chunks_of(shapes, axes, self.part)
        d = lax.axis_index("dp")
        y, c = d // 2, d % 2
        self.core = {"dp": y * 2 + (1 - c)}
        self.ahead = [{"dp": lax.rem(y + o, self.ring) * 2 + c} for o in range(1, self.ring)]

    def at(self, n, slot):
        m = self.chunks[n][0]
        return chunk_at(
            self.full[m], self.axes[m], self.shapes[m], self.chunks[n], slot, self.part
        )

    def y_copy(self, n, step, source):
        target = self.at(n, 2 * ((self.ring - step) % self.ring))
        return to(
            source, target, self.y_send.at[n, step - 1], self.y_recv.at[n, step - 1],
            self.ahead[step - 1],
        )

    def c_copy(self, n, o, source):
        target = self.at(n, 2 * o + 1)
        return to(source, target, self.c_send.at[n, o], self.c_recv.at[n, o], self.core)

    def begin(self, n, source):
        for step in range(1, self.ring):
            self.y_copy(n, step, source).start()
        self.c_copy(n, 0, source).start()

    def forward(self, n):
        for step in range(1, self.ring):
            o = (self.ring - step) % self.ring
            self.y_copy(n, step, self.at(n, 0)).wait_recv()
            self.c_copy(n, o, self.at(n, 2 * o)).start()

    def finish(self):
        for n in range(len(self.chunks)):
            for step in range(1, self.ring):
                self.y_copy(n, step, self.at(n, 0)).wait_send()
            for o in range(self.ring):
                self.c_copy(n, o, self.at(n, 2 * o)).wait()

    @staticmethod
    def semaphores(pieces, ways):
        dma = pltpu.SemaphoreType.DMA
        return [dma((pieces, ways // 2 - 1))] * 2 + [dma((pieces, ways // 2))] * 2


def gather_kernel(
    ways, nt, axes,
    given, small, s0, s1, s2, s3,
    other, small_all, f0, f1, f2, f3, o0, o1, o2, o3,
    x_send, x_recv, y_send, y_recv, c_send, c_recv, z_send, z_recv,
    b0, b1, b2, b3, local,
):
    shards, bounce = (s0, s1, s2, s3), (b0, b1, b2, b3)
    shapes = [s.shape for s in shards]
    full, later = (f0, f1, f2, f3), (o0, o1, o2, o3)
    p, t = lax.axis_index("pipe"), lax.axis_index("tensor")
    sems = (y_send, y_recv, c_send, c_recv)
    now = Spread(full, shapes, axes, ways, sems)
    then = Spread(later, shapes, axes, ways, sems)
    ring, chunks, part = now.ring, now.chunks, now.part
    rows = given.shape[1]
    across = {"pipe": 1 - p}
    others = [{"tensor": lax.rem(t + step, nt)} for step in range(1, nt)]

    loads = [pltpu.make_async_copy(shards[m], bounce[m], local.at[m]) for m in range(4)]
    for load in loads:
        load.start()
    greet([across, now.core] + now.ahead + others)

    def in_shard(n):
        m, row, col = chunks[n]
        return shards[m].at[pl.ds(row, part), pl.ds(col, part)]

    def small_at(slot):
        return small_all.at[pl.ds(slot * small.shape[0], small.shape[0]), :]

    def x_given():
        mine = other.at[:, pl.ds(pl.multiple_of(t * rows, rows), rows), :]
        return to(given, mine, x_send.at[0], x_recv.at[0], across)

    def x_copy(n, target):
        return to(in_shard(n), target, x_send.at[n + 1], x_recv.at[n + 1], across)

    def small_y(step, source):
        target = small_at(2 * ((ring - step) % ring))
        return to(
            source, target, y_send.at[last, step - 1], y_recv.at[last, step - 1],
            now.ahead[step - 1],
        )

    def small_c(o, source):
        return to(source, small_at(2 * o + 1), c_send.at[last, o], c_recv.at[last, o], now.core)

    def stores(matrices):
        return [
            pltpu.make_async_copy(
                bounce[m],
                matrices[m].at[pl.ds(0, shapes[m][0]), :]
                if axes[m] == 0
                else matrices[m].at[:, pl.ds(0, shapes[m][1])],
                local.at[m],
            )
            for m in range(4)
        ]

    last = len(chunks)
    small_own = pltpu.make_async_copy(small, small_at(0), local.at[4])
    small_own.start()
    x_given().start()
    for step in range(1, ring):
        small_y(step, small).start()
    small_c(0, small).start()
    for load in loads:
        load.wait()

    @pl.when(p == 0)
    def _():
        for store in stores(full):
            store.start()
        for n in range(last):
            x_copy(n, now.at(n, 0)).start()
            now.begin(n, in_shard(n))

    @pl.when(p == 1)
    def _():
        for store in stores(later):
            store.start()
        for n in range(last):
            x_copy(n, then.at(n, 0)).start()

    x_given().wait_recv()
    here = other.at[:, pl.ds(pl.multiple_of(t * rows, rows), rows), :]
    z_copies = []
    for step in range(1, nt):
        z_copies.append(
            to(here, here, z_send.at[step - 1], z_recv.at[step - 1], others[step - 1])
        )
        z_copies[-1].start()
    for step in range(1, ring):
        o = (ring - step) % ring
        small_y(step, small).wait_recv()
        small_c(o, small_at(2 * o)).start()
    for n in range(last):
        x_copy(n, now.at(n, 0)).wait_recv()

        @pl.when(p == 1)
        def _():
            now.begin(n, now.at(n, 0))

        if n > 0:
            now.forward(n - 1)
    now.forward(last - 1)

    now.finish()
    for n in range(last):
        x_copy(n, now.at(n, 0)).wait_send()
    for step in range(1, ring):
        small_y(step, small).wait_send()
    for o in range(ring):
        small_c(o, small).wait()
    x_given().wait_send()
    for copy in z_copies:
        copy.wait()
    for store in stores(full):
        store.wait()
    small_own.wait()


def gather_section(given, small, shards, axes, ways, nt):
    hbm = pl.BlockSpec(memory_space=pl.ANY)
    shape = jax.ShapeDtypeStruct
    part = shards[3].shape[1]
    pieces = len(chunks_of([s.shape for s in shards], axes, part))
    full = [
        shape((s.shape[0] * ways, s.shape[1]) if axis == 0 else (s.shape[0], s.shape[1] * ways), bf16)
        for s, axis in zip(shards, axes)
    ]
    dma = pltpu.SemaphoreType.DMA
    out = pl.pallas_call(
        functools.partial(gather_kernel, ways, nt, axes),
        in_specs=[hbm] * 6,
        out_specs=[hbm] * 10,
        out_shape=[
            shape((given.shape[0], given.shape[1] * nt, given.shape[2]), bf16),
            shape((small.shape[0] * ways, small.shape[1]), bf16),
            *full,
            *full,
        ],
        scratch_shapes=[
            dma((pieces + 1,)),
            dma((pieces + 1,)),
            *Spread.semaphores(pieces + 1, ways),
            dma((nt - 1,)),
            dma((nt - 1,)),
            *[pltpu.VMEM(s.shape, bf16) for s in shards],
            dma((5,)),
        ],
        compiler_params=pltpu.CompilerParams(
            collective_id=1, has_side_effects=True, vmem_limit_bytes=16 << 20
        ),
        cost_estimate=pl.CostEstimate(flops=0, bytes_accessed=600 << 20, transcendentals=0),
        name="gather_section",
    )(given, small, *shards)
    return out[0], out[1], out[2:6], out[6:10]


SUBS = 8


class LineSum:
    def __init__(self, n, partial, right, left, sems, finished, out=None):
        self.n, self.partial, self.right, self.left = n, partial, right, left
        self.finished, self.out = finished, out
        self.r_send, self.r_recv, self.l_send, self.l_recv = sems[:4]
        self.spread = sems[4:]
        self.i = lax.axis_index("tensor")
        self.rows = partial.shape[0] // n
        self.sub = self.rows // SUBS
        self.after = {"tensor": lax.rem(self.i + 1, n)}
        self.before = {"tensor": lax.rem(self.i + n - 1, n)}

    def at(self, ref, j, s):
        start = pl.multiple_of(j * self.rows + s * self.sub, self.sub)
        return ref.at[pl.ds(start, self.sub), :]

    def r_copy(self, j, s, source):
        target = self.at(self.right, j, s)
        return to(source, target, self.r_send.at[j, s], self.r_recv.at[j, s], self.after)

    def l_copy(self, j, s, source):
        target = self.at(self.left, j, s)
        return to(source, target, self.l_send.at[j, s], self.l_recv.at[j, s], self.before)

    def ar_copy(self, j, s):
        rows = self.at(self.out, j, s)
        return to(rows, rows, self.spread[0].at[j, s], self.spread[1].at[j, s], self.after)

    def al_copy(self, j, s):
        rows = self.at(self.out, j, s)
        return to(rows, rows, self.spread[2].at[j, s], self.spread[3].at[j, s], self.before)

    def add(self, ref, j, s):
        ref = self.at(ref, j, s)
        own = self.at(self.partial, j, s)[...].astype(f32)
        ref[...] = (ref[...].astype(f32) + own).astype(bf16)

    def reduce(self, s):
        i, n = self.i, self.n
        for k in range(n - 1):
            j = n - 1 - k

            @pl.when(i == 0)
            def _():
                self.r_copy(j, s, self.at(self.partial, j, s)).start()

            @pl.when((i > 0) & (i < j))
            def _():
                self.r_copy(j, s, self.at(self.right, j, s)).wait_recv()
                self.add(self.right, j, s)
                self.r_copy(j, s, self.at(self.right, j, s)).start()

        for k in range(n - 1):

            @pl.when(i == n - 1)
            def _():
                self.l_copy(k, s, self.at(self.partial, k, s)).start()

            @pl.when((i < n - 1) & (i > k))
            def _():
                self.l_copy(k, s, self.at(self.left, k, s)).wait_recv()
                self.add(self.left, k, s)
                self.l_copy(k, s, self.at(self.left, k, s)).start()

    def finish(self, s):
        i, n = self.i, self.n

        @pl.when(i > 0)
        def _():
            self.r_copy(i, s, self.at(self.right, i, s)).wait_recv()
            self.add(self.right, i, s)

        @pl.when(i == 0)
        def _():
            self.at(self.right, i, s)[...] = self.at(self.partial, i, s)[...]

        @pl.when(i < n - 1)
        def _():
            self.l_copy(i, s, self.at(self.left, i, s)).wait_recv()

        @pl.when(i == n - 1)
        def _():
            self.at(self.left, i, s)[...] = jnp.zeros((self.sub, self.left.shape[1]), bf16)

        total = self.at(self.right, i, s)[...].astype(f32)
        total = total + self.at(self.left, i, s)[...].astype(f32)
        self.finished(self, s, total)
        if self.out is not None:

            @pl.when(i < n - 1)
            def _():
                self.ar_copy(i, s).start()

            @pl.when(i > 0)
            def _():
                self.al_copy(i, s).start()

    def pass_on(self, step, s):
        i, n = self.i, self.n

        @pl.when(i >= step)
        def _():
            self.ar_copy(i - step, s).wait_recv()

            @pl.when(i < n - 1)
            def _():
                self.ar_copy(i - step, s).start()

        @pl.when(i + step < n)
        def _():
            self.al_copy(i + step, s).wait_recv()

            @pl.when(i > 0)
            def _():
                self.al_copy(i + step, s).start()

    @property
    def turns(self):
        return SUBS + (self.n if self.out is not None else 1)

    def turn(self, it):
        @pl.when(it < SUBS)
        def _():
            self.reduce(it)

        @pl.when((it >= 1) & (it < SUBS + 1))
        def _():
            self.finish(it - 1)

        if self.out is not None:
            for step in range(1, self.n):
                s = it - 1 - step

                @pl.when((s >= 0) & (s < SUBS))
                def _():
                    self.pass_on(step, s)

    def drain(self):
        i, n = self.i, self.n

        def body(s, _):
            for j in range(n):

                @pl.when(i < j)
                def _():
                    self.r_copy(j, s, self.at(self.partial, j, s)).wait_send()

                @pl.when(i > j)
                def _():
                    self.l_copy(j, s, self.at(self.partial, j, s)).wait_send()

                if self.out is not None:

                    @pl.when((i >= j) & (i < n - 1))
                    def _():
                        self.ar_copy(j, s).wait_send()

                    @pl.when((i <= j) & (i > 0))
                    def _():
                        self.al_copy(j, s).wait_send()

            return 0

        lax.fori_loop(0, SUBS, body, 0)

    @staticmethod
    def scratch(n, tokens, width, spread):
        return [pltpu.VMEM((tokens, width), bf16)] * 2 + [
            pltpu.SemaphoreType.DMA((n, SUBS))
        ] * (8 if spread else 4)


def sum_spread_kernel(n, ways, axes, shapes, partial, base, *refs):
    out, full, right, left = refs[4], refs[5:9], refs[9], refs[10]
    line_sems, parts_sems = refs[11:19], refs[19:23]

    def finished(line, s, total):
        mine = pl.ds(pl.multiple_of(s * line.sub, line.sub), line.sub)
        line.at(out, line.i, s)[...] = (base[mine, :] + total).astype(bf16)

    line = LineSum(n, partial, right, left, line_sems, finished, out)
    parts = Spread(full, shapes, axes, ways, parts_sems)
    greet([line.after, line.before, parts.core] + parts.ahead)
    count = len(parts.chunks)
    for m in range(count):
        parts.begin(m, parts.at(m, 0))

    def turn_(it, _):
        line.turn(it)
        for m in range(count):

            @pl.when(it == m + 1)
            def _():
                parts.forward(m)

        return 0

    lax.fori_loop(0, max(line.turns, count + 1), turn_, 0)
    line.drain()
    parts.finish()


def sum_spread(partial, base, n, full, shapes, axes, ways):
    tokens, width = partial.shape
    vmem = pl.BlockSpec(memory_space=pltpu.VMEM)
    hbm = pl.BlockSpec(memory_space=pl.ANY)
    pieces = len(chunks_of(shapes, axes, shapes[3][1]))
    out = pl.pallas_call(
        functools.partial(sum_spread_kernel, n, ways, axes, shapes),
        in_specs=[vmem, vmem] + [hbm] * 4,
        out_specs=[vmem] + [hbm] * 4,
        out_shape=[jax.ShapeDtypeStruct((tokens, width), bf16)]
        + [jax.ShapeDtypeStruct(w.shape, bf16) for w in full],
        input_output_aliases={2 + m: 1 + m for m in range(4)},
        scratch_shapes=LineSum.scratch(n, tokens, width, True)
        + Spread.semaphores(pieces, ways),
        compiler_params=pltpu.CompilerParams(
            collective_id=2, has_side_effects=True, vmem_limit_bytes=32 << 20
        ),
        cost_estimate=pl.CostEstimate(flops=0, bytes_accessed=360 << 20, transcendentals=0),
        name="sum_spread",
    )(partial, base, *full)
    return out[0], out[1:]


class GradSum:
    def __init__(self, k, ways, xh, g, sides, outs, vec, vec_out, scratch):
        (
            self.load, self.away, self.held, self.round, self.across, self.done,
            self.v_held, self.v_round, self.v_across,
            self.load_sem, self.c_send, self.c_recv, self.y_send, self.y_recv,
            self.x_send, self.x_recv, self.out_sem,
        ) = scratch
        self.k, self.ring = k, ways // 2
        self.xh, self.g, self.sides, self.outs = xh, g, sides, outs
        self.vec, self.vec_out = vec, vec_out
        self.part = self.load.shape[2]
        self.counts = [side.shape[1] // self.part for side in sides]
        self.starts = [sum(self.counts[:m]) for m in range(4)]
        self.count = sum(self.counts)
        p, d = lax.axis_index("pipe"), lax.axis_index("dp")
        y, c = d // 2, d % 2
        self.p = p
        self.core = {"dp": y * 2 + (1 - c)}
        self.ahead = [{"dp": lax.rem(y + o, self.ring) * 2 + c} for o in range(1, self.ring)]
        self.other = {"pipe": 1 - p}

    def each(self, c, act):
        for m in range(4):

            @pl.when((c >= self.starts[m]) & (c < self.starts[m] + self.counts[m]))
            def _():
                act(m, pl.multiple_of((c - self.starts[m]) * self.part, self.part))

    def fetch(self, c):
        def act(m, at):
            pltpu.make_async_copy(
                self.sides[m].at[:, pl.ds(at, self.part)],
                self.load.at[lax.rem(c, 3)],
                self.load_sem.at[lax.rem(c, 3)],
            ).start()

        self.each(c, act)

    def fetched(self, c):
        slot = lax.rem(c, 3)
        pltpu.make_async_copy(
            self.sides[0].at[:, pl.ds(0, self.part)], self.load.at[slot], self.load_sem.at[slot]
        ).wait()

    def piece(self, c, slot, use):
        side = self.load.at[lax.rem(c, 3)]
        cols = pl.ds(slot * self.part, self.part)

        @pl.when(c < self.starts[2])
        def _():
            use(dot(side[...], self.g[:, cols], ((0,), (0,))))

        @pl.when(c >= self.starts[2])
        def _():
            use(dot(self.xh[:, cols], side[...], ((0,), (0,))))

    def c_copy(self, c, o):
        return to(
            self.away.at[lax.rem(c, 2), o], self.held.at[c, o],
            self.c_send.at[c, o], self.c_recv.at[c, o], self.core,
        )

    def y_copy(self, c, o):
        return to(
            self.held.at[c, o], self.round.at[c, o - 1],
            self.y_send.at[c, o - 1], self.y_recv.at[c, o - 1], self.ahead[o - 1],
        )

    def x_copy(self, c):
        return to(
            self.held.at[c, 0], self.across.at[c], self.x_send.at[c], self.x_recv.at[c], self.other
        )

    def chunk_sum(self, c):
        total = self.held[c, 0].astype(f32)
        for o in range(1, self.ring):
            total = total + self.round[c, o - 1].astype(f32)
        return total

    def store(self, c, start):
        slot = lax.rem(c, 2)

        def act(m, at):
            out = self.outs[m]
            if m < 2:
                out = out.at[pl.ds(at, self.part), :]
            else:
                out = out.at[:, pl.ds(at, self.part)]
            copy = pltpu.make_async_copy(self.done.at[slot], out, self.out_sem.at[slot])
            copy.start() if start else copy.wait()

        self.each(c, act)

    @property
    def turns(self):
        return self.count + 5

    def begin(self):
        self.fetch(0)
        self.fetch(1)
        self.v_copy(0).start()

    def v_copy(self, stage, o=1):
        last = self.count
        if stage == 0:
            return to(
                self.vec, self.v_held, self.c_send.at[last, 0], self.c_recv.at[last, 0], self.core
            )
        if stage == 1:
            return to(
                self.v_held, self.v_round.at[o - 1],
                self.y_send.at[last, o - 1], self.y_recv.at[last, o - 1], self.ahead[o - 1],
            )
        return to(
            self.vec_out, self.v_across, self.x_send.at[last], self.x_recv.at[last], self.other
        )

    def turn(self, it):
        @pl.when(it < self.count)
        def _():
            c = it
            self.fetched(c)
            for o in range(self.ring):

                @pl.when(c >= 2)
                def _():
                    self.c_copy(c - 2, o).wait_send()

                def use(value):
                    self.away[lax.rem(c, 2), o] = value.astype(bf16)

                self.piece(c, 2 * o + 1, use)
                self.c_copy(c, o).start()

        @pl.when((it >= 1) & (it < self.count + 1))
        def _():
            c = it - 1
            for o in range(self.ring - 1, -1, -1):
                self.c_copy(c, o).wait_recv()

                def use(value):
                    value = value + self.held[c, o].astype(f32)
                    self.held[c, o] = value.astype(bf16)

                self.piece(c, 2 * o, use)
                if o > 0:
                    self.y_copy(c, o).start()

            @pl.when(c + 3 < self.count + 1)
            def _():
                @pl.when(c + 2 < self.count)
                def _():
                    self.fetch(c + 2)

        @pl.when((it >= 3) & (it < self.count + 3))
        def _():
            c = it - 3
            for o in range(1, self.ring):
                self.y_copy(c, o).wait_recv()

            @pl.when(self.p != self.k)
            def _():
                self.held[c, 0] = self.chunk_sum(c).astype(bf16)
                self.x_copy(c).start()

        @pl.when((it >= 5) & (self.p == self.k))
        def _():
            c = it - 5

            @pl.when(c >= 2)
            def _():
                self.store(c - 2, False)

            self.x_copy(c).wait_recv()
            self.done[lax.rem(c, 2)] = self.chunk_sum(c) + self.across[c].astype(f32)
            self.store(c, True)

        @pl.when(it == 3)
        def _():
            self.v_copy(0).wait()
            self.v_held[...] = self.v_held[...] + self.vec[...]
            for o in range(1, self.ring):
                self.v_copy(1, o).start()

        @pl.when(it == 6)
        def _():
            total = self.v_held[...]
            for o in range(1, self.ring):
                self.v_copy(1, o).wait()
                total = total + self.v_round[o - 1]
            self.vec_out[...] = total

            @pl.when(self.p != self.k)
            def _():
                self.v_copy(2).start()

        @pl.when((it == 9) & (self.p == self.k))
        def _():
            self.v_copy(2).wait_recv()
            self.vec_out[...] = self.vec_out[...] + self.v_across[...]

    def drain(self):
        last = self.count
        for c in (last - 2, last - 1):
            for o in range(self.ring):
                self.c_copy(c, o).wait_send()

        @pl.when(self.p == self.k)
        def _():
            for c in (last - 2, last - 1):
                self.store(jnp.int32(c), False)

        @pl.when(self.p != self.k)
        def _():
            self.v_copy(2).wait_send()

        def body(c, _):
            for o in range(1, self.ring):
                self.y_copy(c, o).wait_send()

            @pl.when(self.p != self.k)
            def _():
                self.x_copy(c).wait_send()

            return 0

        lax.fori_loop(0, last, body, 0)

    @staticmethod
    def scratch(ways, part, tokens, count, vec):
        ring = ways // 2
        dma = pltpu.SemaphoreType.DMA
        return [
            pltpu.VMEM((3, tokens, part), bf16),
            pltpu.VMEM((2, ring, part, part), bf16),
            pltpu.VMEM((count, ring, part, part), bf16),
            pltpu.VMEM((count, ring - 1, part, part), bf16),
            pltpu.VMEM((count, part, part), bf16),
            pltpu.VMEM((2, part, part), f32),
            pltpu.VMEM(vec.shape, f32),
            pltpu.VMEM((ring - 1, *vec.shape), f32),
            pltpu.VMEM(vec.shape, f32),
            dma((3,)),
            dma((count + 1, ring)),
            dma((count + 1, ring)),
            dma((count + 1, ring - 1)),
            dma((count + 1, ring - 1)),
            dma((count + 1,)),
            dma((count + 1,)),
            dma((2,)),
        ]


def back_kernel(n, ways, k, partial, inv_std, xh, g, vec, *refs):
    sides, refs = refs[:4], refs[4:]
    if k == 0:
        refs = refs[4:]
        rows_out, rows_away, vec_out, outs, refs = refs[0], refs[1], refs[2], refs[3:7], refs[7:]
        out = None
    else:
        out, vec_out, outs, refs = refs[0], refs[1], refs[2:6], refs[6:]
    count = 8 if k else 4
    right, left, line_sems, refs = refs[0], refs[1], refs[2 : 2 + count], refs[2 + count :]
    if k == 0:
        handed, d_send, d_recv, refs = refs[0], refs[1], refs[2], refs[3:]
    p = lax.axis_index("pipe")
    other = {"pipe": 1 - p}

    def d_copy(s, sub):
        mine = pl.ds(pl.multiple_of(s * sub, sub), sub)
        return to(handed.at[mine, :], rows_away.at[mine, :], d_send.at[s], d_recv.at[s], other)

    def finished(line, s, total):
        mine = pl.ds(pl.multiple_of(s * line.sub, line.sub), line.sub)
        xr = line.at(xh, line.i, s)[...].astype(f32)
        mean = jnp.mean(total, axis=1, keepdims=True)
        proj = jnp.mean(total * xr, axis=1, keepdims=True)
        total = inv_std[mine, :] * (total - mean - xr * proj)
        total = line.at(g, line.i, s)[...].astype(f32) + total
        if k == 1:
            line.at(out, line.i, s)[...] = total.astype(bf16)
        else:
            rows_out[mine, :] = total
            handed[mine, :] = total.astype(bf16)

            @pl.when(p == 1)
            def _():
                d_copy(s, line.sub).start()

    line = LineSum(n, partial, right, left, line_sems, finished, out)
    grads = GradSum(k, ways, xh, g, sides, outs, vec, vec_out, refs)
    greet([line.after, line.before, grads.core, grads.other] + grads.ahead)
    grads.begin()

    def turn_(it, _):
        line.turn(it)
        grads.turn(it)
        return 0

    lax.fori_loop(0, grads.turns, turn_, 0)
    line.drain()
    grads.drain()
    if k == 0:
        for s in range(SUBS):

            @pl.when(p == 1)
            def _():
                d_copy(s, line.sub).wait_send()

            @pl.when(p == 0)
            def _():
                d_copy(s, line.sub).wait_recv()


def back_sums(k, partial, inv_std, xh, g, vec, sides, n, ways, outs=None):
    tokens, width = partial.shape
    part = width // ways
    rows = tokens // n
    vmem = pl.BlockSpec(memory_space=pltpu.VMEM)
    hbm = pl.BlockSpec(memory_space=pl.ANY)
    shape = jax.ShapeDtypeStruct
    count = sum(side.shape[1] for side in sides) // part
    grad_shapes = [
        shape((side.shape[1], part) if m < 2 else (part, side.shape[1]), f32)
        for m, side in enumerate(sides)
    ]
    if k == 0:
        lead = [shape((rows, width), f32), shape((rows, width), bf16)]
        lead_specs = [vmem, vmem]
        extra = [pltpu.VMEM((rows, width), bf16)] + [pltpu.SemaphoreType.DMA((SUBS,))] * 2
    else:
        lead, lead_specs, extra = [shape((tokens, width), bf16)], [vmem], []
    lead, lead_specs = lead + [shape(vec.shape, f32)], lead_specs + [vmem]
    return pl.pallas_call(
        functools.partial(back_kernel, n, ways, k),
        in_specs=[vmem] * 5 + [hbm] * (4 if k else 8),
        out_specs=lead_specs + [hbm] * 4,
        out_shape=lead + grad_shapes,
        input_output_aliases={} if k else {9 + m: len(lead) + m for m in range(4)},
        scratch_shapes=LineSum.scratch(n, tokens, width, k == 1)
        + extra
        + GradSum.scratch(ways, part, tokens, count, vec),
        compiler_params=pltpu.CompilerParams(
            collective_id=3 + k, has_side_effects=True, vmem_limit_bytes=60 << 20
        ),
        cost_estimate=pl.CostEstimate(flops=0, bytes_accessed=500 << 20, transcendentals=0),
        name="back_sums",
    )(partial, inv_std, xh, g, vec, *sides, *(outs or ()))


def normalize(values):
    average = jnp.mean(values, axis=-1, keepdims=True)
    centred = values - average
    spread = jnp.mean(centred * centred, axis=-1, keepdims=True)
    inv_std = lax.rsqrt(spread + norm_epsilon)
    return (centred * inv_std, inv_std)


def rotary_tables(seg):
    seqs, length = seg.shape
    places = jnp.arange(length, dtype=jnp.int32)[None, :]
    change = jnp.concatenate(
        [jnp.ones_like(seg[:, :1]) > 0, seg[:, 1:] != seg[:, :-1]],
        axis=1,
    )
    starts = lax.cummax(jnp.where(change, places, 0), axis=1)
    offsets = (places - starts).astype(f32).reshape(seqs * length, 1)
    frequency = jnp.exp(-math.log(10000.0) * 2.0 * jnp.arange(32, dtype=f32) / 64)
    angles = offsets * frequency
    cos, sin = jnp.cos(angles), jnp.sin(angles)
    one, zero = jnp.ones((seqs * length, ROT - 64), f32), jnp.zeros((seqs * length, 32), f32)
    return (
        jnp.concatenate([cos, cos, one], axis=1),
        jnp.concatenate([-sin, zero, zero, zero], axis=1),
        jnp.concatenate([zero, sin, zero, zero], axis=1),
    )


def per_device(
    boundary,
    segments,
    ln1_gain,
    ln1_bias,
    ln2_gain,
    ln2_bias,
    qkv_weight,
    qkv_bias,
    dense_weight,
    dense_bias,
    fc1_weight,
    fc1_bias,
    fc2_weight,
    fc2_bias,
):
    pipe, d, t = lax.axis_index("pipe"), lax.axis_index("dp"), lax.axis_index("tensor")
    ways, ring = lax.axis_size("dp"), lax.axis_size("dp") // 2
    nt = lax.axis_size("tensor")
    first = pipe == 0
    seqs, length, width = boundary.shape[1] // 2, boundary.shape[2], boundary.shape[3]
    tokens, rows, part = seqs * length, length // nt, width // ways
    heads, size = qkv_weight.shape[2], qkv_weight.shape[3] // 3
    y, c = d // 2, d % 2

    def pipe_swap(v):
        return lax.ppermute(v, "pipe", [(0, 1), (1, 0)])

    def pipe_send(v, source):
        return lax.ppermute(v, "pipe", [(source, 1 - source)])

    def own_order(v):
        parts = []
        for o in range(ring):
            for b in range(2):
                place = ((y + o) % ring) * 2 + (c ^ b)
                parts.append(lax.dynamic_slice_in_dim(v, place * part, part, v.ndim - 1))
        return jnp.concatenate(parts, axis=-1)

    def true_order(v):
        parts = []
        for j in range(ways):
            place = ((j // 2 - y) % ring) * 2 + (c ^ (j % 2))
            parts.append(lax.dynamic_slice_in_dim(v, place * part, part, v.ndim - 1))
        return jnp.concatenate(parts, axis=-1)

    def in_true_order(parts):
        stacked = jnp.stack(parts)
        places = [((j // 2 - y) % ring) * 2 + (c ^ (j % 2)) for j in range(ways)]
        return [lax.dynamic_index_in_dim(stacked, place, 0, False) for place in places]

    def together(*values):
        return list(lax.optimization_barrier(values))

    kept = lax.dynamic_slice_in_dim(boundary[0], pipe * seqs, seqs, 0)
    given = lax.dynamic_slice(
        boundary[0], ((1 - pipe) * seqs, t * rows, 0), (seqs, rows, width)
    )
    kept, given = own_order(kept), own_order(given)
    seg = lax.dynamic_slice_in_dim(segments, pipe * seqs, seqs, 0)
    tables = rotary_tables(seg)

    shards = (
        qkv_weight[0].reshape(part, heads * 3 * size),
        fc1_weight[0],
        fc2_weight[0],
        dense_weight[0],
    )
    axes = (0, 0, 1, 1)
    small = [
        v[0].reshape(-1)
        for v in (ln1_gain, ln1_bias, ln2_gain, ln2_bias, dense_bias, fc2_bias, fc1_bias, qkv_bias)
    ]
    flat = jnp.concatenate(small)
    flat = jnp.pad(flat, (0, -flat.shape[0] % 2048)).reshape(-1, 128)
    flat_across = pipe_swap(flat)
    flat = jnp.concatenate(
        [jnp.where(first, flat, flat_across), jnp.where(first, flat_across, flat)], axis=0
    )
    other, flat_all, weights_0, weights_1 = gather_section(given, flat, shards, axes, ways, nt)
    source = jnp.where(first, kept, other).reshape(tokens, width)
    cotangent = jnp.where(first, other, kept).reshape(tokens, width)
    flat_all = flat_all.reshape(ways, 2, -1).astype(f32)
    flat_parts = [flat_all[r] for r in range(ways)]

    def vectors(k):
        at, found = 0, []
        for index, v in enumerate(small):
            blocks = [v_part[k : k + 1, at : at + v.shape[0]] for v_part in flat_parts]
            at += v.shape[0]
            if index >= 6:
                blocks = in_true_order(blocks)
            if index == 7:
                blocks = [v_part.reshape(heads, -1) for v_part in blocks]
            found.append(jnp.concatenate(blocks, axis=-1).reshape(1, -1))
        return found

    def scatter_rows(v):
        return lax.psum_scatter(
            v.reshape(seqs, length, width), "tensor", scatter_dimension=1, tiled=True
        )

    def own_rows(v):
        return lax.dynamic_slice_in_dim(v.reshape(seqs, length, width), t * rows, rows, 1)

    def own_rows_of(v):
        return lax.dynamic_slice_in_dim(v, t * rows, rows, 0)

    def enter(k, x):
        g1, b1, g2, b2 = vectors(k)[:4]
        xhat, inv_std = normalize(x.astype(f32))
        n1 = (xhat * g1 + b1).astype(bf16)
        n2 = (xhat * g2 + b2).astype(bf16)
        return n1, n2, xhat.astype(bf16), own_rows_of(inv_std)

    tn, nt_ = ((0,), (0,)), ((1,), (1,))

    def sums_of(qkv_sum, d_hidden, g):
        g_sum = true_order(jnp.sum(g.astype(f32), axis=0, keepdims=True))[0]
        found = jnp.concatenate([qkv_sum, jnp.sum(d_hidden.astype(f32), axis=0), g_sum])
        return jnp.pad(found, (0, -found.shape[0] % 1024)).reshape(-1, 128)

    wq0, w10, w20, wd0 = weights_0
    n1, n2, xh0, inv0 = enter(0, source)
    ar0, qr0, kr0, vr0 = attend(dot(n1, wq0), vectors(0)[7], tables, seg, heads, length)
    act0, slope0 = gelu_matmul(n2, w10, vectors(0)[6])
    branch = (dot(ar0, wd0) + dot(act0, w20)).astype(bf16)
    base = (own_rows(source).astype(f32) + (vectors(0)[4] + vectors(0)[5])).reshape(-1, width)
    x1, weights_1 = sum_spread(
        branch, base, nt, weights_1, [shard.shape for shard in shards], axes, ways
    )
    wq1, w11, w21, wd1 = weights_1

    n1, n2, xh1, inv1 = enter(1, x1)
    g1, _, g2, _ = vectors(1)[:4]
    ar1, qr1, kr1, vr1 = attend(dot(n1, wq1), vectors(1)[7], tables, seg, heads, length)
    d_ar = dot(cotangent, wd1, nt_).astype(bf16)
    d_qkv1, qkv_sum1 = attend_back(qr1, kr1, vr1, d_ar, tables, seg, heads, length)
    act1, slope1 = gelu_matmul(n2, w11, vectors(1)[6])
    d_hidden1 = (slope1.astype(f32) * dot(cotangent, w21, nt_)).astype(bf16)
    u = (dot(d_qkv1, wq1, nt_) * g1 + dot(d_hidden1, w11, nt_) * g2).astype(bf16)
    g0, sums_1, *grads = back_sums(
        1, u, inv1, xh1, cotangent, sums_of(qkv_sum1, d_hidden1, cotangent),
        (act1, ar1, d_hidden1, d_qkv1), nt, ways,
    )

    act1, ar1, g0 = together(act1, ar1, g0)
    branch = (dot(ar1, wd1) + dot(act1, w21)).astype(bf16)
    summed = scatter_rows(branch).astype(f32)
    g1, _, g2, _ = vectors(0)[:4]
    d_ar = dot(g0, wd0, nt_).astype(bf16)
    d_hidden0 = (slope0.astype(f32) * dot(g0, w20, nt_)).astype(bf16)
    d_qkv0, qkv_sum0 = attend_back(qr0, kr0, vr0, d_ar, tables, seg, heads, length)
    u = (dot(d_qkv0, wq0, nt_) * g1 + dot(d_hidden0, w10, nt_) * g2).astype(bf16)
    y_rows = own_rows(x1).astype(f32) + (summed + (vectors(1)[4] + vectors(1)[5]))
    u, y_rows = together(u, y_rows)
    dx_rows, dx_away, sums_0, *grads = back_sums(
        0, u, inv0, xh0, g0, sums_of(qkv_sum0, d_hidden0, g0),
        (act0, ar0, d_hidden0, d_qkv0), nt, ways, grads,
    )
    dx_rows = dx_rows.reshape(seqs, rows, width)
    dx_away = dx_away.reshape(seqs, rows, width).astype(f32)

    y_away = pipe_send(y_rows.astype(bf16), 0).astype(f32)
    boundary_out = true_order(
        jnp.where(
            first,
            jnp.concatenate([dx_rows, dx_away], axis=0),
            jnp.concatenate([y_away, y_rows], axis=0),
        )
    )[None]

    fc2_grad, dense_grad, fc1_core, qkv_core = grads
    sums = jnp.where(first, sums_0, sums_1).reshape(-1)
    cut = heads * 3 * size
    end = cut + shards[1].shape[1]
    qkv_sum, fc1_sum, g_sum = sums[:cut], sums[cut:end], sums[end : end + width]

    def norm_grads(weight, core, sum_):
        w = weight.astype(f32)
        return jnp.sum(w * core, axis=1), jnp.sum(w * sum_[None], axis=1)

    norms = norm_grads(shards[0], qkv_core, qkv_sum) + norm_grads(shards[1], fc1_core, fc1_sum)
    norms = jnp.stack(norms)

    def for_place(step):
        place = lax.rem(t + step, nt) * (part // nt)
        return lax.dynamic_slice_in_dim(norms, place, part // nt, 1)

    norms = for_place(0) + sum(
        lax.ppermute(for_place(step), "tensor", [(i, (i + step) % nt) for i in range(nt)])
        for step in range(1, nt)
    )

    def finish(core, gain, bias, sum_):
        gain, bias = gain[0].astype(f32)[:, None], bias[0].astype(f32)[:, None]
        return gain * core + bias * sum_[None]

    qkv_grad = finish(qkv_core, ln1_gain, ln1_bias, qkv_sum).reshape(part, heads, 3 * size)
    fc1_grad = finish(fc1_core, ln2_gain, ln2_bias, fc1_sum)

    def own_part(v, axis):
        step = v.shape[axis] // ways
        return lax.dynamic_slice_in_dim(v, d * step, step, axis)

    bias_grad = own_part(g_sum, 0)[None]
    return (
        boundary_out,
        norms[0][None],
        norms[1][None],
        norms[2][None],
        norms[3][None],
        qkv_grad[None],
        own_part(qkv_sum.reshape(heads, 3 * size), 1)[None],
        dense_grad[None],
        bias_grad,
        fc1_grad[None],
        own_part(fc1_sum, 0)[None],
        fc2_grad[None],
        bias_grad,
    )


def solution(mesh):
    in_specs = (
        P("pipe", "dp", None, None),
        P("dp", None),
        P("pipe", "dp"),
        P("pipe", "dp"),
        P("pipe", "dp"),
        P("pipe", "dp"),
        P("pipe", "dp", "tensor", None),
        P("pipe", "tensor", "dp"),
        P("pipe", "tensor", "dp"),
        P("pipe", "dp"),
        P("pipe", "dp", "tensor"),
        P("pipe", ("tensor", "dp")),
        P("pipe", "tensor", "dp"),
        P("pipe", "dp"),
    )
    out_specs = (
        P("pipe", "dp", "tensor", None),
        P("pipe", ("dp", "tensor")),
        P("pipe", ("dp", "tensor")),
        P("pipe", ("dp", "tensor")),
        P("pipe", ("dp", "tensor")),
        P("pipe", "dp", "tensor", None),
        P("pipe", "tensor", "dp"),
        P("pipe", "tensor", "dp"),
        P("pipe", "dp"),
        P("pipe", "dp", "tensor"),
        P("pipe", ("tensor", "dp")),
        P("pipe", "tensor", "dp"),
        P("pipe", "dp"),
    )
    return jax.shard_map(
        per_device, mesh=mesh, in_specs=in_specs, out_specs=out_specs, check_vma=False
    )
```

```python
import functools
import math

import jax
import jax.numpy as jnp
from jax import lax
from jax.experimental import pallas as pl
from jax.experimental.pallas import tpu as pltpu
from jax.sharding import PartitionSpec as P

norm_epsilon = 1e-05
mask_fill = -1e30
BAND = 256
ROT = 128
f32, bf16 = jnp.float32, jnp.bfloat16


def dot(a, b, contract=((1,), (0,))):
    return lax.dot_general(a, b, (contract, ((), ())), preferred_element_type=f32)


def allowed(seg_col, seg_row, block):
    low = max(block - 1, 0) * BAND
    size = (block + 1) * BAND - low
    own = lax.broadcasted_iota(jnp.int32, (BAND, size), 0) + (block * BAND - low)
    key = lax.broadcasted_iota(jnp.int32, (BAND, size), 1)
    rows = pl.ds(block * BAND, BAND)
    return (own >= key) & (seg_col[rows, :] == seg_row[:, pl.ds(low, size)])


def turn(values, cos, forward, backward):
    head = values[:, :ROT]
    head = (
        head * cos
        + pltpu.roll(head, ROT - 32, 1) * forward
        + pltpu.roll(head, 32, 1) * backward
    )
    return jnp.concatenate([head, values[:, ROT:]], axis=1)


def attend_kernel(scale, qkv, bias, cos, sin_a, sin_b, seg_col, seg_row, out, qr, kr, vr):
    size = out.shape[1]
    for block in range(out.shape[0] // BAND):
        rows = pl.ds(block * BAND, BAND)
        c, a, b = cos[rows, :], sin_a[rows, :], sin_b[rows, :]
        q = turn(qkv[rows, :size] + bias[:, :size], c, a, b).astype(bf16)
        k = turn(qkv[rows, size : 2 * size] + bias[:, size : 2 * size], c, a, b).astype(bf16)
        qr[rows, :] = q
        kr[rows, :] = k
        vr[rows, :] = (qkv[rows, 2 * size :] + bias[:, 2 * size :]).astype(bf16)
        low = max(block - 1, 0) * BAND
        keys = pl.ds(low, (block + 1) * BAND - low)
        scores = dot(q, kr[keys, :], ((1,), (1,))) * scale
        scores = jnp.where(allowed(seg_col, seg_row, block), scores, mask_fill)
        weights = jnp.exp(scores - jnp.max(scores, axis=1, keepdims=True))
        weights = weights * (1.0 / jnp.sum(weights, axis=1, keepdims=True))
        out[rows, :] = dot(weights.astype(bf16), vr[keys, :]).astype(bf16)


def attend(qkv, bias, tables, seg, heads, length):
    size = qkv.shape[1] // heads // 3
    seqs = qkv.shape[0] // length
    block = pl.BlockSpec((length, size), lambda b, h: (b, h))
    table = pl.BlockSpec((length, ROT), lambda b, h: (b, 0))
    return pl.pallas_call(
        functools.partial(attend_kernel, 1.0 / math.sqrt(size)),
        grid=(seqs, heads),
        in_specs=[
            pl.BlockSpec((length, 3 * size), lambda b, h: (b, h)),
            pl.BlockSpec((1, 3 * size), lambda b, h: (0, h)),
            table,
            table,
            table,
            pl.BlockSpec((length, 1), lambda b, h: (b, 0)),
            pl.BlockSpec((1, length), lambda b, h: (0, b)),
        ],
        out_specs=[block] * 4,
        out_shape=[jax.ShapeDtypeStruct((qkv.shape[0], heads * size), bf16)] * 4,
        compiler_params=pltpu.CompilerParams(vmem_limit_bytes=48 << 20),
        cost_estimate=pl.CostEstimate(
            flops=2 * 2 * qkv.shape[0] * 2 * BAND * heads * size,
            bytes_accessed=qkv.size * 4 + qkv.shape[0] * heads * size * 8,
            transcendentals=qkv.shape[0] * heads * 2 * BAND,
        ),
        name="attend",
    )(qkv, bias, *tables, seg.reshape(-1, 1), seg.reshape(1, -1))


def attend_back_kernel(
    scale, qr, kr, vr, grad, cos, sin_a, sin_b, seg_col, seg_row, out, out_sum, dk_acc, dv_acc
):
    size = grad.shape[1]
    blocks = grad.shape[0] // BAND
    sums = [jnp.zeros((1, size), f32)] * 3

    def emit(place, part, values):
        rows = pl.ds(place * BAND, BAND)
        if part < 2:
            values = turn(values, cos[rows, :], -sin_a[rows, :], -sin_b[rows, :])
        values = values.astype(bf16)
        out[rows, part * size : (part + 1) * size] = values
        sums[part] = sums[part] + jnp.sum(values.astype(f32), axis=0, keepdims=True)

    for block in range(blocks):
        rows = pl.ds(block * BAND, BAND)
        low = max(block - 1, 0) * BAND
        keys = pl.ds(low, (block + 1) * BAND - low)
        q, k, v, g = qr[rows, :], kr[keys, :], vr[keys, :], grad[rows, :]
        scores = dot(q, k, ((1,), (1,))) * scale
        scores = jnp.where(allowed(seg_col, seg_row, block), scores, mask_fill)
        weights = jnp.exp(scores - jnp.max(scores, axis=1, keepdims=True))
        weights = weights * (1.0 / jnp.sum(weights, axis=1, keepdims=True))
        grad_weights = dot(g, v, ((1,), (1,)))
        row_dot = jnp.sum(weights * grad_weights, axis=1, keepdims=True)
        grad_scores = (weights * (grad_weights - row_dot)).astype(bf16)
        emit(block, 0, dot(grad_scores, k) * scale)
        dk = dot(grad_scores, q, ((0,), (0,))) * scale
        dv = dot(weights.astype(bf16), g, ((0,), (0,)))
        if block > 0:
            emit(block - 1, 1, dk_acc[...] + dk[:BAND])
            emit(block - 1, 2, dv_acc[...] + dv[:BAND])
            dk, dv = dk[BAND:], dv[BAND:]
        if block == blocks - 1:
            emit(block, 1, dk)
            emit(block, 2, dv)
        else:
            dk_acc[...] = dk
            dv_acc[...] = dv
    out_sum[0] = jnp.concatenate(sums, axis=1)


def attend_back(qr, kr, vr, grad, tables, seg, heads, length):
    size = qr.shape[1] // heads
    tokens = qr.shape[0]
    seqs = tokens // length
    block = pl.BlockSpec((length, size), lambda b, h: (b, h))
    table = pl.BlockSpec((length, ROT), lambda b, h: (b, 0))
    out, sums = pl.pallas_call(
        functools.partial(attend_back_kernel, 1.0 / math.sqrt(size)),
        grid=(seqs, heads),
        in_specs=[block] * 4
        + [table] * 3
        + [
            pl.BlockSpec((length, 1), lambda b, h: (b, 0)),
            pl.BlockSpec((1, length), lambda b, h: (0, b)),
        ],
        out_specs=[
            pl.BlockSpec((length, 3 * size), lambda b, h: (b, h)),
            pl.BlockSpec((1, 1, 3 * size), lambda b, h: (b, 0, h)),
        ],
        out_shape=[
            jax.ShapeDtypeStruct((tokens, heads * 3 * size), bf16),
            jax.ShapeDtypeStruct((seqs, 1, heads * 3 * size), f32),
        ],
        scratch_shapes=[pltpu.VMEM((BAND, size), f32)] * 2,
        compiler_params=pltpu.CompilerParams(vmem_limit_bytes=48 << 20),
        cost_estimate=pl.CostEstimate(
            flops=2 * 5 * tokens * 2 * BAND * heads * size,
            bytes_accessed=tokens * heads * size * 14,
            transcendentals=tokens * heads * 2 * BAND,
        ),
        name="attend_back",
    )(qr, kr, vr, grad, *tables, seg.reshape(-1, 1), seg.reshape(1, -1))
    return out, jnp.sum(sums, axis=(0, 1))


def gelu_parts(h):
    t = 1.0 / (1.0 + (0.3275911 * math.sqrt(0.5)) * jnp.abs(h))
    poly = 1.061405429 * t - 1.453152027
    poly = poly * t + 1.421413741
    poly = poly * t - 0.284496736
    poly = poly * t + 0.254829592
    bell = jnp.exp(-0.5 * h * h)
    tail = 0.5 * poly * t * bell
    cdf = jnp.where(h >= 0.0, 1.0 - tail, tail)
    slope = cdf + h * bell * (1.0 / math.sqrt(2.0 * math.pi))
    return (h * cdf).astype(bf16), slope.astype(bf16)


def gelu_kernel(x, w, bias, act, slope):
    for row in range(0, x.shape[0], BAND):
        rows = pl.ds(row, BAND)
        act[rows, :], slope[rows, :] = gelu_parts(dot(x[rows, :], w[...]) + bias[...])


def gelu_matmul(x, w, bias):
    tokens, depth = x.shape
    width = w.shape[1]
    cols = min(512, width)
    block = pl.BlockSpec((tokens, cols), lambda j: (0, j))
    return pl.pallas_call(
        gelu_kernel,
        grid=(width // cols,),
        in_specs=[
            pl.BlockSpec((tokens, depth), lambda j: (0, 0)),
            pl.BlockSpec((depth, cols), lambda j: (0, j)),
            pl.BlockSpec((1, cols), lambda j: (0, j)),
        ],
        out_specs=[block, block],
        out_shape=[jax.ShapeDtypeStruct((tokens, width), bf16)] * 2,
        compiler_params=pltpu.CompilerParams(vmem_limit_bytes=48 << 20),
        cost_estimate=pl.CostEstimate(
            flops=2 * tokens * depth * width,
            bytes_accessed=2 * (tokens * depth + depth * width + 2 * tokens * width),
            transcendentals=2 * tokens * width,
        ),
        name="gelu_matmul",
    )(x, w, bias)


def to(source, target, send, recv, place):
    return pltpu.make_async_remote_copy(
        src_ref=source,
        dst_ref=target,
        send_sem=send,
        recv_sem=recv,
        device_id=place,
        device_id_type=pl.DeviceIdType.MESH,
    )


def greet(places):
    barrier = pltpu.get_barrier_semaphore()
    for place in places:
        pl.semaphore_signal(
            barrier, inc=1, device_id=place, device_id_type=pl.DeviceIdType.MESH
        )
    pl.semaphore_wait(barrier, len(places))


def chunks_of(shapes, axes, part):
    return [
        (m, row, col)
        for m, (shape, axis) in enumerate(zip(shapes, axes))
        for row in range(0, shape[0], part)
        for col in range(0, shape[1], part)
    ]


def chunk_at(ref, axis, shape, chunk, slot, part):
    _, row, col = chunk
    row, col = (row + slot * shape[0], col) if axis == 0 else (row, col + slot * shape[1])
    return ref.at[pl.ds(row, part), pl.ds(col, part)]


class Spread:
    def __init__(self, full, shapes, axes, ways, sems):
        self.full, self.shapes, self.axes = full, shapes, axes
        self.ring = ways // 2
        self.y_send, self.y_recv, self.c_send, self.c_recv = sems
        self.part = shapes[3][1]
        self.chunks = chunks_of(shapes, axes, self.part)
        d = lax.axis_index("dp")
        y, c = d // 2, d % 2
        self.core = {"dp": y * 2 + (1 - c)}
        self.ahead = [{"dp": lax.rem(y + o, self.ring) * 2 + c} for o in range(1, self.ring)]

    def at(self, n, slot):
        m = self.chunks[n][0]
        return chunk_at(
            self.full[m], self.axes[m], self.shapes[m], self.chunks[n], slot, self.part
        )

    def y_copy(self, n, step, source):
        target = self.at(n, 2 * ((self.ring - step) % self.ring))
        return to(
            source, target, self.y_send.at[n, step - 1], self.y_recv.at[n, step - 1],
            self.ahead[step - 1],
        )

    def c_copy(self, n, o, source):
        target = self.at(n, 2 * o + 1)
        return to(source, target, self.c_send.at[n, o], self.c_recv.at[n, o], self.core)

    def begin(self, n, source):
        for step in range(1, self.ring):
            self.y_copy(n, step, source).start()
        self.c_copy(n, 0, source).start()

    def forward(self, n):
        for step in range(1, self.ring):
            o = (self.ring - step) % self.ring
            self.y_copy(n, step, self.at(n, 0)).wait_recv()
            self.c_copy(n, o, self.at(n, 2 * o)).start()

    def arrived(self, m):
        for n in range(len(self.chunks)):
            if self.chunks[n][0] == m:
                for o in range(self.ring):
                    self.c_copy(n, o, self.at(n, 2 * o)).wait_recv()

    def finish(self, waited=()):
        for n in range(len(self.chunks)):
            for step in range(1, self.ring):
                self.y_copy(n, step, self.at(n, 0)).wait_send()
            for o in range(self.ring):
                self.c_copy(n, o, self.at(n, 2 * o)).wait_send()
        for m in range(4):
            if m not in waited:
                self.arrived(m)

    @staticmethod
    def semaphores(pieces, ways):
        dma = pltpu.SemaphoreType.DMA
        return [dma((pieces, ways // 2 - 1))] * 2 + [dma((pieces, ways // 2))] * 2


def small_rows(sm, m, count, slots, part, scattered=False):
    def block(slot):
        return sm[pl.ds(slot * 32, 16), :].astype(f32)

    if not scattered:
        return jnp.concatenate([block(slot)[m : m + 1] for slot in range(slots)], axis=1)
    total = block(0)
    for slot in range(1, slots):
        total = total + block(slot)
    return jnp.concatenate([total[m + j : m + j + 1] for j in range(count)], axis=1)


def enter_kernel(
    ways, nt, axes, heads,
    boundary, small, s0, s1, s2, s3, seg_col, seg_row, frequency,
    source, cotangent, small_all, f0, f1, f2, f3, o0, o1, o2, o3,
    cos_out, sin_a_out, sin_b_out, xh_out, inv_out,
    ar_out, qr_out, kr_out, vr_out, act_out, slope_out,
    x_send, x_recv, y_send, y_recv, c_send, c_recv, z_send, z_recv,
    b0, b1, b2, b3, local, keep_sem, out_sem,
    xv, sm, n1, n2, wq, w1, packed, cos, sin_a, sin_b, xh, inv, ar, qr, kr, vr, act, slope,
):
    shards, bounce = (s0, s1, s2, s3), (b0, b1, b2, b3)
    shapes = [s.shape for s in shards]
    full, later = (f0, f1, f2, f3), (o0, o1, o2, o3)
    p, d, t = lax.axis_index("pipe"), lax.axis_index("dp"), lax.axis_index("tensor")
    sems = (y_send, y_recv, c_send, c_recv)
    now = Spread(full, shapes, axes, ways, sems)
    then = Spread(later, shapes, axes, ways, sems)
    ring, chunks, part = now.ring, now.chunks, now.part
    length = boundary.shape[1]
    rows = length // nt
    across = {"pipe": 1 - p}
    others = [{"tensor": lax.rem(t + step, nt)} for step in range(1, nt)]
    places = [
        (lax.rem(d // 2 + o, ring) * 2 + lax.rem(d + b, 2)) * part
        for o in range(ring)
        for b in range(2)
    ]
    mine = pl.ds(pl.multiple_of(t * rows, rows), rows)

    loads = [pltpu.make_async_copy(shards[m], bounce[m], local.at[m]) for m in range(4)]
    for load in loads:
        load.start()
    keeps = [
        pltpu.make_async_copy(
            boundary.at[p, :, pl.ds(pl.multiple_of(places[r], part), part)],
            xv.at[:, pl.ds(r * part, part)],
            keep_sem.at[r],
        )
        for r in range(ways)
    ]
    greet([across, now.core] + now.ahead + others)

    def in_shard(n):
        m, row, col = chunks[n]
        return shards[m].at[pl.ds(row, part), pl.ds(col, part)]

    def small_at(slot, count=32, row=0):
        return small_all.at[pl.ds(slot * 32 + row, count), :]

    def x_given(r, target):
        return to(
            boundary.at[1 - p, mine, pl.ds(pl.multiple_of(places[r], part), part)],
            target.at[mine, pl.ds(r * part, part)],
            x_send.at[r], x_recv.at[r], across,
        )

    def x_small():
        here = small_all.at[pl.ds(pl.multiple_of(p * 16, 16), 16), :]
        return to(small, here, x_send.at[ways], x_recv.at[ways], across)

    def x_copy(n, target):
        at = ways + 1 + n
        return to(in_shard(n), target, x_send.at[at], x_recv.at[at], across)

    def small_y(step):
        target = small_at(2 * ((ring - step) % ring))
        return to(
            small_at(0), target, y_send.at[last, step - 1], y_recv.at[last, step - 1],
            now.ahead[step - 1],
        )

    def small_c(o):
        target = small_at(2 * o + 1)
        return to(small_at(2 * o), target, c_send.at[last, o], c_recv.at[last, o], now.core)

    def stores(matrices):
        return [
            pltpu.make_async_copy(
                bounce[m],
                matrices[m].at[pl.ds(0, shapes[m][0]), :]
                if axes[m] == 0
                else matrices[m].at[:, pl.ds(0, shapes[m][1])],
                local.at[m],
            )
            for m in range(4)
        ]

    last = len(chunks)
    small_own = pltpu.make_async_copy(
        small, small_all.at[pl.ds(pl.multiple_of(p * 16, 16), 16), :], local.at[4]
    )
    small_own.start()
    x_small().start()

    @pl.when(p == 0)
    def _():
        for r in range(ways):
            x_given(r, source).start()

    @pl.when(p == 1)
    def _():
        for r in range(ways):
            x_given(r, cotangent).start()

    for keep in keeps:
        keep.start()
    for load in loads:
        load.wait()

    @pl.when(p == 0)
    def _():
        for store in stores(full):
            store.start()
        for n in range(last):
            x_copy(n, now.at(n, 0)).start()
            now.begin(n, in_shard(n))

    @pl.when(p == 1)
    def _():
        for store in stores(later):
            store.start()
        for n in range(last):
            x_copy(n, then.at(n, 0)).start()

    for keep in keeps:
        keep.wait()

    def kept_store(target):
        return pltpu.make_async_copy(xv, target, keep_sem.at[0])

    @pl.when(p == 0)
    def _():
        kept_store(source).start()

    @pl.when(p == 1)
    def _():
        kept_store(cotangent).start()

    small_own.wait()
    x_small().wait_recv()
    for step in range(1, ring):
        small_y(step).start()
    small_c(0).start()

    def table(block, _):
        at = pl.ds(pl.multiple_of(block * BAND, BAND), BAND)
        same = seg_col[at, :] == seg_row[...]
        key = lax.broadcasted_iota(jnp.int32, (BAND, length), 1)
        start = jnp.min(jnp.where(same, key, length), axis=1, keepdims=True)
        place = lax.broadcasted_iota(jnp.int32, (BAND, 1), 0) + block * BAND
        angle = (place - start).astype(f32) * frequency[...]
        lane = lax.broadcasted_iota(jnp.int32, (BAND, ROT), 1)
        sine = jnp.sin(angle)
        cos[at, :] = jnp.cos(angle)
        sin_a[at, :] = jnp.where(lane < 32, -sine, 0.0)
        sin_b[at, :] = jnp.where((lane >= 32) & (lane < 64), sine, 0.0)
        return 0

    lax.fori_loop(0, length // BAND, table, 0)
    outs = []

    def give(at, ref, target):
        outs.append(pltpu.make_async_copy(ref, target, out_sem.at[at]))
        outs[-1].start()

    give(0, cos, cos_out)
    give(1, sin_a, sin_a_out)
    give(2, sin_b, sin_b_out)

    kept_store(source).wait()
    for r in range(ways):
        x_given(r, source).wait_recv()

    def z_copy(step, ref):
        return to(
            ref.at[mine, :], ref.at[mine, :], z_send.at[step - 1], z_recv.at[step - 1],
            others[step - 1],
        )

    @pl.when(p == 0)
    def _():
        for step in range(1, nt):
            z_copy(step, cotangent).start()

    @pl.when(p == 1)
    def _():
        for step in range(1, nt):
            z_copy(step, source).start()

    for step in range(1, ring):
        small_y(step).wait_recv()
        small_c((ring - step) % ring).start()

    def norm():
        for step in range(1, nt):
            z_copy(step, source).wait_recv()
        for o in range(ring):
            small_c(o).wait()
        vectors = pltpu.make_async_copy(small_all, sm, keep_sem.at[1])
        vectors.start()

        @pl.when(p == 1)
        def _():
            whole = pltpu.make_async_copy(source, xv, keep_sem.at[0])
            whole.start()
            whole.wait()

        vectors.wait()
        g1, b1, g2, b2 = (small_rows(sm, m, 1, ways, part) for m in range(4))

        def block(step, _):
            at = pl.ds(pl.multiple_of(step * 128, 128), 128)
            x = xv[at, :].astype(f32)
            x = x - jnp.mean(x, axis=1, keepdims=True)
            inv_std = lax.rsqrt(jnp.mean(x * x, axis=1, keepdims=True) + norm_epsilon)
            x = x * inv_std
            inv[at, :] = inv_std
            xh[at, :] = x.astype(bf16)
            n1[at, :] = (x * g1 + b1).astype(bf16)
            n2[at, :] = (x * g2 + b2).astype(bf16)
            return 0

        lax.fori_loop(0, length // 128, block, 0)
        give(3, xh, xh_out)
        give(4, inv, inv_out)
        now.arrived(0)
        stores(full)[0].wait()
        pltpu.make_async_copy(full[0], wq, keep_sem.at[2]).start()

    size = wq.shape[1] // heads // 3

    def attention(h):
        if h == 0:
            pltpu.make_async_copy(full[0], wq, keep_sem.at[2]).wait()
            now.arrived(1)
            stores(full)[1].wait()
            pltpu.make_async_copy(full[1], w1, keep_sem.at[3]).start()
        cols = pl.ds(h * 3 * size, 3 * size)

        def block(step, _):
            at = pl.ds(pl.multiple_of(step * BAND, BAND), BAND)
            packed[at, :] = dot(n1[at, :], wq[:, cols])
            return 0

        lax.fori_loop(0, length // BAND, block, 0)
        bias = small_rows(sm, 6, heads * 3 * size // part, ways, part, True)
        bias = bias[:, h * 3 * size : (h + 1) * 3 * size]
        at = pl.ds(h * size, size)
        attend_kernel(
            1.0 / math.sqrt(size), packed, bias, cos, sin_a, sin_b, seg_col, seg_row,
            ar.at[:, at], qr.at[:, at], kr.at[:, at], vr.at[:, at],
        )
        if h == heads - 1:
            for n, (ref, target) in enumerate(
                ((ar, ar_out), (qr, qr_out), (kr, kr_out), (vr, vr_out))
            ):
                give(5 + n, ref, target)

    hidden = w1.shape[1] // part
    bias_row = 6 + heads * 3 * size // part

    def feed(j):
        if j == 0:
            pltpu.make_async_copy(full[1], w1, keep_sem.at[3]).wait()
        cols = pl.ds(j * part, part)
        bias = small_rows(sm, bias_row + j, 1, ways, part, True)

        def block(step, _):
            at = pl.ds(pl.multiple_of(step * BAND, BAND), BAND)
            act[at, cols], slope[at, cols] = gelu_parts(dot(n2[at, :], w1[:, cols]) + bias)
            return 0

        lax.fori_loop(0, length // BAND, block, 0)
        if j == hidden - 1:
            give(9, act, act_out)
            give(10, slope, slope_out)

    work = [[] for _ in range(last)]
    begin = min(7, last - 1)
    steps = [norm] + [functools.partial(attention, h) for h in range(heads)]
    for n, step in enumerate(steps):
        work[min(begin + n, last - 1)].append(step)
    for j in range(hidden):
        work[min(begin + len(steps) + j // 2, last - 1)].append(functools.partial(feed, j))

    for n in range(last):
        x_copy(n, now.at(n, 0)).wait_recv()

        @pl.when(p == 1)
        def _():
            now.begin(n, now.at(n, 0))

        if n > 0:
            now.forward(n - 1)
        for step in work[n]:
            step()
    now.forward(last - 1)

    now.finish((0, 1))
    for n in range(last):
        x_copy(n, now.at(n, 0)).wait_send()
    for step in range(1, ring):
        small_y(step).wait_send()
    x_small().wait_send()
    for r in range(ways):
        x_given(r, source).wait_send()
    for step in range(1, nt):
        z_copy(step, source).wait_send()
    for store in stores(full)[2:]:
        store.wait()
    for out in outs:
        out.wait()


def enter_section(boundary, small, shards, seg, axes, ways, nt, heads):
    hbm, vmem = pl.BlockSpec(memory_space=pl.ANY), pl.BlockSpec(memory_space=pltpu.VMEM)
    shape = jax.ShapeDtypeStruct
    part = shards[3].shape[1]
    length, width = boundary.shape[1:]
    pieces = len(chunks_of([s.shape for s in shards], axes, part))
    full = [
        shape((s.shape[0] * ways, s.shape[1]) if axis == 0 else (s.shape[0], s.shape[1] * ways), bf16)
        for s, axis in zip(shards, axes)
    ]
    dma = pltpu.SemaphoreType.DMA
    lane = jnp.arange(ROT, dtype=f32)
    frequency = jnp.exp(-math.log(10000.0) * 2.0 * (lane % 32) / 64)
    frequency = jnp.where(lane < 64, frequency, 0.0)[None]
    inner, columns = shards[0].shape[1], shards[1].shape[1]
    results = (
        [shape((length, ROT), f32)] * 3
        + [shape((length, width), bf16), shape((length, 1), f32)]
        + [shape((length, inner // 3), bf16)] * 4
        + [shape((length, columns), bf16)] * 2
    )
    out = pl.pallas_call(
        functools.partial(enter_kernel, ways, nt, axes, heads),
        in_specs=[hbm] * 6 + [vmem] * 3,
        out_specs=[hbm] * (11 + len(results)),
        out_shape=[
            shape((length, width), bf16),
            shape((length, width), bf16),
            shape((32 * ways, part), bf16),
            *full,
            *full,
            *results,
        ],
        scratch_shapes=[
            dma((ways + 1 + pieces,)),
            dma((ways + 1 + pieces,)),
            *Spread.semaphores(pieces + 1, ways),
            dma((nt - 1,)),
            dma((nt - 1,)),
            *[pltpu.VMEM(s.shape, bf16) for s in shards],
            dma((5,)),
            dma((max(ways, 4),)),
            dma((11,)),
            pltpu.VMEM((length, width), bf16),
            pltpu.VMEM((32 * ways, part), bf16),
            pltpu.VMEM((length, width), bf16),
            pltpu.VMEM((length, width), bf16),
            pltpu.VMEM(full[0].shape, bf16),
            pltpu.VMEM(full[1].shape, bf16),
            pltpu.VMEM((length, inner // heads), f32),
            *[pltpu.VMEM(r.shape, r.dtype) for r in results],
        ],
        compiler_params=pltpu.CompilerParams(
            collective_id=1, has_side_effects=True, vmem_limit_bytes=62 << 20
        ),
        cost_estimate=pl.CostEstimate(flops=0, bytes_accessed=600 << 20, transcendentals=0),
        name="enter_section",
    )(boundary, small, *shards, seg.reshape(-1, 1), seg.reshape(1, -1), frequency)
    return out[0], out[1], out[2], out[3:7], out[7:11], out[11:]


SUBS = 8


class LineSum:
    def __init__(self, n, partial, right, left, sems, finished, out=None):
        self.n, self.partial, self.right, self.left = n, partial, right, left
        self.finished, self.out = finished, out
        self.r_send, self.r_recv, self.l_send, self.l_recv = sems[:4]
        self.spread = sems[4:]
        self.i = lax.axis_index("tensor")
        self.rows = partial.shape[0] // n
        self.sub = self.rows // SUBS
        self.after = {"tensor": lax.rem(self.i + 1, n)}
        self.before = {"tensor": lax.rem(self.i + n - 1, n)}

    def at(self, ref, j, s):
        start = pl.multiple_of(j * self.rows + s * self.sub, self.sub)
        return ref.at[pl.ds(start, self.sub), :]

    def r_copy(self, j, s, source):
        target = self.at(self.right, j, s)
        return to(source, target, self.r_send.at[j, s], self.r_recv.at[j, s], self.after)

    def l_copy(self, j, s, source):
        target = self.at(self.left, j, s)
        return to(source, target, self.l_send.at[j, s], self.l_recv.at[j, s], self.before)

    def ar_copy(self, j, s):
        rows = self.at(self.out, j, s)
        return to(rows, rows, self.spread[0].at[j, s], self.spread[1].at[j, s], self.after)

    def al_copy(self, j, s):
        rows = self.at(self.out, j, s)
        return to(rows, rows, self.spread[2].at[j, s], self.spread[3].at[j, s], self.before)

    def add(self, ref, j, s):
        ref = self.at(ref, j, s)
        own = self.at(self.partial, j, s)[...].astype(f32)
        ref[...] = (ref[...].astype(f32) + own).astype(bf16)

    def reduce_right(self, s):
        for k in range(self.n - 1):
            j = self.n - 1 - k

            @pl.when(self.i == 0)
            def _():
                self.r_copy(j, s, self.at(self.partial, j, s)).start()

            @pl.when((self.i > 0) & (self.i < j))
            def _():
                self.r_copy(j, s, self.at(self.right, j, s)).wait_recv()
                self.add(self.right, j, s)
                self.r_copy(j, s, self.at(self.right, j, s)).start()

    def reduce_left(self, s):
        for k in range(self.n - 1):

            @pl.when(self.i == self.n - 1)
            def _():
                self.l_copy(k, s, self.at(self.partial, k, s)).start()

            @pl.when((self.i < self.n - 1) & (self.i > k))
            def _():
                self.l_copy(k, s, self.at(self.left, k, s)).wait_recv()
                self.add(self.left, k, s)
                self.l_copy(k, s, self.at(self.left, k, s)).start()

    def finish(self, s):
        i, n = self.i, self.n

        @pl.when(i > 0)
        def _():
            self.r_copy(i, s, self.at(self.right, i, s)).wait_recv()
            self.add(self.right, i, s)

        @pl.when(i == 0)
        def _():
            self.at(self.right, i, s)[...] = self.at(self.partial, i, s)[...]

        @pl.when(i < n - 1)
        def _():
            self.l_copy(i, s, self.at(self.left, i, s)).wait_recv()

        @pl.when(i == n - 1)
        def _():
            self.at(self.left, i, s)[...] = jnp.zeros((self.sub, self.left.shape[1]), bf16)

        total = self.at(self.right, i, s)[...].astype(f32)
        total = total + self.at(self.left, i, s)[...].astype(f32)
        self.finished(self, s, total)
        if self.out is not None:

            @pl.when(i < n - 1)
            def _():
                self.ar_copy(i, s).start()

            @pl.when(i > 0)
            def _():
                self.al_copy(i, s).start()

    def pass_on(self, step, s):
        i, n = self.i, self.n

        @pl.when(i >= step)
        def _():
            self.ar_copy(i - step, s).wait_recv()

            @pl.when(i < n - 1)
            def _():
                self.ar_copy(i - step, s).start()

        @pl.when(i + step < n)
        def _():
            self.al_copy(i + step, s).wait_recv()

            @pl.when(i > 0)
            def _():
                self.al_copy(i + step, s).start()

    @property
    def turns(self):
        return SUBS + (2 * self.n - 2 if self.out is not None else self.n - 1)

    def turn(self, it):
        def when_piece(s, act):
            @pl.when((s >= 0) & (s < SUBS))
            def _():
                act(s)

        when_piece(it - self.i, self.reduce_right)
        when_piece(it - (self.n - 1 - self.i), self.reduce_left)
        when_piece(it - (self.n - 1), self.finish)
        if self.out is not None:
            for step in range(1, self.n):
                when_piece(it - (self.n - 1) - step, functools.partial(self.pass_on, step))

    def drain(self):
        i, n = self.i, self.n

        def body(s, _):
            for j in range(n):

                @pl.when(i < j)
                def _():
                    self.r_copy(j, s, self.at(self.partial, j, s)).wait_send()

                @pl.when(i > j)
                def _():
                    self.l_copy(j, s, self.at(self.partial, j, s)).wait_send()

                if self.out is not None:

                    @pl.when((i >= j) & (i < n - 1))
                    def _():
                        self.ar_copy(j, s).wait_send()

                    @pl.when((i <= j) & (i > 0))
                    def _():
                        self.al_copy(j, s).wait_send()

            return 0

        lax.fori_loop(0, SUBS, body, 0)

    @staticmethod
    def scratch(n, tokens, width, spread):
        return [pltpu.VMEM((tokens, width), bf16)] * 2 + [
            pltpu.SemaphoreType.DMA((n, SUBS))
        ] * (8 if spread else 4)


def sum_spread_kernel(n, ways, axes, shapes, partial, base, *refs):
    out, full, right, left = refs[4], refs[5:9], refs[9], refs[10]
    line_sems, parts_sems = refs[11:19], refs[19:23]

    def finished(line, s, total):
        mine = pl.ds(pl.multiple_of(s * line.sub, line.sub), line.sub)
        line.at(out, line.i, s)[...] = (base[mine, :] + total).astype(bf16)

    line = LineSum(n, partial, right, left, line_sems, finished, out)
    parts = Spread(full, shapes, axes, ways, parts_sems)
    greet([line.after, line.before, parts.core] + parts.ahead)
    count = len(parts.chunks)
    for m in range(count):
        parts.begin(m, parts.at(m, 0))

    def turn_(it, _):
        line.turn(it)
        for m in range(count):

            @pl.when(it == m + 1)
            def _():
                parts.forward(m)

        return 0

    lax.fori_loop(0, max(line.turns, count + 1), turn_, 0)
    line.drain()
    parts.finish()


def sum_spread(partial, base, n, full, shapes, axes, ways):
    tokens, width = partial.shape
    vmem = pl.BlockSpec(memory_space=pltpu.VMEM)
    hbm = pl.BlockSpec(memory_space=pl.ANY)
    pieces = len(chunks_of(shapes, axes, shapes[3][1]))
    out = pl.pallas_call(
        functools.partial(sum_spread_kernel, n, ways, axes, shapes),
        in_specs=[vmem, vmem] + [hbm] * 4,
        out_specs=[vmem] + [hbm] * 4,
        out_shape=[jax.ShapeDtypeStruct((tokens, width), bf16)]
        + [jax.ShapeDtypeStruct(w.shape, bf16) for w in full],
        input_output_aliases={2 + m: 1 + m for m in range(4)},
        scratch_shapes=LineSum.scratch(n, tokens, width, True)
        + Spread.semaphores(pieces, ways),
        compiler_params=pltpu.CompilerParams(
            collective_id=2, has_side_effects=True, vmem_limit_bytes=32 << 20
        ),
        cost_estimate=pl.CostEstimate(flops=0, bytes_accessed=360 << 20, transcendentals=0),
        name="sum_spread",
    )(partial, base, *full)
    return out[0], out[1:]


class GradSum:
    def __init__(self, k, ways, xh, g, sides, outs, vec, vec_out, scratch):
        (
            self.load, self.away, self.held, self.round, self.across, self.done,
            self.v_held, self.v_round, self.v_across,
            self.load_sem, self.c_send, self.c_recv, self.y_send, self.y_recv,
            self.x_send, self.x_recv, self.out_sem,
        ) = scratch
        self.k, self.ring = k, ways // 2
        self.xh, self.g, self.sides, self.outs = xh, g, sides, outs
        self.vec, self.vec_out = vec, vec_out
        self.part = self.load.shape[2]
        self.counts = [side.shape[1] // self.part for side in sides]
        self.starts = [sum(self.counts[:m]) for m in range(4)]
        self.count = sum(self.counts)
        p, d = lax.axis_index("pipe"), lax.axis_index("dp")
        y, c = d // 2, d % 2
        self.p = p
        self.core = {"dp": y * 2 + (1 - c)}
        self.ahead = [{"dp": lax.rem(y + o, self.ring) * 2 + c} for o in range(1, self.ring)]
        self.other = {"pipe": 1 - p}

    def each(self, c, act):
        for m in range(4):

            @pl.when((c >= self.starts[m]) & (c < self.starts[m] + self.counts[m]))
            def _():
                act(m, pl.multiple_of((c - self.starts[m]) * self.part, self.part))

    def fetch(self, c):
        def act(m, at):
            pltpu.make_async_copy(
                self.sides[m].at[:, pl.ds(at, self.part)],
                self.load.at[lax.rem(c, 3)],
                self.load_sem.at[lax.rem(c, 3)],
            ).start()

        self.each(c, act)

    def fetched(self, c):
        slot = lax.rem(c, 3)
        pltpu.make_async_copy(
            self.sides[0].at[:, pl.ds(0, self.part)], self.load.at[slot], self.load_sem.at[slot]
        ).wait()

    def piece(self, c, slot, use):
        side = self.load.at[lax.rem(c, 3)]
        cols = pl.ds(slot * self.part, self.part)

        @pl.when(c < self.starts[2])
        def _():
            use(dot(side[...], self.g[:, cols], ((0,), (0,))))

        @pl.when(c >= self.starts[2])
        def _():
            use(dot(self.xh[:, cols], side[...], ((0,), (0,))))

    def c_copy(self, c, o):
        return to(
            self.away.at[lax.rem(c, 2), o], self.held.at[c, o],
            self.c_send.at[c, o], self.c_recv.at[c, o], self.core,
        )

    def y_copy(self, c, o):
        return to(
            self.held.at[c, o], self.round.at[c, o - 1],
            self.y_send.at[c, o - 1], self.y_recv.at[c, o - 1], self.ahead[o - 1],
        )

    def x_copy(self, c):
        return to(
            self.held.at[c, 0], self.across.at[c], self.x_send.at[c], self.x_recv.at[c], self.other
        )

    def chunk_sum(self, c):
        total = self.held[c, 0].astype(f32)
        for o in range(1, self.ring):
            total = total + self.round[c, o - 1].astype(f32)
        return total

    def store(self, c, start):
        slot = lax.rem(c, 2)

        def act(m, at):
            out = self.outs[m]
            if m < 2:
                out = out.at[pl.ds(at, self.part), :]
            else:
                out = out.at[:, pl.ds(at, self.part)]
            copy = pltpu.make_async_copy(self.done.at[slot], out, self.out_sem.at[slot])
            copy.start() if start else copy.wait()

        self.each(c, act)

    @property
    def turns(self):
        return self.count + 5

    def begin(self):
        self.fetch(0)
        self.fetch(1)
        self.v_copy(0).start()

    def v_copy(self, stage, o=1):
        last = self.count
        if stage == 0:
            return to(
                self.vec, self.v_held, self.c_send.at[last, 0], self.c_recv.at[last, 0], self.core
            )
        if stage == 1:
            return to(
                self.v_held, self.v_round.at[o - 1],
                self.y_send.at[last, o - 1], self.y_recv.at[last, o - 1], self.ahead[o - 1],
            )
        return to(
            self.vec_out, self.v_across, self.x_send.at[last], self.x_recv.at[last], self.other
        )

    def turn(self, it):
        @pl.when(it < self.count)
        def _():
            c = it
            self.fetched(c)
            for o in range(self.ring):

                @pl.when(c >= 2)
                def _():
                    self.c_copy(c - 2, o).wait_send()

                def use(value):
                    self.away[lax.rem(c, 2), o] = value.astype(bf16)

                self.piece(c, 2 * o + 1, use)
                self.c_copy(c, o).start()

        @pl.when((it >= 1) & (it < self.count + 1))
        def _():
            c = it - 1
            for o in range(self.ring - 1, -1, -1):
                self.c_copy(c, o).wait_recv()

                def use(value):
                    value = value + self.held[c, o].astype(f32)
                    self.held[c, o] = value.astype(bf16)

                self.piece(c, 2 * o, use)
                if o > 0:
                    self.y_copy(c, o).start()

            @pl.when(c + 3 < self.count + 1)
            def _():
                @pl.when(c + 2 < self.count)
                def _():
                    self.fetch(c + 2)

        @pl.when((it >= 3) & (it < self.count + 3))
        def _():
            c = it - 3
            for o in range(1, self.ring):
                self.y_copy(c, o).wait_recv()

            @pl.when(self.p != self.k)
            def _():
                self.held[c, 0] = self.chunk_sum(c).astype(bf16)
                self.x_copy(c).start()

        @pl.when((it >= 5) & (it < self.count + 5) & (self.p == self.k))
        def _():
            c = it - 5

            @pl.when(c >= 2)
            def _():
                self.store(c - 2, False)

            self.x_copy(c).wait_recv()
            self.done[lax.rem(c, 2)] = self.chunk_sum(c) + self.across[c].astype(f32)
            self.store(c, True)

        @pl.when(it == 3)
        def _():
            self.v_copy(0).wait()
            self.v_held[...] = self.v_held[...] + self.vec[...]
            for o in range(1, self.ring):
                self.v_copy(1, o).start()

        @pl.when(it == 6)
        def _():
            total = self.v_held[...]
            for o in range(1, self.ring):
                self.v_copy(1, o).wait()
                total = total + self.v_round[o - 1]
            self.vec_out[...] = total

            @pl.when(self.p != self.k)
            def _():
                self.v_copy(2).start()

        @pl.when((it == 9) & (self.p == self.k))
        def _():
            self.v_copy(2).wait_recv()
            self.vec_out[...] = self.vec_out[...] + self.v_across[...]

    def drain(self):
        last = self.count
        for c in (last - 2, last - 1):
            for o in range(self.ring):
                self.c_copy(c, o).wait_send()

        @pl.when(self.p == self.k)
        def _():
            for c in (last - 2, last - 1):
                self.store(jnp.int32(c), False)

        @pl.when(self.p != self.k)
        def _():
            self.v_copy(2).wait_send()

        def body(c, _):
            for o in range(1, self.ring):
                self.y_copy(c, o).wait_send()

            @pl.when(self.p != self.k)
            def _():
                self.x_copy(c).wait_send()

            return 0

        lax.fori_loop(0, last, body, 0)

    @staticmethod
    def scratch(ways, part, tokens, count, vec):
        ring = ways // 2
        dma = pltpu.SemaphoreType.DMA
        return [
            pltpu.VMEM((3, tokens, part), bf16),
            pltpu.VMEM((2, ring, part, part), bf16),
            pltpu.VMEM((count, ring, part, part), bf16),
            pltpu.VMEM((count, ring - 1, part, part), bf16),
            pltpu.VMEM((count, part, part), bf16),
            pltpu.VMEM((2, part, part), f32),
            pltpu.VMEM(vec.shape, f32),
            pltpu.VMEM((ring - 1, *vec.shape), f32),
            pltpu.VMEM(vec.shape, f32),
            dma((3,)),
            dma((count + 1, ring)),
            dma((count + 1, ring)),
            dma((count + 1, ring - 1)),
            dma((count + 1, ring - 1)),
            dma((count + 1,)),
            dma((count + 1,)),
            dma((2,)),
        ]


def back_kernel(n, ways, k, partial, inv_std, xh, g, vec, *refs):
    sides, refs = refs[:4], refs[4:]
    if k == 0:
        refs = refs[4:]
        rows_out, rows_away, vec_out, outs, refs = refs[0], refs[1], refs[2], refs[3:7], refs[7:]
        out = None
    else:
        out, vec_out, outs, refs = refs[0], refs[1], refs[2:6], refs[6:]
    count = 8 if k else 4
    right, left, line_sems, refs = refs[0], refs[1], refs[2 : 2 + count], refs[2 + count :]
    if k == 0:
        handed, d_send, d_recv, refs = refs[0], refs[1], refs[2], refs[3:]
    p = lax.axis_index("pipe")
    other = {"pipe": 1 - p}

    def d_copy(s, sub):
        mine = pl.ds(pl.multiple_of(s * sub, sub), sub)
        return to(handed.at[mine, :], rows_away.at[mine, :], d_send.at[s], d_recv.at[s], other)

    def finished(line, s, total):
        mine = pl.ds(pl.multiple_of(s * line.sub, line.sub), line.sub)
        xr = line.at(xh, line.i, s)[...].astype(f32)
        mean = jnp.mean(total, axis=1, keepdims=True)
        proj = jnp.mean(total * xr, axis=1, keepdims=True)
        total = inv_std[mine, :] * (total - mean - xr * proj)
        total = line.at(g, line.i, s)[...].astype(f32) + total
        if k == 1:
            line.at(out, line.i, s)[...] = total.astype(bf16)
        else:
            rows_out[mine, :] = total
            handed[mine, :] = total.astype(bf16)

            @pl.when(p == 1)
            def _():
                d_copy(s, line.sub).start()

    line = LineSum(n, partial, right, left, line_sems, finished, out)
    grads = GradSum(k, ways, xh, g, sides, outs, vec, vec_out, refs)
    greet([line.after, line.before, grads.core, grads.other] + grads.ahead)
    grads.begin()

    def turn_(it, _):
        line.turn(it)
        grads.turn(it)
        return 0

    lax.fori_loop(0, max(line.turns, grads.turns), turn_, 0)
    line.drain()
    grads.drain()
    if k == 0:
        for s in range(SUBS):

            @pl.when(p == 1)
            def _():
                d_copy(s, line.sub).wait_send()

            @pl.when(p == 0)
            def _():
                d_copy(s, line.sub).wait_recv()


def back_sums(k, partial, inv_std, xh, g, vec, sides, n, ways, outs=None):
    tokens, width = partial.shape
    part = width // ways
    rows = tokens // n
    vmem = pl.BlockSpec(memory_space=pltpu.VMEM)
    hbm = pl.BlockSpec(memory_space=pl.ANY)
    shape = jax.ShapeDtypeStruct
    count = sum(side.shape[1] for side in sides) // part
    grad_shapes = [
        shape((side.shape[1], part) if m < 2 else (part, side.shape[1]), f32)
        for m, side in enumerate(sides)
    ]
    if k == 0:
        lead = [shape((rows, width), f32), shape((rows, width), bf16)]
        lead_specs = [vmem, vmem]
        extra = [pltpu.VMEM((rows, width), bf16)] + [pltpu.SemaphoreType.DMA((SUBS,))] * 2
    else:
        lead, lead_specs, extra = [shape((tokens, width), bf16)], [vmem], []
    lead, lead_specs = lead + [shape(vec.shape, f32)], lead_specs + [vmem]
    return pl.pallas_call(
        functools.partial(back_kernel, n, ways, k),
        in_specs=[vmem] * 5 + [hbm] * (4 if k else 8),
        out_specs=lead_specs + [hbm] * 4,
        out_shape=lead + grad_shapes,
        input_output_aliases={} if k else {9 + m: len(lead) + m for m in range(4)},
        scratch_shapes=LineSum.scratch(n, tokens, width, k == 1)
        + extra
        + GradSum.scratch(ways, part, tokens, count, vec),
        compiler_params=pltpu.CompilerParams(
            collective_id=3 + k, has_side_effects=True, vmem_limit_bytes=60 << 20
        ),
        cost_estimate=pl.CostEstimate(flops=0, bytes_accessed=500 << 20, transcendentals=0),
        name="back_sums",
    )(partial, inv_std, xh, g, vec, *sides, *(outs or ()))


def normalize(values):
    average = jnp.mean(values, axis=-1, keepdims=True)
    centred = values - average
    spread = jnp.mean(centred * centred, axis=-1, keepdims=True)
    inv_std = lax.rsqrt(spread + norm_epsilon)
    return (centred * inv_std, inv_std)


def per_device(
    boundary,
    segments,
    ln1_gain,
    ln1_bias,
    ln2_gain,
    ln2_bias,
    qkv_weight,
    qkv_bias,
    dense_weight,
    dense_bias,
    fc1_weight,
    fc1_bias,
    fc2_weight,
    fc2_bias,
):
    pipe, d, t = lax.axis_index("pipe"), lax.axis_index("dp"), lax.axis_index("tensor")
    ways, ring = lax.axis_size("dp"), lax.axis_size("dp") // 2
    nt = lax.axis_size("tensor")
    first = pipe == 0
    seqs, length, width = boundary.shape[1] // 2, boundary.shape[2], boundary.shape[3]
    tokens, rows, part = seqs * length, length // nt, width // ways
    heads, size = qkv_weight.shape[2], qkv_weight.shape[3] // 3
    y, c = d // 2, d % 2

    def pipe_send(v, source):
        return lax.ppermute(v, "pipe", [(source, 1 - source)])

    def true_order(v):
        parts = []
        for j in range(ways):
            place = ((j // 2 - y) % ring) * 2 + (c ^ (j % 2))
            parts.append(lax.dynamic_slice_in_dim(v, place * part, part, v.ndim - 1))
        return jnp.concatenate(parts, axis=-1)

    def together(*values):
        return list(lax.optimization_barrier(values))

    seg = lax.dynamic_slice_in_dim(segments, pipe * seqs, seqs, 0)
    shards = (
        qkv_weight[0].reshape(part, heads * 3 * size),
        fc1_weight[0],
        fc2_weight[0],
        dense_weight[0],
    )
    axes = (0, 0, 1, 1)
    def in_place(v):
        whole = jnp.zeros((v.shape[0], v.shape[1] * ways), bf16)
        whole = lax.dynamic_update_slice_in_dim(whole, v, d * v.shape[1], 1)
        return whole.reshape(-1, part)

    small = [ln1_gain, ln1_bias, ln2_gain, ln2_bias, dense_bias, fc2_bias]
    small = jnp.concatenate(small + [in_place(qkv_bias[0]), in_place(fc1_bias)], axis=0)
    small = jnp.pad(small, ((0, 16 - small.shape[0]), (0, 0)))
    source, cotangent, small_all, weights_0, weights_1, found = enter_section(
        boundary[0], small, shards, seg, axes, ways, nt, heads
    )
    tables, (xh0, inv0, ar0, qr0, kr0, vr0, act0, slope0) = found[:3], found[3:]
    small_all = small_all.reshape(ways, 2, 16, part).astype(f32)
    cut = heads * 3 * size

    def vectors(k):
        rows_ = small_all[:, k]
        found = [rows_[:, m].reshape(1, width) for m in range(6)]
        in_place = jnp.sum(rows_[:, 6:], axis=0).reshape(1, -1)
        return found + [in_place[:, cut : cut + fc1_weight.shape[2]], in_place[:, :cut]]

    def scatter_rows(v):
        return lax.psum_scatter(
            v.reshape(seqs, length, width), "tensor", scatter_dimension=1, tiled=True
        )

    def own_rows(v):
        return lax.dynamic_slice_in_dim(v.reshape(seqs, length, width), t * rows, rows, 1)

    def own_rows_of(v):
        return lax.dynamic_slice_in_dim(v, t * rows, rows, 0)

    def enter(k, x):
        g1, b1, g2, b2 = vectors(k)[:4]
        xhat, inv_std = normalize(x.astype(f32))
        n1 = (xhat * g1 + b1).astype(bf16)
        n2 = (xhat * g2 + b2).astype(bf16)
        return n1, n2, xhat.astype(bf16), inv_std

    tn, nt_ = ((0,), (0,)), ((1,), (1,))

    def sums_of(qkv_sum, d_hidden, g):
        g_sum = true_order(jnp.sum(g.astype(f32), axis=0, keepdims=True))[0]
        found = jnp.concatenate([qkv_sum, jnp.sum(d_hidden.astype(f32), axis=0), g_sum])
        return jnp.pad(found, (0, -found.shape[0] % 1024)).reshape(-1, 128)

    wq0, w10, w20, wd0 = weights_0
    branch = (dot(ar0, wd0) + dot(act0, w20)).astype(bf16)
    base = (own_rows(source).astype(f32) + (vectors(0)[4] + vectors(0)[5])).reshape(-1, width)
    x1, weights_1 = sum_spread(
        branch, base, nt, weights_1, [shard.shape for shard in shards], axes, ways
    )
    wq1, w11, w21, wd1 = weights_1

    n1, n2, xh1, inv1 = enter(1, x1)
    g1, _, g2, _ = vectors(1)[:4]
    ar1, qr1, kr1, vr1 = attend(dot(n1, wq1), vectors(1)[7], tables, seg, heads, length)
    d_ar = dot(cotangent, wd1, nt_).astype(bf16)
    d_qkv1, qkv_sum1 = attend_back(qr1, kr1, vr1, d_ar, tables, seg, heads, length)
    act1, slope1 = gelu_matmul(n2, w11, vectors(1)[6])
    d_hidden1 = (slope1.astype(f32) * dot(cotangent, w21, nt_)).astype(bf16)
    u = (dot(d_qkv1, wq1, nt_) * g1 + dot(d_hidden1, w11, nt_) * g2).astype(bf16)
    branch = (dot(ar1, wd1) + dot(act1, w21)).astype(bf16)
    u, branch = together(u, branch)
    g0, sums_1, *grads = back_sums(
        1, u, own_rows_of(inv1), xh1, cotangent, sums_of(qkv_sum1, d_hidden1, cotangent),
        (act1, ar1, d_hidden1, d_qkv1), nt, ways,
    )

    branch, g0 = together(branch, g0)
    summed = scatter_rows(branch).astype(f32)
    g1, _, g2, _ = vectors(0)[:4]
    d_ar = dot(g0, wd0, nt_).astype(bf16)
    d_hidden0 = (slope0.astype(f32) * dot(g0, w20, nt_)).astype(bf16)
    d_qkv0, qkv_sum0 = attend_back(qr0, kr0, vr0, d_ar, tables, seg, heads, length)
    u = (dot(d_qkv0, wq0, nt_) * g1 + dot(d_hidden0, w10, nt_) * g2).astype(bf16)
    y_rows = own_rows(x1).astype(f32) + (summed + (vectors(1)[4] + vectors(1)[5]))
    y_away = pipe_send(y_rows.astype(bf16), 0)
    u, y_away = together(u, y_away)
    dx_rows, dx_away, sums_0, *grads = back_sums(
        0, u, own_rows_of(inv0), xh0, g0, sums_of(qkv_sum0, d_hidden0, g0),
        (act0, ar0, d_hidden0, d_qkv0), nt, ways, grads,
    )
    dx_rows = dx_rows.reshape(seqs, rows, width)
    dx_away = dx_away.reshape(seqs, rows, width).astype(f32)

    y_away = y_away.astype(f32)
    boundary_out = true_order(
        jnp.where(
            first,
            jnp.concatenate([dx_rows, dx_away], axis=0),
            jnp.concatenate([y_away, y_rows], axis=0),
        )
    )[None]

    fc2_grad, dense_grad, fc1_core, qkv_core = grads
    sums = jnp.where(first, sums_0, sums_1).reshape(-1)
    end = cut + shards[1].shape[1]
    qkv_sum, fc1_sum, g_sum = sums[:cut], sums[cut:end], sums[end : end + width]

    def norm_grads(weight, core, sum_):
        w = weight.astype(f32)
        return jnp.sum(w * core, axis=1), jnp.sum(w * sum_[None], axis=1)

    norms = norm_grads(shards[0], qkv_core, qkv_sum) + norm_grads(shards[1], fc1_core, fc1_sum)
    norms = jnp.stack(norms)

    def for_place(step):
        place = lax.rem(t + step, nt) * (part // nt)
        return lax.dynamic_slice_in_dim(norms, place, part // nt, 1)

    norms = for_place(0) + sum(
        lax.ppermute(for_place(step), "tensor", [(i, (i + step) % nt) for i in range(nt)])
        for step in range(1, nt)
    )

    def finish(core, gain, bias, sum_):
        gain, bias = gain[0].astype(f32)[:, None], bias[0].astype(f32)[:, None]
        return gain * core + bias * sum_[None]

    qkv_grad = finish(qkv_core, ln1_gain, ln1_bias, qkv_sum).reshape(part, heads, 3 * size)
    fc1_grad = finish(fc1_core, ln2_gain, ln2_bias, fc1_sum)

    def own_part(v, axis):
        step = v.shape[axis] // ways
        return lax.dynamic_slice_in_dim(v, d * step, step, axis)

    bias_grad = own_part(g_sum, 0)[None]
    return (
        boundary_out,
        norms[0][None],
        norms[1][None],
        norms[2][None],
        norms[3][None],
        qkv_grad[None],
        own_part(qkv_sum.reshape(heads, 3 * size), 1)[None],
        dense_grad[None],
        bias_grad,
        fc1_grad[None],
        own_part(fc1_sum, 0)[None],
        fc2_grad[None],
        bias_grad,
    )


def solution(mesh):
    in_specs = (
        P("pipe", "dp", None, None),
        P("dp", None),
        P("pipe", "dp"),
        P("pipe", "dp"),
        P("pipe", "dp"),
        P("pipe", "dp"),
        P("pipe", "dp", "tensor", None),
        P("pipe", "tensor", "dp"),
        P("pipe", "tensor", "dp"),
        P("pipe", "dp"),
        P("pipe", "dp", "tensor"),
        P("pipe", ("tensor", "dp")),
        P("pipe", "tensor", "dp"),
        P("pipe", "dp"),
    )
    out_specs = (
        P("pipe", "dp", "tensor", None),
        P("pipe", ("dp", "tensor")),
        P("pipe", ("dp", "tensor")),
        P("pipe", ("dp", "tensor")),
        P("pipe", ("dp", "tensor")),
        P("pipe", "dp", "tensor", None),
        P("pipe", "tensor", "dp"),
        P("pipe", "tensor", "dp"),
        P("pipe", "dp"),
        P("pipe", "dp", "tensor"),
        P("pipe", ("tensor", "dp")),
        P("pipe", "tensor", "dp"),
        P("pipe", "dp"),
    )
    return jax.shard_map(
        per_device, mesh=mesh, in_specs=in_specs, out_specs=out_specs, check_vma=False
    )
```

```python
import functools
import math

import jax
import jax.numpy as jnp
from jax import lax
from jax.experimental import pallas as pl
from jax.experimental.pallas import tpu as pltpu
from jax.sharding import PartitionSpec as P

norm_epsilon = 1e-05
mask_fill = -1e30
BAND = 256
ROT = 128
f32, bf16 = jnp.float32, jnp.bfloat16


def dot(a, b, contract=((1,), (0,))):
    return lax.dot_general(a, b, (contract, ((), ())), preferred_element_type=f32)


def allowed(seg_col, seg_row, block):
    low = max(block - 1, 0) * BAND
    size = (block + 1) * BAND - low
    own = lax.broadcasted_iota(jnp.int32, (BAND, size), 0) + (block * BAND - low)
    key = lax.broadcasted_iota(jnp.int32, (BAND, size), 1)
    rows = pl.ds(block * BAND, BAND)
    return (own >= key) & (seg_col[rows, :] == seg_row[:, pl.ds(low, size)])


def turn(values, cos, forward, backward):
    head = values[:, :ROT]
    head = (
        head * cos
        + pltpu.roll(head, ROT - 32, 1) * forward
        + pltpu.roll(head, 32, 1) * backward
    )
    return jnp.concatenate([head, values[:, ROT:]], axis=1)


def attend_kernel(scale, qkv, bias, cos, sin_a, sin_b, seg_col, seg_row, out, qr, kr, vr):
    size = out.shape[1]
    for block in range(out.shape[0] // BAND):
        rows = pl.ds(block * BAND, BAND)
        c, a, b = cos[rows, :], sin_a[rows, :], sin_b[rows, :]
        q = turn(qkv[rows, :size] + bias[:, :size], c, a, b).astype(bf16)
        k = turn(qkv[rows, size : 2 * size] + bias[:, size : 2 * size], c, a, b).astype(bf16)
        qr[rows, :] = q
        kr[rows, :] = k
        vr[rows, :] = (qkv[rows, 2 * size :] + bias[:, 2 * size :]).astype(bf16)
        low = max(block - 1, 0) * BAND
        keys = pl.ds(low, (block + 1) * BAND - low)
        scores = dot(q, kr[keys, :], ((1,), (1,))) * scale
        scores = jnp.where(allowed(seg_col, seg_row, block), scores, mask_fill)
        weights = jnp.exp(scores - jnp.max(scores, axis=1, keepdims=True))
        weights = weights * (1.0 / jnp.sum(weights, axis=1, keepdims=True))
        out[rows, :] = dot(weights.astype(bf16), vr[keys, :]).astype(bf16)


def attend(qkv, bias, tables, seg, heads, length):
    size = qkv.shape[1] // heads // 3
    seqs = qkv.shape[0] // length
    block = pl.BlockSpec((length, size), lambda b, h: (b, h))
    table = pl.BlockSpec((length, ROT), lambda b, h: (b, 0))
    return pl.pallas_call(
        functools.partial(attend_kernel, 1.0 / math.sqrt(size)),
        grid=(seqs, heads),
        in_specs=[
            pl.BlockSpec((length, 3 * size), lambda b, h: (b, h)),
            pl.BlockSpec((1, 3 * size), lambda b, h: (0, h)),
            table,
            table,
            table,
            pl.BlockSpec((length, 1), lambda b, h: (b, 0)),
            pl.BlockSpec((1, length), lambda b, h: (0, b)),
        ],
        out_specs=[block] * 4,
        out_shape=[jax.ShapeDtypeStruct((qkv.shape[0], heads * size), bf16)] * 4,
        compiler_params=pltpu.CompilerParams(vmem_limit_bytes=48 << 20),
        cost_estimate=pl.CostEstimate(
            flops=2 * 2 * qkv.shape[0] * 2 * BAND * heads * size,
            bytes_accessed=qkv.size * 4 + qkv.shape[0] * heads * size * 8,
            transcendentals=qkv.shape[0] * heads * 2 * BAND,
        ),
        name="attend",
    )(qkv, bias, *tables, seg.reshape(-1, 1), seg.reshape(1, -1))


def attend_back_kernel(
    scale, qr, kr, vr, grad, cos, sin_a, sin_b, seg_col, seg_row, out, out_sum, dk_acc, dv_acc
):
    size = grad.shape[1]
    blocks = grad.shape[0] // BAND
    sums = [jnp.zeros((1, size), f32)] * 3

    def emit(place, part, values):
        rows = pl.ds(place * BAND, BAND)
        if part < 2:
            values = turn(values, cos[rows, :], -sin_a[rows, :], -sin_b[rows, :])
        values = values.astype(bf16)
        out[rows, part * size : (part + 1) * size] = values
        sums[part] = sums[part] + jnp.sum(values.astype(f32), axis=0, keepdims=True)

    for block in range(blocks):
        rows = pl.ds(block * BAND, BAND)
        low = max(block - 1, 0) * BAND
        keys = pl.ds(low, (block + 1) * BAND - low)
        q, k, v, g = qr[rows, :], kr[keys, :], vr[keys, :], grad[rows, :]
        scores = dot(q, k, ((1,), (1,))) * scale
        scores = jnp.where(allowed(seg_col, seg_row, block), scores, mask_fill)
        weights = jnp.exp(scores - jnp.max(scores, axis=1, keepdims=True))
        weights = weights * (1.0 / jnp.sum(weights, axis=1, keepdims=True))
        grad_weights = dot(g, v, ((1,), (1,)))
        row_dot = jnp.sum(weights * grad_weights, axis=1, keepdims=True)
        grad_scores = (weights * (grad_weights - row_dot)).astype(bf16)
        emit(block, 0, dot(grad_scores, k) * scale)
        dk = dot(grad_scores, q, ((0,), (0,))) * scale
        dv = dot(weights.astype(bf16), g, ((0,), (0,)))
        if block > 0:
            emit(block - 1, 1, dk_acc[...] + dk[:BAND])
            emit(block - 1, 2, dv_acc[...] + dv[:BAND])
            dk, dv = dk[BAND:], dv[BAND:]
        if block == blocks - 1:
            emit(block, 1, dk)
            emit(block, 2, dv)
        else:
            dk_acc[...] = dk
            dv_acc[...] = dv
    out_sum[0] = jnp.concatenate(sums, axis=1)


def attend_back(qr, kr, vr, grad, tables, seg, heads, length):
    size = qr.shape[1] // heads
    tokens = qr.shape[0]
    seqs = tokens // length
    block = pl.BlockSpec((length, size), lambda b, h: (b, h))
    table = pl.BlockSpec((length, ROT), lambda b, h: (b, 0))
    out, sums = pl.pallas_call(
        functools.partial(attend_back_kernel, 1.0 / math.sqrt(size)),
        grid=(seqs, heads),
        in_specs=[block] * 4
        + [table] * 3
        + [
            pl.BlockSpec((length, 1), lambda b, h: (b, 0)),
            pl.BlockSpec((1, length), lambda b, h: (0, b)),
        ],
        out_specs=[
            pl.BlockSpec((length, 3 * size), lambda b, h: (b, h)),
            pl.BlockSpec((1, 1, 3 * size), lambda b, h: (b, 0, h)),
        ],
        out_shape=[
            jax.ShapeDtypeStruct((tokens, heads * 3 * size), bf16),
            jax.ShapeDtypeStruct((seqs, 1, heads * 3 * size), f32),
        ],
        scratch_shapes=[pltpu.VMEM((BAND, size), f32)] * 2,
        compiler_params=pltpu.CompilerParams(vmem_limit_bytes=48 << 20),
        cost_estimate=pl.CostEstimate(
            flops=2 * 5 * tokens * 2 * BAND * heads * size,
            bytes_accessed=tokens * heads * size * 14,
            transcendentals=tokens * heads * 2 * BAND,
        ),
        name="attend_back",
    )(qr, kr, vr, grad, *tables, seg.reshape(-1, 1), seg.reshape(1, -1))
    return out, jnp.sum(sums, axis=(0, 1))


def gelu_parts(h):
    t = 1.0 / (1.0 + (0.3275911 * math.sqrt(0.5)) * jnp.abs(h))
    poly = 1.061405429 * t - 1.453152027
    poly = poly * t + 1.421413741
    poly = poly * t - 0.284496736
    poly = poly * t + 0.254829592
    bell = jnp.exp(-0.5 * h * h)
    tail = 0.5 * poly * t * bell
    cdf = jnp.where(h >= 0.0, 1.0 - tail, tail)
    slope = cdf + h * bell * (1.0 / math.sqrt(2.0 * math.pi))
    return (h * cdf).astype(bf16), slope.astype(bf16)


def gelu_kernel(x, w, bias, act, slope):
    for row in range(0, x.shape[0], BAND):
        rows = pl.ds(row, BAND)
        act[rows, :], slope[rows, :] = gelu_parts(dot(x[rows, :], w[...]) + bias[...])


def gelu_matmul(x, w, bias):
    tokens, depth = x.shape
    width = w.shape[1]
    cols = min(512, width)
    block = pl.BlockSpec((tokens, cols), lambda j: (0, j))
    return pl.pallas_call(
        gelu_kernel,
        grid=(width // cols,),
        in_specs=[
            pl.BlockSpec((tokens, depth), lambda j: (0, 0)),
            pl.BlockSpec((depth, cols), lambda j: (0, j)),
            pl.BlockSpec((1, cols), lambda j: (0, j)),
        ],
        out_specs=[block, block],
        out_shape=[jax.ShapeDtypeStruct((tokens, width), bf16)] * 2,
        compiler_params=pltpu.CompilerParams(vmem_limit_bytes=48 << 20),
        cost_estimate=pl.CostEstimate(
            flops=2 * tokens * depth * width,
            bytes_accessed=2 * (tokens * depth + depth * width + 2 * tokens * width),
            transcendentals=2 * tokens * width,
        ),
        name="gelu_matmul",
    )(x, w, bias)


def to(source, target, send, recv, place):
    return pltpu.make_async_remote_copy(
        src_ref=source,
        dst_ref=target,
        send_sem=send,
        recv_sem=recv,
        device_id=place,
        device_id_type=pl.DeviceIdType.MESH,
    )


def greet(places):
    barrier = pltpu.get_barrier_semaphore()
    for place in places:
        pl.semaphore_signal(
            barrier, inc=1, device_id=place, device_id_type=pl.DeviceIdType.MESH
        )
    pl.semaphore_wait(barrier, len(places))


def chunks_of(shapes, axes, part):
    return [
        (m, row, col)
        for m, (shape, axis) in enumerate(zip(shapes, axes))
        for row in range(0, shape[0], part)
        for col in range(0, shape[1], part)
    ]


def chunk_at(ref, axis, shape, chunk, slot, part):
    _, row, col = chunk
    row, col = (row + slot * shape[0], col) if axis == 0 else (row, col + slot * shape[1])
    return ref.at[pl.ds(row, part), pl.ds(col, part)]


class Spread:
    def __init__(self, full, shapes, axes, ways, sems):
        self.full, self.shapes, self.axes = full, shapes, axes
        self.ring = ways // 2
        self.y_send, self.y_recv, self.c_send, self.c_recv = sems
        self.part = shapes[3][1]
        self.chunks = chunks_of(shapes, axes, self.part)
        d = lax.axis_index("dp")
        y, c = d // 2, d % 2
        self.core = {"dp": y * 2 + (1 - c)}
        self.ahead = [{"dp": lax.rem(y + o, self.ring) * 2 + c} for o in range(1, self.ring)]

    def at(self, n, slot):
        m = self.chunks[n][0]
        return chunk_at(
            self.full[m], self.axes[m], self.shapes[m], self.chunks[n], slot, self.part
        )

    def y_copy(self, n, step, source):
        target = self.at(n, 2 * ((self.ring - step) % self.ring))
        return to(
            source, target, self.y_send.at[n, step - 1], self.y_recv.at[n, step - 1],
            self.ahead[step - 1],
        )

    def c_copy(self, n, o, source):
        target = self.at(n, 2 * o + 1)
        return to(source, target, self.c_send.at[n, o], self.c_recv.at[n, o], self.core)

    def begin(self, n, source):
        for step in range(1, self.ring):
            self.y_copy(n, step, source).start()
        self.c_copy(n, 0, source).start()

    def forward(self, n):
        for step in range(1, self.ring):
            o = (self.ring - step) % self.ring
            self.y_copy(n, step, self.at(n, 0)).wait_recv()
            self.c_copy(n, o, self.at(n, 2 * o)).start()

    def arrived(self, m):
        for n in range(len(self.chunks)):
            if self.chunks[n][0] == m:
                for o in range(self.ring):
                    self.c_copy(n, o, self.at(n, 2 * o)).wait_recv()

    def finish(self, waited=()):
        for n in range(len(self.chunks)):
            for step in range(1, self.ring):
                self.y_copy(n, step, self.at(n, 0)).wait_send()
            for o in range(self.ring):
                self.c_copy(n, o, self.at(n, 2 * o)).wait_send()
        for m in range(4):
            if m not in waited:
                self.arrived(m)

    @staticmethod
    def semaphores(pieces, ways):
        dma = pltpu.SemaphoreType.DMA
        return [dma((pieces, ways // 2 - 1))] * 2 + [dma((pieces, ways // 2))] * 2


def small_rows(sm, m, count, slots, part, scattered=False):
    def block(slot):
        return sm[pl.ds(slot * 32, 16), :].astype(f32)

    if not scattered:
        return jnp.concatenate([block(slot)[m : m + 1] for slot in range(slots)], axis=1)
    total = block(0)
    for slot in range(1, slots):
        total = total + block(slot)
    return jnp.concatenate([total[m + j : m + j + 1] for j in range(count)], axis=1)


def enter_kernel(
    ways, nt, axes, heads,
    boundary, small, s0, s1, s2, s3, seg_col, seg_row, frequency,
    source, cotangent, small_all, f0, f1, f2, f3, o0, o1, o2, o3,
    cos_out, sin_a_out, sin_b_out, xh_out, inv_out,
    ar_out, qr_out, kr_out, vr_out, act_out, slope_out,
    x_send, x_recv, y_send, y_recv, c_send, c_recv, z_send, z_recv,
    b0, b1, b2, b3, local, keep_sem, out_sem,
    xv, sm, n1, n2, wq, w1, packed, cos, sin_a, sin_b, xh, inv, ar, qr, kr, vr, act, slope,
):
    shards, bounce = (s0, s1, s2, s3), (b0, b1, b2, b3)
    shapes = [s.shape for s in shards]
    full, later = (f0, f1, f2, f3), (o0, o1, o2, o3)
    p, d, t = lax.axis_index("pipe"), lax.axis_index("dp"), lax.axis_index("tensor")
    sems = (y_send, y_recv, c_send, c_recv)
    now = Spread(full, shapes, axes, ways, sems)
    then = Spread(later, shapes, axes, ways, sems)
    ring, chunks, part = now.ring, now.chunks, now.part
    length = boundary.shape[1]
    rows = length // nt
    across = {"pipe": 1 - p}
    others = [{"tensor": lax.rem(t + step, nt)} for step in range(1, nt)]
    places = [
        (lax.rem(d // 2 + o, ring) * 2 + lax.rem(d + b, 2)) * part
        for o in range(ring)
        for b in range(2)
    ]
    mine = pl.ds(pl.multiple_of(t * rows, rows), rows)

    loads = [pltpu.make_async_copy(shards[m], bounce[m], local.at[m]) for m in range(4)]
    for load in loads:
        load.start()
    keeps = [
        pltpu.make_async_copy(
            boundary.at[p, :, pl.ds(pl.multiple_of(places[r], part), part)],
            xv.at[:, pl.ds(r * part, part)],
            keep_sem.at[r],
        )
        for r in range(ways)
    ]
    greet([across, now.core] + now.ahead + others)

    def in_shard(n):
        m, row, col = chunks[n]
        return shards[m].at[pl.ds(row, part), pl.ds(col, part)]

    def small_at(slot, count=32, row=0):
        return small_all.at[pl.ds(slot * 32 + row, count), :]

    def x_given(r, target):
        return to(
            boundary.at[1 - p, mine, pl.ds(pl.multiple_of(places[r], part), part)],
            target.at[mine, pl.ds(r * part, part)],
            x_send.at[r], x_recv.at[r], across,
        )

    def x_small():
        here = small_all.at[pl.ds(pl.multiple_of(p * 16, 16), 16), :]
        return to(small, here, x_send.at[ways], x_recv.at[ways], across)

    def x_copy(n, target):
        at = ways + 1 + n
        return to(in_shard(n), target, x_send.at[at], x_recv.at[at], across)

    def small_y(step):
        target = small_at(2 * ((ring - step) % ring))
        return to(
            small_at(0), target, y_send.at[last, step - 1], y_recv.at[last, step - 1],
            now.ahead[step - 1],
        )

    def small_c(o):
        target = small_at(2 * o + 1)
        return to(small_at(2 * o), target, c_send.at[last, o], c_recv.at[last, o], now.core)

    def stores(matrices):
        return [
            pltpu.make_async_copy(
                bounce[m],
                matrices[m].at[pl.ds(0, shapes[m][0]), :]
                if axes[m] == 0
                else matrices[m].at[:, pl.ds(0, shapes[m][1])],
                local.at[m],
            )
            for m in range(4)
        ]

    last = len(chunks)
    small_own = pltpu.make_async_copy(
        small, small_all.at[pl.ds(pl.multiple_of(p * 16, 16), 16), :], local.at[4]
    )
    small_own.start()
    x_small().start()

    @pl.when(p == 0)
    def _():
        for r in range(ways):
            x_given(r, source).start()

    @pl.when(p == 1)
    def _():
        for r in range(ways):
            x_given(r, cotangent).start()

    for keep in keeps:
        keep.start()
    for load in loads:
        load.wait()

    @pl.when(p == 0)
    def _():
        for store in stores(full):
            store.start()
        for n in range(last):
            x_copy(n, now.at(n, 0)).start()
            now.begin(n, in_shard(n))

    @pl.when(p == 1)
    def _():
        for store in stores(later):
            store.start()
        for n in range(last):
            x_copy(n, then.at(n, 0)).start()

    for keep in keeps:
        keep.wait()

    def kept_store(target):
        return pltpu.make_async_copy(xv, target, keep_sem.at[0])

    @pl.when(p == 0)
    def _():
        kept_store(source).start()

    @pl.when(p == 1)
    def _():
        kept_store(cotangent).start()

    small_own.wait()
    x_small().wait_recv()
    for step in range(1, ring):
        small_y(step).start()
    small_c(0).start()

    def table(block, _):
        at = pl.ds(pl.multiple_of(block * BAND, BAND), BAND)
        same = seg_col[at, :] == seg_row[...]
        key = lax.broadcasted_iota(jnp.int32, (BAND, length), 1)
        start = jnp.min(jnp.where(same, key, length), axis=1, keepdims=True)
        place = lax.broadcasted_iota(jnp.int32, (BAND, 1), 0) + block * BAND
        angle = (place - start).astype(f32) * frequency[...]
        lane = lax.broadcasted_iota(jnp.int32, (BAND, ROT), 1)
        sine = jnp.sin(angle)
        cos[at, :] = jnp.cos(angle)
        sin_a[at, :] = jnp.where(lane < 32, -sine, 0.0)
        sin_b[at, :] = jnp.where((lane >= 32) & (lane < 64), sine, 0.0)
        return 0

    lax.fori_loop(0, length // BAND, table, 0)
    outs = []

    def give(at, ref, target):
        outs.append(pltpu.make_async_copy(ref, target, out_sem.at[at]))
        outs[-1].start()

    give(0, cos, cos_out)
    give(1, sin_a, sin_a_out)
    give(2, sin_b, sin_b_out)

    kept_store(source).wait()
    for r in range(ways):
        x_given(r, source).wait_recv()

    def z_copy(step, ref):
        return to(
            ref.at[mine, :], ref.at[mine, :], z_send.at[step - 1], z_recv.at[step - 1],
            others[step - 1],
        )

    @pl.when(p == 0)
    def _():
        for step in range(1, nt):
            z_copy(step, cotangent).start()

    @pl.when(p == 1)
    def _():
        for step in range(1, nt):
            z_copy(step, source).start()

    for step in range(1, ring):
        small_y(step).wait_recv()
        small_c((ring - step) % ring).start()

    def norm():
        for step in range(1, nt):
            z_copy(step, source).wait_recv()
        for o in range(ring):
            small_c(o).wait()
        vectors = pltpu.make_async_copy(small_all, sm, keep_sem.at[1])
        vectors.start()

        @pl.when(p == 1)
        def _():
            whole = pltpu.make_async_copy(source, xv, keep_sem.at[0])
            whole.start()
            whole.wait()

        vectors.wait()
        g1, b1, g2, b2 = (small_rows(sm, m, 1, ways, part) for m in range(4))

        def block(step, _):
            at = pl.ds(pl.multiple_of(step * 128, 128), 128)
            x = xv[at, :].astype(f32)
            x = x - jnp.mean(x, axis=1, keepdims=True)
            inv_std = lax.rsqrt(jnp.mean(x * x, axis=1, keepdims=True) + norm_epsilon)
            x = x * inv_std
            inv[at, :] = inv_std
            xh[at, :] = x.astype(bf16)
            n1[at, :] = (x * g1 + b1).astype(bf16)
            n2[at, :] = (x * g2 + b2).astype(bf16)
            return 0

        lax.fori_loop(0, length // 128, block, 0)
        give(3, xh, xh_out)
        give(4, inv, inv_out)
        now.arrived(0)
        stores(full)[0].wait()
        pltpu.make_async_copy(full[0], wq, keep_sem.at[2]).start()

    size = wq.shape[1] // heads // 3

    def attention(h):
        if h == 0:
            pltpu.make_async_copy(full[0], wq, keep_sem.at[2]).wait()
            now.arrived(1)
            stores(full)[1].wait()
            pltpu.make_async_copy(full[1], w1, keep_sem.at[3]).start()
        cols = pl.ds(h * 3 * size, 3 * size)

        def block(step, _):
            at = pl.ds(pl.multiple_of(step * BAND, BAND), BAND)
            packed[at, :] = dot(n1[at, :], wq[:, cols])
            return 0

        lax.fori_loop(0, length // BAND, block, 0)
        bias = small_rows(sm, 6, heads * 3 * size // part, ways, part, True)
        bias = bias[:, h * 3 * size : (h + 1) * 3 * size]
        at = pl.ds(h * size, size)
        attend_kernel(
            1.0 / math.sqrt(size), packed, bias, cos, sin_a, sin_b, seg_col, seg_row,
            ar.at[:, at], qr.at[:, at], kr.at[:, at], vr.at[:, at],
        )
        if h == heads - 1:
            for n, (ref, target) in enumerate(
                ((ar, ar_out), (qr, qr_out), (kr, kr_out), (vr, vr_out))
            ):
                give(5 + n, ref, target)

    hidden = w1.shape[1] // part
    bias_row = 6 + heads * 3 * size // part

    def feed(j):
        if j == 0:
            pltpu.make_async_copy(full[1], w1, keep_sem.at[3]).wait()
        cols = pl.ds(j * part, part)
        bias = small_rows(sm, bias_row + j, 1, ways, part, True)

        def block(step, _):
            at = pl.ds(pl.multiple_of(step * BAND, BAND), BAND)
            act[at, cols], slope[at, cols] = gelu_parts(dot(n2[at, :], w1[:, cols]) + bias)
            return 0

        lax.fori_loop(0, length // BAND, block, 0)
        if j == hidden - 1:
            give(9, act, act_out)
            give(10, slope, slope_out)

    work = [[] for _ in range(last)]
    begin = min(7, last - 1)
    steps = [norm] + [functools.partial(attention, h) for h in range(heads)]
    for n, step in enumerate(steps):
        work[min(begin + n, last - 1)].append(step)
    for j in range(hidden):
        work[min(begin + len(steps) + j // 2, last - 1)].append(functools.partial(feed, j))

    for n in range(last):
        x_copy(n, now.at(n, 0)).wait_recv()

        @pl.when(p == 1)
        def _():
            now.begin(n, now.at(n, 0))

        if n > 0:
            now.forward(n - 1)
        for step in work[n]:
            step()
    now.forward(last - 1)

    now.finish((0, 1))
    for n in range(last):
        x_copy(n, now.at(n, 0)).wait_send()
    for step in range(1, ring):
        small_y(step).wait_send()
    x_small().wait_send()
    for r in range(ways):
        x_given(r, source).wait_send()
    for step in range(1, nt):
        z_copy(step, source).wait_send()
    for store in stores(full)[2:]:
        store.wait()
    for out in outs:
        out.wait()


def enter_section(boundary, small, shards, seg, axes, ways, nt, heads):
    hbm, vmem = pl.BlockSpec(memory_space=pl.ANY), pl.BlockSpec(memory_space=pltpu.VMEM)
    shape = jax.ShapeDtypeStruct
    part = shards[3].shape[1]
    length, width = boundary.shape[1:]
    pieces = len(chunks_of([s.shape for s in shards], axes, part))
    full = [
        shape((s.shape[0] * ways, s.shape[1]) if axis == 0 else (s.shape[0], s.shape[1] * ways), bf16)
        for s, axis in zip(shards, axes)
    ]
    dma = pltpu.SemaphoreType.DMA
    lane = jnp.arange(ROT, dtype=f32)
    frequency = jnp.exp(-math.log(10000.0) * 2.0 * (lane % 32) / 64)
    frequency = jnp.where(lane < 64, frequency, 0.0)[None]
    inner, columns = shards[0].shape[1], shards[1].shape[1]
    results = (
        [shape((length, ROT), f32)] * 3
        + [shape((length, width), bf16), shape((length, 1), f32)]
        + [shape((length, inner // 3), bf16)] * 4
        + [shape((length, columns), bf16)] * 2
    )
    out = pl.pallas_call(
        functools.partial(enter_kernel, ways, nt, axes, heads),
        in_specs=[hbm] * 6 + [vmem] * 3,
        out_specs=[hbm] * (11 + len(results)),
        out_shape=[
            shape((length, width), bf16),
            shape((length, width), bf16),
            shape((32 * ways, part), bf16),
            *full,
            *full,
            *results,
        ],
        scratch_shapes=[
            dma((ways + 1 + pieces,)),
            dma((ways + 1 + pieces,)),
            *Spread.semaphores(pieces + 1, ways),
            dma((nt - 1,)),
            dma((nt - 1,)),
            *[pltpu.VMEM(s.shape, bf16) for s in shards],
            dma((5,)),
            dma((max(ways, 4),)),
            dma((11,)),
            pltpu.VMEM((length, width), bf16),
            pltpu.VMEM((32 * ways, part), bf16),
            pltpu.VMEM((length, width), bf16),
            pltpu.VMEM((length, width), bf16),
            pltpu.VMEM(full[0].shape, bf16),
            pltpu.VMEM(full[1].shape, bf16),
            pltpu.VMEM((length, inner // heads), f32),
            *[pltpu.VMEM(r.shape, r.dtype) for r in results],
        ],
        compiler_params=pltpu.CompilerParams(
            collective_id=1, has_side_effects=True, vmem_limit_bytes=62 << 20
        ),
        cost_estimate=pl.CostEstimate(flops=0, bytes_accessed=600 << 20, transcendentals=0),
        name="enter_section",
    )(boundary, small, *shards, seg.reshape(-1, 1), seg.reshape(1, -1), frequency)
    return out[0], out[1], out[2], out[3:7], out[7:11], out[11:]


SUBS = 8


class LineSum:
    def __init__(self, n, partial, right, left, sems, finished, out=None):
        self.n, self.partial, self.right, self.left = n, partial, right, left
        self.finished, self.out = finished, out
        self.r_send, self.r_recv, self.l_send, self.l_recv = sems[:4]
        self.spread = sems[4:]
        self.i = lax.axis_index("tensor")
        self.rows = partial.shape[0] // n
        self.sub = self.rows // SUBS
        self.after = {"tensor": lax.rem(self.i + 1, n)}
        self.before = {"tensor": lax.rem(self.i + n - 1, n)}

    def at(self, ref, j, s):
        start = pl.multiple_of(j * self.rows + s * self.sub, self.sub)
        return ref.at[pl.ds(start, self.sub), :]

    def r_copy(self, j, s, source):
        target = self.at(self.right, j, s)
        return to(source, target, self.r_send.at[j, s], self.r_recv.at[j, s], self.after)

    def l_copy(self, j, s, source):
        target = self.at(self.left, j, s)
        return to(source, target, self.l_send.at[j, s], self.l_recv.at[j, s], self.before)

    def ar_copy(self, j, s):
        rows = self.at(self.out, j, s)
        return to(rows, rows, self.spread[0].at[j, s], self.spread[1].at[j, s], self.after)

    def al_copy(self, j, s):
        rows = self.at(self.out, j, s)
        return to(rows, rows, self.spread[2].at[j, s], self.spread[3].at[j, s], self.before)

    def add(self, ref, j, s):
        ref = self.at(ref, j, s)
        own = self.at(self.partial, j, s)[...].astype(f32)
        ref[...] = (ref[...].astype(f32) + own).astype(bf16)

    def reduce_right(self, s):
        for k in range(self.n - 1):
            j = self.n - 1 - k

            @pl.when(self.i == 0)
            def _():
                self.r_copy(j, s, self.at(self.partial, j, s)).start()

            @pl.when((self.i > 0) & (self.i < j))
            def _():
                self.r_copy(j, s, self.at(self.right, j, s)).wait_recv()
                self.add(self.right, j, s)
                self.r_copy(j, s, self.at(self.right, j, s)).start()

    def reduce_left(self, s):
        for k in range(self.n - 1):

            @pl.when(self.i == self.n - 1)
            def _():
                self.l_copy(k, s, self.at(self.partial, k, s)).start()

            @pl.when((self.i < self.n - 1) & (self.i > k))
            def _():
                self.l_copy(k, s, self.at(self.left, k, s)).wait_recv()
                self.add(self.left, k, s)
                self.l_copy(k, s, self.at(self.left, k, s)).start()

    def finish(self, s):
        i, n = self.i, self.n

        @pl.when(i > 0)
        def _():
            self.r_copy(i, s, self.at(self.right, i, s)).wait_recv()
            self.add(self.right, i, s)

        @pl.when(i == 0)
        def _():
            self.at(self.right, i, s)[...] = self.at(self.partial, i, s)[...]

        @pl.when(i < n - 1)
        def _():
            self.l_copy(i, s, self.at(self.left, i, s)).wait_recv()

        @pl.when(i == n - 1)
        def _():
            self.at(self.left, i, s)[...] = jnp.zeros((self.sub, self.left.shape[1]), bf16)

        total = self.at(self.right, i, s)[...].astype(f32)
        total = total + self.at(self.left, i, s)[...].astype(f32)
        self.finished(self, s, total)
        if self.out is not None:

            @pl.when(i < n - 1)
            def _():
                self.ar_copy(i, s).start()

            @pl.when(i > 0)
            def _():
                self.al_copy(i, s).start()

    def pass_on(self, step, s):
        i, n = self.i, self.n

        @pl.when(i >= step)
        def _():
            self.ar_copy(i - step, s).wait_recv()

            @pl.when(i < n - 1)
            def _():
                self.ar_copy(i - step, s).start()

        @pl.when(i + step < n)
        def _():
            self.al_copy(i + step, s).wait_recv()

            @pl.when(i > 0)
            def _():
                self.al_copy(i + step, s).start()

    @property
    def turns(self):
        return SUBS + (2 * self.n - 2 if self.out is not None else self.n - 1)

    def turn(self, it):
        def when_piece(s, act):
            @pl.when((s >= 0) & (s < SUBS))
            def _():
                act(s)

        when_piece(it - self.i, self.reduce_right)
        when_piece(it - (self.n - 1 - self.i), self.reduce_left)
        when_piece(it - (self.n - 1), self.finish)
        if self.out is not None:
            for step in range(1, self.n):
                when_piece(it - (self.n - 1) - step, functools.partial(self.pass_on, step))

    def drain(self):
        i, n = self.i, self.n

        def body(s, _):
            for j in range(n):

                @pl.when(i < j)
                def _():
                    self.r_copy(j, s, self.at(self.partial, j, s)).wait_send()

                @pl.when(i > j)
                def _():
                    self.l_copy(j, s, self.at(self.partial, j, s)).wait_send()

                if self.out is not None:

                    @pl.when((i >= j) & (i < n - 1))
                    def _():
                        self.ar_copy(j, s).wait_send()

                    @pl.when((i <= j) & (i > 0))
                    def _():
                        self.al_copy(j, s).wait_send()

            return 0

        lax.fori_loop(0, SUBS, body, 0)

    @staticmethod
    def scratch(n, tokens, width, spread):
        return [pltpu.VMEM((tokens, width), bf16)] * 2 + [
            pltpu.SemaphoreType.DMA((n, SUBS))
        ] * (8 if spread else 4)


def sum_spread_kernel(n, ways, axes, shapes, partial, base, *refs):
    out, full, right, left = refs[4], refs[5:9], refs[9], refs[10]
    line_sems, parts_sems = refs[11:19], refs[19:23]

    def finished(line, s, total):
        mine = pl.ds(pl.multiple_of(s * line.sub, line.sub), line.sub)
        line.at(out, line.i, s)[...] = (base[mine, :] + total).astype(bf16)

    line = LineSum(n, partial, right, left, line_sems, finished, out)
    parts = Spread(full, shapes, axes, ways, parts_sems)
    greet([line.after, line.before, parts.core] + parts.ahead)
    count = len(parts.chunks)
    for m in range(count):
        parts.begin(m, parts.at(m, 0))

    def turn_(it, _):
        line.turn(it)
        for m in range(count):

            @pl.when(it == m + 1)
            def _():
                parts.forward(m)

        return 0

    lax.fori_loop(0, max(line.turns, count + 1), turn_, 0)
    line.drain()
    parts.finish()


def sum_spread(partial, base, n, full, shapes, axes, ways):
    tokens, width = partial.shape
    vmem = pl.BlockSpec(memory_space=pltpu.VMEM)
    hbm = pl.BlockSpec(memory_space=pl.ANY)
    pieces = len(chunks_of(shapes, axes, shapes[3][1]))
    out = pl.pallas_call(
        functools.partial(sum_spread_kernel, n, ways, axes, shapes),
        in_specs=[vmem, vmem] + [hbm] * 4,
        out_specs=[vmem] + [hbm] * 4,
        out_shape=[jax.ShapeDtypeStruct((tokens, width), bf16)]
        + [jax.ShapeDtypeStruct(w.shape, bf16) for w in full],
        input_output_aliases={2 + m: 1 + m for m in range(4)},
        scratch_shapes=LineSum.scratch(n, tokens, width, True)
        + Spread.semaphores(pieces, ways),
        compiler_params=pltpu.CompilerParams(
            collective_id=2, has_side_effects=True, vmem_limit_bytes=32 << 20
        ),
        cost_estimate=pl.CostEstimate(flops=0, bytes_accessed=360 << 20, transcendentals=0),
        name="sum_spread",
    )(partial, base, *full)
    return out[0], out[1:]


class GradSum:
    def __init__(self, k, ways, xh, g, lefts, rights, outs, own, scales, vec_out, norms, refs):
        (
            self.from_core, self.from_ring, self.from_pipe,
            self.load, self.away, self.near, self.far, self.core_in, self.ring_in, self.pipe_in,
            self.done, self.weight, self.vec, self.v_held, self.v_round, self.v_across,
            self.load_sem, self.c_send, self.c_recv, self.y_send, self.y_recv,
            self.x_send, self.x_recv, self.out_sem, self.in_sem,
        ) = refs
        self.k, self.ring = k, ways // 2
        self.xh, self.g, self.lefts, self.rights, self.outs = xh, g, lefts, rights, outs
        self.own, self.scales, self.vec_out, self.norms = own, scales, vec_out, norms
        self.part = self.load.shape[2]
        self.counts = [side.shape[1] // self.part for side in (*lefts, *rights)]
        self.starts = [sum(self.counts[:m]) for m in range(4)]
        self.count = sum(self.counts)
        p, d = lax.axis_index("pipe"), lax.axis_index("dp")
        y, c = d // 2, d % 2
        self.p = p
        self.core = {"dp": y * 2 + (1 - c)}
        self.ahead = [{"dp": lax.rem(y + o, self.ring) * 2 + c} for o in range(1, self.ring)]
        self.other = {"pipe": 1 - p}

    def each(self, c, act, matrices=range(4)):
        for m in matrices:

            @pl.when((c >= self.starts[m]) & (c < self.starts[m] + self.counts[m]))
            def _():
                act(m, pl.multiple_of((c - self.starts[m]) * self.part, self.part))

    def fetch(self, c):
        def act(m, at):
            pltpu.make_async_copy(
                self.lefts[m].at[:, pl.ds(at, self.part)],
                self.load.at[lax.rem(c, 3)],
                self.load_sem.at[lax.rem(c, 3)],
            ).start()

        self.each(c, act, (0, 1))

    def fetched(self, c):
        slot = lax.rem(c, 3)
        pltpu.make_async_copy(
            self.lefts[0].at[:, pl.ds(0, self.part)], self.load.at[slot], self.load_sem.at[slot]
        ).wait()

    def piece(self, c, slot, use):
        cols = pl.ds(slot * self.part, self.part)

        @pl.when(c < self.starts[2])
        def _():
            use(dot(self.load[lax.rem(c, 3)], self.g[:, cols], ((0,), (0,))))

        def right(m, at):
            side = self.rights[m - 2][:, pl.ds(at, self.part)]
            use(dot(self.xh[:, cols], side, ((0,), (0,))))

        self.each(c, right, (2, 3))

    def c_copy(self, c, o):
        return to(
            self.away.at[lax.rem(c, 2), o], self.from_core.at[c, o],
            self.c_send.at[c, o], self.c_recv.at[c, o], self.core,
        )

    def y_copy(self, c, o):
        return to(
            self.far.at[lax.rem(c, 3), o - 1], self.from_ring.at[c, o - 1],
            self.y_send.at[c, o - 1], self.y_recv.at[c, o - 1], self.ahead[o - 1],
        )

    def x_copy(self, c):
        return to(
            self.near.at[lax.rem(c, 6)], self.from_pipe.at[c],
            self.x_send.at[c], self.x_recv.at[c], self.other,
        )

    def core_load(self, c, o):
        return pltpu.make_async_copy(
            self.from_core.at[c, o], self.core_in.at[o], self.in_sem.at[0, o]
        )

    def ring_load(self, c, o):
        return pltpu.make_async_copy(
            self.from_ring.at[c, o - 1], self.ring_in.at[o - 1], self.in_sem.at[1, o]
        )

    def pipe_load(self, c):
        return pltpu.make_async_copy(self.from_pipe.at[c], self.pipe_in, self.in_sem.at[1, 0])

    def weight_load(self, m, at):
        return pltpu.make_async_copy(
            self.own[m - 2].at[:, pl.ds(at, self.part)], self.weight, self.in_sem.at[2, 0]
        )

    def store(self, c, start):
        def act(m, at):
            out = self.outs[m]
            if m < 2:
                out = out.at[pl.ds(at, self.part), :]
            else:
                out = out.at[:, pl.ds(at, self.part)]
            copy = pltpu.make_async_copy(self.done, out, self.out_sem.at[0])
            copy.start() if start else copy.wait()

        self.each(c, act)

    @property
    def turns(self):
        return self.count + 5

    def begin(self):
        self.fetch(0)
        self.fetch(1)
        self.vec[...] = jnp.zeros(self.vec.shape, f32)

    def v_copy(self, stage, o=1):
        last = self.count
        if stage == 0:
            return to(
                self.vec, self.v_held, self.c_send.at[last, 0], self.c_recv.at[last, 0], self.core
            )
        if stage == 1:
            return to(
                self.v_held, self.v_round.at[o - 1],
                self.y_send.at[last, o - 1], self.y_recv.at[last, o - 1], self.ahead[o - 1],
            )
        return to(
            self.vec_out, self.v_across, self.x_send.at[last], self.x_recv.at[last], self.other
        )

    def turn(self, it, v_start):
        @pl.when((it >= 1) & (it < self.count + 1))
        def _():
            for o in range(self.ring):
                self.c_copy(it - 1, o).wait_recv()
                self.core_load(it - 1, o).start()

        @pl.when((it >= 3) & (it < self.count + 3))
        def _():
            for o in range(1, self.ring):
                self.y_copy(it - 3, o).wait_recv()
                self.ring_load(it - 3, o).start()

        at_end = (it >= 5) & (it < self.count + 5) & (self.p == self.k)

        @pl.when(at_end)
        def _():
            self.x_copy(it - 5).wait_recv()
            self.pipe_load(it - 5).start()
            self.each(it - 5, lambda m, at: self.weight_load(m, at).start(), (2, 3))

        @pl.when(it < self.count)
        def _():
            c = it

            @pl.when(c < self.starts[2])
            def _():
                self.fetched(c)

            for o in range(self.ring):

                @pl.when(c >= 2)
                def _():
                    self.c_copy(c - 2, o).wait_send()

                def use(value):
                    self.away[lax.rem(c, 2), o] = value.astype(bf16)

                self.piece(c, 2 * o + 1, use)
                self.c_copy(c, o).start()

        @pl.when((it >= 1) & (it < self.count + 1))
        def _():
            c = it - 1
            for o in range(self.ring - 1, -1, -1):
                self.core_load(c, o).wait()
                if o > 0:

                    @pl.when(c >= 3)
                    def _():
                        self.y_copy(c - 3, o).wait_send()

                    def use(value):
                        value = value + self.core_in[o].astype(f32)
                        self.far[lax.rem(c, 3), o - 1] = value.astype(bf16)

                    self.piece(c, 2 * o, use)
                    self.y_copy(c, o).start()
                else:

                    @pl.when((c >= 6) & (self.p != self.k))
                    def _():
                        self.x_copy(c - 6).wait_send()

                    def use(value):
                        value = value + self.core_in[o].astype(f32)
                        self.near[lax.rem(c, 6)] = value.astype(bf16)

                    self.piece(c, 0, use)
            self.fetch(c + 2)

        @pl.when((it >= 3) & (it < self.count + 3))
        def _():
            c = it - 3
            total = self.near[lax.rem(c, 6)].astype(f32)
            for o in range(1, self.ring):
                self.ring_load(c, o).wait()
                total = total + self.ring_in[o - 1].astype(f32)
            self.near[lax.rem(c, 6)] = total.astype(bf16)

            @pl.when(self.p != self.k)
            def _():
                self.x_copy(c).start()

        @pl.when(at_end)
        def _():
            c = it - 5

            @pl.when(c >= 1)
            def _():
                self.store(c - 1, False)

            self.pipe_load(c).wait()
            core = self.near[lax.rem(c, 6)].astype(f32) + self.pipe_in[...].astype(f32)

            @pl.when(c < self.starts[2])
            def _():
                self.done[...] = core

            def finish(m, at):
                gain, bias = self.scales[:, 2 * m - 4 : 2 * m - 3], self.scales[:, 2 * m - 3 : 2 * m - 2]
                row = self.vec_out[pl.ds(c - self.starts[2], 1), :]
                self.done[...] = gain * core + bias * row
                self.weight_load(m, at).wait()
                weight = self.weight[...].astype(f32)
                lane = lax.broadcasted_iota(jnp.int32, self.norms.shape, 1)
                gain_sum = jnp.sum(weight * core, axis=1, keepdims=True)
                bias_sum = jnp.sum(weight * row, axis=1, keepdims=True)
                both = jnp.where(lane == 2 * m - 4, gain_sum, 0.0)
                both = both + jnp.where(lane == 2 * m - 3, bias_sum, 0.0)
                self.norms[...] = self.norms[...] + both

            self.each(c, finish, (2, 3))
            self.store(c, True)

        @pl.when(it == v_start)
        def _():
            self.v_copy(0).start()

        @pl.when(it == v_start + 1)
        def _():
            self.v_copy(0).wait()
            self.v_held[...] = self.v_held[...] + self.vec[...]
            for o in range(1, self.ring):
                self.v_copy(1, o).start()

        @pl.when(it == v_start + 3)
        def _():
            total = self.v_held[...]
            for o in range(1, self.ring):
                self.v_copy(1, o).wait()
                total = total + self.v_round[o - 1]
            self.vec_out[...] = total

            @pl.when(self.p != self.k)
            def _():
                self.v_copy(2).start()

        @pl.when((it == v_start + 5) & (self.p == self.k))
        def _():
            self.v_copy(2).wait_recv()
            self.vec_out[...] = self.vec_out[...] + self.v_across[...]

    def drain(self):
        last = self.count
        for o in range(self.ring):
            for c in (last - 2, last - 1):
                self.c_copy(c, o).wait_send()
            for c in (last - 3, last - 2, last - 1):
                if o > 0:
                    self.y_copy(c, o).wait_send()

        @pl.when(self.p == self.k)
        def _():
            self.store(jnp.int32(last - 1), False)

        @pl.when(self.p != self.k)
        def _():
            self.v_copy(2).wait_send()
            for c in range(last - 6, last):
                self.x_copy(c).wait_send()

    @staticmethod
    def landing(ways, part, count):
        ring = ways // 2
        return [
            jax.ShapeDtypeStruct((count, *lead, part, part), bf16)
            for lead in ((ring,), (ring - 1,), ())
        ]

    @staticmethod
    def scratch(ways, part, tokens, count):
        ring = ways // 2
        dma = pltpu.SemaphoreType.DMA
        return [
            pltpu.VMEM((3, tokens, part), bf16),
            pltpu.VMEM((2, ring, part, part), bf16),
            pltpu.VMEM((6, part, part), bf16),
            pltpu.VMEM((3, ring - 1, part, part), bf16),
            pltpu.VMEM((ring, part, part), bf16),
            pltpu.VMEM((ring - 1, part, part), bf16),
            pltpu.VMEM((part, part), bf16),
            pltpu.VMEM((part, part), f32),
            pltpu.VMEM((part, part), bf16),
            pltpu.VMEM((16, part), f32),
            pltpu.VMEM((16, part), f32),
            pltpu.VMEM((ring - 1, 16, part), f32),
            pltpu.VMEM((16, part), f32),
            dma((3,)),
            dma((count + 1, ring)),
            dma((count + 1, ring)),
            dma((count + 1, ring - 1)),
            dma((count + 1, ring - 1)),
            dma((count + 1,)),
            dma((count + 1,)),
            dma((1,)),
            dma((3, max(ring, 2))),
        ]


class BackWork:
    def __init__(self, ways, heads, g, tables, segs, gains, hbm, dq, dh, u, vec, refs):
        self.wq, self.w1, self.w2, self.wd, self.qr, self.kr, self.vr, self.slope = hbm
        (
            self.wa, self.wb, self.hq, self.hk, self.hv, self.sl, self.d_ar,
            self.q_sum, self.dk, self.dv, self.sem,
        ) = refs
        self.ways, self.heads, self.g, self.vec = ways, heads, g, vec
        self.tables, self.segs, self.gains = tables, segs, gains
        self.dq, self.dh, self.u_rows = dq, dh, u
        self.part = g.shape[1] // ways
        self.size = self.qr.shape[1] // heads
        pieces = [("head", h) for h in range(heads)]
        pieces += [("hidden", j) for j in range(dh.shape[1] // self.part)]
        pieces += [("rows", j) for j in range(ways)]
        self.pieces = pieces

    def loads(self, n):
        kind, j = self.pieces[n]
        slot, part, size = n % 2, self.part, self.size
        width, hidden, inner = self.g.shape[1], self.dh.shape[1], self.dq.shape[1]
        if kind == "head":
            cols = pl.ds(j * size, size)
            pairs = [(self.wd.at[cols, :], self.wa.at[slot, pl.ds(0, size), pl.ds(0, width)])]
            pairs += [
                (ref.at[:, cols], held.at[slot])
                for ref, held in ((self.qr, self.hq), (self.kr, self.hk), (self.vr, self.hv))
            ]
        elif kind == "hidden":
            at = pl.ds(j * part, part)
            pairs = [
                (self.w2.at[at, :], self.wa.at[slot, pl.ds(0, part), pl.ds(0, width)]),
                (self.slope.at[:, at], self.sl.at[slot]),
            ]
        else:
            at = pl.ds(j * part, part)
            pairs = [
                (self.w1.at[at, :], self.wa.at[slot, pl.ds(0, part), pl.ds(0, hidden)]),
                (self.wq.at[at, :], self.wb.at[slot, :, pl.ds(0, inner)]),
            ]
        return [
            pltpu.make_async_copy(source, target, self.sem.at[slot, i])
            for i, (source, target) in enumerate(pairs)
        ]

    def begin(self, n):
        if n < len(self.pieces):
            for load in self.loads(n):
                load.start()

    def run(self, n):
        for load in self.loads(n):
            load.wait()
        self.begin(n + 1)
        kind, j = self.pieces[n]
        getattr(self, kind)(j, n % 2)

    def blocks(self, act):
        def body(step, _):
            act(pl.ds(pl.multiple_of(step * BAND, BAND), BAND))
            return 0

        lax.fori_loop(0, self.g.shape[0] // BAND, body, 0)

    def head(self, h, slot):
        size, width = self.size, self.g.shape[1]
        weight = self.wa.at[slot, pl.ds(0, size), pl.ds(0, width)]

        def act(at):
            self.d_ar[at, :] = dot(self.g[at, :], weight[...], ((1,), (1,))).astype(bf16)

        self.blocks(act)
        attend_back_kernel(
            1.0 / math.sqrt(size), self.hq.at[slot], self.hk.at[slot], self.hv.at[slot],
            self.d_ar, *self.tables, *self.segs,
            self.dq.at[:, pl.ds(h * 3 * size, 3 * size)], self.q_sum.at[pl.ds(h, 1)],
            self.dk, self.dv,
        )
        if h == self.heads - 1:
            sums = jnp.concatenate([self.q_sum[i] for i in range(self.heads)], axis=1)
            for row in range(sums.shape[1] // self.part):
                self.vec[row : row + 1, :] = sums[:, row * self.part : (row + 1) * self.part]

    def hidden(self, j, slot):
        part, width = self.part, self.g.shape[1]
        weight = self.wa.at[slot, pl.ds(0, part), pl.ds(0, width)]
        cols = pl.ds(j * part, part)
        first = self.dq.shape[1] // part
        row = first + j
        self.vec[row : row + 1, :] = jnp.zeros((1, part), f32)

        def act(at):
            value = dot(self.g[at, :], weight[...], ((1,), (1,)))
            value = (self.sl[slot, at, :].astype(f32) * value).astype(bf16)
            self.dh[at, cols] = value
            self.vec[row : row + 1, :] += jnp.sum(value.astype(f32), axis=0, keepdims=True)

        self.blocks(act)
        if j == 0:
            d = lax.axis_index("dp")
            ring = self.ways // 2
            for r in range(self.ways):
                place = lax.rem(d // 2 + r // 2, ring) * 2 + lax.rem(d + r % 2, 2)
                total = jnp.sum(self.g[:, pl.ds(r * part, part)].astype(f32), axis=0, keepdims=True)
                self.vec[pl.ds(first + self.dh.shape[1] // part + place, 1), :] = total

    def rows(self, j, slot):
        part, hidden, inner = self.part, self.dh.shape[1], self.dq.shape[1]
        weight_1 = self.wa.at[slot, pl.ds(0, part), pl.ds(0, hidden)]
        weight_q = self.wb.at[slot, :, pl.ds(0, inner)]
        cols = pl.ds(j * part, part)
        gain_1, gain_2 = (gain[:, cols] for gain in self.gains)

        def act(at):
            value = dot(self.dq[at, :], weight_q[...], ((1,), (1,))) * gain_1
            value = value + dot(self.dh[at, :], weight_1[...], ((1,), (1,))) * gain_2
            self.u_rows[at, cols] = value.astype(bf16)

        self.blocks(act)

    @staticmethod
    def scratch(ways, heads, tokens, width, hidden, size):
        part = width // ways
        return [
            pltpu.VMEM((2, max(part, size), max(width, hidden)), bf16),
            pltpu.VMEM((2, part, 3 * heads * size), bf16),
            *[pltpu.VMEM((2, tokens, size), bf16)] * 3,
            pltpu.VMEM((2, tokens, part), bf16),
            pltpu.VMEM((tokens, size), bf16),
            pltpu.VMEM((heads, 1, 3 * size), f32),
            *[pltpu.VMEM((BAND, size), f32)] * 2,
            pltpu.SemaphoreType.DMA((2, 4)),
        ]


def back_kernel(n, ways, heads, k, *refs):
    take = iter(refs)

    def some(count):
        return [next(take) for _ in range(count)]

    g, xh, inv_std, scales = some(4)
    tables, segs, gains = some(3), some(2), some(2)
    weights, attended, slope = some(4), some(3), next(take)
    lefts, own = some(2), some(2)
    if k == 0:
        y_part, y_base = some(2)
        norms_in = next(take)
        some(4)
    vec_out, norms, outs = next(take), next(take), some(4)
    if k == 0:
        rows_out, rows_away, y_rows, y_away, y_land = some(5)
    else:
        out, branch = some(2)
    landing = some(3)
    dq, dh, u, right, left = some(5)
    line_sems = some(4 if k == 0 else 8)
    work_refs = some(11)
    grad_refs = landing + some(22)
    p, t = lax.axis_index("pipe"), lax.axis_index("tensor")
    other = {"pipe": 1 - p}
    if k == 0:
        stage, handed, d_send, d_recv, stage_sem = some(5)
        y_in, y_stage, y_handed, yz_send, yz_recv, yx_send, yx_recv, y_sem = some(8)

    def d_copy(s, sub):
        mine = pl.ds(pl.multiple_of(s * sub, sub), sub)
        return to(handed.at[mine, :], rows_away.at[mine, :], d_send.at[s], d_recv.at[s], other)

    def d_store(s, sub):
        mine = pl.ds(pl.multiple_of(s * sub, sub), sub)
        slot = lax.rem(s, 2)
        return pltpu.make_async_copy(stage.at[slot], rows_out.at[mine, :], stage_sem.at[slot])

    def finished(line, s, total):
        mine = pl.ds(pl.multiple_of(s * line.sub, line.sub), line.sub)
        xr = line.at(xh, line.i, s)[...].astype(f32)
        mean = jnp.mean(total, axis=1, keepdims=True)
        proj = jnp.mean(total * xr, axis=1, keepdims=True)
        total = inv_std[mine, :] * (total - mean - xr * proj)
        total = line.at(g, line.i, s)[...].astype(f32) + total
        if k == 1:
            line.at(out, line.i, s)[...] = total.astype(bf16)
        else:

            @pl.when(s >= 2)
            def _():
                d_store(s - 2, line.sub).wait()

            stage[lax.rem(s, 2)] = total
            d_store(s, line.sub).start()
            handed[mine, :] = total.astype(bf16)

            @pl.when(p == 1)
            def _():
                d_copy(s, line.sub).start()

    line = LineSum(n, u, right, left, line_sems, finished, out if k else None)
    vec = grad_refs[12]
    work = BackWork(
        ways, heads, g, tables, segs, gains, (*weights, *attended, slope), dq, dh, u, vec,
        work_refs,
    )
    grads = GradSum(k, ways, xh, g, lefts, (dq, dh), outs, own, scales, vec_out, norms, grad_refs)
    places = [line.after, line.before, grads.core, grads.other] + grads.ahead
    if k == 0:
        along = [{"tensor": lax.rem(t + step, n)} for step in range(1, n)]
        places = places[2:] + along
    greet(places)
    grads.begin()
    norms[...] = norms_in[...] if k == 0 else jnp.zeros(norms.shape, f32)
    work.begin(0)

    count = len(work.pieces)
    last_hidden = heads + dh.shape[1] // work.part
    middle = (last_hidden + count) // 2
    if k == 1:
        plan = [
            range(0, 0), range(0, heads), range(heads, last_hidden),
            range(last_hidden, middle), range(middle, count),
        ]
    else:
        per = -(-count // 6)
        plan = [range(0, 0)] + [range(at, min(at + per, count)) for at in range(0, count, per)]
    v_start = 1 + next(i for i, some_ in enumerate(plan) if last_hidden - 1 in some_)
    begin = len(plan)

    if k == 0:
        block = y_base.shape[0] // 4
        width = y_base.shape[1]

        def yz_copy(step):
            owner = lax.rem(t + step, n)
            rows = y_base.shape[0]
            theirs = pl.ds(pl.multiple_of(owner * rows, rows), rows)
            return to(
                y_part.at[theirs, :], y_land.at[step - 1], yz_send.at[step - 1],
                yz_recv.at[step - 1], along[step - 1],
            )

        def yx_copy(q):
            mine = pl.ds(q * block, block)
            return to(y_handed.at[mine, :], y_away.at[mine, :], yx_send.at[q], yx_recv.at[q], other)

        def y_store(q):
            mine = pl.ds(q * block, block)
            return pltpu.make_async_copy(y_stage, y_rows.at[mine, :], y_sem.at[n + 1])

        def y_finish(q):
            mine = pl.ds(q * block, block)
            if q == 0:
                for step in range(1, n):
                    yz_copy(step).wait_recv()
            else:
                y_store(q - 1).wait()
            start = pl.multiple_of(t * y_base.shape[0] + q * block, block)
            loads = [pltpu.make_async_copy(y_part.at[pl.ds(start, block), :], y_in.at[0], y_sem.at[0])]
            loads += [
                pltpu.make_async_copy(y_land.at[step - 1, mine, :], y_in.at[step], y_sem.at[step])
                for step in range(1, n)
            ]
            loads.append(pltpu.make_async_copy(y_base.at[mine, :], y_stage, y_sem.at[n]))
            for load in loads:
                load.start()
            for load in loads:
                load.wait()
            total = y_stage[...]
            for step in range(n):
                total = total + y_in[step].astype(f32)
            y_stage[...] = total
            y_store(q).start()
            y_handed[mine, :] = total.astype(bf16)

            @pl.when(p == 0)
            def _():
                yx_copy(q).start()

        for step in range(1, n):
            yz_copy(step).start()

    b_start = grads.count + 1

    def b_loads(j):
        part = work.part
        cols = pl.ds(j * part, part)
        tokens, hidden = g.shape[0], dh.shape[1]
        half = min(tokens, hidden)
        pairs = [
            (weights[2].at[pl.ds(i * half, half), cols], grads.load.at[i, pl.ds(0, half), :])
            for i in range(hidden // half)
        ]
        rows = weights[3].shape[0]
        pairs.append((weights[3].at[:, cols], work.wb.at[j % 2, pl.ds(0, rows), pl.ds(0, part)]))
        if j == 0:
            pairs += [(lefts[0], dh), (lefts[1], dq.at[:, pl.ds(0, rows)])]
        return [
            pltpu.make_async_copy(source, target, work.sem.at[i // 4, i % 4])
            for i, (source, target) in enumerate(pairs)
        ]

    def b_store(j):
        part = work.part
        return pltpu.make_async_copy(
            work.sl.at[j % 2], branch.at[:, pl.ds(j * part, part)], grads.load_sem.at[j % 2]
        )

    def b_block(j):
        part, hidden = work.part, dh.shape[1]
        half = min(g.shape[0], hidden)
        rows = weights[3].shape[0]
        loads = b_loads(j)
        for load in loads:
            load.start()
        if j >= 2:
            b_store(j - 2).wait()
        for load in loads:
            load.wait()

        def act(at):
            value = dot(dq[at, pl.ds(0, rows)], work.wb[j % 2, pl.ds(0, rows), pl.ds(0, part)])
            for i in range(hidden // half):
                value = value + dot(
                    dh[at, pl.ds(i * half, half)], grads.load[i, pl.ds(0, half), :]
                )
            work.sl[j % 2, at, :] = value.astype(bf16)

        work.blocks(act)
        b_store(j).start()

    def turn_(it, _):
        @pl.when(it >= begin)
        def _():
            line.turn(it - begin)

        grads.turn(it, v_start)
        for at, some_ in enumerate(plan):
            if len(some_):

                @pl.when(it == at)
                def _():
                    for piece in some_:
                        work.run(piece)

        if k == 0:
            for q in range(4):

                @pl.when(it == begin + 1 + q)
                def _():
                    y_finish(q)

        else:
            for j in range(ways):

                @pl.when(it == b_start + j)
                def _():
                    b_block(j)

        return 0

    total = max(begin + line.turns, grads.turns, b_start + ways if k else 0)
    lax.fori_loop(0, total, turn_, 0)
    line.drain()
    grads.drain()
    if k == 1:
        b_store(ways - 2).wait()
        b_store(ways - 1).wait()
        return
    y_store(3).wait()
    for step in range(1, n):
        yz_copy(step).wait_send()
    for s in (SUBS - 2, SUBS - 1):
        d_store(s, line.sub).wait()

    @pl.when(p == 1)
    def _():
        for s in range(SUBS):
            d_copy(s, line.sub).wait_send()
        for q in range(4):
            yx_copy(q).wait_recv()

    @pl.when(p == 0)
    def _():
        for s in range(SUBS):
            d_copy(s, line.sub).wait_recv()
        for q in range(4):
            yx_copy(q).wait_send()


def back_section(
    k, g, xh, inv_std, scales, tables, seg, gains, weights, attended, slope, lefts, own, heads,
    n, ways, y=None, held=None,
):
    tokens, width = g.shape
    part, rows = width // ways, tokens // n
    hidden, inner = slope.shape[1], 3 * attended[0].shape[1]
    size = inner // 3 // heads
    vmem, hbm = pl.BlockSpec(memory_space=pltpu.VMEM), pl.BlockSpec(memory_space=pl.ANY)
    shape, dma = jax.ShapeDtypeStruct, pltpu.SemaphoreType.DMA
    sides = (lefts[0].shape[1], lefts[1].shape[1], inner, hidden)
    count = sum(sides) // part
    out_shape = [shape((16, part), f32), shape((part, 128), f32)]
    out_specs = [vmem, vmem] + [hbm] * 4
    out_shape += [
        shape((side, part) if m < 2 else (part, side), f32) for m, side in enumerate(sides)
    ]
    if k == 0:
        out_shape += [shape((rows, width), f32), shape((rows, width), bf16)] * 2
        out_shape += [shape((n - 1, rows, width), bf16)]
        out_specs += [hbm] * 5
        block = rows // 4
        extra = [
            pltpu.VMEM((2, rows // SUBS, width), f32),
            pltpu.VMEM((rows, width), bf16),
            dma((SUBS,)),
            dma((SUBS,)),
            dma((2,)),
            pltpu.VMEM((n, block, width), bf16),
            pltpu.VMEM((block, width), f32),
            pltpu.VMEM((rows, width), bf16),
            dma((n - 1,)),
            dma((n - 1,)),
            dma((4,)),
            dma((4,)),
            dma((n + 2,)),
        ]
    else:
        out_shape += [shape((tokens, width), bf16)] * 2
        out_specs += [vmem, hbm]
        extra = []
    landing = GradSum.landing(ways, part, count)
    args = [
        g, xh, inv_std, scales, *tables, seg.reshape(-1, 1), seg.reshape(1, -1), *gains,
        *weights, *attended, slope, *lefts, *own, *(y or ()),
    ]
    specs = [vmem] * 11 + [hbm] * (len(args) - 11)
    aliases = {}
    if k == 0:
        aliases = {len(args) + 1 + m: 2 + m for m in range(4)}
        args += held
        specs += [vmem] + [hbm] * 4
    line = LineSum.scratch(n, tokens, width, k == 1)
    return pl.pallas_call(
        functools.partial(back_kernel, n, ways, heads, k),
        in_specs=specs,
        out_specs=out_specs + [hbm] * 3,
        out_shape=out_shape + landing,
        input_output_aliases=aliases,
        scratch_shapes=[
            pltpu.VMEM((tokens, inner), bf16),
            pltpu.VMEM((tokens, hidden), bf16),
            pltpu.VMEM((tokens, width), bf16),
            *line,
            *BackWork.scratch(ways, heads, tokens, width, hidden, size),
            *GradSum.scratch(ways, part, tokens, count),
            *extra,
        ],
        compiler_params=pltpu.CompilerParams(
            collective_id=3 + k, has_side_effects=True, vmem_limit_bytes=63 << 20
        ),
        cost_estimate=pl.CostEstimate(flops=0, bytes_accessed=600 << 20, transcendentals=0),
        name="back_section",
    )(*args)


def normalize(values):
    average = jnp.mean(values, axis=-1, keepdims=True)
    centred = values - average
    spread = jnp.mean(centred * centred, axis=-1, keepdims=True)
    inv_std = lax.rsqrt(spread + norm_epsilon)
    return (centred * inv_std, inv_std)


def per_device(
    boundary,
    segments,
    ln1_gain,
    ln1_bias,
    ln2_gain,
    ln2_bias,
    qkv_weight,
    qkv_bias,
    dense_weight,
    dense_bias,
    fc1_weight,
    fc1_bias,
    fc2_weight,
    fc2_bias,
):
    pipe, d, t = lax.axis_index("pipe"), lax.axis_index("dp"), lax.axis_index("tensor")
    ways, ring = lax.axis_size("dp"), lax.axis_size("dp") // 2
    nt = lax.axis_size("tensor")
    first = pipe == 0
    seqs, length, width = boundary.shape[1] // 2, boundary.shape[2], boundary.shape[3]
    tokens, rows, part = seqs * length, length // nt, width // ways
    heads, size = qkv_weight.shape[2], qkv_weight.shape[3] // 3
    y, c = d // 2, d % 2

    def pipe_send(v, source):
        return lax.ppermute(v, "pipe", [(source, 1 - source)])

    def true_order(v):
        parts = []
        for j in range(ways):
            place = ((j // 2 - y) % ring) * 2 + (c ^ (j % 2))
            parts.append(lax.dynamic_slice_in_dim(v, place * part, part, v.ndim - 1))
        return jnp.concatenate(parts, axis=-1)

    def together(*values):
        return list(lax.optimization_barrier(values))

    seg = lax.dynamic_slice_in_dim(segments, pipe * seqs, seqs, 0)
    shards = (
        qkv_weight[0].reshape(part, heads * 3 * size),
        fc1_weight[0],
        fc2_weight[0],
        dense_weight[0],
    )
    axes = (0, 0, 1, 1)
    def in_place(v):
        whole = jnp.zeros((v.shape[0], v.shape[1] * ways), bf16)
        whole = lax.dynamic_update_slice_in_dim(whole, v, d * v.shape[1], 1)
        return whole.reshape(-1, part)

    small = [ln1_gain, ln1_bias, ln2_gain, ln2_bias, dense_bias, fc2_bias]
    small = jnp.concatenate(small + [in_place(qkv_bias[0]), in_place(fc1_bias)], axis=0)
    small = jnp.pad(small, ((0, 16 - small.shape[0]), (0, 0)))
    source, cotangent, small_all, weights_0, weights_1, found = enter_section(
        boundary[0], small, shards, seg, axes, ways, nt, heads
    )
    tables, (xh0, inv0, ar0, qr0, kr0, vr0, act0, slope0) = found[:3], found[3:]
    small_all = small_all.reshape(ways, 2, 16, part).astype(f32)
    cut = heads * 3 * size

    def vectors(k):
        rows_ = small_all[:, k]
        found = [rows_[:, m].reshape(1, width) for m in range(6)]
        in_place = jnp.sum(rows_[:, 6:], axis=0).reshape(1, -1)
        return found + [in_place[:, cut : cut + fc1_weight.shape[2]], in_place[:, :cut]]

    def own_rows(v):
        return lax.dynamic_slice_in_dim(v.reshape(seqs, length, width), t * rows, rows, 1)

    def own_rows_of(v):
        return lax.dynamic_slice_in_dim(v, t * rows, rows, 0)

    def enter(k, x):
        g1, b1, g2, b2 = vectors(k)[:4]
        xhat, inv_std = normalize(x.astype(f32))
        n1 = (xhat * g1 + b1).astype(bf16)
        n2 = (xhat * g2 + b2).astype(bf16)
        return n1, n2, xhat.astype(bf16), inv_std

    wq0, w10, w20, wd0 = weights_0
    branch = (dot(ar0, wd0) + dot(act0, w20)).astype(bf16)
    base = (own_rows(source).astype(f32) + (vectors(0)[4] + vectors(0)[5])).reshape(-1, width)
    x1, weights_1 = sum_spread(
        branch, base, nt, weights_1, [shard.shape for shard in shards], axes, ways
    )
    wq1, w11, w21, wd1 = weights_1

    n1, n2, xh1, inv1 = enter(1, x1)
    g1, _, g2, _ = vectors(1)[:4]
    ar1, qr1, kr1, vr1 = attend(dot(n1, wq1), vectors(1)[7], tables, seg, heads, length)
    act1, slope1 = gelu_matmul(n2, w11, vectors(1)[6])

    def column(v):
        return v[0].astype(f32)[:, None]

    scales = jnp.concatenate([column(v) for v in (ln1_gain, ln1_bias, ln2_gain, ln2_bias)], axis=1)
    sums_1, norms, fc2_grad, dense_grad, qkv_grad, fc1_grad, g0, branch, *_ = back_section(
        1, cotangent, xh1, own_rows_of(inv1), scales, tables, seg, (g1, g2), (wq1, w11, w21, wd1),
        (qr1, kr1, vr1), slope1, (act1, ar1), shards[:2], heads, nt, ways,
    )

    g1, _, g2, _ = vectors(0)[:4]
    base = (own_rows(x1).astype(f32) + (vectors(1)[4] + vectors(1)[5])).reshape(-1, width)
    found = back_section(
        0, g0, xh0, own_rows_of(inv0), scales, tables, seg, (g1, g2), weights_0,
        (qr0, kr0, vr0), slope0, (act0, ar0), shards[:2], heads, nt, ways,
        (branch, base), [norms, fc2_grad, dense_grad, qkv_grad, fc1_grad],
    )
    sums_0, norms, fc2_grad, dense_grad, qkv_grad, fc1_grad = found[:6]
    dx_rows, dx_away, y_rows, y_away = (v.reshape(seqs, rows, width) for v in found[6:10])
    dx_away, y_away = dx_away.astype(f32), y_away.astype(f32)

    boundary_out = true_order(
        jnp.where(
            first,
            jnp.concatenate([dx_rows, dx_away], axis=0),
            jnp.concatenate([y_away, y_rows], axis=0),
        )
    )[None]

    sums = jnp.where(first, sums_0, sums_1).reshape(-1)
    end = cut + shards[1].shape[1]
    qkv_sum, fc1_sum, g_sum = sums[:cut], sums[cut:end], sums[end : end + width]
    norms = norms[:, :4].T

    def for_place(step):
        place = lax.rem(t + step, nt) * (part // nt)
        return lax.dynamic_slice_in_dim(norms, place, part // nt, 1)

    norms = for_place(0) + sum(
        lax.ppermute(for_place(step), "tensor", [(i, (i + step) % nt) for i in range(nt)])
        for step in range(1, nt)
    )

    qkv_grad = qkv_grad.reshape(part, heads, 3 * size)

    def own_part(v, axis):
        step = v.shape[axis] // ways
        return lax.dynamic_slice_in_dim(v, d * step, step, axis)

    bias_grad = own_part(g_sum, 0)[None]
    return (
        boundary_out,
        norms[0][None],
        norms[1][None],
        norms[2][None],
        norms[3][None],
        qkv_grad[None],
        own_part(qkv_sum.reshape(heads, 3 * size), 1)[None],
        dense_grad[None],
        bias_grad,
        fc1_grad[None],
        own_part(fc1_sum, 0)[None],
        fc2_grad[None],
        bias_grad,
    )


def solution(mesh):
    in_specs = (
        P("pipe", "dp", None, None),
        P("dp", None),
        P("pipe", "dp"),
        P("pipe", "dp"),
        P("pipe", "dp"),
        P("pipe", "dp"),
        P("pipe", "dp", "tensor", None),
        P("pipe", "tensor", "dp"),
        P("pipe", "tensor", "dp"),
        P("pipe", "dp"),
        P("pipe", "dp", "tensor"),
        P("pipe", ("tensor", "dp")),
        P("pipe", "tensor", "dp"),
        P("pipe", "dp"),
    )
    out_specs = (
        P("pipe", "dp", "tensor", None),
        P("pipe", ("dp", "tensor")),
        P("pipe", ("dp", "tensor")),
        P("pipe", ("dp", "tensor")),
        P("pipe", ("dp", "tensor")),
        P("pipe", "dp", "tensor", None),
        P("pipe", "tensor", "dp"),
        P("pipe", "tensor", "dp"),
        P("pipe", "dp"),
        P("pipe", "dp", "tensor"),
        P("pipe", ("tensor", "dp")),
        P("pipe", "tensor", "dp"),
        P("pipe", "dp"),
    )
    return jax.shard_map(
        per_device, mesh=mesh, in_specs=in_specs, out_specs=out_specs, check_vma=False
    )
```

```python
import functools
import math

import jax
import jax.numpy as jnp
from jax import lax
from jax.experimental import pallas as pl
from jax.experimental.pallas import tpu as pltpu
from jax.sharding import PartitionSpec as P

norm_epsilon = 1e-05
mask_fill = -1e30
BAND = 256
ROT = 128
f32, bf16 = jnp.float32, jnp.bfloat16


def dot(a, b, contract=((1,), (0,))):
    return lax.dot_general(a, b, (contract, ((), ())), preferred_element_type=f32)


def allowed(seg_col, seg_row, block):
    low = max(block - 1, 0) * BAND
    size = (block + 1) * BAND - low
    own = lax.broadcasted_iota(jnp.int32, (BAND, size), 0) + (block * BAND - low)
    key = lax.broadcasted_iota(jnp.int32, (BAND, size), 1)
    rows = pl.ds(block * BAND, BAND)
    return (own >= key) & (seg_col[rows, :] == seg_row[:, pl.ds(low, size)])


def turn(values, cos, forward, backward):
    head = values[:, :ROT]
    head = (
        head * cos
        + pltpu.roll(head, ROT - 32, 1) * forward
        + pltpu.roll(head, 32, 1) * backward
    )
    return jnp.concatenate([head, values[:, ROT:]], axis=1)


def attend_kernel(scale, qkv, bias, cos, sin_a, sin_b, seg_col, seg_row, out, qr, kr, vr):
    size = out.shape[1]
    for block in range(out.shape[0] // BAND):
        rows = pl.ds(block * BAND, BAND)
        c, a, b = cos[rows, :], sin_a[rows, :], sin_b[rows, :]
        q = turn(qkv[rows, :size] + bias[:, :size], c, a, b).astype(bf16)
        k = turn(qkv[rows, size : 2 * size] + bias[:, size : 2 * size], c, a, b).astype(bf16)
        qr[rows, :] = q
        kr[rows, :] = k
        vr[rows, :] = (qkv[rows, 2 * size :] + bias[:, 2 * size :]).astype(bf16)
        low = max(block - 1, 0) * BAND
        keys = pl.ds(low, (block + 1) * BAND - low)
        scores = dot(q, kr[keys, :], ((1,), (1,))) * scale
        scores = jnp.where(allowed(seg_col, seg_row, block), scores, mask_fill)
        weights = jnp.exp(scores - jnp.max(scores, axis=1, keepdims=True))
        weights = weights * (1.0 / jnp.sum(weights, axis=1, keepdims=True))
        out[rows, :] = dot(weights.astype(bf16), vr[keys, :]).astype(bf16)


def attend(qkv, bias, tables, seg, heads, length):
    size = qkv.shape[1] // heads // 3
    seqs = qkv.shape[0] // length
    block = pl.BlockSpec((length, size), lambda b, h: (b, h))
    table = pl.BlockSpec((length, ROT), lambda b, h: (b, 0))
    return pl.pallas_call(
        functools.partial(attend_kernel, 1.0 / math.sqrt(size)),
        grid=(seqs, heads),
        in_specs=[
            pl.BlockSpec((length, 3 * size), lambda b, h: (b, h)),
            pl.BlockSpec((1, 3 * size), lambda b, h: (0, h)),
            table,
            table,
            table,
            pl.BlockSpec((length, 1), lambda b, h: (b, 0)),
            pl.BlockSpec((1, length), lambda b, h: (0, b)),
        ],
        out_specs=[block] * 4,
        out_shape=[jax.ShapeDtypeStruct((qkv.shape[0], heads * size), bf16)] * 4,
        compiler_params=pltpu.CompilerParams(vmem_limit_bytes=48 << 20),
        cost_estimate=pl.CostEstimate(
            flops=2 * 2 * qkv.shape[0] * 2 * BAND * heads * size,
            bytes_accessed=qkv.size * 4 + qkv.shape[0] * heads * size * 8,
            transcendentals=qkv.shape[0] * heads * 2 * BAND,
        ),
        name="attend",
    )(qkv, bias, *tables, seg.reshape(-1, 1), seg.reshape(1, -1))


def attend_back_kernel(
    scale, qr, kr, vr, grad, cos, sin_a, sin_b, seg_col, seg_row, out, out_sum, dk_acc, dv_acc
):
    size = grad.shape[1]
    blocks = grad.shape[0] // BAND
    sums = [jnp.zeros((1, size), f32)] * 3

    def emit(place, part, values):
        rows = pl.ds(place * BAND, BAND)
        if part < 2:
            values = turn(values, cos[rows, :], -sin_a[rows, :], -sin_b[rows, :])
        values = values.astype(bf16)
        out[rows, part * size : (part + 1) * size] = values
        sums[part] = sums[part] + jnp.sum(values.astype(f32), axis=0, keepdims=True)

    for block in range(blocks):
        rows = pl.ds(block * BAND, BAND)
        low = max(block - 1, 0) * BAND
        keys = pl.ds(low, (block + 1) * BAND - low)
        q, k, v, g = qr[rows, :], kr[keys, :], vr[keys, :], grad[rows, :]
        scores = dot(q, k, ((1,), (1,))) * scale
        scores = jnp.where(allowed(seg_col, seg_row, block), scores, mask_fill)
        weights = jnp.exp(scores - jnp.max(scores, axis=1, keepdims=True))
        weights = weights * (1.0 / jnp.sum(weights, axis=1, keepdims=True))
        grad_weights = dot(g, v, ((1,), (1,)))
        row_dot = jnp.sum(weights * grad_weights, axis=1, keepdims=True)
        grad_scores = (weights * (grad_weights - row_dot)).astype(bf16)
        emit(block, 0, dot(grad_scores, k) * scale)
        dk = dot(grad_scores, q, ((0,), (0,))) * scale
        dv = dot(weights.astype(bf16), g, ((0,), (0,)))
        if block > 0:
            emit(block - 1, 1, dk_acc[...] + dk[:BAND])
            emit(block - 1, 2, dv_acc[...] + dv[:BAND])
            dk, dv = dk[BAND:], dv[BAND:]
        if block == blocks - 1:
            emit(block, 1, dk)
            emit(block, 2, dv)
        else:
            dk_acc[...] = dk
            dv_acc[...] = dv
    out_sum[0] = jnp.concatenate(sums, axis=1)


def attend_back(qr, kr, vr, grad, tables, seg, heads, length):
    size = qr.shape[1] // heads
    tokens = qr.shape[0]
    seqs = tokens // length
    block = pl.BlockSpec((length, size), lambda b, h: (b, h))
    table = pl.BlockSpec((length, ROT), lambda b, h: (b, 0))
    out, sums = pl.pallas_call(
        functools.partial(attend_back_kernel, 1.0 / math.sqrt(size)),
        grid=(seqs, heads),
        in_specs=[block] * 4
        + [table] * 3
        + [
            pl.BlockSpec((length, 1), lambda b, h: (b, 0)),
            pl.BlockSpec((1, length), lambda b, h: (0, b)),
        ],
        out_specs=[
            pl.BlockSpec((length, 3 * size), lambda b, h: (b, h)),
            pl.BlockSpec((1, 1, 3 * size), lambda b, h: (b, 0, h)),
        ],
        out_shape=[
            jax.ShapeDtypeStruct((tokens, heads * 3 * size), bf16),
            jax.ShapeDtypeStruct((seqs, 1, heads * 3 * size), f32),
        ],
        scratch_shapes=[pltpu.VMEM((BAND, size), f32)] * 2,
        compiler_params=pltpu.CompilerParams(vmem_limit_bytes=48 << 20),
        cost_estimate=pl.CostEstimate(
            flops=2 * 5 * tokens * 2 * BAND * heads * size,
            bytes_accessed=tokens * heads * size * 14,
            transcendentals=tokens * heads * 2 * BAND,
        ),
        name="attend_back",
    )(qr, kr, vr, grad, *tables, seg.reshape(-1, 1), seg.reshape(1, -1))
    return out, jnp.sum(sums, axis=(0, 1))


def gelu_parts(h):
    t = 1.0 / (1.0 + (0.3275911 * math.sqrt(0.5)) * jnp.abs(h))
    poly = 1.061405429 * t - 1.453152027
    poly = poly * t + 1.421413741
    poly = poly * t - 0.284496736
    poly = poly * t + 0.254829592
    bell = jnp.exp(-0.5 * h * h)
    tail = 0.5 * poly * t * bell
    cdf = jnp.where(h >= 0.0, 1.0 - tail, tail)
    slope = cdf + h * bell * (1.0 / math.sqrt(2.0 * math.pi))
    return (h * cdf).astype(bf16), slope.astype(bf16)


def gelu_back_kernel(x, w, bias, grad, act, d_hidden):
    for row in range(0, x.shape[0], BAND):
        rows = pl.ds(row, BAND)
        act[rows, :], slope = gelu_parts(dot(x[rows, :], w[...]) + bias[...])
        d_hidden[rows, :] = (slope.astype(f32) * grad[rows, :].astype(f32)).astype(bf16)


def gelu_matmul(x, w, bias, grad):
    tokens, depth = x.shape
    width = w.shape[1]
    cols = min(512, width)
    block = pl.BlockSpec((tokens, cols), lambda j: (0, j))
    return pl.pallas_call(
        gelu_back_kernel,
        grid=(width // cols,),
        in_specs=[
            pl.BlockSpec((tokens, depth), lambda j: (0, 0)),
            pl.BlockSpec((depth, cols), lambda j: (0, j)),
            pl.BlockSpec((1, cols), lambda j: (0, j)),
            block,
        ],
        out_specs=[block, block],
        out_shape=[jax.ShapeDtypeStruct((tokens, width), bf16)] * 2,
        compiler_params=pltpu.CompilerParams(vmem_limit_bytes=48 << 20),
        cost_estimate=pl.CostEstimate(
            flops=2 * tokens * depth * width,
            bytes_accessed=2 * (tokens * depth + depth * width + 2 * tokens * width),
            transcendentals=2 * tokens * width,
        ),
        name="gelu_matmul",
    )(x, w, bias, grad)


def to(source, target, send, recv, place):
    return pltpu.make_async_remote_copy(
        src_ref=source,
        dst_ref=target,
        send_sem=send,
        recv_sem=recv,
        device_id=place,
        device_id_type=pl.DeviceIdType.MESH,
    )


def greet(places):
    barrier = pltpu.get_barrier_semaphore()
    for place in places:
        pl.semaphore_signal(
            barrier, inc=1, device_id=place, device_id_type=pl.DeviceIdType.MESH
        )
    pl.semaphore_wait(barrier, len(places))


def chunks_of(shapes, axes, part):
    return [
        (m, row, col)
        for m, (shape, axis) in enumerate(zip(shapes, axes))
        for row in range(0, shape[0], part)
        for col in range(0, shape[1], part)
    ]


def chunk_at(ref, axis, shape, chunk, slot, part):
    _, row, col = chunk
    row, col = (row + slot * shape[0], col) if axis == 0 else (row, col + slot * shape[1])
    return ref.at[pl.ds(row, part), pl.ds(col, part)]


class Spread:
    def __init__(self, full, shapes, axes, ways, sems):
        self.full, self.shapes, self.axes = full, shapes, axes
        self.ring = ways // 2
        self.y_send, self.y_recv, self.c_send, self.c_recv = sems
        self.part = shapes[3][1]
        self.chunks = chunks_of(shapes, axes, self.part)
        d = lax.axis_index("dp")
        y, c = d // 2, d % 2
        self.core = {"dp": y * 2 + (1 - c)}
        self.ahead = [{"dp": lax.rem(y + o, self.ring) * 2 + c} for o in range(1, self.ring)]

    def at(self, n, slot):
        m = self.chunks[n][0]
        return chunk_at(
            self.full[m], self.axes[m], self.shapes[m], self.chunks[n], slot, self.part
        )

    def y_copy(self, n, step, source):
        target = self.at(n, 2 * ((self.ring - step) % self.ring))
        return to(
            source, target, self.y_send.at[n, step - 1], self.y_recv.at[n, step - 1],
            self.ahead[step - 1],
        )

    def c_copy(self, n, o, source):
        target = self.at(n, 2 * o + 1)
        return to(source, target, self.c_send.at[n, o], self.c_recv.at[n, o], self.core)

    def begin(self, n, source):
        for step in range(1, self.ring):
            self.y_copy(n, step, source).start()
        self.c_copy(n, 0, source).start()

    def forward(self, n):
        for step in range(1, self.ring):
            o = (self.ring - step) % self.ring
            self.y_copy(n, step, self.at(n, 0)).wait_recv()
            self.c_copy(n, o, self.at(n, 2 * o)).start()

    def arrived(self, m):
        for n in range(len(self.chunks)):
            if self.chunks[n][0] == m:
                for o in range(self.ring):
                    self.c_copy(n, o, self.at(n, 2 * o)).wait_recv()

    def finish(self, waited=()):
        for n in range(len(self.chunks)):
            for step in range(1, self.ring):
                self.y_copy(n, step, self.at(n, 0)).wait_send()
            for o in range(self.ring):
                self.c_copy(n, o, self.at(n, 2 * o)).wait_send()
        for m in range(4):
            if m not in waited:
                self.arrived(m)

    @staticmethod
    def semaphores(pieces, ways):
        dma = pltpu.SemaphoreType.DMA
        return [dma((pieces, ways // 2 - 1))] * 2 + [dma((pieces, ways // 2))] * 2


def small_rows(sm, m, count, slots, part, scattered=False):
    def block(slot):
        return sm[pl.ds(slot * 32, 16), :].astype(f32)

    if not scattered:
        return jnp.concatenate([block(slot)[m : m + 1] for slot in range(slots)], axis=1)
    total = block(0)
    for slot in range(1, slots):
        total = total + block(slot)
    return jnp.concatenate([total[m + j : m + j + 1] for j in range(count)], axis=1)


def enter_kernel(
    ways, nt, axes, heads,
    boundary, small, s0, s1, s2, s3, seg_col, seg_row, frequency,
    source, cotangent, small_all, f0, f1, f2, f3, o0, o1, o2, o3,
    cos_out, sin_a_out, sin_b_out, xh_out, inv_out,
    ar_out, qr_out, kr_out, vr_out, act_out, slope_out,
    x_send, x_recv, y_send, y_recv, c_send, c_recv, z_send, z_recv,
    b0, b1, b2, b3, local, keep_sem, out_sem,
    xv, sm, n1, n2, wq, w1, packed, cos, sin_a, sin_b, xh, inv, ar, qr, kr, vr, act, slope,
):
    shards, bounce = (s0, s1, s2, s3), (b0, b1, b2, b3)
    shapes = [s.shape for s in shards]
    full, later = (f0, f1, f2, f3), (o0, o1, o2, o3)
    p, d, t = lax.axis_index("pipe"), lax.axis_index("dp"), lax.axis_index("tensor")
    sems = (y_send, y_recv, c_send, c_recv)
    now = Spread(full, shapes, axes, ways, sems)
    then = Spread(later, shapes, axes, ways, sems)
    ring, chunks, part = now.ring, now.chunks, now.part
    length = boundary.shape[1]
    rows = length // nt
    across = {"pipe": 1 - p}
    others = [{"tensor": lax.rem(t + step, nt)} for step in range(1, nt)]
    places = [
        (lax.rem(d // 2 + o, ring) * 2 + lax.rem(d + b, 2)) * part
        for o in range(ring)
        for b in range(2)
    ]
    mine = pl.ds(pl.multiple_of(t * rows, rows), rows)

    loads = [pltpu.make_async_copy(shards[m], bounce[m], local.at[m]) for m in range(4)]
    for load in loads:
        load.start()
    keeps = [
        pltpu.make_async_copy(
            boundary.at[p, :, pl.ds(pl.multiple_of(places[r], part), part)],
            xv.at[:, pl.ds(r * part, part)],
            keep_sem.at[r],
        )
        for r in range(ways)
    ]
    greet([across, now.core] + now.ahead + others)

    def in_shard(n):
        m, row, col = chunks[n]
        return shards[m].at[pl.ds(row, part), pl.ds(col, part)]

    def small_at(slot, count=32, row=0):
        return small_all.at[pl.ds(slot * 32 + row, count), :]

    def x_given(r, target):
        return to(
            boundary.at[1 - p, mine, pl.ds(pl.multiple_of(places[r], part), part)],
            target.at[mine, pl.ds(r * part, part)],
            x_send.at[r], x_recv.at[r], across,
        )

    def x_small():
        here = small_all.at[pl.ds(pl.multiple_of(p * 16, 16), 16), :]
        return to(small, here, x_send.at[ways], x_recv.at[ways], across)

    def x_copy(n, target):
        at = ways + 1 + n
        return to(in_shard(n), target, x_send.at[at], x_recv.at[at], across)

    def small_y(step):
        target = small_at(2 * ((ring - step) % ring))
        return to(
            small_at(0), target, y_send.at[last, step - 1], y_recv.at[last, step - 1],
            now.ahead[step - 1],
        )

    def small_c(o):
        target = small_at(2 * o + 1)
        return to(small_at(2 * o), target, c_send.at[last, o], c_recv.at[last, o], now.core)

    def stores(matrices):
        return [
            pltpu.make_async_copy(
                bounce[m],
                matrices[m].at[pl.ds(0, shapes[m][0]), :]
                if axes[m] == 0
                else matrices[m].at[:, pl.ds(0, shapes[m][1])],
                local.at[m],
            )
            for m in range(4)
        ]

    last = len(chunks)
    small_own = pltpu.make_async_copy(
        small, small_all.at[pl.ds(pl.multiple_of(p * 16, 16), 16), :], local.at[4]
    )
    small_own.start()
    x_small().start()

    @pl.when(p == 0)
    def _():
        for r in range(ways):
            x_given(r, source).start()

    @pl.when(p == 1)
    def _():
        for r in range(ways):
            x_given(r, cotangent).start()

    for keep in keeps:
        keep.start()
    for load in loads:
        load.wait()

    @pl.when(p == 0)
    def _():
        for store in stores(full):
            store.start()
        for n in range(last):
            x_copy(n, now.at(n, 0)).start()
            now.begin(n, in_shard(n))

    @pl.when(p == 1)
    def _():
        for store in stores(later):
            store.start()
        for n in range(last):
            x_copy(n, then.at(n, 0)).start()

    for keep in keeps:
        keep.wait()

    def kept_store(target):
        return pltpu.make_async_copy(xv, target, keep_sem.at[0])

    @pl.when(p == 0)
    def _():
        kept_store(source).start()

    @pl.when(p == 1)
    def _():
        kept_store(cotangent).start()

    small_own.wait()
    x_small().wait_recv()
    for step in range(1, ring):
        small_y(step).start()
    small_c(0).start()

    def table(block, _):
        at = pl.ds(pl.multiple_of(block * BAND, BAND), BAND)
        same = seg_col[at, :] == seg_row[...]
        key = lax.broadcasted_iota(jnp.int32, (BAND, length), 1)
        start = jnp.min(jnp.where(same, key, length), axis=1, keepdims=True)
        place = lax.broadcasted_iota(jnp.int32, (BAND, 1), 0) + block * BAND
        angle = (place - start).astype(f32) * frequency[...]
        lane = lax.broadcasted_iota(jnp.int32, (BAND, ROT), 1)
        sine = jnp.sin(angle)
        cos[at, :] = jnp.cos(angle)
        sin_a[at, :] = jnp.where(lane < 32, -sine, 0.0)
        sin_b[at, :] = jnp.where((lane >= 32) & (lane < 64), sine, 0.0)
        return 0

    lax.fori_loop(0, length // BAND, table, 0)
    outs = []

    def give(at, ref, target):
        outs.append(pltpu.make_async_copy(ref, target, out_sem.at[at]))
        outs[-1].start()

    give(0, cos, cos_out)
    give(1, sin_a, sin_a_out)
    give(2, sin_b, sin_b_out)

    kept_store(source).wait()
    for r in range(ways):
        x_given(r, source).wait_recv()

    def z_copy(step, ref):
        return to(
            ref.at[mine, :], ref.at[mine, :], z_send.at[step - 1], z_recv.at[step - 1],
            others[step - 1],
        )

    @pl.when(p == 0)
    def _():
        for step in range(1, nt):
            z_copy(step, cotangent).start()

    @pl.when(p == 1)
    def _():
        for step in range(1, nt):
            z_copy(step, source).start()

    for step in range(1, ring):
        small_y(step).wait_recv()
        small_c((ring - step) % ring).start()

    def norm():
        for step in range(1, nt):
            z_copy(step, source).wait_recv()
        for o in range(ring):
            small_c(o).wait()
        vectors = pltpu.make_async_copy(small_all, sm, keep_sem.at[1])
        vectors.start()

        @pl.when(p == 1)
        def _():
            whole = pltpu.make_async_copy(source, xv, keep_sem.at[0])
            whole.start()
            whole.wait()

        vectors.wait()
        g1, b1, g2, b2 = (small_rows(sm, m, 1, ways, part) for m in range(4))

        def block(step, _):
            at = pl.ds(pl.multiple_of(step * 128, 128), 128)
            x = xv[at, :].astype(f32)
            x = x - jnp.mean(x, axis=1, keepdims=True)
            inv_std = lax.rsqrt(jnp.mean(x * x, axis=1, keepdims=True) + norm_epsilon)
            x = x * inv_std
            inv[at, :] = inv_std
            xh[at, :] = x.astype(bf16)
            n1[at, :] = (x * g1 + b1).astype(bf16)
            n2[at, :] = (x * g2 + b2).astype(bf16)
            return 0

        lax.fori_loop(0, length // 128, block, 0)
        give(3, xh, xh_out)
        give(4, inv, inv_out)
        now.arrived(0)
        stores(full)[0].wait()
        pltpu.make_async_copy(full[0], wq, keep_sem.at[2]).start()

    size = wq.shape[1] // heads // 3

    def attention(h):
        if h == 0:
            pltpu.make_async_copy(full[0], wq, keep_sem.at[2]).wait()
            now.arrived(1)
            stores(full)[1].wait()
            pltpu.make_async_copy(full[1], w1, keep_sem.at[3]).start()
        cols = pl.ds(h * 3 * size, 3 * size)

        def block(step, _):
            at = pl.ds(pl.multiple_of(step * BAND, BAND), BAND)
            packed[at, :] = dot(n1[at, :], wq[:, cols])
            return 0

        lax.fori_loop(0, length // BAND, block, 0)
        bias = small_rows(sm, 6, heads * 3 * size // part, ways, part, True)
        bias = bias[:, h * 3 * size : (h + 1) * 3 * size]
        at = pl.ds(h * size, size)
        attend_kernel(
            1.0 / math.sqrt(size), packed, bias, cos, sin_a, sin_b, seg_col, seg_row,
            ar.at[:, at], qr.at[:, at], kr.at[:, at], vr.at[:, at],
        )
        if h == heads - 1:
            for n, (ref, target) in enumerate(
                ((ar, ar_out), (qr, qr_out), (kr, kr_out), (vr, vr_out))
            ):
                give(5 + n, ref, target)

    hidden = w1.shape[1] // part
    bias_row = 6 + heads * 3 * size // part

    def feed(j):
        if j == 0:
            pltpu.make_async_copy(full[1], w1, keep_sem.at[3]).wait()
        cols = pl.ds(j * part, part)
        bias = small_rows(sm, bias_row + j, 1, ways, part, True)

        def block(step, _):
            at = pl.ds(pl.multiple_of(step * BAND, BAND), BAND)
            act[at, cols], slope[at, cols] = gelu_parts(dot(n2[at, :], w1[:, cols]) + bias)
            return 0

        lax.fori_loop(0, length // BAND, block, 0)
        if j == hidden - 1:
            give(9, act, act_out)
            give(10, slope, slope_out)

    work = [[] for _ in range(last)]
    begin = min(7, last - 1)
    steps = [norm] + [functools.partial(attention, h) for h in range(heads)]
    for n, step in enumerate(steps):
        work[min(begin + n, last - 1)].append(step)
    for j in range(hidden):
        work[min(begin + len(steps) + j // 2, last - 1)].append(functools.partial(feed, j))

    for n in range(last):
        x_copy(n, now.at(n, 0)).wait_recv()

        @pl.when(p == 1)
        def _():
            now.begin(n, now.at(n, 0))

        if n > 0:
            now.forward(n - 1)
        for step in work[n]:
            step()
    now.forward(last - 1)

    now.finish((0, 1))
    for n in range(last):
        x_copy(n, now.at(n, 0)).wait_send()
    for step in range(1, ring):
        small_y(step).wait_send()
    x_small().wait_send()
    for r in range(ways):
        x_given(r, source).wait_send()
    for step in range(1, nt):
        z_copy(step, source).wait_send()
    for store in stores(full)[2:]:
        store.wait()
    for out in outs:
        out.wait()


def enter_section(boundary, small, shards, seg, axes, ways, nt, heads):
    hbm, vmem = pl.BlockSpec(memory_space=pl.ANY), pl.BlockSpec(memory_space=pltpu.VMEM)
    shape = jax.ShapeDtypeStruct
    part = shards[3].shape[1]
    length, width = boundary.shape[1:]
    pieces = len(chunks_of([s.shape for s in shards], axes, part))
    full = [
        shape((s.shape[0] * ways, s.shape[1]) if axis == 0 else (s.shape[0], s.shape[1] * ways), bf16)
        for s, axis in zip(shards, axes)
    ]
    dma = pltpu.SemaphoreType.DMA
    lane = jnp.arange(ROT, dtype=f32)
    frequency = jnp.exp(-math.log(10000.0) * 2.0 * (lane % 32) / 64)
    frequency = jnp.where(lane < 64, frequency, 0.0)[None]
    inner, columns = shards[0].shape[1], shards[1].shape[1]
    results = (
        [shape((length, ROT), f32)] * 3
        + [shape((length, width), bf16), shape((length, 1), f32)]
        + [shape((length, inner // 3), bf16)] * 4
        + [shape((length, columns), bf16)] * 2
    )
    out = pl.pallas_call(
        functools.partial(enter_kernel, ways, nt, axes, heads),
        in_specs=[hbm] * 6 + [vmem] * 3,
        out_specs=[hbm] * (11 + len(results)),
        out_shape=[
            shape((length, width), bf16),
            shape((length, width), bf16),
            shape((32 * ways, part), bf16),
            *full,
            *full,
            *results,
        ],
        scratch_shapes=[
            dma((ways + 1 + pieces,)),
            dma((ways + 1 + pieces,)),
            *Spread.semaphores(pieces + 1, ways),
            dma((nt - 1,)),
            dma((nt - 1,)),
            *[pltpu.VMEM(s.shape, bf16) for s in shards],
            dma((5,)),
            dma((max(ways, 4),)),
            dma((11,)),
            pltpu.VMEM((length, width), bf16),
            pltpu.VMEM((32 * ways, part), bf16),
            pltpu.VMEM((length, width), bf16),
            pltpu.VMEM((length, width), bf16),
            pltpu.VMEM(full[0].shape, bf16),
            pltpu.VMEM(full[1].shape, bf16),
            pltpu.VMEM((length, inner // heads), f32),
            *[pltpu.VMEM(r.shape, r.dtype) for r in results],
        ],
        compiler_params=pltpu.CompilerParams(
            collective_id=1, has_side_effects=True, vmem_limit_bytes=62 << 20
        ),
        cost_estimate=pl.CostEstimate(flops=0, bytes_accessed=600 << 20, transcendentals=0),
        name="enter_section",
    )(boundary, small, *shards, seg.reshape(-1, 1), seg.reshape(1, -1), frequency)
    return out[0], out[1], out[2], out[3:7], out[7:11], out[11:]


def subs_of(rows):
    return max(1, min(16, rows // 16))


class LineSum:
    def __init__(self, n, partial, right, left, sems, finished, out=None):
        self.n, self.partial, self.right, self.left = n, partial, right, left
        self.finished, self.out = finished, out
        self.r_send, self.r_recv, self.l_send, self.l_recv = sems[:4]
        self.spread = sems[4:]
        self.i = lax.axis_index("tensor")
        self.rows = partial.shape[0] // n
        self.subs = subs_of(self.rows)
        self.sub = self.rows // self.subs
        self.after = {"tensor": lax.rem(self.i + 1, n)}
        self.before = {"tensor": lax.rem(self.i + n - 1, n)}

    def at(self, ref, j, s):
        start = pl.multiple_of(j * self.rows + s * self.sub, self.sub)
        return ref.at[pl.ds(start, self.sub), :]

    def r_copy(self, j, s, source):
        target = self.at(self.right, j, s)
        return to(source, target, self.r_send.at[j, s], self.r_recv.at[j, s], self.after)

    def l_copy(self, j, s, source):
        target = self.at(self.left, j, s)
        return to(source, target, self.l_send.at[j, s], self.l_recv.at[j, s], self.before)

    def ar_copy(self, j, s):
        rows = self.at(self.out, j, s)
        return to(rows, rows, self.spread[0].at[j, s], self.spread[1].at[j, s], self.after)

    def al_copy(self, j, s):
        rows = self.at(self.out, j, s)
        return to(rows, rows, self.spread[2].at[j, s], self.spread[3].at[j, s], self.before)

    def add(self, ref, j, s):
        ref = self.at(ref, j, s)
        own = self.at(self.partial, j, s)[...].astype(f32)
        ref[...] = (ref[...].astype(f32) + own).astype(bf16)

    def reduce_right(self, s):
        for k in range(self.n - 1):
            j = self.n - 1 - k

            @pl.when(self.i == 0)
            def _():
                self.r_copy(j, s, self.at(self.partial, j, s)).start()

            @pl.when((self.i > 0) & (self.i < j))
            def _():
                self.r_copy(j, s, self.at(self.right, j, s)).wait_recv()
                self.add(self.right, j, s)
                self.r_copy(j, s, self.at(self.right, j, s)).start()

    def reduce_left(self, s):
        for k in range(self.n - 1):

            @pl.when(self.i == self.n - 1)
            def _():
                self.l_copy(k, s, self.at(self.partial, k, s)).start()

            @pl.when((self.i < self.n - 1) & (self.i > k))
            def _():
                self.l_copy(k, s, self.at(self.left, k, s)).wait_recv()
                self.add(self.left, k, s)
                self.l_copy(k, s, self.at(self.left, k, s)).start()

    def finish(self, s):
        i, n = self.i, self.n

        @pl.when(i > 0)
        def _():
            self.r_copy(i, s, self.at(self.right, i, s)).wait_recv()
            self.add(self.right, i, s)

        @pl.when(i == 0)
        def _():
            self.at(self.right, i, s)[...] = self.at(self.partial, i, s)[...]

        @pl.when(i < n - 1)
        def _():
            self.l_copy(i, s, self.at(self.left, i, s)).wait_recv()

        @pl.when(i == n - 1)
        def _():
            self.at(self.left, i, s)[...] = jnp.zeros((self.sub, self.left.shape[1]), bf16)

        total = self.at(self.right, i, s)[...].astype(f32)
        total = total + self.at(self.left, i, s)[...].astype(f32)
        self.finished(self, s, total)
        if self.out is not None:

            @pl.when(i < n - 1)
            def _():
                self.ar_copy(i, s).start()

            @pl.when(i > 0)
            def _():
                self.al_copy(i, s).start()

    def pass_on(self, step, s):
        i, n = self.i, self.n

        @pl.when(i >= step)
        def _():
            self.ar_copy(i - step, s).wait_recv()

            @pl.when(i < n - 1)
            def _():
                self.ar_copy(i - step, s).start()

        @pl.when(i + step < n)
        def _():
            self.al_copy(i + step, s).wait_recv()

            @pl.when(i > 0)
            def _():
                self.al_copy(i + step, s).start()

    @property
    def turns(self):
        return self.subs + (2 * self.n - 2 if self.out is not None else self.n - 1)

    def turn(self, it):
        def when_piece(s, act):
            @pl.when((s >= 0) & (s < self.subs))
            def _():
                act(s)

        when_piece(it - self.i, self.reduce_right)
        when_piece(it - (self.n - 1 - self.i), self.reduce_left)
        when_piece(it - (self.n - 1), self.finish)
        if self.out is not None:
            for step in range(1, self.n):
                when_piece(it - (self.n - 1) - step, functools.partial(self.pass_on, step))

    def drain(self):
        i, n = self.i, self.n

        def body(s, _):
            for j in range(n):

                @pl.when(i < j)
                def _():
                    self.r_copy(j, s, self.at(self.partial, j, s)).wait_send()

                @pl.when(i > j)
                def _():
                    self.l_copy(j, s, self.at(self.partial, j, s)).wait_send()

                if self.out is not None:

                    @pl.when((i >= j) & (i < n - 1))
                    def _():
                        self.ar_copy(j, s).wait_send()

                    @pl.when((i <= j) & (i > 0))
                    def _():
                        self.al_copy(j, s).wait_send()

            return 0

        lax.fori_loop(0, self.subs, body, 0)

    @staticmethod
    def scratch(n, tokens, width, spread):
        return [pltpu.VMEM((tokens, width), bf16)] * 2 + [
            pltpu.SemaphoreType.DMA((n, subs_of(tokens // n)))
        ] * (8 if spread else 4)


def sum_spread_kernel(n, ways, axes, shapes, order, partial, base, g, *refs):
    out, full, d_ar, d_act = refs[4], refs[5:9], refs[9], refs[10]
    right, left = refs[11], refs[12]
    line_sems, parts_sems = refs[13:21], refs[21:25]
    x_send, x_recv, weight, result, ar_result, w_sem, r_sem = refs[25:]
    p = lax.axis_index("pipe")

    def finished(line, s, total):
        mine = pl.ds(pl.multiple_of(s * line.sub, line.sub), line.sub)
        line.at(out, line.i, s)[...] = (base[mine, :] + total).astype(bf16)

    line = LineSum(n, partial, right, left, line_sems, finished, out)
    parts = Spread(full, shapes, axes, ways, parts_sems)
    ring, part = parts.ring, parts.part
    across = {"pipe": 1 - p}
    greet([line.after, line.before, parts.core, across] + parts.ahead)
    count = len(parts.chunks)

    def x_copy(m, o):
        chunk = parts.at(m, 2 * o)
        return to(chunk, chunk, x_send.at[m, o - 1], x_recv.at[m, o - 1], across)

    for place, m in enumerate(order):
        parts.c_copy(m, 0, parts.at(m, 0)).start()

        @pl.when(p == place % 2)
        def _():
            for step in range(1, ring):
                parts.y_copy(m, step, parts.at(m, 0)).start()

    def from_ring(m):
        for step in range(1, ring):
            o = (ring - step) % ring
            parts.y_copy(m, step, parts.at(m, 0)).wait_recv()
            x_copy(m, o).start()
            parts.c_copy(m, o, parts.at(m, 2 * o)).start()

    def from_across(m):
        for o in range(1, ring):
            x_copy(m, o).wait_recv()
            parts.c_copy(m, o, parts.at(m, 2 * o)).start()

    hidden, inner = d_act.shape[1], d_ar.shape[1]
    blocks = [("act", j) for j in range(hidden // part)] + [("ar", 0)]
    wd_rows = full[3].shape[0]

    def weight_load(i):
        kind, j = blocks[i]
        if kind == "act":
            source, target = full[2].at[pl.ds(j * part, part), :], weight.at[i % 2]
        else:
            source, target = full[3], weight.at[i % 2, pl.ds(0, wd_rows), :]
        return pltpu.make_async_copy(source, target, w_sem.at[i % 2])

    def store(i):
        kind, j = blocks[i]
        if kind == "act":
            at = pl.ds(j * part, part)
            return pltpu.make_async_copy(result.at[i % 2], d_act.at[:, at], r_sem.at[i % 2])
        return pltpu.make_async_copy(ar_result, d_ar, r_sem.at[2])

    def product(i):
        if i == 0:
            for m in (2, 3):
                parts.arrived(m)
            weight_load(0).start()
        weight_load(i).wait()
        if i + 1 < len(blocks):
            weight_load(i + 1).start()
        kind, _ = blocks[i]
        if kind == "act" and i >= 2:
            store(i - 2).wait()

        def body(step, _):
            at = pl.ds(pl.multiple_of(step * BAND, BAND), BAND)
            if kind == "act":
                result[i % 2, at, :] = dot(g[at, :], weight[i % 2], ((1,), (1,))).astype(bf16)
            else:
                value = dot(g[at, :], weight[i % 2, pl.ds(0, wd_rows), :], ((1,), (1,)))
                ar_result[at, :] = value.astype(bf16)
            return 0

        lax.fori_loop(0, g.shape[0] // BAND, body, 0)
        store(i).start()

    early = sum(parts.chunks[m][0] in (2, 3) for m in range(count))
    ready = 2 * (-(-early // 2) + 2)
    pairs = -(-count // 2)

    def turn_(half, _):
        line.turn(half)
        for pair in range(pairs):
            both = list(enumerate(order))[2 * pair : 2 * pair + 2]

            @pl.when(half == 2 * pair + 2)
            def _():
                for place, m in both:

                    @pl.when(p == place % 2)
                    def _():
                        from_ring(m)

            @pl.when(half == 2 * pair + 4)
            def _():
                for place, m in both:

                    @pl.when(p != place % 2)
                    def _():
                        from_across(m)

        for i in range(len(blocks)):

            @pl.when(half == ready + i)
            def _():
                product(i)

        return 0

    total = max(line.turns, 2 * pairs + 4, ready + len(blocks))
    lax.fori_loop(0, total, turn_, 0)
    line.drain()
    for place, m in enumerate(order):

        @pl.when(p == place % 2)
        def _():
            for step in range(1, ring):
                parts.y_copy(m, step, parts.at(m, 0)).wait_send()
                x_copy(m, step).wait_send()

        for o in range(ring):
            parts.c_copy(m, o, parts.at(m, 2 * o)).wait_send()
    for m in (0, 1):
        parts.arrived(m)
    store(len(blocks) - 1).wait()
    for i in range(max(len(blocks) - 3, 0), len(blocks) - 1):
        store(i).wait()


def sum_spread(partial, base, g, n, full, shapes, axes, ways):
    tokens, width = partial.shape
    vmem = pl.BlockSpec(memory_space=pltpu.VMEM)
    hbm = pl.BlockSpec(memory_space=pl.ANY)
    shape, dma = jax.ShapeDtypeStruct, pltpu.SemaphoreType.DMA
    part = shapes[3][1]
    chunks = chunks_of(shapes, axes, part)
    pieces = len(chunks)
    order = sorted(range(pieces), key=lambda m: (2, 3, 0, 1)[chunks[m][0]])
    inner, hidden = shapes[3][0], shapes[2][0]
    out = pl.pallas_call(
        functools.partial(sum_spread_kernel, n, ways, axes, shapes, order),
        in_specs=[vmem, vmem, vmem] + [hbm] * 4,
        out_specs=[vmem] + [hbm] * 6,
        out_shape=[shape((tokens, width), bf16)]
        + [shape(w.shape, bf16) for w in full]
        + [shape((tokens, inner), bf16), shape((tokens, hidden), bf16)],
        input_output_aliases={3 + m: 1 + m for m in range(4)},
        scratch_shapes=LineSum.scratch(n, tokens, width, True)
        + Spread.semaphores(pieces, ways)
        + [dma((pieces, ways // 2 - 1))] * 2
        + [
            pltpu.VMEM((2, max(part, inner), width), bf16),
            pltpu.VMEM((2, tokens, part), bf16),
            pltpu.VMEM((tokens, inner), bf16),
            dma((2,)),
            dma((3,)),
        ],
        compiler_params=pltpu.CompilerParams(
            collective_id=2, has_side_effects=True, vmem_limit_bytes=40 << 20
        ),
        cost_estimate=pl.CostEstimate(flops=0, bytes_accessed=360 << 20, transcendentals=0),
        name="sum_spread",
    )(partial, base, g, *full)
    return out[0], out[1:5], out[5], out[6]


class GradSum:
    def __init__(self, k, ways, xh, g, lefts, rights, outs, own, scales, vec_out, norms, refs):
        (
            self.from_core, self.from_ring, self.from_pipe,
            self.load, self.away, self.near, self.far, self.core_in, self.ring_in, self.pipe_in,
            self.done, self.weight, self.vec, self.v_held, self.v_round, self.v_across,
            self.load_sem, self.c_send, self.c_recv, self.y_send, self.y_recv,
            self.x_send, self.x_recv, self.out_sem, self.in_sem,
        ) = refs
        self.k, self.ring = k, ways // 2
        self.xh, self.g, self.lefts, self.rights, self.outs = xh, g, lefts, rights, outs
        self.own, self.scales, self.vec_out, self.norms = own, scales, vec_out, norms
        self.part = self.load.shape[2]
        self.counts = [side.shape[1] // self.part for side in (*lefts, *rights)]
        self.starts = [sum(self.counts[:m]) for m in range(4)]
        self.count = sum(self.counts)
        p, d = lax.axis_index("pipe"), lax.axis_index("dp")
        y, c = d // 2, d % 2
        self.p = p
        self.core = {"dp": y * 2 + (1 - c)}
        self.ahead = [{"dp": lax.rem(y + o, self.ring) * 2 + c} for o in range(1, self.ring)]
        self.other = {"pipe": 1 - p}

    def each(self, c, act, matrices=range(4)):
        for m in matrices:

            @pl.when((c >= self.starts[m]) & (c < self.starts[m] + self.counts[m]))
            def _():
                act(m, pl.multiple_of((c - self.starts[m]) * self.part, self.part))

    def fetch(self, c):
        def act(m, at):
            pltpu.make_async_copy(
                self.lefts[m].at[:, pl.ds(at, self.part)],
                self.load.at[lax.rem(c, 3)],
                self.load_sem.at[lax.rem(c, 3)],
            ).start()

        self.each(c, act, (0, 1))

    def fetched(self, c):
        slot = lax.rem(c, 3)
        pltpu.make_async_copy(
            self.lefts[0].at[:, pl.ds(0, self.part)], self.load.at[slot], self.load_sem.at[slot]
        ).wait()

    def piece(self, c, slot, use):
        cols = pl.ds(slot * self.part, self.part)

        @pl.when(c < self.starts[2])
        def _():
            use(dot(self.load[lax.rem(c, 3)], self.g[:, cols], ((0,), (0,))))

        def right(m, at):
            side = self.rights[m - 2][:, pl.ds(at, self.part)]
            use(dot(self.xh[:, cols], side, ((0,), (0,))))

        self.each(c, right, (2, 3))

    def c_copy(self, c, o):
        return to(
            self.away.at[lax.rem(c, 2), o], self.from_core.at[c, o],
            self.c_send.at[c, o], self.c_recv.at[c, o], self.core,
        )

    def y_copy(self, c, o):
        return to(
            self.far.at[lax.rem(c, 3), o - 1], self.from_ring.at[c, o - 1],
            self.y_send.at[c, o - 1], self.y_recv.at[c, o - 1], self.ahead[o - 1],
        )

    def x_copy(self, c):
        return to(
            self.near.at[lax.rem(c, 5)], self.from_pipe.at[c],
            self.x_send.at[c], self.x_recv.at[c], self.other,
        )

    def core_load(self, c, o):
        return pltpu.make_async_copy(
            self.from_core.at[c, o], self.core_in.at[o], self.in_sem.at[0, o]
        )

    def ring_load(self, c, o):
        return pltpu.make_async_copy(
            self.from_ring.at[c, o - 1], self.ring_in.at[o - 1], self.in_sem.at[1, o]
        )

    def pipe_load(self, c):
        return pltpu.make_async_copy(self.from_pipe.at[c], self.pipe_in, self.in_sem.at[1, 0])

    def weight_load(self, m, at):
        return pltpu.make_async_copy(
            self.own[m - 2].at[:, pl.ds(at, self.part)], self.weight, self.in_sem.at[2, 0]
        )

    def store(self, c, start):
        def act(m, at):
            out = self.outs[m]
            if m < 2:
                out = out.at[pl.ds(at, self.part), :]
            else:
                out = out.at[:, pl.ds(at, self.part)]
            copy = pltpu.make_async_copy(self.done, out, self.out_sem.at[0])
            copy.start() if start else copy.wait()

        self.each(c, act)

    @property
    def turns(self):
        return self.count + 5

    def begin(self):
        self.fetch(0)
        self.fetch(1)
        self.vec[...] = jnp.zeros(self.vec.shape, f32)

    def v_copy(self, stage, o=1):
        last = self.count
        if stage == 0:
            return to(
                self.vec, self.v_held, self.c_send.at[last, 0], self.c_recv.at[last, 0], self.core
            )
        if stage == 1:
            return to(
                self.v_held, self.v_round.at[o - 1],
                self.y_send.at[last, o - 1], self.y_recv.at[last, o - 1], self.ahead[o - 1],
            )
        return to(
            self.vec_out, self.v_across, self.x_send.at[last], self.x_recv.at[last], self.other
        )

    def turn(self, it, v_start):
        @pl.when((it >= 1) & (it < self.count + 1))
        def _():
            for o in range(self.ring):
                self.c_copy(it - 1, o).wait_recv()
                self.core_load(it - 1, o).start()

        @pl.when((it >= 3) & (it < self.count + 3))
        def _():
            for o in range(1, self.ring):
                self.y_copy(it - 3, o).wait_recv()
                self.ring_load(it - 3, o).start()

        at_end = (it >= 5) & (it < self.count + 5) & (self.p == self.k)

        @pl.when(at_end)
        def _():
            self.x_copy(it - 5).wait_recv()
            self.pipe_load(it - 5).start()
            self.each(it - 5, lambda m, at: self.weight_load(m, at).start(), (2, 3))

        @pl.when(it < self.count)
        def _():
            c = it

            @pl.when(c < self.starts[2])
            def _():
                self.fetched(c)

            for o in range(self.ring):

                @pl.when(c >= 2)
                def _():
                    self.c_copy(c - 2, o).wait_send()

                def use(value):
                    self.away[lax.rem(c, 2), o] = value.astype(bf16)

                self.piece(c, 2 * o + 1, use)
                self.c_copy(c, o).start()

        @pl.when((it >= 1) & (it < self.count + 1))
        def _():
            c = it - 1
            for o in range(self.ring - 1, -1, -1):
                self.core_load(c, o).wait()
                if o > 0:

                    @pl.when(c >= 3)
                    def _():
                        self.y_copy(c - 3, o).wait_send()

                    def use(value):
                        value = value + self.core_in[o].astype(f32)
                        self.far[lax.rem(c, 3), o - 1] = value.astype(bf16)

                    self.piece(c, 2 * o, use)
                    self.y_copy(c, o).start()
                else:

                    @pl.when((c >= 5) & (self.p != self.k))
                    def _():
                        self.x_copy(c - 5).wait_send()

                    def use(value):
                        value = value + self.core_in[o].astype(f32)
                        self.near[lax.rem(c, 5)] = value.astype(bf16)

                    self.piece(c, 0, use)
            self.fetch(c + 2)

        @pl.when((it >= 3) & (it < self.count + 3))
        def _():
            c = it - 3
            total = self.near[lax.rem(c, 5)].astype(f32)
            for o in range(1, self.ring):
                self.ring_load(c, o).wait()
                total = total + self.ring_in[o - 1].astype(f32)
            self.near[lax.rem(c, 5)] = total.astype(bf16)

            @pl.when(self.p != self.k)
            def _():
                self.x_copy(c).start()

        @pl.when(at_end)
        def _():
            c = it - 5

            @pl.when(c >= 1)
            def _():
                self.store(c - 1, False)

            self.pipe_load(c).wait()
            core = self.near[lax.rem(c, 5)].astype(f32) + self.pipe_in[...].astype(f32)

            @pl.when(c < self.starts[2])
            def _():
                self.done[...] = core

            def finish(m, at):
                gain, bias = self.scales[:, 2 * m - 4 : 2 * m - 3], self.scales[:, 2 * m - 3 : 2 * m - 2]
                row = self.vec_out[pl.ds(c - self.starts[2], 1), :]
                self.done[...] = gain * core + bias * row
                self.weight_load(m, at).wait()
                weight = self.weight[...].astype(f32)
                lane = lax.broadcasted_iota(jnp.int32, self.norms.shape, 1)
                gain_sum = jnp.sum(weight * core, axis=1, keepdims=True)
                bias_sum = jnp.sum(weight * row, axis=1, keepdims=True)
                both = jnp.where(lane == 2 * m - 4, gain_sum, 0.0)
                both = both + jnp.where(lane == 2 * m - 3, bias_sum, 0.0)
                self.norms[...] = self.norms[...] + both

            self.each(c, finish, (2, 3))
            self.store(c, True)

        @pl.when(it == v_start)
        def _():
            self.v_copy(0).start()

        @pl.when(it == v_start + 1)
        def _():
            self.v_copy(0).wait()
            self.v_held[...] = self.v_held[...] + self.vec[...]
            for o in range(1, self.ring):
                self.v_copy(1, o).start()

        @pl.when(it == v_start + 2)
        def _():
            total = self.v_held[...]
            for o in range(1, self.ring):
                self.v_copy(1, o).wait()
                total = total + self.v_round[o - 1]
            self.vec_out[...] = total

            @pl.when(self.p != self.k)
            def _():
                self.v_copy(2).start()

        @pl.when((it == v_start + 3) & (self.p == self.k))
        def _():
            self.v_copy(2).wait_recv()
            self.vec_out[...] = self.vec_out[...] + self.v_across[...]

    def drain(self):
        last = self.count
        for o in range(self.ring):
            for c in (last - 2, last - 1):
                self.c_copy(c, o).wait_send()
            for c in (last - 3, last - 2, last - 1):
                if o > 0:
                    self.y_copy(c, o).wait_send()

        @pl.when(self.p == self.k)
        def _():
            self.store(jnp.int32(last - 1), False)

        @pl.when(self.p != self.k)
        def _():
            self.v_copy(2).wait_send()
            for c in range(last - 5, last):
                self.x_copy(c).wait_send()

    @staticmethod
    def landing(ways, part, count):
        ring = ways // 2
        return [
            jax.ShapeDtypeStruct((count, *lead, part, part), bf16)
            for lead in ((ring,), (ring - 1,), ())
        ]

    @staticmethod
    def scratch(ways, part, tokens, count):
        ring = ways // 2
        dma = pltpu.SemaphoreType.DMA
        return [
            pltpu.VMEM((3, tokens, part), bf16),
            pltpu.VMEM((2, ring, part, part), bf16),
            pltpu.VMEM((5, part, part), bf16),
            pltpu.VMEM((3, ring - 1, part, part), bf16),
            pltpu.VMEM((ring, part, part), bf16),
            pltpu.VMEM((ring - 1, part, part), bf16),
            pltpu.VMEM((part, part), bf16),
            pltpu.VMEM((part, part), f32),
            pltpu.VMEM((part, part), bf16),
            pltpu.VMEM((16, part), f32),
            pltpu.VMEM((16, part), f32),
            pltpu.VMEM((ring - 1, 16, part), f32),
            pltpu.VMEM((16, part), f32),
            dma((3,)),
            dma((count + 1, ring)),
            dma((count + 1, ring)),
            dma((count + 1, ring - 1)),
            dma((count + 1, ring - 1)),
            dma((count + 1,)),
            dma((count + 1,)),
            dma((1,)),
            dma((3, max(ring, 2))),
        ]


class BackWork:
    def __init__(self, given, ways, heads, g, tables, segs, gains, hbm, dq, dh, u, vec, refs):
        self.given = given
        self.wq, self.w1, self.w2, self.wd, self.qr, self.kr, self.vr, self.slope = hbm
        (
            self.wa, self.wb, self.hq, self.hk, self.hv, self.sl, self.d_ar,
            self.q_sum, self.dk, self.dv, self.sem,
        ) = refs
        self.ways, self.heads, self.g, self.vec = ways, heads, g, vec
        self.tables, self.segs, self.gains = tables, segs, gains
        self.dq, self.dh, self.u_rows = dq, dh, u
        self.part = g.shape[1] // ways
        self.size = self.qr.shape[1] // heads
        pieces = [("head", h) for h in range(heads)]
        pieces += [("hidden", j) for j in range(dh.shape[1] // self.part)]
        pieces += [("rows", j) for j in range(ways)]
        self.pieces = pieces

    def loads(self, n):
        kind, j = self.pieces[n]
        slot, part, size = n % 2, self.part, self.size
        width, hidden, inner = self.g.shape[1], self.dh.shape[1], self.dq.shape[1]
        if kind == "head":
            cols = pl.ds(j * size, size)
            if self.given:
                pairs = [(self.wd.at[:, cols], self.d_ar.at[slot])]
            else:
                pairs = [(self.wd.at[cols, :], self.wa.at[slot, pl.ds(0, size), pl.ds(0, width)])]
            pairs += [
                (ref.at[:, cols], held.at[slot])
                for ref, held in ((self.qr, self.hq), (self.kr, self.hk), (self.vr, self.hv))
            ]
        elif kind == "hidden":
            at = pl.ds(j * part, part)
            pairs = [(self.slope.at[:, at], self.dh.at[:, at])] if self.given else [
                (self.w2.at[at, :], self.wa.at[slot, pl.ds(0, part), pl.ds(0, width)]),
                (self.slope.at[:, at], self.sl.at[slot]),
            ]
        else:
            at = pl.ds(j * part, part)
            pairs = [
                (self.w1.at[at, :], self.wa.at[slot, pl.ds(0, part), pl.ds(0, hidden)]),
                (self.wq.at[at, :], self.wb.at[slot, :, pl.ds(0, inner)]),
            ]
        return [
            pltpu.make_async_copy(source, target, self.sem.at[slot, i])
            for i, (source, target) in enumerate(pairs)
        ]

    def begin(self, n):
        if n < len(self.pieces):
            for load in self.loads(n):
                load.start()

    def run(self, n):
        for load in self.loads(n):
            load.wait()
        self.begin(n + 1)
        kind, j = self.pieces[n]
        getattr(self, kind)(j, n % 2)

    def blocks(self, act):
        def body(step, _):
            act(pl.ds(pl.multiple_of(step * BAND, BAND), BAND))
            return 0

        lax.fori_loop(0, self.g.shape[0] // BAND, body, 0)

    def head(self, h, slot):
        size, width = self.size, self.g.shape[1]
        weight = self.wa.at[slot, pl.ds(0, size), pl.ds(0, width)]

        def act(at):
            self.d_ar[0, at, :] = dot(self.g[at, :], weight[...], ((1,), (1,))).astype(bf16)

        if not self.given:
            self.blocks(act)
        attend_back_kernel(
            1.0 / math.sqrt(size), self.hq.at[slot], self.hk.at[slot], self.hv.at[slot],
            self.d_ar.at[slot if self.given else 0], *self.tables, *self.segs,
            self.dq.at[:, pl.ds(h * 3 * size, 3 * size)], self.q_sum.at[pl.ds(h, 1)],
            self.dk, self.dv,
        )
        if h == self.heads - 1:
            sums = jnp.concatenate([self.q_sum[i] for i in range(self.heads)], axis=1)
            for row in range(sums.shape[1] // self.part):
                self.vec[row : row + 1, :] = sums[:, row * self.part : (row + 1) * self.part]

    def hidden(self, j, slot):
        part, width = self.part, self.g.shape[1]
        weight = self.wa.at[slot, pl.ds(0, part), pl.ds(0, width)]
        cols = pl.ds(j * part, part)
        first = self.dq.shape[1] // part
        row = first + j
        self.vec[row : row + 1, :] = jnp.zeros((1, part), f32)

        def act(at):
            if self.given:
                value = self.dh[at, cols]
            else:
                value = dot(self.g[at, :], weight[...], ((1,), (1,)))
                value = (self.sl[slot, at, :].astype(f32) * value).astype(bf16)
                self.dh[at, cols] = value
            self.vec[row : row + 1, :] += jnp.sum(value.astype(f32), axis=0, keepdims=True)

        self.blocks(act)
        if j == 0:
            d = lax.axis_index("dp")
            ring = self.ways // 2
            for r in range(self.ways):
                place = lax.rem(d // 2 + r // 2, ring) * 2 + lax.rem(d + r % 2, 2)
                total = jnp.sum(self.g[:, pl.ds(r * part, part)].astype(f32), axis=0, keepdims=True)
                self.vec[pl.ds(first + self.dh.shape[1] // part + place, 1), :] = total

    def rows(self, j, slot):
        part, hidden, inner = self.part, self.dh.shape[1], self.dq.shape[1]
        weight_1 = self.wa.at[slot, pl.ds(0, part), pl.ds(0, hidden)]
        weight_q = self.wb.at[slot, :, pl.ds(0, inner)]
        cols = pl.ds(j * part, part)
        gain_1, gain_2 = (gain[:, cols] for gain in self.gains)

        def act(at):
            value = dot(self.dq[at, :], weight_q[...], ((1,), (1,))) * gain_1
            value = value + dot(self.dh[at, :], weight_1[...], ((1,), (1,))) * gain_2
            self.u_rows[at, cols] = value.astype(bf16)

        self.blocks(act)

    @staticmethod
    def scratch(given, ways, heads, tokens, width, hidden, size):
        part = width // ways
        return [
            pltpu.VMEM((2, max(part, size), max(width, hidden)), bf16),
            pltpu.VMEM((2, part, 3 * heads * size), bf16),
            *[pltpu.VMEM((2, tokens, size), bf16)] * 3,
            pltpu.VMEM((2, tokens, part), bf16),
            pltpu.VMEM((2 if given else 1, tokens, size), bf16),
            pltpu.VMEM((heads, 1, 3 * size), f32),
            *[pltpu.VMEM((BAND, size), f32)] * 2,
            pltpu.SemaphoreType.DMA((2, 4)),
        ]


def back_kernel(n, ways, heads, k, *refs):
    take = iter(refs)

    def some(count):
        return [next(take) for _ in range(count)]

    g, xh, inv_std, scales = some(4)
    tables, segs, gains = some(3), some(2), some(2)
    weights, attended, slope = some(4), some(3), next(take)
    lefts, own = some(2), some(2)
    outward = weights[2:]
    if k == 1:
        weights = weights[:2] + [None, next(take)]
    if k == 0:
        y_part, y_base = some(2)
        norms_in = next(take)
        some(4)
    vec_out, norms, outs = next(take), next(take), some(4)
    if k == 0:
        norm_rows, rows_out, rows_away, y_rows, y_away, y_land = some(6)
    else:
        out, branch = some(2)
    landing = some(3)
    dq, dh, u, right, left = some(5)
    line_sems = some(4 if k == 0 else 8)
    work_refs = some(11)
    grad_refs = landing + some(22)
    p, t = lax.axis_index("pipe"), lax.axis_index("tensor")
    other = {"pipe": 1 - p}
    if k == 0:
        stage, handed, d_send, d_recv, stage_sem = some(5)
        y_in, y_stage, y_handed, yz_send, yz_recv, yx_send, yx_recv, y_sem = some(8)
        n_land, n_send, n_recv = some(3)

    def d_copy(s, sub):
        mine = pl.ds(pl.multiple_of(s * sub, sub), sub)
        return to(handed.at[mine, :], rows_away.at[mine, :], d_send.at[s], d_recv.at[s], other)

    def d_store(s, sub):
        mine = pl.ds(pl.multiple_of(s * sub, sub), sub)
        slot = lax.rem(s, 2)
        return pltpu.make_async_copy(stage.at[slot], rows_out.at[mine, :], stage_sem.at[slot])

    def finished(line, s, total):
        mine = pl.ds(pl.multiple_of(s * line.sub, line.sub), line.sub)
        xr = line.at(xh, line.i, s)[...].astype(f32)
        mean = jnp.mean(total, axis=1, keepdims=True)
        proj = jnp.mean(total * xr, axis=1, keepdims=True)
        total = inv_std[mine, :] * (total - mean - xr * proj)
        total = line.at(g, line.i, s)[...].astype(f32) + total
        if k == 1:
            line.at(out, line.i, s)[...] = total.astype(bf16)
        else:

            @pl.when(s >= 2)
            def _():
                d_store(s - 2, line.sub).wait()

            stage[lax.rem(s, 2)] = total
            d_store(s, line.sub).start()
            handed[mine, :] = total.astype(bf16)

            @pl.when(p == 1)
            def _():
                d_copy(s, line.sub).start()

    line = LineSum(n, u, right, left, line_sems, finished, out if k else None)
    vec = grad_refs[12]
    work = BackWork(
        k == 1, ways, heads, g, tables, segs, gains, (*weights, *attended, slope), dq, dh, u, vec,
        work_refs,
    )
    grads = GradSum(k, ways, xh, g, lefts, (dq, dh), outs, own, scales, vec_out, norms, grad_refs)
    places = [line.after, line.before, grads.core, grads.other] + grads.ahead
    if k == 0:
        along = [{"tensor": lax.rem(t + step, n)} for step in range(1, n)]
        places = places[2:] + along
    greet(places)
    grads.begin()
    norms[...] = norms_in[...] if k == 0 else jnp.zeros(norms.shape, f32)
    work.begin(0)

    count = len(work.pieces)
    last_hidden = heads + dh.shape[1] // work.part
    middle = (last_hidden + count) // 2
    if k == 1:
        step = -(-(count - last_hidden) // 4)
        plan = {1: (0, 1), 3: (1, heads), 4: (heads, last_hidden)}
        plan |= {5 + i: (last_hidden + i * step, last_hidden + (i + 1) * step) for i in range(4)}
        begin, v_start = 9, 3
    else:
        mid_hidden = (heads + last_hidden) // 2
        plan = {
            3: (0, 1), 7: (1, heads), 9: (heads, mid_hidden), 11: (mid_hidden, last_hidden),
            13: (last_hidden, middle), 15: (middle, count),
        }
        begin, v_start = 16, 6

    if k == 0:
        block = y_base.shape[0] // 4
        width = y_base.shape[1]

        def yz_copy(step):
            owner = lax.rem(t + step, n)
            rows = y_base.shape[0]
            theirs = pl.ds(pl.multiple_of(owner * rows, rows), rows)
            return to(
                y_part.at[theirs, :], y_land.at[step - 1], yz_send.at[step - 1],
                yz_recv.at[step - 1], along[step - 1],
            )

        def yx_copy(q):
            mine = pl.ds(q * block, block)
            return to(y_handed.at[mine, :], y_away.at[mine, :], yx_send.at[q], yx_recv.at[q], other)

        def y_store(q):
            mine = pl.ds(q * block, block)
            return pltpu.make_async_copy(y_stage, y_rows.at[mine, :], y_sem.at[n + 1])

        def y_finish(q):
            mine = pl.ds(q * block, block)
            if q == 0:
                for step in range(1, n):
                    yz_copy(step).wait_recv()
            else:
                y_store(q - 1).wait()
            start = pl.multiple_of(t * y_base.shape[0] + q * block, block)
            loads = [pltpu.make_async_copy(y_part.at[pl.ds(start, block), :], y_in.at[0], y_sem.at[0])]
            loads += [
                pltpu.make_async_copy(y_land.at[step - 1, mine, :], y_in.at[step], y_sem.at[step])
                for step in range(1, n)
            ]
            loads.append(pltpu.make_async_copy(y_base.at[mine, :], y_stage, y_sem.at[n]))
            for load in loads:
                load.start()
            for load in loads:
                load.wait()
            total = y_stage[...]
            for step in range(n):
                total = total + y_in[step].astype(f32)
            y_stage[...] = total
            y_store(q).start()
            y_handed[mine, :] = total.astype(bf16)

            @pl.when(p == 0)
            def _():
                yx_copy(q).start()

        for step in range(1, n):
            yz_copy(step).start()

    b_start = grads.count + 1

    def b_loads(j):
        part = work.part
        cols = pl.ds(j * part, part)
        tokens, hidden = g.shape[0], dh.shape[1]
        half = min(tokens, hidden)
        pairs = [
            (outward[0].at[pl.ds(i * half, half), cols], grads.load.at[i, pl.ds(0, half), :])
            for i in range(hidden // half)
        ]
        rows = outward[1].shape[0]
        pairs.append((outward[1].at[:, cols], work.wb.at[j % 2, pl.ds(0, rows), pl.ds(0, part)]))
        if j == 0:
            pairs += [(lefts[0], dh), (lefts[1], dq.at[:, pl.ds(0, rows)])]
        return [
            pltpu.make_async_copy(source, target, work.sem.at[i // 4, i % 4])
            for i, (source, target) in enumerate(pairs)
        ]

    def b_store(j):
        part = work.part
        return pltpu.make_async_copy(
            work.sl.at[j % 2], branch.at[:, pl.ds(j * part, part)], grads.load_sem.at[j % 2]
        )

    def b_block(j):
        part, hidden = work.part, dh.shape[1]
        half = min(g.shape[0], hidden)
        rows = outward[1].shape[0]
        loads = b_loads(j)
        for load in loads:
            load.start()
        if j >= 2:
            b_store(j - 2).wait()
        for load in loads:
            load.wait()

        def act(at):
            value = dot(dq[at, pl.ds(0, rows)], work.wb[j % 2, pl.ds(0, rows), pl.ds(0, part)])
            for i in range(hidden // half):
                value = value + dot(
                    dh[at, pl.ds(i * half, half)], grads.load[i, pl.ds(0, half), :]
                )
            work.sl[j % 2, at, :] = value.astype(bf16)

        work.blocks(act)
        b_store(j).start()

    def turn_(half, _):
        @pl.when(half >= begin)
        def _():
            line.turn(half - begin)

        @pl.when(lax.rem(half, 2) == 0)
        def _():
            grads.turn(half // 2, v_start)

        for at, (low, high) in plan.items():

            @pl.when(half == at)
            def _():
                for piece in range(low, high):
                    work.run(piece)

        if k == 0:
            for q in range(4):

                @pl.when(half == 2 * q + 17)
                def _():
                    y_finish(q)

        else:
            for j in range(ways):

                @pl.when(half == 2 * b_start + 1 + j)
                def _():
                    b_block(j)

        return 0

    total = max(begin + line.turns, 2 * grads.turns)
    total = max(total, 2 * b_start + 1 + ways if k else 25)
    lax.fori_loop(0, total, turn_, 0)
    line.drain()
    grads.drain()
    if k == 1:
        b_store(ways - 2).wait()
        b_store(ways - 1).wait()
        return
    y_store(3).wait()
    share = norms.shape[0] // n

    def n_copy(step):
        owner = lax.rem(t + step, n)
        theirs = norms.at[pl.ds(pl.multiple_of(owner * share, share), share), :]
        return to(
            theirs, n_land.at[step - 1], n_send.at[step - 1], n_recv.at[step - 1], along[step - 1]
        )

    for step in range(1, n):
        n_copy(step).start()
    mine = norms[pl.ds(pl.multiple_of(t * share, share), share), :]
    for step in range(1, n):
        n_copy(step).wait()
        mine = mine + n_land[step - 1]
    norm_rows[...] = mine
    for step in range(1, n):
        yz_copy(step).wait_send()
    for s in range(max(line.subs - 2, 0), line.subs):
        d_store(s, line.sub).wait()

    @pl.when(p == 1)
    def _():
        for s in range(line.subs):
            d_copy(s, line.sub).wait_send()
        for q in range(4):
            yx_copy(q).wait_recv()

    @pl.when(p == 0)
    def _():
        for s in range(line.subs):
            d_copy(s, line.sub).wait_recv()
        for q in range(4):
            yx_copy(q).wait_send()


def back_section(
    k, g, xh, inv_std, scales, tables, seg, gains, weights, attended, slope, lefts, own, heads,
    n, ways, extra_in, held=None,
):
    tokens, width = g.shape
    part, rows = width // ways, tokens // n
    hidden, inner = slope.shape[1], 3 * attended[0].shape[1]
    size = inner // 3 // heads
    vmem, hbm = pl.BlockSpec(memory_space=pltpu.VMEM), pl.BlockSpec(memory_space=pl.ANY)
    shape, dma = jax.ShapeDtypeStruct, pltpu.SemaphoreType.DMA
    sides = (lefts[0].shape[1], lefts[1].shape[1], inner, hidden)
    count = sum(sides) // part
    out_shape = [shape((16, part), f32), shape((part, 128), f32)]
    out_specs = [vmem, vmem] + [hbm] * 4
    out_shape += [
        shape((side, part) if m < 2 else (part, side), f32) for m, side in enumerate(sides)
    ]
    if k == 0:
        out_shape += [shape((part // n, 128), f32)]
        out_shape += [shape((rows, width), f32), shape((rows, width), bf16)] * 2
        out_shape += [shape((n - 1, rows, width), bf16)]
        out_specs += [vmem] + [hbm] * 5
        block = rows // 4
        extra = [
            pltpu.VMEM((2, rows // subs_of(rows), width), f32),
            pltpu.VMEM((rows, width), bf16),
            dma((subs_of(rows),)),
            dma((subs_of(rows),)),
            dma((2,)),
            pltpu.VMEM((n, block, width), bf16),
            pltpu.VMEM((block, width), f32),
            pltpu.VMEM((rows, width), bf16),
            dma((n - 1,)),
            dma((n - 1,)),
            dma((4,)),
            dma((4,)),
            dma((n + 2,)),
            pltpu.VMEM((n - 1, part // n, 128), f32),
            dma((n - 1,)),
            dma((n - 1,)),
        ]
    else:
        out_shape += [shape((tokens, width), bf16)] * 2
        out_specs += [vmem, hbm]
        extra = []
    landing = GradSum.landing(ways, part, count)
    args = [
        g, xh, inv_std, scales, *tables, seg.reshape(-1, 1), seg.reshape(1, -1), *gains,
        *weights, *attended, slope, *lefts, *own, *(extra_in or ()),
    ]
    specs = [vmem] * 11 + [hbm] * (len(args) - 11)
    aliases = {}
    if k == 0:
        aliases = {len(args) + 1 + m: 2 + m for m in range(4)}
        args += held
        specs += [vmem] + [hbm] * 4
    line = LineSum.scratch(n, tokens, width, k == 1)
    return pl.pallas_call(
        functools.partial(back_kernel, n, ways, heads, k),
        in_specs=specs,
        out_specs=out_specs + [hbm] * 3,
        out_shape=out_shape + landing,
        input_output_aliases=aliases,
        scratch_shapes=[
            pltpu.VMEM((tokens, inner), bf16),
            pltpu.VMEM((tokens, hidden), bf16),
            pltpu.VMEM((tokens, width), bf16),
            *line,
            *BackWork.scratch(k == 1, ways, heads, tokens, width, hidden, size),
            *GradSum.scratch(ways, part, tokens, count),
            *extra,
        ],
        compiler_params=pltpu.CompilerParams(
            collective_id=3 + k, has_side_effects=True, vmem_limit_bytes=63 << 20
        ),
        cost_estimate=pl.CostEstimate(flops=0, bytes_accessed=600 << 20, transcendentals=0),
        name="back_section",
    )(*args)


def normalize(values):
    average = jnp.mean(values, axis=-1, keepdims=True)
    centred = values - average
    spread = jnp.mean(centred * centred, axis=-1, keepdims=True)
    inv_std = lax.rsqrt(spread + norm_epsilon)
    return (centred * inv_std, inv_std)


def per_device(
    boundary,
    segments,
    ln1_gain,
    ln1_bias,
    ln2_gain,
    ln2_bias,
    qkv_weight,
    qkv_bias,
    dense_weight,
    dense_bias,
    fc1_weight,
    fc1_bias,
    fc2_weight,
    fc2_bias,
):
    pipe, d, t = lax.axis_index("pipe"), lax.axis_index("dp"), lax.axis_index("tensor")
    ways, ring = lax.axis_size("dp"), lax.axis_size("dp") // 2
    nt = lax.axis_size("tensor")
    first = pipe == 0
    seqs, length, width = boundary.shape[1] // 2, boundary.shape[2], boundary.shape[3]
    tokens, rows, part = seqs * length, length // nt, width // ways
    heads, size = qkv_weight.shape[2], qkv_weight.shape[3] // 3
    y, c = d // 2, d % 2

    def pipe_send(v, source):
        return lax.ppermute(v, "pipe", [(source, 1 - source)])

    def true_order(v):
        parts = []
        for j in range(ways):
            place = ((j // 2 - y) % ring) * 2 + (c ^ (j % 2))
            parts.append(lax.dynamic_slice_in_dim(v, place * part, part, v.ndim - 1))
        return jnp.concatenate(parts, axis=-1)

    def together(*values):
        return list(lax.optimization_barrier(values))

    seg = lax.dynamic_slice_in_dim(segments, pipe * seqs, seqs, 0)
    shards = (
        qkv_weight[0].reshape(part, heads * 3 * size),
        fc1_weight[0],
        fc2_weight[0],
        dense_weight[0],
    )
    axes = (0, 0, 1, 1)
    def in_place(v):
        whole = jnp.zeros((v.shape[0], v.shape[1] * ways), bf16)
        whole = lax.dynamic_update_slice_in_dim(whole, v, d * v.shape[1], 1)
        return whole.reshape(-1, part)

    small = [ln1_gain, ln1_bias, ln2_gain, ln2_bias, dense_bias, fc2_bias]
    small = jnp.concatenate(small + [in_place(qkv_bias[0]), in_place(fc1_bias)], axis=0)
    small = jnp.pad(small, ((0, 16 - small.shape[0]), (0, 0)))
    source, cotangent, small_all, weights_0, weights_1, found = enter_section(
        boundary[0], small, shards, seg, axes, ways, nt, heads
    )
    tables, (xh0, inv0, ar0, qr0, kr0, vr0, act0, slope0) = found[:3], found[3:]
    small_all = small_all.reshape(ways, 2, 16, part).astype(f32)
    cut = heads * 3 * size

    def vectors(k):
        rows_ = small_all[:, k]
        found = [rows_[:, m].reshape(1, width) for m in range(6)]
        in_place = jnp.sum(rows_[:, 6:], axis=0).reshape(1, -1)
        return found + [in_place[:, cut : cut + fc1_weight.shape[2]], in_place[:, :cut]]

    def own_rows(v):
        return lax.dynamic_slice_in_dim(v.reshape(seqs, length, width), t * rows, rows, 1)

    def own_rows_of(v):
        return lax.dynamic_slice_in_dim(v, t * rows, rows, 0)

    def enter(k, x):
        g1, b1, g2, b2 = vectors(k)[:4]
        xhat, inv_std = normalize(x.astype(f32))
        n1 = (xhat * g1 + b1).astype(bf16)
        n2 = (xhat * g2 + b2).astype(bf16)
        return n1, n2, xhat.astype(bf16), inv_std

    wq0, w10, w20, wd0 = weights_0
    branch = (dot(ar0, wd0) + dot(act0, w20)).astype(bf16)
    base = (own_rows(source).astype(f32) + (vectors(0)[4] + vectors(0)[5])).reshape(-1, width)
    x1, weights_1, d_ar1, d_act1 = sum_spread(
        branch, base, cotangent, nt, weights_1, [shard.shape for shard in shards], axes, ways
    )
    wq1, w11, w21, wd1 = weights_1

    n1, n2, xh1, inv1 = enter(1, x1)
    g1, _, g2, _ = vectors(1)[:4]
    ar1, qr1, kr1, vr1 = attend(dot(n1, wq1), vectors(1)[7], tables, seg, heads, length)
    act1, d_hidden1 = gelu_matmul(n2, w11, vectors(1)[6], d_act1)

    def column(v):
        return v[0].astype(f32)[:, None]

    scales = jnp.concatenate([column(v) for v in (ln1_gain, ln1_bias, ln2_gain, ln2_bias)], axis=1)
    sums_1, norms, fc2_grad, dense_grad, qkv_grad, fc1_grad, g0, branch, *_ = back_section(
        1, cotangent, xh1, own_rows_of(inv1), scales, tables, seg, (g1, g2), (wq1, w11, w21, wd1),
        (qr1, kr1, vr1), d_hidden1, (act1, ar1), shards[:2], heads, nt, ways, (d_ar1,),
    )

    g1, _, g2, _ = vectors(0)[:4]
    base = (own_rows(x1).astype(f32) + (vectors(1)[4] + vectors(1)[5])).reshape(-1, width)
    found = back_section(
        0, g0, xh0, own_rows_of(inv0), scales, tables, seg, (g1, g2), weights_0,
        (qr0, kr0, vr0), slope0, (act0, ar0), shards[:2], heads, nt, ways,
        (branch, base), [norms, fc2_grad, dense_grad, qkv_grad, fc1_grad],
    )
    sums_0, norms, fc2_grad, dense_grad, qkv_grad, fc1_grad = found[:6]
    dx_rows, dx_away, y_rows, y_away = (v.reshape(seqs, rows, width) for v in found[7:11])
    dx_away, y_away = dx_away.astype(f32), y_away.astype(f32)

    boundary_out = true_order(
        jnp.where(
            first,
            jnp.concatenate([dx_rows, dx_away], axis=0),
            jnp.concatenate([y_away, y_rows], axis=0),
        )
    )[None]

    sums = jnp.where(first, sums_0, sums_1).reshape(-1)
    end = cut + shards[1].shape[1]
    qkv_sum, fc1_sum, g_sum = sums[:cut], sums[cut:end], sums[end : end + width]
    norms = found[6][:, :4].T

    qkv_grad = qkv_grad.reshape(part, heads, 3 * size)

    def own_part(v, axis):
        step = v.shape[axis] // ways
        return lax.dynamic_slice_in_dim(v, d * step, step, axis)

    bias_grad = own_part(g_sum, 0)[None]
    return (
        boundary_out,
        norms[0][None],
        norms[1][None],
        norms[2][None],
        norms[3][None],
        qkv_grad[None],
        own_part(qkv_sum.reshape(heads, 3 * size), 1)[None],
        dense_grad[None],
        bias_grad,
        fc1_grad[None],
        own_part(fc1_sum, 0)[None],
        fc2_grad[None],
        bias_grad,
    )


def solution(mesh):
    in_specs = (
        P("pipe", "dp", None, None),
        P("dp", None),
        P("pipe", "dp"),
        P("pipe", "dp"),
        P("pipe", "dp"),
        P("pipe", "dp"),
        P("pipe", "dp", "tensor", None),
        P("pipe", "tensor", "dp"),
        P("pipe", "tensor", "dp"),
        P("pipe", "dp"),
        P("pipe", "dp", "tensor"),
        P("pipe", ("tensor", "dp")),
        P("pipe", "tensor", "dp"),
        P("pipe", "dp"),
    )
    out_specs = (
        P("pipe", "dp", "tensor", None),
        P("pipe", ("dp", "tensor")),
        P("pipe", ("dp", "tensor")),
        P("pipe", ("dp", "tensor")),
        P("pipe", ("dp", "tensor")),
        P("pipe", "dp", "tensor", None),
        P("pipe", "tensor", "dp"),
        P("pipe", "tensor", "dp"),
        P("pipe", "dp"),
        P("pipe", "dp", "tensor"),
        P("pipe", ("tensor", "dp")),
        P("pipe", "tensor", "dp"),
        P("pipe", "dp"),
    )
    return jax.shard_map(
        per_device, mesh=mesh, in_specs=in_specs, out_specs=out_specs, check_vma=False
    )
```

```python
import functools
import math

import jax
import jax.numpy as jnp
from jax import lax
from jax.experimental import pallas as pl
from jax.experimental.pallas import tpu as pltpu
from jax.sharding import PartitionSpec as P

norm_epsilon = 1e-05
mask_fill = -1e30
BAND = 256
ROT = 128
f32, bf16 = jnp.float32, jnp.bfloat16


def dot(a, b, contract=((1,), (0,))):
    return lax.dot_general(a, b, (contract, ((), ())), preferred_element_type=f32)


def allowed(seg_col, seg_row, block):
    low = max(block - 1, 0) * BAND
    size = (block + 1) * BAND - low
    own = lax.broadcasted_iota(jnp.int32, (BAND, size), 0) + (block * BAND - low)
    key = lax.broadcasted_iota(jnp.int32, (BAND, size), 1)
    rows = pl.ds(block * BAND, BAND)
    return (own >= key) & (seg_col[rows, :] == seg_row[:, pl.ds(low, size)])


def turn(values, cos, forward, backward):
    head = values[:, :ROT]
    head = (
        head * cos
        + pltpu.roll(head, ROT - 32, 1) * forward
        + pltpu.roll(head, 32, 1) * backward
    )
    return jnp.concatenate([head, values[:, ROT:]], axis=1)


def attend_kernel(scale, qkv, bias, cos, sin_a, sin_b, seg_col, seg_row, out, qr, kr, vr):
    size = out.shape[1]
    for block in range(out.shape[0] // BAND):
        rows = pl.ds(block * BAND, BAND)
        c, a, b = cos[rows, :], sin_a[rows, :], sin_b[rows, :]
        q = turn(qkv[rows, :size] + bias[:, :size], c, a, b).astype(bf16)
        k = turn(qkv[rows, size : 2 * size] + bias[:, size : 2 * size], c, a, b).astype(bf16)
        qr[rows, :] = q
        kr[rows, :] = k
        vr[rows, :] = (qkv[rows, 2 * size :] + bias[:, 2 * size :]).astype(bf16)
        low = max(block - 1, 0) * BAND
        keys = pl.ds(low, (block + 1) * BAND - low)
        scores = dot(q, kr[keys, :], ((1,), (1,))) * scale
        scores = jnp.where(allowed(seg_col, seg_row, block), scores, mask_fill)
        weights = jnp.exp(scores - jnp.max(scores, axis=1, keepdims=True))
        weights = weights * (1.0 / jnp.sum(weights, axis=1, keepdims=True))
        out[rows, :] = dot(weights.astype(bf16), vr[keys, :]).astype(bf16)


def attend_back_kernel(
    scale, qr, kr, vr, grad, cos, sin_a, sin_b, seg_col, seg_row, out, out_sum, dk_acc, dv_acc
):
    size = grad.shape[1]
    blocks = grad.shape[0] // BAND
    sums = [jnp.zeros((1, size), f32)] * 3

    def emit(place, part, values):
        rows = pl.ds(place * BAND, BAND)
        if part < 2:
            values = turn(values, cos[rows, :], -sin_a[rows, :], -sin_b[rows, :])
        values = values.astype(bf16)
        out[rows, part * size : (part + 1) * size] = values
        sums[part] = sums[part] + jnp.sum(values.astype(f32), axis=0, keepdims=True)

    for block in range(blocks):
        rows = pl.ds(block * BAND, BAND)
        low = max(block - 1, 0) * BAND
        keys = pl.ds(low, (block + 1) * BAND - low)
        q, k, v, g = qr[rows, :], kr[keys, :], vr[keys, :], grad[rows, :]
        scores = dot(q, k, ((1,), (1,))) * scale
        scores = jnp.where(allowed(seg_col, seg_row, block), scores, mask_fill)
        weights = jnp.exp(scores - jnp.max(scores, axis=1, keepdims=True))
        weights = weights * (1.0 / jnp.sum(weights, axis=1, keepdims=True))
        grad_weights = dot(g, v, ((1,), (1,)))
        row_dot = jnp.sum(weights * grad_weights, axis=1, keepdims=True)
        grad_scores = (weights * (grad_weights - row_dot)).astype(bf16)
        emit(block, 0, dot(grad_scores, k) * scale)
        dk = dot(grad_scores, q, ((0,), (0,))) * scale
        dv = dot(weights.astype(bf16), g, ((0,), (0,)))
        if block > 0:
            emit(block - 1, 1, dk_acc[...] + dk[:BAND])
            emit(block - 1, 2, dv_acc[...] + dv[:BAND])
            dk, dv = dk[BAND:], dv[BAND:]
        if block == blocks - 1:
            emit(block, 1, dk)
            emit(block, 2, dv)
        else:
            dk_acc[...] = dk
            dv_acc[...] = dv
    out_sum[0] = jnp.concatenate(sums, axis=1)


def gelu_parts(h):
    t = 1.0 / (1.0 + (0.3275911 * math.sqrt(0.5)) * jnp.abs(h))
    poly = 1.061405429 * t - 1.453152027
    poly = poly * t + 1.421413741
    poly = poly * t - 0.284496736
    poly = poly * t + 0.254829592
    bell = jnp.exp(-0.5 * h * h)
    tail = 0.5 * poly * t * bell
    cdf = jnp.where(h >= 0.0, 1.0 - tail, tail)
    slope = cdf + h * bell * (1.0 / math.sqrt(2.0 * math.pi))
    return (h * cdf).astype(bf16), slope.astype(bf16)


def to(source, target, send, recv, place):
    return pltpu.make_async_remote_copy(
        src_ref=source,
        dst_ref=target,
        send_sem=send,
        recv_sem=recv,
        device_id=place,
        device_id_type=pl.DeviceIdType.MESH,
    )


def greet(places):
    barrier = pltpu.get_barrier_semaphore()
    for place in places:
        pl.semaphore_signal(
            barrier, inc=1, device_id=place, device_id_type=pl.DeviceIdType.MESH
        )
    pl.semaphore_wait(barrier, len(places))


def chunks_of(shapes, axes, part):
    return [
        (m, row, col)
        for m, (shape, axis) in enumerate(zip(shapes, axes))
        for row in range(0, shape[0], part)
        for col in range(0, shape[1], part)
    ]


def chunk_at(ref, axis, shape, chunk, slot, part):
    _, row, col = chunk
    row, col = (row + slot * shape[0], col) if axis == 0 else (row, col + slot * shape[1])
    return ref.at[pl.ds(row, part), pl.ds(col, part)]


class Spread:
    def __init__(self, full, shapes, axes, ways, sems):
        self.full, self.shapes, self.axes = full, shapes, axes
        self.ring = ways // 2
        self.y_send, self.y_recv, self.c_send, self.c_recv = sems
        self.part = shapes[3][1]
        self.chunks = chunks_of(shapes, axes, self.part)
        d = lax.axis_index("dp")
        y, c = d // 2, d % 2
        self.core = {"dp": y * 2 + (1 - c)}
        self.ahead = [{"dp": lax.rem(y + o, self.ring) * 2 + c} for o in range(1, self.ring)]

    def at(self, n, slot):
        m = self.chunks[n][0]
        return chunk_at(
            self.full[m], self.axes[m], self.shapes[m], self.chunks[n], slot, self.part
        )

    def y_copy(self, n, step, source):
        target = self.at(n, 2 * ((self.ring - step) % self.ring))
        return to(
            source, target, self.y_send.at[n, step - 1], self.y_recv.at[n, step - 1],
            self.ahead[step - 1],
        )

    def c_copy(self, n, o, source):
        target = self.at(n, 2 * o + 1)
        return to(source, target, self.c_send.at[n, o], self.c_recv.at[n, o], self.core)

    def begin(self, n, source):
        for step in range(1, self.ring):
            self.y_copy(n, step, source).start()
        self.c_copy(n, 0, source).start()

    def forward(self, n):
        for step in range(1, self.ring):
            o = (self.ring - step) % self.ring
            self.y_copy(n, step, self.at(n, 0)).wait_recv()
            self.c_copy(n, o, self.at(n, 2 * o)).start()

    def arrived(self, m):
        for n in range(len(self.chunks)):
            if self.chunks[n][0] == m:
                for o in range(self.ring):
                    self.c_copy(n, o, self.at(n, 2 * o)).wait_recv()

    def finish(self, waited=()):
        for n in range(len(self.chunks)):
            for step in range(1, self.ring):
                self.y_copy(n, step, self.at(n, 0)).wait_send()
            for o in range(self.ring):
                self.c_copy(n, o, self.at(n, 2 * o)).wait_send()
        for m in range(4):
            if m not in waited:
                self.arrived(m)

    @staticmethod
    def semaphores(pieces, ways):
        dma = pltpu.SemaphoreType.DMA
        return [dma((pieces, ways // 2 - 1))] * 2 + [dma((pieces, ways // 2))] * 2


def small_rows(sm, m, count, slots, part, scattered=False):
    def block(slot):
        return sm[pl.ds(slot * 32, 16), :].astype(f32)

    if not scattered:
        return jnp.concatenate([block(slot)[m : m + 1] for slot in range(slots)], axis=1)
    total = block(0)
    for slot in range(1, slots):
        total = total + block(slot)
    return jnp.concatenate([total[m + j : m + j + 1] for j in range(count)], axis=1)


def enter_kernel(
    ways, nt, axes, heads,
    boundary, small, s0, s1, s2, s3, seg_col, seg_row, frequency,
    source, cotangent, small_all, f0, f1, f2, f3, o0, o1, o2, o3,
    cos_out, sin_a_out, sin_b_out, xh_out, inv_out,
    ar_out, qr_out, kr_out, vr_out, act_out, slope_out,
    x_send, x_recv, y_send, y_recv, c_send, c_recv, z_send, z_recv,
    b0, b1, b2, b3, local, keep_sem, out_sem,
    xv, sm, n1, n2, wq, w1, packed, cos, sin_a, sin_b, xh, inv, ar, qr, kr, vr, act, slope,
):
    shards, bounce = (s0, s1, s2, s3), (b0, b1, b2, b3)
    shapes = [s.shape for s in shards]
    full, later = (f0, f1, f2, f3), (o0, o1, o2, o3)
    p, d, t = lax.axis_index("pipe"), lax.axis_index("dp"), lax.axis_index("tensor")
    sems = (y_send, y_recv, c_send, c_recv)
    now = Spread(full, shapes, axes, ways, sems)
    then = Spread(later, shapes, axes, ways, sems)
    ring, chunks, part = now.ring, now.chunks, now.part
    length = boundary.shape[1]
    rows = length // nt
    across = {"pipe": 1 - p}
    others = [{"tensor": lax.rem(t + step, nt)} for step in range(1, nt)]
    places = [
        (lax.rem(d // 2 + o, ring) * 2 + lax.rem(d + b, 2)) * part
        for o in range(ring)
        for b in range(2)
    ]
    mine = pl.ds(pl.multiple_of(t * rows, rows), rows)

    loads = [pltpu.make_async_copy(shards[m], bounce[m], local.at[m]) for m in range(4)]
    for load in loads:
        load.start()
    keeps = [
        pltpu.make_async_copy(
            boundary.at[p, :, pl.ds(pl.multiple_of(places[r], part), part)],
            xv.at[:, pl.ds(r * part, part)],
            keep_sem.at[r],
        )
        for r in range(ways)
    ]
    greet([across, now.core] + now.ahead + others)

    def in_shard(n):
        m, row, col = chunks[n]
        return shards[m].at[pl.ds(row, part), pl.ds(col, part)]

    def small_at(slot, count=32, row=0):
        return small_all.at[pl.ds(slot * 32 + row, count), :]

    def x_given(r, target):
        return to(
            boundary.at[1 - p, mine, pl.ds(pl.multiple_of(places[r], part), part)],
            target.at[mine, pl.ds(r * part, part)],
            x_send.at[r], x_recv.at[r], across,
        )

    def x_small():
        here = small_all.at[pl.ds(pl.multiple_of(p * 16, 16), 16), :]
        return to(small, here, x_send.at[ways], x_recv.at[ways], across)

    def x_copy(n, target):
        at = ways + 1 + n
        return to(in_shard(n), target, x_send.at[at], x_recv.at[at], across)

    def small_y(step):
        target = small_at(2 * ((ring - step) % ring))
        return to(
            small_at(0), target, y_send.at[last, step - 1], y_recv.at[last, step - 1],
            now.ahead[step - 1],
        )

    def small_c(o):
        target = small_at(2 * o + 1)
        return to(small_at(2 * o), target, c_send.at[last, o], c_recv.at[last, o], now.core)

    def stores(matrices):
        return [
            pltpu.make_async_copy(
                bounce[m],
                matrices[m].at[pl.ds(0, shapes[m][0]), :]
                if axes[m] == 0
                else matrices[m].at[:, pl.ds(0, shapes[m][1])],
                local.at[m],
            )
            for m in range(4)
        ]

    last = len(chunks)
    small_own = pltpu.make_async_copy(
        small, small_all.at[pl.ds(pl.multiple_of(p * 16, 16), 16), :], local.at[4]
    )
    small_own.start()
    x_small().start()

    @pl.when(p == 0)
    def _():
        for r in range(ways):
            x_given(r, source).start()

    @pl.when(p == 1)
    def _():
        for r in range(ways):
            x_given(r, cotangent).start()

    for keep in keeps:
        keep.start()
    for load in loads:
        load.wait()

    @pl.when(p == 0)
    def _():
        for store in stores(full):
            store.start()
        for n in range(last):
            x_copy(n, now.at(n, 0)).start()
            now.begin(n, in_shard(n))

    @pl.when(p == 1)
    def _():
        for store in stores(later):
            store.start()
        for n in range(last):
            x_copy(n, then.at(n, 0)).start()

    for keep in keeps:
        keep.wait()

    def kept_store(target):
        return pltpu.make_async_copy(xv, target, keep_sem.at[0])

    @pl.when(p == 0)
    def _():
        kept_store(source).start()

    @pl.when(p == 1)
    def _():
        kept_store(cotangent).start()

    small_own.wait()
    x_small().wait_recv()
    for step in range(1, ring):
        small_y(step).start()
    small_c(0).start()

    def table(block, _):
        at = pl.ds(pl.multiple_of(block * BAND, BAND), BAND)
        same = seg_col[at, :] == seg_row[...]
        key = lax.broadcasted_iota(jnp.int32, (BAND, length), 1)
        start = jnp.min(jnp.where(same, key, length), axis=1, keepdims=True)
        place = lax.broadcasted_iota(jnp.int32, (BAND, 1), 0) + block * BAND
        angle = (place - start).astype(f32) * frequency[...]
        lane = lax.broadcasted_iota(jnp.int32, (BAND, ROT), 1)
        sine = jnp.sin(angle)
        cos[at, :] = jnp.cos(angle)
        sin_a[at, :] = jnp.where(lane < 32, -sine, 0.0)
        sin_b[at, :] = jnp.where((lane >= 32) & (lane < 64), sine, 0.0)
        return 0

    lax.fori_loop(0, length // BAND, table, 0)
    outs = []

    def give(at, ref, target):
        outs.append(pltpu.make_async_copy(ref, target, out_sem.at[at]))
        outs[-1].start()

    give(0, cos, cos_out)
    give(1, sin_a, sin_a_out)
    give(2, sin_b, sin_b_out)

    kept_store(source).wait()
    for r in range(ways):
        x_given(r, source).wait_recv()

    def z_copy(step, ref):
        return to(
            ref.at[mine, :], ref.at[mine, :], z_send.at[step - 1], z_recv.at[step - 1],
            others[step - 1],
        )

    @pl.when(p == 0)
    def _():
        for step in range(1, nt):
            z_copy(step, cotangent).start()

    @pl.when(p == 1)
    def _():
        for step in range(1, nt):
            z_copy(step, source).start()

    for step in range(1, ring):
        small_y(step).wait_recv()
        small_c((ring - step) % ring).start()

    def norm():
        for step in range(1, nt):
            z_copy(step, source).wait_recv()
        for o in range(ring):
            small_c(o).wait()
        vectors = pltpu.make_async_copy(small_all, sm, keep_sem.at[1])
        vectors.start()

        @pl.when(p == 1)
        def _():
            whole = pltpu.make_async_copy(source, xv, keep_sem.at[0])
            whole.start()
            whole.wait()

        vectors.wait()
        g1, b1, g2, b2 = (small_rows(sm, m, 1, ways, part) for m in range(4))

        def block(step, _):
            at = pl.ds(pl.multiple_of(step * 128, 128), 128)
            x = xv[at, :].astype(f32)
            x = x - jnp.mean(x, axis=1, keepdims=True)
            inv_std = lax.rsqrt(jnp.mean(x * x, axis=1, keepdims=True) + norm_epsilon)
            x = x * inv_std
            inv[at, :] = inv_std
            xh[at, :] = x.astype(bf16)
            n1[at, :] = (x * g1 + b1).astype(bf16)
            n2[at, :] = (x * g2 + b2).astype(bf16)
            return 0

        lax.fori_loop(0, length // 128, block, 0)
        give(3, xh, xh_out)
        give(4, inv, inv_out)
        now.arrived(0)
        stores(full)[0].wait()
        pltpu.make_async_copy(full[0], wq, keep_sem.at[2]).start()

    size = wq.shape[1] // heads // 3

    def attention(h):
        if h == 0:
            pltpu.make_async_copy(full[0], wq, keep_sem.at[2]).wait()
            now.arrived(1)
            stores(full)[1].wait()
            pltpu.make_async_copy(full[1], w1, keep_sem.at[3]).start()
        cols = pl.ds(h * 3 * size, 3 * size)

        def block(step, _):
            at = pl.ds(pl.multiple_of(step * BAND, BAND), BAND)
            packed[at, :] = dot(n1[at, :], wq[:, cols])
            return 0

        lax.fori_loop(0, length // BAND, block, 0)
        bias = small_rows(sm, 6, heads * 3 * size // part, ways, part, True)
        bias = bias[:, h * 3 * size : (h + 1) * 3 * size]
        at = pl.ds(h * size, size)
        attend_kernel(
            1.0 / math.sqrt(size), packed, bias, cos, sin_a, sin_b, seg_col, seg_row,
            ar.at[:, at], qr.at[:, at], kr.at[:, at], vr.at[:, at],
        )
        if h == heads - 1:
            for n, (ref, target) in enumerate(
                ((ar, ar_out), (qr, qr_out), (kr, kr_out), (vr, vr_out))
            ):
                give(5 + n, ref, target)

    hidden = w1.shape[1] // part
    bias_row = 6 + heads * 3 * size // part

    def feed(j):
        if j == 0:
            pltpu.make_async_copy(full[1], w1, keep_sem.at[3]).wait()
        cols = pl.ds(j * part, part)
        bias = small_rows(sm, bias_row + j, 1, ways, part, True)

        def block(step, _):
            at = pl.ds(pl.multiple_of(step * BAND, BAND), BAND)
            act[at, cols], slope[at, cols] = gelu_parts(dot(n2[at, :], w1[:, cols]) + bias)
            return 0

        lax.fori_loop(0, length // BAND, block, 0)
        if j == hidden - 1:
            give(9, act, act_out)
            give(10, slope, slope_out)

    work = [[] for _ in range(last)]
    begin = min(7, last - 1)
    steps = [norm] + [functools.partial(attention, h) for h in range(heads)]
    for n, step in enumerate(steps):
        work[min(begin + n, last - 1)].append(step)
    for j in range(hidden):
        work[min(begin + len(steps) + j // 2, last - 1)].append(functools.partial(feed, j))

    for n in range(last):
        x_copy(n, now.at(n, 0)).wait_recv()

        @pl.when(p == 1)
        def _():
            now.begin(n, now.at(n, 0))

        if n > 0:
            now.forward(n - 1)
        for step in work[n]:
            step()
    now.forward(last - 1)

    now.finish((0, 1))
    for n in range(last):
        x_copy(n, now.at(n, 0)).wait_send()
    for step in range(1, ring):
        small_y(step).wait_send()
    x_small().wait_send()
    for r in range(ways):
        x_given(r, source).wait_send()
    for step in range(1, nt):
        z_copy(step, source).wait_send()
    for store in stores(full)[2:]:
        store.wait()
    for out in outs:
        out.wait()


def enter_section(boundary, small, shards, seg, axes, ways, nt, heads):
    hbm, vmem = pl.BlockSpec(memory_space=pl.ANY), pl.BlockSpec(memory_space=pltpu.VMEM)
    shape = jax.ShapeDtypeStruct
    part = shards[3].shape[1]
    length, width = boundary.shape[1:]
    pieces = len(chunks_of([s.shape for s in shards], axes, part))
    full = [
        shape((s.shape[0] * ways, s.shape[1]) if axis == 0 else (s.shape[0], s.shape[1] * ways), bf16)
        for s, axis in zip(shards, axes)
    ]
    dma = pltpu.SemaphoreType.DMA
    lane = jnp.arange(ROT, dtype=f32)
    frequency = jnp.exp(-math.log(10000.0) * 2.0 * (lane % 32) / 64)
    frequency = jnp.where(lane < 64, frequency, 0.0)[None]
    inner, columns = shards[0].shape[1], shards[1].shape[1]
    results = (
        [shape((length, ROT), f32)] * 3
        + [shape((length, width), bf16), shape((length, 1), f32)]
        + [shape((length, inner // 3), bf16)] * 4
        + [shape((length, columns), bf16)] * 2
    )
    out = pl.pallas_call(
        functools.partial(enter_kernel, ways, nt, axes, heads),
        in_specs=[hbm] * 6 + [vmem] * 3,
        out_specs=[hbm] * (11 + len(results)),
        out_shape=[
            shape((length, width), bf16),
            shape((length, width), bf16),
            shape((32 * ways, part), bf16),
            *full,
            *full,
            *results,
        ],
        scratch_shapes=[
            dma((ways + 1 + pieces,)),
            dma((ways + 1 + pieces,)),
            *Spread.semaphores(pieces + 1, ways),
            dma((nt - 1,)),
            dma((nt - 1,)),
            *[pltpu.VMEM(s.shape, bf16) for s in shards],
            dma((5,)),
            dma((max(ways, 4),)),
            dma((11,)),
            pltpu.VMEM((length, width), bf16),
            pltpu.VMEM((32 * ways, part), bf16),
            pltpu.VMEM((length, width), bf16),
            pltpu.VMEM((length, width), bf16),
            pltpu.VMEM(full[0].shape, bf16),
            pltpu.VMEM(full[1].shape, bf16),
            pltpu.VMEM((length, inner // heads), f32),
            *[pltpu.VMEM(r.shape, r.dtype) for r in results],
        ],
        compiler_params=pltpu.CompilerParams(
            collective_id=1, has_side_effects=True, vmem_limit_bytes=62 << 20
        ),
        cost_estimate=pl.CostEstimate(flops=0, bytes_accessed=600 << 20, transcendentals=0),
        name="enter_section",
    )(boundary, small, *shards, seg.reshape(-1, 1), seg.reshape(1, -1), frequency)
    return out[0], out[1], out[2], out[3:7], out[7:11], out[11:]


def subs_of(rows):
    return max(1, min(16, rows // 16))


class LineSum:
    def __init__(self, n, partial, right, left, sems, finished, out=None):
        self.n, self.partial, self.right, self.left = n, partial, right, left
        self.finished, self.out = finished, out
        self.r_send, self.r_recv, self.l_send, self.l_recv = sems[:4]
        self.spread = sems[4:]
        self.i = lax.axis_index("tensor")
        self.rows = partial.shape[0] // n
        self.subs = subs_of(self.rows)
        self.sub = self.rows // self.subs
        self.after = {"tensor": lax.rem(self.i + 1, n)}
        self.before = {"tensor": lax.rem(self.i + n - 1, n)}

    def at(self, ref, j, s):
        start = pl.multiple_of(j * self.rows + s * self.sub, self.sub)
        return ref.at[pl.ds(start, self.sub), :]

    def r_copy(self, j, s, source):
        target = self.at(self.right, j, s)
        return to(source, target, self.r_send.at[j, s], self.r_recv.at[j, s], self.after)

    def l_copy(self, j, s, source):
        target = self.at(self.left, j, s)
        return to(source, target, self.l_send.at[j, s], self.l_recv.at[j, s], self.before)

    def ar_copy(self, j, s):
        rows = self.at(self.out, j, s)
        return to(rows, rows, self.spread[0].at[j, s], self.spread[1].at[j, s], self.after)

    def al_copy(self, j, s):
        rows = self.at(self.out, j, s)
        return to(rows, rows, self.spread[2].at[j, s], self.spread[3].at[j, s], self.before)

    def add(self, ref, j, s):
        ref = self.at(ref, j, s)
        own = self.at(self.partial, j, s)[...].astype(f32)
        ref[...] = (ref[...].astype(f32) + own).astype(bf16)

    def reduce_right(self, s):
        for k in range(self.n - 1):
            j = self.n - 1 - k

            @pl.when(self.i == 0)
            def _():
                self.r_copy(j, s, self.at(self.partial, j, s)).start()

            @pl.when((self.i > 0) & (self.i < j))
            def _():
                self.r_copy(j, s, self.at(self.right, j, s)).wait_recv()
                self.add(self.right, j, s)
                self.r_copy(j, s, self.at(self.right, j, s)).start()

    def reduce_left(self, s):
        for k in range(self.n - 1):

            @pl.when(self.i == self.n - 1)
            def _():
                self.l_copy(k, s, self.at(self.partial, k, s)).start()

            @pl.when((self.i < self.n - 1) & (self.i > k))
            def _():
                self.l_copy(k, s, self.at(self.left, k, s)).wait_recv()
                self.add(self.left, k, s)
                self.l_copy(k, s, self.at(self.left, k, s)).start()

    def finish(self, s):
        i, n = self.i, self.n

        @pl.when(i > 0)
        def _():
            self.r_copy(i, s, self.at(self.right, i, s)).wait_recv()
            self.add(self.right, i, s)

        @pl.when(i == 0)
        def _():
            self.at(self.right, i, s)[...] = self.at(self.partial, i, s)[...]

        @pl.when(i < n - 1)
        def _():
            self.l_copy(i, s, self.at(self.left, i, s)).wait_recv()

        @pl.when(i == n - 1)
        def _():
            self.at(self.left, i, s)[...] = jnp.zeros((self.sub, self.left.shape[1]), bf16)

        total = self.at(self.right, i, s)[...].astype(f32)
        total = total + self.at(self.left, i, s)[...].astype(f32)
        self.finished(self, s, total)
        if self.out is not None:

            @pl.when(i < n - 1)
            def _():
                self.ar_copy(i, s).start()

            @pl.when(i > 0)
            def _():
                self.al_copy(i, s).start()

    def pass_on(self, step, s):
        i, n = self.i, self.n

        @pl.when(i >= step)
        def _():
            self.ar_copy(i - step, s).wait_recv()

            @pl.when(i < n - 1)
            def _():
                self.ar_copy(i - step, s).start()

        @pl.when(i + step < n)
        def _():
            self.al_copy(i + step, s).wait_recv()

            @pl.when(i > 0)
            def _():
                self.al_copy(i + step, s).start()

    @property
    def turns(self):
        return self.subs + (2 * self.n - 2 if self.out is not None else self.n - 1)

    def turn(self, it):
        def when_piece(s, act):
            @pl.when((s >= 0) & (s < self.subs))
            def _():
                act(s)

        when_piece(it - self.i, self.reduce_right)
        when_piece(it - (self.n - 1 - self.i), self.reduce_left)
        when_piece(it - (self.n - 1), self.finish)
        if self.out is not None:
            for step in range(1, self.n):
                when_piece(it - (self.n - 1) - step, functools.partial(self.pass_on, step))

    def drain(self):
        i, n = self.i, self.n

        def body(s, _):
            for j in range(n):

                @pl.when(i < j)
                def _():
                    self.r_copy(j, s, self.at(self.partial, j, s)).wait_send()

                @pl.when(i > j)
                def _():
                    self.l_copy(j, s, self.at(self.partial, j, s)).wait_send()

                if self.out is not None:

                    @pl.when((i >= j) & (i < n - 1))
                    def _():
                        self.ar_copy(j, s).wait_send()

                    @pl.when((i <= j) & (i > 0))
                    def _():
                        self.al_copy(j, s).wait_send()

            return 0

        lax.fori_loop(0, self.subs, body, 0)

    @staticmethod
    def scratch(n, tokens, width, spread):
        return [pltpu.VMEM((tokens, width), bf16)] * 2 + [
            pltpu.SemaphoreType.DMA((n, subs_of(tokens // n)))
        ] * (8 if spread else 4)


def middle_kernel(n, ways, axes, shapes, order, heads, *refs):
    take = iter(refs)

    def some(count):
        return [next(take) for _ in range(count)]

    base, shift, g, gains, q_bias, h_bias = some(6)
    tables, segs = some(3), some(2)
    act_in, ar_in, w2_in, wd_in = some(4)
    some(4)
    out, full, d_ar, d_act = next(take), some(4), next(take), next(take)
    results = some(8)
    partial, right, left = some(3)
    line_sems, parts_sems = some(8), some(4)
    x_send, x_recv, weight, result, w_sem, r_sem = some(6)
    big, wd, act, ar, wq, packed, qr, kr, vr, dh, inv, load_sem, out_sem = some(13)
    p = lax.axis_index("pipe")
    tokens, width = partial.shape
    hidden, inner = d_act.shape[1], d_ar.shape[1]
    size = inner // heads
    w2 = big.at[pl.ds(0, hidden), pl.ds(0, width)]
    w1 = big.at[pl.ds(0, width), pl.ds(0, hidden)]

    loads = [
        pltpu.make_async_copy(source, target, load_sem.at[i])
        for i, (source, target) in enumerate(
            ((ar_in, ar), (wd_in, wd), (act_in, act), (w2_in, w2))
        )
    ]
    for load in loads:
        load.start()

    def finished(line, s, total):
        mine = pl.ds(pl.multiple_of(s * line.sub, line.sub), line.sub)
        total = total + (base[mine, :].astype(f32) + shift[...])
        line.at(out, line.i, s)[...] = total.astype(bf16)

    line = LineSum(n, partial, right, left, line_sems, finished, out)
    parts = Spread(full, shapes, axes, ways, parts_sems)
    ring, part = parts.ring, parts.part
    across = {"pipe": 1 - p}
    greet([line.after, line.before, parts.core, across] + parts.ahead)
    count = len(parts.chunks)

    def x_copy(m, o):
        chunk = parts.at(m, 2 * o)
        return to(chunk, chunk, x_send.at[m, o - 1], x_recv.at[m, o - 1], across)

    for place, m in enumerate(order):
        parts.c_copy(m, 0, parts.at(m, 0)).start()

        @pl.when(p == place % 2)
        def _():
            for step in range(1, ring):
                parts.y_copy(m, step, parts.at(m, 0)).start()

    def from_ring(m):
        for step in range(1, ring):
            o = (ring - step) % ring
            parts.y_copy(m, step, parts.at(m, 0)).wait_recv()
            x_copy(m, o).start()
            parts.c_copy(m, o, parts.at(m, 2 * o)).start()

    def from_across(m):
        for o in range(1, ring):
            x_copy(m, o).wait_recv()
            parts.c_copy(m, o, parts.at(m, 2 * o)).start()

    groups = min(4, line.subs)
    height = line.rows // groups

    def last_matmul(group):
        def rows_of(ref):
            return jnp.concatenate(
                [ref[pl.ds(j * line.rows + group * height, height), :] for j in range(n)], axis=0
            )

        heads_rows, act_rows = rows_of(ar), rows_of(act)

        def column(step, _):
            cols = pl.ds(pl.multiple_of(step * part, part), part)
            value = dot(heads_rows, wd[:, cols]) + dot(act_rows, w2[:, cols])
            value = value.astype(bf16)
            for j in range(n):
                partial[pl.ds(j * line.rows + group * height, height), cols] = value[
                    j * height : (j + 1) * height
                ]
            return 0

        lax.fori_loop(0, ways, column, 0)

    for load in loads:
        load.wait()
    last_matmul(0)

    blocks = [("act", j) for j in range(hidden // part)] + [("ar", 0)]
    wd_rows = full[3].shape[0]

    def weight_load(i):
        kind, j = blocks[i]
        if kind == "act":
            source, target = full[2].at[pl.ds(j * part, part), :], weight.at[i % 2]
        else:
            source, target = full[3], weight.at[i % 2, pl.ds(0, wd_rows), :]
        return pltpu.make_async_copy(source, target, w_sem.at[i % 2])

    def store(i):
        kind, j = blocks[i]
        if kind == "act":
            at = pl.ds(j * part, part)
            return pltpu.make_async_copy(result.at[i % 2], d_act.at[:, at], r_sem.at[i % 2])
        return pltpu.make_async_copy(qr, d_ar, r_sem.at[2])

    def product(i):
        if i == 0:
            for m in (2, 3):
                parts.arrived(m)
            weight_load(0).start()
        weight_load(i).wait()
        if i + 1 < len(blocks):
            weight_load(i + 1).start()
        kind, _ = blocks[i]
        if kind == "act" and i >= 2:
            store(i - 2).wait()

        def body(step, _):
            at = pl.ds(pl.multiple_of(step * BAND, BAND), BAND)
            if kind == "act":
                result[i % 2, at, :] = dot(g[at, :], weight[i % 2], ((1,), (1,))).astype(bf16)
            else:
                value = dot(g[at, :], weight[i % 2, pl.ds(0, wd_rows), :], ((1,), (1,)))
                qr[at, :] = value.astype(bf16)
            return 0

        lax.fori_loop(0, g.shape[0] // BAND, body, 0)
        store(i).start()

    early = sum(parts.chunks[m][0] in (2, 3) for m in range(count))
    ready = 2 * (-(-early // 2) + 2)
    pairs = -(-count // 2)

    fetch_at = 2 * pairs + 4
    q_load = pltpu.make_async_copy(full[0], wq, load_sem.at[0])
    h_load = pltpu.make_async_copy(full[1], w1, load_sem.at[1])

    def turn_(half, _):
        line.turn(half)
        for pair in range(pairs):
            both = list(enumerate(order))[2 * pair : 2 * pair + 2]

            @pl.when(half == 2 * pair + 2)
            def _():
                for place, m in both:

                    @pl.when(p == place % 2)
                    def _():
                        from_ring(m)

            @pl.when(half == 2 * pair + 4)
            def _():
                for place, m in both:

                    @pl.when(p != place % 2)
                    def _():
                        from_across(m)

        for group in range(1, groups):

            @pl.when(half == line.subs // groups * group - 3)
            def _():
                last_matmul(group)

        for i in range(len(blocks)):

            @pl.when(half == ready + i)
            def _():
                product(i)

        @pl.when(half == fetch_at)
        def _():
            for m in (0, 1):
                parts.arrived(m)
            q_load.start()
            h_load.start()

        return 0

    total = max(line.turns, fetch_at + 1, ready + len(blocks))
    lax.fori_loop(0, total, turn_, 0)
    line.drain()
    store(len(blocks) - 1).wait()
    for i in range(max(len(blocks) - 3, 0), len(blocks) - 1):
        store(i).wait()

    xh, n1, n2 = partial, right, left
    given = []

    def give(at, ref):
        given.append(pltpu.make_async_copy(ref, results[at], out_sem.at[at]))
        given[-1].start()

    def grad_load(j):
        return pltpu.make_async_copy(
            d_act.at[:, pl.ds(j * part, part)], result.at[j % 2], r_sem.at[j % 2]
        )

    grad_load(0).start()
    g1, b1, g2, b2 = (gains[m : m + 1, :] for m in range(4))

    def norm(step, _):
        at = pl.ds(pl.multiple_of(step * 128, 128), 128)
        x = out[at, :].astype(f32)
        x = x - jnp.mean(x, axis=1, keepdims=True)
        inv_std = lax.rsqrt(jnp.mean(x * x, axis=1, keepdims=True) + norm_epsilon)
        x = x * inv_std
        inv[at, :] = inv_std
        xh[at, :] = x.astype(bf16)
        n1[at, :] = (x * g1 + b1).astype(bf16)
        n2[at, :] = (x * g2 + b2).astype(bf16)
        return 0

    lax.fori_loop(0, tokens // 128, norm, 0)
    give(0, xh)
    give(1, inv)
    q_load.wait()
    for h in range(heads):
        cols = pl.ds(h * 3 * size, 3 * size)

        def project(step, _):
            at = pl.ds(pl.multiple_of(step * BAND, BAND), BAND)
            packed[at, :] = dot(n1[at, :], wq[:, cols])
            return 0

        lax.fori_loop(0, tokens // BAND, project, 0)
        at = pl.ds(h * size, size)
        attend_kernel(
            1.0 / math.sqrt(size), packed, q_bias[:, h * 3 * size : (h + 1) * 3 * size],
            *tables, *segs, ar.at[:, at], qr.at[:, at], kr.at[:, at], vr.at[:, at],
        )
    for at, ref in enumerate((ar, qr, kr, vr)):
        give(2 + at, ref)
    h_load.wait()
    for j in range(hidden // part):
        cols = pl.ds(j * part, part)
        grad_load(j).wait()
        if j + 1 < hidden // part:
            grad_load(j + 1).start()

        def feed(step, _):
            at = pl.ds(pl.multiple_of(step * BAND, BAND), BAND)
            act[at, cols], slope = gelu_parts(dot(n2[at, :], w1[:, cols]) + h_bias[:, cols])
            grad = result[j % 2, at, :].astype(f32)
            dh[at, cols] = (slope.astype(f32) * grad).astype(bf16)
            return 0

        lax.fori_loop(0, tokens // BAND, feed, 0)
    give(6, act)
    give(7, dh)
    for place, m in enumerate(order):

        @pl.when(p == place % 2)
        def _():
            for step in range(1, ring):
                parts.y_copy(m, step, parts.at(m, 0)).wait_send()
                x_copy(m, step).wait_send()

        for o in range(ring):
            parts.c_copy(m, o, parts.at(m, 2 * o)).wait_send()
    for copy in given:
        copy.wait()


def middle(base, shift, g, gains, q_bias, h_bias, tables, seg, act, ar, w2, wd, full, shapes, axes,
           heads, n, ways):
    tokens, width = g.shape
    vmem = pl.BlockSpec(memory_space=pltpu.VMEM)
    hbm = pl.BlockSpec(memory_space=pl.ANY)
    shape, dma = jax.ShapeDtypeStruct, pltpu.SemaphoreType.DMA
    part = shapes[3][1]
    chunks = chunks_of(shapes, axes, part)
    pieces = len(chunks)
    order = sorted(range(pieces), key=lambda m: (2, 3, 0, 1)[chunks[m][0]])
    inner, hidden = shapes[3][0], shapes[2][0]
    large = max(hidden, width)
    results = [shape((tokens, width), bf16), shape((tokens, 1), f32)]
    results += [shape((tokens, inner), bf16)] * 4 + [shape((tokens, hidden), bf16)] * 2
    args = [base, shift, g, gains, q_bias, h_bias, *tables, seg.reshape(-1, 1), seg.reshape(1, -1)]
    args += [act, ar, w2, wd]
    out = pl.pallas_call(
        functools.partial(middle_kernel, n, ways, axes, shapes, order, heads),
        in_specs=[vmem] * 11 + [hbm] * 8,
        out_specs=[vmem] + [hbm] * 14,
        out_shape=[shape((tokens, width), bf16)]
        + [shape(w.shape, bf16) for w in full]
        + [shape((tokens, inner), bf16), shape((tokens, hidden), bf16)]
        + results,
        input_output_aliases={15 + m: 1 + m for m in range(4)},
        scratch_shapes=[pltpu.VMEM((tokens, width), bf16)]
        + LineSum.scratch(n, tokens, width, True)
        + Spread.semaphores(pieces, ways)
        + [dma((pieces, ways // 2 - 1))] * 2
        + [
            pltpu.VMEM((2, max(part, inner), width), bf16),
            pltpu.VMEM((2, tokens, part), bf16),
            dma((2,)),
            dma((3,)),
            pltpu.VMEM((large, large), bf16),
            pltpu.VMEM((inner, width), bf16),
            pltpu.VMEM((tokens, hidden), bf16),
            pltpu.VMEM((tokens, inner), bf16),
            pltpu.VMEM((width, 3 * inner), bf16),
            pltpu.VMEM((tokens, 3 * inner // heads), f32),
            *[pltpu.VMEM((tokens, inner), bf16)] * 3,
            pltpu.VMEM((tokens, hidden), bf16),
            pltpu.VMEM((tokens, 1), f32),
            dma((4,)),
            dma((8,)),
        ],
        compiler_params=pltpu.CompilerParams(
            collective_id=2, has_side_effects=True, vmem_limit_bytes=(63 << 20) + (256 << 10)
        ),
        cost_estimate=pl.CostEstimate(flops=0, bytes_accessed=600 << 20, transcendentals=0),
        name="middle",
    )(*args, *full)
    return out[0], out[1:5], out[5], out[7:]


class GradSum:
    def __init__(self, k, ways, xh, g, lefts, rights, outs, own, scales, vec_out, norms, refs):
        (
            self.from_core, self.from_ring, self.from_pipe,
            self.load, self.away, self.near, self.far, self.core_in, self.ring_in, self.pipe_in,
            self.done, self.weight, self.vec, self.v_held, self.v_round, self.v_across,
            self.load_sem, self.c_send, self.c_recv, self.y_send, self.y_recv,
            self.x_send, self.x_recv, self.out_sem, self.in_sem,
        ) = refs
        self.k, self.ring = k, ways // 2
        self.xh, self.g, self.lefts, self.rights, self.outs = xh, g, lefts, rights, outs
        self.own, self.scales, self.vec_out, self.norms = own, scales, vec_out, norms
        self.part = self.load.shape[2]
        self.counts = [side.shape[1] // self.part for side in (*lefts, *rights)]
        self.starts = [sum(self.counts[:m]) for m in range(4)]
        self.count = sum(self.counts)
        p, d = lax.axis_index("pipe"), lax.axis_index("dp")
        y, c = d // 2, d % 2
        self.p = p
        self.core = {"dp": y * 2 + (1 - c)}
        self.ahead = [{"dp": lax.rem(y + o, self.ring) * 2 + c} for o in range(1, self.ring)]
        self.other = {"pipe": 1 - p}

    def each(self, c, act, matrices=range(4)):
        for m in matrices:

            @pl.when((c >= self.starts[m]) & (c < self.starts[m] + self.counts[m]))
            def _():
                act(m, pl.multiple_of((c - self.starts[m]) * self.part, self.part))

    def fetch(self, c):
        def act(m, at):
            pltpu.make_async_copy(
                self.lefts[m].at[:, pl.ds(at, self.part)],
                self.load.at[lax.rem(c, 3)],
                self.load_sem.at[lax.rem(c, 3)],
            ).start()

        self.each(c, act, (0, 1))

    def fetched(self, c):
        slot = lax.rem(c, 3)
        pltpu.make_async_copy(
            self.lefts[0].at[:, pl.ds(0, self.part)], self.load.at[slot], self.load_sem.at[slot]
        ).wait()

    def piece(self, c, slot, use):
        cols = pl.ds(slot * self.part, self.part)

        @pl.when(c < self.starts[2])
        def _():
            use(dot(self.load[lax.rem(c, 3)], self.g[:, cols], ((0,), (0,))))

        def right(m, at):
            side = self.rights[m - 2][:, pl.ds(at, self.part)]
            use(dot(self.xh[:, cols], side, ((0,), (0,))))

        self.each(c, right, (2, 3))

    def c_copy(self, c, o):
        return to(
            self.away.at[lax.rem(c, 2), o], self.from_core.at[c, o],
            self.c_send.at[c, o], self.c_recv.at[c, o], self.core,
        )

    def y_copy(self, c, o):
        return to(
            self.far.at[lax.rem(c, 3), o - 1], self.from_ring.at[c, o - 1],
            self.y_send.at[c, o - 1], self.y_recv.at[c, o - 1], self.ahead[o - 1],
        )

    def x_copy(self, c):
        return to(
            self.near.at[lax.rem(c, 5)], self.from_pipe.at[c],
            self.x_send.at[c], self.x_recv.at[c], self.other,
        )

    def core_load(self, c, o):
        return pltpu.make_async_copy(
            self.from_core.at[c, o], self.core_in.at[o], self.in_sem.at[0, o]
        )

    def ring_load(self, c, o):
        return pltpu.make_async_copy(
            self.from_ring.at[c, o - 1], self.ring_in.at[o - 1], self.in_sem.at[1, o]
        )

    def pipe_load(self, c):
        return pltpu.make_async_copy(self.from_pipe.at[c], self.pipe_in, self.in_sem.at[1, 0])

    def weight_load(self, m, at):
        return pltpu.make_async_copy(
            self.own[m - 2].at[:, pl.ds(at, self.part)], self.weight, self.in_sem.at[2, 0]
        )

    def store(self, c, start):
        def act(m, at):
            out = self.outs[m]
            if m < 2:
                out = out.at[pl.ds(at, self.part), :]
            else:
                out = out.at[:, pl.ds(at, self.part)]
            copy = pltpu.make_async_copy(self.done, out, self.out_sem.at[0])
            copy.start() if start else copy.wait()

        self.each(c, act)

    @property
    def turns(self):
        return self.count + 5

    def begin(self):
        self.fetch(0)
        self.fetch(1)
        self.vec[...] = jnp.zeros(self.vec.shape, f32)

    def v_copy(self, stage, o=1):
        last = self.count
        if stage == 0:
            return to(
                self.vec, self.v_held, self.c_send.at[last, 0], self.c_recv.at[last, 0], self.core
            )
        if stage == 1:
            return to(
                self.v_held, self.v_round.at[o - 1],
                self.y_send.at[last, o - 1], self.y_recv.at[last, o - 1], self.ahead[o - 1],
            )
        return to(
            self.vec_out, self.v_across, self.x_send.at[last], self.x_recv.at[last], self.other
        )

    def turn(self, it, v_start):
        @pl.when((it >= 1) & (it < self.count + 1))
        def _():
            for o in range(self.ring):
                self.c_copy(it - 1, o).wait_recv()
                self.core_load(it - 1, o).start()

        @pl.when((it >= 3) & (it < self.count + 3))
        def _():
            for o in range(1, self.ring):
                self.y_copy(it - 3, o).wait_recv()
                self.ring_load(it - 3, o).start()

        at_end = (it >= 5) & (it < self.count + 5) & (self.p == self.k)

        @pl.when(at_end)
        def _():
            self.x_copy(it - 5).wait_recv()
            self.pipe_load(it - 5).start()
            self.each(it - 5, lambda m, at: self.weight_load(m, at).start(), (2, 3))

        @pl.when(it < self.count)
        def _():
            c = it

            @pl.when(c < self.starts[2])
            def _():
                self.fetched(c)

            for o in range(self.ring):

                @pl.when(c >= 2)
                def _():
                    self.c_copy(c - 2, o).wait_send()

                def use(value):
                    self.away[lax.rem(c, 2), o] = value.astype(bf16)

                self.piece(c, 2 * o + 1, use)
                self.c_copy(c, o).start()

        @pl.when((it >= 1) & (it < self.count + 1))
        def _():
            c = it - 1
            for o in range(self.ring - 1, -1, -1):
                self.core_load(c, o).wait()
                if o > 0:

                    @pl.when(c >= 3)
                    def _():
                        self.y_copy(c - 3, o).wait_send()

                    def use(value):
                        value = value + self.core_in[o].astype(f32)
                        self.far[lax.rem(c, 3), o - 1] = value.astype(bf16)

                    self.piece(c, 2 * o, use)
                    self.y_copy(c, o).start()
                else:

                    @pl.when((c >= 5) & (self.p != self.k))
                    def _():
                        self.x_copy(c - 5).wait_send()

                    def use(value):
                        value = value + self.core_in[o].astype(f32)
                        self.near[lax.rem(c, 5)] = value.astype(bf16)

                    self.piece(c, 0, use)
            self.fetch(c + 2)

        @pl.when((it >= 3) & (it < self.count + 3))
        def _():
            c = it - 3
            total = self.near[lax.rem(c, 5)].astype(f32)
            for o in range(1, self.ring):
                self.ring_load(c, o).wait()
                total = total + self.ring_in[o - 1].astype(f32)
            self.near[lax.rem(c, 5)] = total.astype(bf16)

            @pl.when(self.p != self.k)
            def _():
                self.x_copy(c).start()

        @pl.when(at_end)
        def _():
            c = it - 5

            @pl.when(c >= 1)
            def _():
                self.store(c - 1, False)

            self.pipe_load(c).wait()
            core = self.near[lax.rem(c, 5)].astype(f32) + self.pipe_in[...].astype(f32)

            @pl.when(c < self.starts[2])
            def _():
                self.done[...] = core

            def finish(m, at):
                gain, bias = self.scales[:, 2 * m - 4 : 2 * m - 3], self.scales[:, 2 * m - 3 : 2 * m - 2]
                row = self.vec_out[pl.ds(c - self.starts[2], 1), :]
                self.done[...] = gain * core + bias * row
                self.weight_load(m, at).wait()
                weight = self.weight[...].astype(f32)
                lane = lax.broadcasted_iota(jnp.int32, self.norms.shape, 1)
                gain_sum = jnp.sum(weight * core, axis=1, keepdims=True)
                bias_sum = jnp.sum(weight * row, axis=1, keepdims=True)
                both = jnp.where(lane == 2 * m - 4, gain_sum, 0.0)
                both = both + jnp.where(lane == 2 * m - 3, bias_sum, 0.0)
                self.norms[...] = self.norms[...] + both

            self.each(c, finish, (2, 3))
            self.store(c, True)

        @pl.when(it == v_start)
        def _():
            self.v_copy(0).start()

        @pl.when(it == v_start + 1)
        def _():
            self.v_copy(0).wait()
            self.v_held[...] = self.v_held[...] + self.vec[...]
            for o in range(1, self.ring):
                self.v_copy(1, o).start()

        @pl.when(it == v_start + 2)
        def _():
            total = self.v_held[...]
            for o in range(1, self.ring):
                self.v_copy(1, o).wait()
                total = total + self.v_round[o - 1]
            self.vec_out[...] = total

            @pl.when(self.p != self.k)
            def _():
                self.v_copy(2).start()

        @pl.when((it == v_start + 3) & (self.p == self.k))
        def _():
            self.v_copy(2).wait_recv()
            self.vec_out[...] = self.vec_out[...] + self.v_across[...]

    def drain(self):
        last = self.count
        for o in range(self.ring):
            for c in (last - 2, last - 1):
                self.c_copy(c, o).wait_send()
            for c in (last - 3, last - 2, last - 1):
                if o > 0:
                    self.y_copy(c, o).wait_send()

        @pl.when(self.p == self.k)
        def _():
            self.store(jnp.int32(last - 1), False)

        @pl.when(self.p != self.k)
        def _():
            self.v_copy(2).wait_send()
            for c in range(last - 5, last):
                self.x_copy(c).wait_send()

    @staticmethod
    def landing(ways, part, count):
        ring = ways // 2
        return [
            jax.ShapeDtypeStruct((count, *lead, part, part), bf16)
            for lead in ((ring,), (ring - 1,), ())
        ]

    @staticmethod
    def scratch(ways, part, tokens, count):
        ring = ways // 2
        dma = pltpu.SemaphoreType.DMA
        return [
            pltpu.VMEM((3, tokens, part), bf16),
            pltpu.VMEM((2, ring, part, part), bf16),
            pltpu.VMEM((5, part, part), bf16),
            pltpu.VMEM((3, ring - 1, part, part), bf16),
            pltpu.VMEM((ring, part, part), bf16),
            pltpu.VMEM((ring - 1, part, part), bf16),
            pltpu.VMEM((part, part), bf16),
            pltpu.VMEM((part, part), f32),
            pltpu.VMEM((part, part), bf16),
            pltpu.VMEM((16, part), f32),
            pltpu.VMEM((16, part), f32),
            pltpu.VMEM((ring - 1, 16, part), f32),
            pltpu.VMEM((16, part), f32),
            dma((3,)),
            dma((count + 1, ring)),
            dma((count + 1, ring)),
            dma((count + 1, ring - 1)),
            dma((count + 1, ring - 1)),
            dma((count + 1,)),
            dma((count + 1,)),
            dma((1,)),
            dma((3, max(ring, 2))),
        ]


class BackWork:
    def __init__(self, given, ways, heads, g, tables, segs, gains, hbm, dq, dh, u, vec, refs):
        self.given = given
        self.wq, self.w1, self.w2, self.wd, self.qr, self.kr, self.vr, self.slope = hbm
        (
            self.wa, self.wb, self.hq, self.hk, self.hv, self.sl, self.d_ar,
            self.q_sum, self.dk, self.dv, self.sem,
        ) = refs
        self.ways, self.heads, self.g, self.vec = ways, heads, g, vec
        self.tables, self.segs, self.gains = tables, segs, gains
        self.dq, self.dh, self.u_rows = dq, dh, u
        self.part = g.shape[1] // ways
        self.size = self.qr.shape[1] // heads
        pieces = [("head", h) for h in range(heads)]
        pieces += [("hidden", j) for j in range(dh.shape[1] // self.part)]
        pieces += [("rows", j) for j in range(ways)]
        self.pieces = pieces

    def loads(self, n):
        kind, j = self.pieces[n]
        slot, part, size = n % 2, self.part, self.size
        width, hidden, inner = self.g.shape[1], self.dh.shape[1], self.dq.shape[1]
        if kind == "head":
            cols = pl.ds(j * size, size)
            if self.given:
                pairs = [(self.wd.at[:, cols], self.d_ar.at[slot])]
            else:
                pairs = [(self.wd.at[cols, :], self.wa.at[slot, pl.ds(0, size), pl.ds(0, width)])]
            pairs += [
                (ref.at[:, cols], held.at[slot])
                for ref, held in ((self.qr, self.hq), (self.kr, self.hk), (self.vr, self.hv))
            ]
        elif kind == "hidden":
            at = pl.ds(j * part, part)
            pairs = [(self.slope.at[:, at], self.dh.at[:, at])] if self.given else [
                (self.w2.at[at, :], self.wa.at[slot, pl.ds(0, part), pl.ds(0, width)]),
                (self.slope.at[:, at], self.sl.at[slot]),
            ]
        else:
            at = pl.ds(j * part, part)
            pairs = [
                (self.w1.at[at, :], self.wa.at[slot, pl.ds(0, part), pl.ds(0, hidden)]),
                (self.wq.at[at, :], self.wb.at[slot, :, pl.ds(0, inner)]),
            ]
        return [
            pltpu.make_async_copy(source, target, self.sem.at[slot, i])
            for i, (source, target) in enumerate(pairs)
        ]

    def begin(self, n):
        if n < len(self.pieces):
            for load in self.loads(n):
                load.start()

    def run(self, n):
        for load in self.loads(n):
            load.wait()
        self.begin(n + 1)
        kind, j = self.pieces[n]
        getattr(self, kind)(j, n % 2)

    def blocks(self, act):
        def body(step, _):
            act(pl.ds(pl.multiple_of(step * BAND, BAND), BAND))
            return 0

        lax.fori_loop(0, self.g.shape[0] // BAND, body, 0)

    def head(self, h, slot):
        size, width = self.size, self.g.shape[1]
        weight = self.wa.at[slot, pl.ds(0, size), pl.ds(0, width)]

        def act(at):
            self.d_ar[0, at, :] = dot(self.g[at, :], weight[...], ((1,), (1,))).astype(bf16)

        if not self.given:
            self.blocks(act)
        attend_back_kernel(
            1.0 / math.sqrt(size), self.hq.at[slot], self.hk.at[slot], self.hv.at[slot],
            self.d_ar.at[slot if self.given else 0], *self.tables, *self.segs,
            self.dq.at[:, pl.ds(h * 3 * size, 3 * size)], self.q_sum.at[pl.ds(h, 1)],
            self.dk, self.dv,
        )
        if h == self.heads - 1:
            sums = jnp.concatenate([self.q_sum[i] for i in range(self.heads)], axis=1)
            for row in range(sums.shape[1] // self.part):
                self.vec[row : row + 1, :] = sums[:, row * self.part : (row + 1) * self.part]

    def hidden(self, j, slot):
        part, width = self.part, self.g.shape[1]
        weight = self.wa.at[slot, pl.ds(0, part), pl.ds(0, width)]
        cols = pl.ds(j * part, part)
        first = self.dq.shape[1] // part
        row = first + j
        self.vec[row : row + 1, :] = jnp.zeros((1, part), f32)

        def act(at):
            if self.given:
                value = self.dh[at, cols]
            else:
                value = dot(self.g[at, :], weight[...], ((1,), (1,)))
                value = (self.sl[slot, at, :].astype(f32) * value).astype(bf16)
                self.dh[at, cols] = value
            self.vec[row : row + 1, :] += jnp.sum(value.astype(f32), axis=0, keepdims=True)

        self.blocks(act)
        if j == 0:
            d = lax.axis_index("dp")
            ring = self.ways // 2
            for r in range(self.ways):
                place = lax.rem(d // 2 + r // 2, ring) * 2 + lax.rem(d + r % 2, 2)
                total = jnp.sum(self.g[:, pl.ds(r * part, part)].astype(f32), axis=0, keepdims=True)
                self.vec[pl.ds(first + self.dh.shape[1] // part + place, 1), :] = total

    def rows(self, j, slot):
        part, hidden, inner = self.part, self.dh.shape[1], self.dq.shape[1]
        weight_1 = self.wa.at[slot, pl.ds(0, part), pl.ds(0, hidden)]
        weight_q = self.wb.at[slot, :, pl.ds(0, inner)]
        cols = pl.ds(j * part, part)
        gain_1, gain_2 = (gain[:, cols] for gain in self.gains)

        def act(at):
            value = dot(self.dq[at, :], weight_q[...], ((1,), (1,))) * gain_1
            value = value + dot(self.dh[at, :], weight_1[...], ((1,), (1,))) * gain_2
            self.u_rows[at, cols] = value.astype(bf16)

        self.blocks(act)

    @staticmethod
    def scratch(given, ways, heads, tokens, width, hidden, size):
        part = width // ways
        return [
            pltpu.VMEM((2, max(part, size), max(width, hidden)), bf16),
            pltpu.VMEM((2, part, 3 * heads * size), bf16),
            *[pltpu.VMEM((2, tokens, size), bf16)] * 3,
            pltpu.VMEM((2, tokens, part), bf16),
            pltpu.VMEM((2 if given else 1, tokens, size), bf16),
            pltpu.VMEM((heads, 1, 3 * size), f32),
            *[pltpu.VMEM((BAND, size), f32)] * 2,
            pltpu.SemaphoreType.DMA((2, 4)),
        ]


def back_kernel(n, ways, heads, k, *refs):
    take = iter(refs)

    def some(count):
        return [next(take) for _ in range(count)]

    g, xh, inv_std, scales = some(4)
    tables, segs, gains = some(3), some(2), some(2)
    weights, attended, slope = some(4), some(3), next(take)
    lefts, own = some(2), some(2)
    outward = weights[2:]
    if k == 1:
        weights = weights[:2] + [None, next(take)]
    if k == 0:
        y_part, y_base = some(2)
        norms_in = next(take)
        some(4)
    vec_out, norms, outs = next(take), next(take), some(4)
    if k == 0:
        norm_rows, rows_out, rows_away, y_rows, y_away, y_land = some(6)
    else:
        out, branch = some(2)
    landing = some(3)
    dq, dh, u, right, left = some(5)
    line_sems = some(4 if k == 0 else 8)
    work_refs = some(11)
    grad_refs = landing + some(22)
    p, t = lax.axis_index("pipe"), lax.axis_index("tensor")
    other = {"pipe": 1 - p}
    if k == 0:
        stage, handed, d_send, d_recv, stage_sem = some(5)
        y_in, y_stage, y_handed, yz_send, yz_recv, yx_send, yx_recv, y_sem = some(8)
        n_land, n_send, n_recv = some(3)

    def d_copy(s, sub):
        mine = pl.ds(pl.multiple_of(s * sub, sub), sub)
        return to(handed.at[mine, :], rows_away.at[mine, :], d_send.at[s], d_recv.at[s], other)

    def d_store(s, sub):
        mine = pl.ds(pl.multiple_of(s * sub, sub), sub)
        slot = lax.rem(s, 2)
        return pltpu.make_async_copy(stage.at[slot], rows_out.at[mine, :], stage_sem.at[slot])

    def finished(line, s, total):
        mine = pl.ds(pl.multiple_of(s * line.sub, line.sub), line.sub)
        xr = line.at(xh, line.i, s)[...].astype(f32)
        mean = jnp.mean(total, axis=1, keepdims=True)
        proj = jnp.mean(total * xr, axis=1, keepdims=True)
        total = inv_std[mine, :] * (total - mean - xr * proj)
        total = line.at(g, line.i, s)[...].astype(f32) + total
        if k == 1:
            line.at(out, line.i, s)[...] = total.astype(bf16)
        else:

            @pl.when(s >= 2)
            def _():
                d_store(s - 2, line.sub).wait()

            stage[lax.rem(s, 2)] = total
            d_store(s, line.sub).start()
            handed[mine, :] = total.astype(bf16)

            @pl.when(p == 1)
            def _():
                d_copy(s, line.sub).start()

    line = LineSum(n, u, right, left, line_sems, finished, out if k else None)
    vec = grad_refs[12]
    work = BackWork(
        k == 1, ways, heads, g, tables, segs, gains, (*weights, *attended, slope), dq, dh, u, vec,
        work_refs,
    )
    grads = GradSum(k, ways, xh, g, lefts, (dq, dh), outs, own, scales, vec_out, norms, grad_refs)
    places = [line.after, line.before, grads.core, grads.other] + grads.ahead
    if k == 0:
        along = [{"tensor": lax.rem(t + step, n)} for step in range(1, n)]
        places = places[2:] + along
    greet(places)
    grads.begin()
    norms[...] = norms_in[...] if k == 0 else jnp.zeros(norms.shape, f32)
    work.begin(0)

    count = len(work.pieces)
    last_hidden = heads + dh.shape[1] // work.part
    middle = (last_hidden + count) // 2
    if k == 1:
        step = -(-(count - last_hidden) // 4)
        plan = {1: (0, 1), 3: (1, heads), 4: (heads, last_hidden)}
        plan |= {5 + i: (last_hidden + i * step, last_hidden + (i + 1) * step) for i in range(4)}
        begin, v_start = 9, 3
    else:
        mid_hidden = (heads + last_hidden) // 2
        plan = {
            3: (0, 1), 7: (1, heads), 9: (heads, mid_hidden), 11: (mid_hidden, last_hidden),
            13: (last_hidden, middle), 15: (middle, count),
        }
        begin, v_start = 16, 6

    if k == 0:
        block = y_base.shape[0] // 4
        width = y_base.shape[1]

        def yz_copy(step):
            owner = lax.rem(t + step, n)
            rows = y_base.shape[0]
            theirs = pl.ds(pl.multiple_of(owner * rows, rows), rows)
            return to(
                y_part.at[theirs, :], y_land.at[step - 1], yz_send.at[step - 1],
                yz_recv.at[step - 1], along[step - 1],
            )

        def yx_copy(q):
            mine = pl.ds(q * block, block)
            return to(y_handed.at[mine, :], y_away.at[mine, :], yx_send.at[q], yx_recv.at[q], other)

        def y_store(q):
            mine = pl.ds(q * block, block)
            return pltpu.make_async_copy(y_stage, y_rows.at[mine, :], y_sem.at[n + 1])

        def y_finish(q):
            mine = pl.ds(q * block, block)
            if q == 0:
                for step in range(1, n):
                    yz_copy(step).wait_recv()
            else:
                y_store(q - 1).wait()
            start = pl.multiple_of(t * y_base.shape[0] + q * block, block)
            loads = [pltpu.make_async_copy(y_part.at[pl.ds(start, block), :], y_in.at[0], y_sem.at[0])]
            loads += [
                pltpu.make_async_copy(y_land.at[step - 1, mine, :], y_in.at[step], y_sem.at[step])
                for step in range(1, n)
            ]
            loads.append(pltpu.make_async_copy(y_base.at[mine, :], y_stage, y_sem.at[n]))
            for load in loads:
                load.start()
            for load in loads:
                load.wait()
            total = y_stage[...]
            for step in range(n):
                total = total + y_in[step].astype(f32)
            y_stage[...] = total
            y_store(q).start()
            y_handed[mine, :] = total.astype(bf16)

            @pl.when(p == 0)
            def _():
                yx_copy(q).start()

        for step in range(1, n):
            yz_copy(step).start()

    b_start = grads.count + 1

    def b_loads(j):
        part = work.part
        cols = pl.ds(j * part, part)
        tokens, hidden = g.shape[0], dh.shape[1]
        half = min(tokens, hidden)
        pairs = [
            (outward[0].at[pl.ds(i * half, half), cols], grads.load.at[i, pl.ds(0, half), :])
            for i in range(hidden // half)
        ]
        rows = outward[1].shape[0]
        pairs.append((outward[1].at[:, cols], work.wb.at[j % 2, pl.ds(0, rows), pl.ds(0, part)]))
        if j == 0:
            pairs += [(lefts[0], dh), (lefts[1], dq.at[:, pl.ds(0, rows)])]
        return [
            pltpu.make_async_copy(source, target, work.sem.at[i // 4, i % 4])
            for i, (source, target) in enumerate(pairs)
        ]

    def b_store(j):
        part = work.part
        return pltpu.make_async_copy(
            work.sl.at[j % 2], branch.at[:, pl.ds(j * part, part)], grads.load_sem.at[j % 2]
        )

    def b_block(j):
        part, hidden = work.part, dh.shape[1]
        half = min(g.shape[0], hidden)
        rows = outward[1].shape[0]
        loads = b_loads(j)
        for load in loads:
            load.start()
        if j >= 2:
            b_store(j - 2).wait()
        for load in loads:
            load.wait()

        def act(at):
            value = dot(dq[at, pl.ds(0, rows)], work.wb[j % 2, pl.ds(0, rows), pl.ds(0, part)])
            for i in range(hidden // half):
                value = value + dot(
                    dh[at, pl.ds(i * half, half)], grads.load[i, pl.ds(0, half), :]
                )
            work.sl[j % 2, at, :] = value.astype(bf16)

        work.blocks(act)
        b_store(j).start()

    def turn_(half, _):
        @pl.when(half >= begin)
        def _():
            line.turn(half - begin)

        @pl.when(lax.rem(half, 2) == 0)
        def _():
            grads.turn(half // 2, v_start)

        for at, (low, high) in plan.items():

            @pl.when(half == at)
            def _():
                for piece in range(low, high):
                    work.run(piece)

        if k == 0:
            for q in range(4):

                @pl.when(half == 2 * q + 17)
                def _():
                    y_finish(q)

        else:
            for j in range(ways):

                @pl.when(half == 2 * b_start + 1 + j)
                def _():
                    b_block(j)

        return 0

    total = max(begin + line.turns, 2 * grads.turns)
    total = max(total, 2 * b_start + 1 + ways if k else 25)
    lax.fori_loop(0, total, turn_, 0)
    line.drain()
    grads.drain()
    if k == 1:
        b_store(ways - 2).wait()
        b_store(ways - 1).wait()
        return
    y_store(3).wait()
    share = norms.shape[0] // n

    def n_copy(step):
        owner = lax.rem(t + step, n)
        theirs = norms.at[pl.ds(pl.multiple_of(owner * share, share), share), :]
        return to(
            theirs, n_land.at[step - 1], n_send.at[step - 1], n_recv.at[step - 1], along[step - 1]
        )

    for step in range(1, n):
        n_copy(step).start()
    mine = norms[pl.ds(pl.multiple_of(t * share, share), share), :]
    for step in range(1, n):
        n_copy(step).wait()
        mine = mine + n_land[step - 1]
    norm_rows[...] = mine
    for step in range(1, n):
        yz_copy(step).wait_send()
    for s in range(max(line.subs - 2, 0), line.subs):
        d_store(s, line.sub).wait()

    @pl.when(p == 1)
    def _():
        for s in range(line.subs):
            d_copy(s, line.sub).wait_send()
        for q in range(4):
            yx_copy(q).wait_recv()

    @pl.when(p == 0)
    def _():
        for s in range(line.subs):
            d_copy(s, line.sub).wait_recv()
        for q in range(4):
            yx_copy(q).wait_send()


def back_section(
    k, g, xh, inv_std, scales, tables, seg, gains, weights, attended, slope, lefts, own, heads,
    n, ways, extra_in, held=None,
):
    tokens, width = g.shape
    part, rows = width // ways, tokens // n
    hidden, inner = slope.shape[1], 3 * attended[0].shape[1]
    size = inner // 3 // heads
    vmem, hbm = pl.BlockSpec(memory_space=pltpu.VMEM), pl.BlockSpec(memory_space=pl.ANY)
    shape, dma = jax.ShapeDtypeStruct, pltpu.SemaphoreType.DMA
    sides = (lefts[0].shape[1], lefts[1].shape[1], inner, hidden)
    count = sum(sides) // part
    out_shape = [shape((16, part), f32), shape((part, 128), f32)]
    out_specs = [vmem, vmem] + [hbm] * 4
    out_shape += [
        shape((side, part) if m < 2 else (part, side), f32) for m, side in enumerate(sides)
    ]
    if k == 0:
        out_shape += [shape((part // n, 128), f32)]
        out_shape += [shape((rows, width), f32), shape((rows, width), bf16)] * 2
        out_shape += [shape((n - 1, rows, width), bf16)]
        out_specs += [vmem] + [hbm] * 5
        block = rows // 4
        extra = [
            pltpu.VMEM((2, rows // subs_of(rows), width), f32),
            pltpu.VMEM((rows, width), bf16),
            dma((subs_of(rows),)),
            dma((subs_of(rows),)),
            dma((2,)),
            pltpu.VMEM((n, block, width), bf16),
            pltpu.VMEM((block, width), f32),
            pltpu.VMEM((rows, width), bf16),
            dma((n - 1,)),
            dma((n - 1,)),
            dma((4,)),
            dma((4,)),
            dma((n + 2,)),
            pltpu.VMEM((n - 1, part // n, 128), f32),
            dma((n - 1,)),
            dma((n - 1,)),
        ]
    else:
        out_shape += [shape((tokens, width), bf16)] * 2
        out_specs += [vmem, hbm]
        extra = []
    landing = GradSum.landing(ways, part, count)
    args = [
        g, xh, inv_std, scales, *tables, seg.reshape(-1, 1), seg.reshape(1, -1), *gains,
        *weights, *attended, slope, *lefts, *own, *(extra_in or ()),
    ]
    specs = [vmem] * 11 + [hbm] * (len(args) - 11)
    aliases = {}
    if k == 0:
        aliases = {len(args) + 1 + m: 2 + m for m in range(4)}
        args += held
        specs += [vmem] + [hbm] * 4
    line = LineSum.scratch(n, tokens, width, k == 1)
    return pl.pallas_call(
        functools.partial(back_kernel, n, ways, heads, k),
        in_specs=specs,
        out_specs=out_specs + [hbm] * 3,
        out_shape=out_shape + landing,
        input_output_aliases=aliases,
        scratch_shapes=[
            pltpu.VMEM((tokens, inner), bf16),
            pltpu.VMEM((tokens, hidden), bf16),
            pltpu.VMEM((tokens, width), bf16),
            *line,
            *BackWork.scratch(k == 1, ways, heads, tokens, width, hidden, size),
            *GradSum.scratch(ways, part, tokens, count),
            *extra,
        ],
        compiler_params=pltpu.CompilerParams(
            collective_id=3 + k, has_side_effects=True, vmem_limit_bytes=63 << 20
        ),
        cost_estimate=pl.CostEstimate(flops=0, bytes_accessed=600 << 20, transcendentals=0),
        name="back_section",
    )(*args)


def per_device(
    boundary,
    segments,
    ln1_gain,
    ln1_bias,
    ln2_gain,
    ln2_bias,
    qkv_weight,
    qkv_bias,
    dense_weight,
    dense_bias,
    fc1_weight,
    fc1_bias,
    fc2_weight,
    fc2_bias,
):
    pipe, d, t = lax.axis_index("pipe"), lax.axis_index("dp"), lax.axis_index("tensor")
    ways, ring = lax.axis_size("dp"), lax.axis_size("dp") // 2
    nt = lax.axis_size("tensor")
    first = pipe == 0
    seqs, length, width = boundary.shape[1] // 2, boundary.shape[2], boundary.shape[3]
    tokens, rows, part = seqs * length, length // nt, width // ways
    heads, size = qkv_weight.shape[2], qkv_weight.shape[3] // 3
    y, c = d // 2, d % 2

    def pipe_send(v, source):
        return lax.ppermute(v, "pipe", [(source, 1 - source)])

    def true_order(v):
        parts = []
        for j in range(ways):
            place = ((j // 2 - y) % ring) * 2 + (c ^ (j % 2))
            parts.append(lax.dynamic_slice_in_dim(v, place * part, part, v.ndim - 1))
        return jnp.concatenate(parts, axis=-1)

    def together(*values):
        return list(lax.optimization_barrier(values))

    seg = lax.dynamic_slice_in_dim(segments, pipe * seqs, seqs, 0)
    shards = (
        qkv_weight[0].reshape(part, heads * 3 * size),
        fc1_weight[0],
        fc2_weight[0],
        dense_weight[0],
    )
    axes = (0, 0, 1, 1)
    def in_place(v):
        whole = jnp.zeros((v.shape[0], v.shape[1] * ways), bf16)
        whole = lax.dynamic_update_slice_in_dim(whole, v, d * v.shape[1], 1)
        return whole.reshape(-1, part)

    small = [ln1_gain, ln1_bias, ln2_gain, ln2_bias, dense_bias, fc2_bias]
    small = jnp.concatenate(small + [in_place(qkv_bias[0]), in_place(fc1_bias)], axis=0)
    small = jnp.pad(small, ((0, 16 - small.shape[0]), (0, 0)))
    source, cotangent, small_all, weights_0, weights_1, found = enter_section(
        boundary[0], small, shards, seg, axes, ways, nt, heads
    )
    tables, (xh0, inv0, ar0, qr0, kr0, vr0, act0, slope0) = found[:3], found[3:]
    small_all = small_all.reshape(ways, 2, 16, part).astype(f32)
    cut = heads * 3 * size

    def vectors(k):
        rows_ = small_all[:, k]
        found = [rows_[:, m].reshape(1, width) for m in range(6)]
        in_place = jnp.sum(rows_[:, 6:], axis=0).reshape(1, -1)
        return found + [in_place[:, cut : cut + fc1_weight.shape[2]], in_place[:, :cut]]

    def own_rows(v):
        return lax.dynamic_slice_in_dim(v.reshape(seqs, length, width), t * rows, rows, 1)

    def own_rows_of(v):
        return lax.dynamic_slice_in_dim(v, t * rows, rows, 0)

    wq0, w10, w20, wd0 = weights_0
    v0, v1 = vectors(0), vectors(1)
    x1, weights_1, d_ar1, found = middle(
        own_rows(source).reshape(-1, width), v0[4] + v0[5], cotangent,
        jnp.concatenate(v1[:4], axis=0), v1[7], v1[6], tables, seg, act0, ar0, w20, wd0, weights_1,
        [shard.shape for shard in shards], axes, heads, nt, ways,
    )
    xh1, inv1, ar1, qr1, kr1, vr1, act1, d_hidden1 = found
    wq1, w11, w21, wd1 = weights_1

    g1, _, g2, _ = vectors(1)[:4]

    def column(v):
        return v[0].astype(f32)[:, None]

    scales = jnp.concatenate([column(v) for v in (ln1_gain, ln1_bias, ln2_gain, ln2_bias)], axis=1)
    sums_1, norms, fc2_grad, dense_grad, qkv_grad, fc1_grad, g0, branch, *_ = back_section(
        1, cotangent, xh1, own_rows_of(inv1), scales, tables, seg, (g1, g2), (wq1, w11, w21, wd1),
        (qr1, kr1, vr1), d_hidden1, (act1, ar1), shards[:2], heads, nt, ways, (d_ar1,),
    )

    g1, _, g2, _ = vectors(0)[:4]
    base = (own_rows(x1).astype(f32) + (vectors(1)[4] + vectors(1)[5])).reshape(-1, width)
    found = back_section(
        0, g0, xh0, own_rows_of(inv0), scales, tables, seg, (g1, g2), weights_0,
        (qr0, kr0, vr0), slope0, (act0, ar0), shards[:2], heads, nt, ways,
        (branch, base), [norms, fc2_grad, dense_grad, qkv_grad, fc1_grad],
    )
    sums_0, norms, fc2_grad, dense_grad, qkv_grad, fc1_grad = found[:6]
    dx_rows, dx_away, y_rows, y_away = (v.reshape(seqs, rows, width) for v in found[7:11])
    dx_away, y_away = dx_away.astype(f32), y_away.astype(f32)

    boundary_out = true_order(
        jnp.where(
            first,
            jnp.concatenate([dx_rows, dx_away], axis=0),
            jnp.concatenate([y_away, y_rows], axis=0),
        )
    )[None]

    sums = jnp.where(first, sums_0, sums_1).reshape(-1)
    end = cut + shards[1].shape[1]
    qkv_sum, fc1_sum, g_sum = sums[:cut], sums[cut:end], sums[end : end + width]
    norms = found[6][:, :4].T

    qkv_grad = qkv_grad.reshape(part, heads, 3 * size)

    def own_part(v, axis):
        step = v.shape[axis] // ways
        return lax.dynamic_slice_in_dim(v, d * step, step, axis)

    bias_grad = own_part(g_sum, 0)[None]
    return (
        boundary_out,
        norms[0][None],
        norms[1][None],
        norms[2][None],
        norms[3][None],
        qkv_grad[None],
        own_part(qkv_sum.reshape(heads, 3 * size), 1)[None],
        dense_grad[None],
        bias_grad,
        fc1_grad[None],
        own_part(fc1_sum, 0)[None],
        fc2_grad[None],
        bias_grad,
    )


def solution(mesh):
    in_specs = (
        P("pipe", "dp", None, None),
        P("dp", None),
        P("pipe", "dp"),
        P("pipe", "dp"),
        P("pipe", "dp"),
        P("pipe", "dp"),
        P("pipe", "dp", "tensor", None),
        P("pipe", "tensor", "dp"),
        P("pipe", "tensor", "dp"),
        P("pipe", "dp"),
        P("pipe", "dp", "tensor"),
        P("pipe", ("tensor", "dp")),
        P("pipe", "tensor", "dp"),
        P("pipe", "dp"),
    )
    out_specs = (
        P("pipe", "dp", "tensor", None),
        P("pipe", ("dp", "tensor")),
        P("pipe", ("dp", "tensor")),
        P("pipe", ("dp", "tensor")),
        P("pipe", ("dp", "tensor")),
        P("pipe", "dp", "tensor", None),
        P("pipe", "tensor", "dp"),
        P("pipe", "tensor", "dp"),
        P("pipe", "dp"),
        P("pipe", "dp", "tensor"),
        P("pipe", ("tensor", "dp")),
        P("pipe", "tensor", "dp"),
        P("pipe", "dp"),
    )
    return jax.shard_map(
        per_device, mesh=mesh, in_specs=in_specs, out_specs=out_specs, check_vma=False
    )
```

```python
import functools
import math

import jax
import jax.numpy as jnp
from jax import lax
from jax.experimental import pallas as pl
from jax.experimental.pallas import tpu as pltpu
from jax.sharding import PartitionSpec as P

norm_epsilon = 1e-05
mask_fill = -1e30
BAND = 256
ROT = 128
f32, bf16 = jnp.float32, jnp.bfloat16


def dot(a, b, contract=((1,), (0,))):
    return lax.dot_general(a, b, (contract, ((), ())), preferred_element_type=f32)


def allowed(seg_col, seg_row, block):
    low = max(block - 1, 0) * BAND
    size = (block + 1) * BAND - low
    own = lax.broadcasted_iota(jnp.int32, (BAND, size), 0) + (block * BAND - low)
    key = lax.broadcasted_iota(jnp.int32, (BAND, size), 1)
    rows = pl.ds(block * BAND, BAND)
    return (own >= key) & (seg_col[rows, :] == seg_row[:, pl.ds(low, size)])


def turn(values, cos, forward, backward):
    head = values[:, :ROT]
    head = (
        head * cos
        + pltpu.roll(head, ROT - 32, 1) * forward
        + pltpu.roll(head, 32, 1) * backward
    )
    return jnp.concatenate([head, values[:, ROT:]], axis=1)


def attend_kernel(scale, qkv, bias, cos, sin_a, sin_b, seg_col, seg_row, out, qr, kr, vr):
    size = out.shape[1]
    for block in range(out.shape[0] // BAND):
        rows = pl.ds(block * BAND, BAND)
        c, a, b = cos[rows, :], sin_a[rows, :], sin_b[rows, :]
        q = turn(qkv[rows, :size] + bias[:, :size], c, a, b).astype(bf16)
        k = turn(qkv[rows, size : 2 * size] + bias[:, size : 2 * size], c, a, b).astype(bf16)
        qr[rows, :] = q
        kr[rows, :] = k
        vr[rows, :] = (qkv[rows, 2 * size :] + bias[:, 2 * size :]).astype(bf16)
        low = max(block - 1, 0) * BAND
        keys = pl.ds(low, (block + 1) * BAND - low)
        scores = dot(q, kr[keys, :], ((1,), (1,))) * scale
        scores = jnp.where(allowed(seg_col, seg_row, block), scores, mask_fill)
        weights = jnp.exp(scores - jnp.max(scores, axis=1, keepdims=True))
        weights = weights * (1.0 / jnp.sum(weights, axis=1, keepdims=True))
        out[rows, :] = dot(weights.astype(bf16), vr[keys, :]).astype(bf16)


def attend_back_kernel(
    scale, qr, kr, vr, grad, cos, sin_a, sin_b, seg_col, seg_row, out, out_sum, dk_acc, dv_acc
):
    size = grad.shape[1]
    blocks = grad.shape[0] // BAND
    sums = [jnp.zeros((1, size), f32)] * 3

    def emit(place, part, values):
        rows = pl.ds(place * BAND, BAND)
        if part < 2:
            values = turn(values, cos[rows, :], -sin_a[rows, :], -sin_b[rows, :])
        values = values.astype(bf16)
        out[rows, part * size : (part + 1) * size] = values
        sums[part] = sums[part] + jnp.sum(values.astype(f32), axis=0, keepdims=True)

    for block in range(blocks):
        rows = pl.ds(block * BAND, BAND)
        low = max(block - 1, 0) * BAND
        keys = pl.ds(low, (block + 1) * BAND - low)
        q, k, v, g = qr[rows, :], kr[keys, :], vr[keys, :], grad[rows, :]
        scores = dot(q, k, ((1,), (1,))) * scale
        scores = jnp.where(allowed(seg_col, seg_row, block), scores, mask_fill)
        weights = jnp.exp(scores - jnp.max(scores, axis=1, keepdims=True))
        weights = weights * (1.0 / jnp.sum(weights, axis=1, keepdims=True))
        grad_weights = dot(g, v, ((1,), (1,)))
        row_dot = jnp.sum(weights * grad_weights, axis=1, keepdims=True)
        grad_scores = (weights * (grad_weights - row_dot)).astype(bf16)
        emit(block, 0, dot(grad_scores, k) * scale)
        dk = dot(grad_scores, q, ((0,), (0,))) * scale
        dv = dot(weights.astype(bf16), g, ((0,), (0,)))
        if block > 0:
            emit(block - 1, 1, dk_acc[...] + dk[:BAND])
            emit(block - 1, 2, dv_acc[...] + dv[:BAND])
            dk, dv = dk[BAND:], dv[BAND:]
        if block == blocks - 1:
            emit(block, 1, dk)
            emit(block, 2, dv)
        else:
            dk_acc[...] = dk
            dv_acc[...] = dv
    out_sum[0] = jnp.concatenate(sums, axis=1)


def gelu_parts(h):
    t = 1.0 / (1.0 + (0.3275911 * math.sqrt(0.5)) * jnp.abs(h))
    poly = 1.061405429 * t - 1.453152027
    poly = poly * t + 1.421413741
    poly = poly * t - 0.284496736
    poly = poly * t + 0.254829592
    bell = jnp.exp(-0.5 * h * h)
    tail = 0.5 * poly * t * bell
    cdf = jnp.where(h >= 0.0, 1.0 - tail, tail)
    slope = cdf + h * bell * (1.0 / math.sqrt(2.0 * math.pi))
    return (h * cdf).astype(bf16), slope.astype(bf16)


def to(source, target, send, recv, place):
    return pltpu.make_async_remote_copy(
        src_ref=source,
        dst_ref=target,
        send_sem=send,
        recv_sem=recv,
        device_id=place,
        device_id_type=pl.DeviceIdType.MESH,
    )


def greet(places):
    barrier = pltpu.get_barrier_semaphore()
    for place in places:
        pl.semaphore_signal(
            barrier, inc=1, device_id=place, device_id_type=pl.DeviceIdType.MESH
        )
    pl.semaphore_wait(barrier, len(places))


def chunks_of(shapes, axes, part):
    return [
        (m, row, col)
        for m, (shape, axis) in enumerate(zip(shapes, axes))
        for row in range(0, shape[0], part)
        for col in range(0, shape[1], part)
    ]


def chunk_at(ref, axis, shape, chunk, slot, part):
    _, row, col = chunk
    row, col = (row + slot * shape[0], col) if axis == 0 else (row, col + slot * shape[1])
    return ref.at[pl.ds(row, part), pl.ds(col, part)]


class Spread:
    def __init__(self, full, shapes, axes, ways, sems):
        self.full, self.shapes, self.axes = full, shapes, axes
        self.ring = ways // 2
        self.y_send, self.y_recv, self.c_send, self.c_recv = sems
        self.part = shapes[3][1]
        self.chunks = chunks_of(shapes, axes, self.part)
        d = lax.axis_index("dp")
        y, c = d // 2, d % 2
        self.core = {"dp": y * 2 + (1 - c)}
        self.ahead = [{"dp": lax.rem(y + o, self.ring) * 2 + c} for o in range(1, self.ring)]

    def at(self, n, slot):
        m = self.chunks[n][0]
        return chunk_at(
            self.full[m], self.axes[m], self.shapes[m], self.chunks[n], slot, self.part
        )

    def y_copy(self, n, step, source):
        target = self.at(n, 2 * ((self.ring - step) % self.ring))
        return to(
            source, target, self.y_send.at[n, step - 1], self.y_recv.at[n, step - 1],
            self.ahead[step - 1],
        )

    def c_copy(self, n, o, source):
        target = self.at(n, 2 * o + 1)
        return to(source, target, self.c_send.at[n, o], self.c_recv.at[n, o], self.core)

    def begin(self, n, source):
        for step in range(1, self.ring):
            self.y_copy(n, step, source).start()
        self.c_copy(n, 0, source).start()

    def forward(self, n):
        for step in range(1, self.ring):
            o = (self.ring - step) % self.ring
            self.y_copy(n, step, self.at(n, 0)).wait_recv()
            self.c_copy(n, o, self.at(n, 2 * o)).start()

    def arrived(self, m):
        for n in range(len(self.chunks)):
            if self.chunks[n][0] == m:
                for o in range(self.ring):
                    self.c_copy(n, o, self.at(n, 2 * o)).wait_recv()

    def finish(self, waited=()):
        for n in range(len(self.chunks)):
            for step in range(1, self.ring):
                self.y_copy(n, step, self.at(n, 0)).wait_send()
            for o in range(self.ring):
                self.c_copy(n, o, self.at(n, 2 * o)).wait_send()
        for m in range(4):
            if m not in waited:
                self.arrived(m)

    @staticmethod
    def semaphores(pieces, ways):
        dma = pltpu.SemaphoreType.DMA
        return [dma((pieces, ways // 2 - 1))] * 2 + [dma((pieces, ways // 2))] * 2


def small_rows(sm, m, count, slots, part, scattered=False):
    def block(slot):
        return sm[pl.ds(slot * 32, 16), :].astype(f32)

    if not scattered:
        return jnp.concatenate([block(slot)[m : m + 1] for slot in range(slots)], axis=1)
    total = block(0)
    for slot in range(1, slots):
        total = total + block(slot)
    return jnp.concatenate([total[m + j : m + j + 1] for j in range(count)], axis=1)


def enter_kernel(
    ways, nt, axes, heads,
    boundary, small, s0, s1, s2, s3, seg_col, seg_row, frequency,
    source, cotangent, small_all, f0, f1, f2, f3, o0, o1, o2, o3,
    cos_out, sin_a_out, sin_b_out, xh_out, inv_out,
    ar_out, qr_out, kr_out, vr_out, act_out, slope_out,
    x_send, x_recv, y_send, y_recv, c_send, c_recv, z_send, z_recv,
    b0, b1, b2, b3, local, keep_sem, out_sem,
    xv, sm, n1, n2, wq, w1, packed, cos, sin_a, sin_b, xh, inv, ar, qr, kr, vr, act, slope,
):
    shards, bounce = (s0, s1, s2, s3), (b0, b1, b2, b3)
    shapes = [s.shape for s in shards]
    full, later = (f0, f1, f2, f3), (o0, o1, o2, o3)
    p, d, t = lax.axis_index("pipe"), lax.axis_index("dp"), lax.axis_index("tensor")
    sems = (y_send, y_recv, c_send, c_recv)
    now = Spread(full, shapes, axes, ways, sems)
    then = Spread(later, shapes, axes, ways, sems)
    ring, chunks, part = now.ring, now.chunks, now.part
    length = boundary.shape[1]
    rows = length // nt
    across = {"pipe": 1 - p}
    others = [{"tensor": lax.rem(t + step, nt)} for step in range(1, nt)]
    places = [
        (lax.rem(d // 2 + o, ring) * 2 + lax.rem(d + b, 2)) * part
        for o in range(ring)
        for b in range(2)
    ]
    mine = pl.ds(pl.multiple_of(t * rows, rows), rows)

    loads = [pltpu.make_async_copy(shards[m], bounce[m], local.at[m]) for m in range(4)]
    for load in loads:
        load.start()
    keeps = [
        pltpu.make_async_copy(
            boundary.at[p, :, pl.ds(pl.multiple_of(places[r], part), part)],
            xv.at[:, pl.ds(r * part, part)],
            keep_sem.at[r],
        )
        for r in range(ways)
    ]
    greet([across, now.core] + now.ahead + others)

    def in_shard(n):
        m, row, col = chunks[n]
        return shards[m].at[pl.ds(row, part), pl.ds(col, part)]

    def small_at(slot, count=32, row=0):
        return small_all.at[pl.ds(slot * 32 + row, count), :]

    def x_given(r, target):
        return to(
            boundary.at[1 - p, mine, pl.ds(pl.multiple_of(places[r], part), part)],
            target.at[mine, pl.ds(r * part, part)],
            x_send.at[r], x_recv.at[r], across,
        )

    def x_small():
        here = small_all.at[pl.ds(pl.multiple_of(p * 16, 16), 16), :]
        return to(small, here, x_send.at[ways], x_recv.at[ways], across)

    def x_copy(n, target):
        at = ways + 1 + n
        return to(in_shard(n), target, x_send.at[at], x_recv.at[at], across)

    def small_y(step):
        target = small_at(2 * ((ring - step) % ring))
        return to(
            small_at(0), target, y_send.at[last, step - 1], y_recv.at[last, step - 1],
            now.ahead[step - 1],
        )

    def small_c(o):
        target = small_at(2 * o + 1)
        return to(small_at(2 * o), target, c_send.at[last, o], c_recv.at[last, o], now.core)

    def stores(matrices):
        return [
            pltpu.make_async_copy(
                bounce[m],
                matrices[m].at[pl.ds(0, shapes[m][0]), :]
                if axes[m] == 0
                else matrices[m].at[:, pl.ds(0, shapes[m][1])],
                local.at[m],
            )
            for m in range(4)
        ]

    last = len(chunks)
    small_own = pltpu.make_async_copy(
        small, small_all.at[pl.ds(pl.multiple_of(p * 16, 16), 16), :], local.at[4]
    )
    small_own.start()
    x_small().start()

    @pl.when(p == 0)
    def _():
        for r in range(ways):
            x_given(r, source).start()

    @pl.when(p == 1)
    def _():
        for r in range(ways):
            x_given(r, cotangent).start()

    for keep in keeps:
        keep.start()
    for load in loads:
        load.wait()

    @pl.when(p == 0)
    def _():
        for store in stores(full):
            store.start()
        for n in range(last):
            x_copy(n, now.at(n, 0)).start()
            now.begin(n, in_shard(n))

    @pl.when(p == 1)
    def _():
        for store in stores(later):
            store.start()
        for n in range(last):
            x_copy(n, then.at(n, 0)).start()

    for keep in keeps:
        keep.wait()

    def kept_store(target):
        return pltpu.make_async_copy(xv, target, keep_sem.at[0])

    @pl.when(p == 0)
    def _():
        kept_store(source).start()

    @pl.when(p == 1)
    def _():
        kept_store(cotangent).start()

    small_own.wait()
    x_small().wait_recv()
    for step in range(1, ring):
        small_y(step).start()
    small_c(0).start()

    def table(block, _):
        at = pl.ds(pl.multiple_of(block * BAND, BAND), BAND)
        same = seg_col[at, :] == seg_row[...]
        key = lax.broadcasted_iota(jnp.int32, (BAND, length), 1)
        start = jnp.min(jnp.where(same, key, length), axis=1, keepdims=True)
        place = lax.broadcasted_iota(jnp.int32, (BAND, 1), 0) + block * BAND
        angle = (place - start).astype(f32) * frequency[...]
        lane = lax.broadcasted_iota(jnp.int32, (BAND, ROT), 1)
        sine = jnp.sin(angle)
        cos[at, :] = jnp.cos(angle)
        sin_a[at, :] = jnp.where(lane < 32, -sine, 0.0)
        sin_b[at, :] = jnp.where((lane >= 32) & (lane < 64), sine, 0.0)
        return 0

    lax.fori_loop(0, length // BAND, table, 0)
    outs = []

    def give(at, ref, target):
        outs.append(pltpu.make_async_copy(ref, target, out_sem.at[at]))
        outs[-1].start()

    give(0, cos, cos_out)
    give(1, sin_a, sin_a_out)
    give(2, sin_b, sin_b_out)

    kept_store(source).wait()
    for r in range(ways):
        x_given(r, source).wait_recv()

    def z_copy(step, ref):
        return to(
            ref.at[mine, :], ref.at[mine, :], z_send.at[step - 1], z_recv.at[step - 1],
            others[step - 1],
        )

    @pl.when(p == 0)
    def _():
        for step in range(1, nt):
            z_copy(step, cotangent).start()

    @pl.when(p == 1)
    def _():
        for step in range(1, nt):
            z_copy(step, source).start()

    for step in range(1, ring):
        small_y(step).wait_recv()
        small_c((ring - step) % ring).start()

    def norm():
        for step in range(1, nt):
            z_copy(step, source).wait_recv()
        for o in range(ring):
            small_c(o).wait()
        vectors = pltpu.make_async_copy(small_all, sm, keep_sem.at[1])
        vectors.start()

        @pl.when(p == 1)
        def _():
            whole = pltpu.make_async_copy(source, xv, keep_sem.at[0])
            whole.start()
            whole.wait()

        vectors.wait()
        g1, b1, g2, b2 = (small_rows(sm, m, 1, ways, part) for m in range(4))

        def block(step, _):
            at = pl.ds(pl.multiple_of(step * 128, 128), 128)
            x = xv[at, :].astype(f32)
            x = x - jnp.mean(x, axis=1, keepdims=True)
            inv_std = lax.rsqrt(jnp.mean(x * x, axis=1, keepdims=True) + norm_epsilon)
            x = x * inv_std
            inv[at, :] = inv_std
            xh[at, :] = x.astype(bf16)
            n1[at, :] = (x * g1 + b1).astype(bf16)
            n2[at, :] = (x * g2 + b2).astype(bf16)
            return 0

        lax.fori_loop(0, length // 128, block, 0)
        give(3, xh, xh_out)
        give(4, inv, inv_out)
        now.arrived(0)
        stores(full)[0].wait()
        pltpu.make_async_copy(full[0], wq, keep_sem.at[2]).start()

    size = wq.shape[1] // heads // 3

    def attention(h):
        if h == 0:
            pltpu.make_async_copy(full[0], wq, keep_sem.at[2]).wait()
            now.arrived(1)
            stores(full)[1].wait()
            pltpu.make_async_copy(full[1], w1, keep_sem.at[3]).start()
        cols = pl.ds(h * 3 * size, 3 * size)

        def block(step, _):
            at = pl.ds(pl.multiple_of(step * BAND, BAND), BAND)
            packed[at, :] = dot(n1[at, :], wq[:, cols])
            return 0

        lax.fori_loop(0, length // BAND, block, 0)
        bias = small_rows(sm, 6, heads * 3 * size // part, ways, part, True)
        bias = bias[:, h * 3 * size : (h + 1) * 3 * size]
        at = pl.ds(h * size, size)
        attend_kernel(
            1.0 / math.sqrt(size), packed, bias, cos, sin_a, sin_b, seg_col, seg_row,
            ar.at[:, at], qr.at[:, at], kr.at[:, at], vr.at[:, at],
        )
        if h == heads - 1:
            for n, (ref, target) in enumerate(
                ((ar, ar_out), (qr, qr_out), (kr, kr_out), (vr, vr_out))
            ):
                give(5 + n, ref, target)

    hidden = w1.shape[1] // part
    bias_row = 6 + heads * 3 * size // part

    def feed(j):
        if j == 0:
            pltpu.make_async_copy(full[1], w1, keep_sem.at[3]).wait()
        cols = pl.ds(j * part, part)
        bias = small_rows(sm, bias_row + j, 1, ways, part, True)

        def block(step, _):
            at = pl.ds(pl.multiple_of(step * BAND, BAND), BAND)
            act[at, cols], slope[at, cols] = gelu_parts(dot(n2[at, :], w1[:, cols]) + bias)
            return 0

        lax.fori_loop(0, length // BAND, block, 0)
        if j == hidden - 1:
            give(9, act, act_out)
            give(10, slope, slope_out)

    work = [[] for _ in range(last)]
    begin = min(7, last - 1)
    steps = [norm] + [functools.partial(attention, h) for h in range(heads)]
    for n, step in enumerate(steps):
        work[min(begin + n, last - 1)].append(step)
    for j in range(hidden):
        work[min(begin + len(steps) + j // 2, last - 1)].append(functools.partial(feed, j))

    for n in range(last):
        x_copy(n, now.at(n, 0)).wait_recv()

        @pl.when(p == 1)
        def _():
            now.begin(n, now.at(n, 0))

        if n > 0:
            now.forward(n - 1)
        for step in work[n]:
            step()
    now.forward(last - 1)

    now.finish((0, 1))
    for n in range(last):
        x_copy(n, now.at(n, 0)).wait_send()
    for step in range(1, ring):
        small_y(step).wait_send()
    x_small().wait_send()
    for r in range(ways):
        x_given(r, source).wait_send()
    for step in range(1, nt):
        z_copy(step, source).wait_send()
    for store in stores(full)[2:]:
        store.wait()
    for out in outs:
        out.wait()


def enter_section(boundary, small, shards, seg, axes, ways, nt, heads):
    hbm, vmem = pl.BlockSpec(memory_space=pl.ANY), pl.BlockSpec(memory_space=pltpu.VMEM)
    shape = jax.ShapeDtypeStruct
    part = shards[3].shape[1]
    length, width = boundary.shape[1:]
    pieces = len(chunks_of([s.shape for s in shards], axes, part))
    full = [
        shape((s.shape[0] * ways, s.shape[1]) if axis == 0 else (s.shape[0], s.shape[1] * ways), bf16)
        for s, axis in zip(shards, axes)
    ]
    dma = pltpu.SemaphoreType.DMA
    lane = jnp.arange(ROT, dtype=f32)
    frequency = jnp.exp(-math.log(10000.0) * 2.0 * (lane % 32) / 64)
    frequency = jnp.where(lane < 64, frequency, 0.0)[None]
    inner, columns = shards[0].shape[1], shards[1].shape[1]
    results = (
        [shape((length, ROT), f32)] * 3
        + [shape((length, width), bf16), shape((length, 1), f32)]
        + [shape((length, inner // 3), bf16)] * 4
        + [shape((length, columns), bf16)] * 2
    )
    out = pl.pallas_call(
        functools.partial(enter_kernel, ways, nt, axes, heads),
        in_specs=[hbm] * 6 + [vmem] * 3,
        out_specs=[hbm] * (11 + len(results)),
        out_shape=[
            shape((length, width), bf16),
            shape((length, width), bf16),
            shape((32 * ways, part), bf16),
            *full,
            *full,
            *results,
        ],
        scratch_shapes=[
            dma((ways + 1 + pieces,)),
            dma((ways + 1 + pieces,)),
            *Spread.semaphores(pieces + 1, ways),
            dma((nt - 1,)),
            dma((nt - 1,)),
            *[pltpu.VMEM(s.shape, bf16) for s in shards],
            dma((5,)),
            dma((max(ways, 4),)),
            dma((11,)),
            pltpu.VMEM((length, width), bf16),
            pltpu.VMEM((32 * ways, part), bf16),
            pltpu.VMEM((length, width), bf16),
            pltpu.VMEM((length, width), bf16),
            pltpu.VMEM(full[0].shape, bf16),
            pltpu.VMEM(full[1].shape, bf16),
            pltpu.VMEM((length, inner // heads), f32),
            *[pltpu.VMEM(r.shape, r.dtype) for r in results],
        ],
        compiler_params=pltpu.CompilerParams(
            collective_id=1, has_side_effects=True, vmem_limit_bytes=62 << 20
        ),
        cost_estimate=pl.CostEstimate(flops=0, bytes_accessed=600 << 20, transcendentals=0),
        name="enter_section",
    )(boundary, small, *shards, seg.reshape(-1, 1), seg.reshape(1, -1), frequency)
    return out[0], out[1], out[2], out[3:7], out[7:11], out[11:]


def subs_of(rows):
    return max(1, min(16, rows // 16))


class LineSum:
    def __init__(self, n, partial, right, left, sems, finished, out=None):
        self.n, self.partial, self.right, self.left = n, partial, right, left
        self.finished, self.out = finished, out
        self.r_send, self.r_recv, self.l_send, self.l_recv = sems[:4]
        self.spread = sems[4:]
        self.i = lax.axis_index("tensor")
        self.rows = partial.shape[0] // n
        self.subs = subs_of(self.rows)
        self.sub = self.rows // self.subs
        self.after = {"tensor": lax.rem(self.i + 1, n)}
        self.before = {"tensor": lax.rem(self.i + n - 1, n)}

    def at(self, ref, j, s):
        start = pl.multiple_of(j * self.rows + s * self.sub, self.sub)
        return ref.at[pl.ds(start, self.sub), :]

    def r_copy(self, j, s, source):
        target = self.at(self.right, j, s)
        return to(source, target, self.r_send.at[j, s], self.r_recv.at[j, s], self.after)

    def l_copy(self, j, s, source):
        target = self.at(self.left, j, s)
        return to(source, target, self.l_send.at[j, s], self.l_recv.at[j, s], self.before)

    def ar_copy(self, j, s):
        rows = self.at(self.out, j, s)
        return to(rows, rows, self.spread[0].at[j, s], self.spread[1].at[j, s], self.after)

    def al_copy(self, j, s):
        rows = self.at(self.out, j, s)
        return to(rows, rows, self.spread[2].at[j, s], self.spread[3].at[j, s], self.before)

    def add(self, ref, j, s):
        ref = self.at(ref, j, s)
        own = self.at(self.partial, j, s)[...].astype(f32)
        ref[...] = (ref[...].astype(f32) + own).astype(bf16)

    def reduce_right(self, s):
        for k in range(self.n - 1):
            j = self.n - 1 - k

            @pl.when(self.i == 0)
            def _():
                self.r_copy(j, s, self.at(self.partial, j, s)).start()

            @pl.when((self.i > 0) & (self.i < j))
            def _():
                self.r_copy(j, s, self.at(self.right, j, s)).wait_recv()
                self.add(self.right, j, s)
                self.r_copy(j, s, self.at(self.right, j, s)).start()

    def reduce_left(self, s):
        for k in range(self.n - 1):

            @pl.when(self.i == self.n - 1)
            def _():
                self.l_copy(k, s, self.at(self.partial, k, s)).start()

            @pl.when((self.i < self.n - 1) & (self.i > k))
            def _():
                self.l_copy(k, s, self.at(self.left, k, s)).wait_recv()
                self.add(self.left, k, s)
                self.l_copy(k, s, self.at(self.left, k, s)).start()

    def finish(self, s):
        i, n = self.i, self.n

        @pl.when(i > 0)
        def _():
            self.r_copy(i, s, self.at(self.right, i, s)).wait_recv()
            self.add(self.right, i, s)

        @pl.when(i == 0)
        def _():
            self.at(self.right, i, s)[...] = self.at(self.partial, i, s)[...]

        @pl.when(i < n - 1)
        def _():
            self.l_copy(i, s, self.at(self.left, i, s)).wait_recv()

        @pl.when(i == n - 1)
        def _():
            self.at(self.left, i, s)[...] = jnp.zeros((self.sub, self.left.shape[1]), bf16)

        total = self.at(self.right, i, s)[...].astype(f32)
        total = total + self.at(self.left, i, s)[...].astype(f32)
        self.finished(self, s, total)
        if self.out is not None:

            @pl.when(i < n - 1)
            def _():
                self.ar_copy(i, s).start()

            @pl.when(i > 0)
            def _():
                self.al_copy(i, s).start()

    def pass_on(self, step, s):
        i, n = self.i, self.n

        @pl.when(i >= step)
        def _():
            self.ar_copy(i - step, s).wait_recv()

            @pl.when(i < n - 1)
            def _():
                self.ar_copy(i - step, s).start()

        @pl.when(i + step < n)
        def _():
            self.al_copy(i + step, s).wait_recv()

            @pl.when(i > 0)
            def _():
                self.al_copy(i + step, s).start()

    @property
    def turns(self):
        return self.subs + (2 * self.n - 2 if self.out is not None else self.n - 1)

    def turn(self, it):
        def when_piece(s, act):
            @pl.when((s >= 0) & (s < self.subs))
            def _():
                act(s)

        when_piece(it - self.i, self.reduce_right)
        when_piece(it - (self.n - 1 - self.i), self.reduce_left)
        when_piece(it - (self.n - 1), self.finish)
        if self.out is not None:
            for step in range(1, self.n):
                when_piece(it - (self.n - 1) - step, functools.partial(self.pass_on, step))

    def drain(self):
        i, n = self.i, self.n

        def body(s, _):
            for j in range(n):

                @pl.when(i < j)
                def _():
                    self.r_copy(j, s, self.at(self.partial, j, s)).wait_send()

                @pl.when(i > j)
                def _():
                    self.l_copy(j, s, self.at(self.partial, j, s)).wait_send()

                if self.out is not None:

                    @pl.when((i >= j) & (i < n - 1))
                    def _():
                        self.ar_copy(j, s).wait_send()

                    @pl.when((i <= j) & (i > 0))
                    def _():
                        self.al_copy(j, s).wait_send()

            return 0

        lax.fori_loop(0, self.subs, body, 0)

    @staticmethod
    def scratch(n, tokens, width, spread):
        return [pltpu.VMEM((tokens, width), bf16)] * 2 + [
            pltpu.SemaphoreType.DMA((n, subs_of(tokens // n)))
        ] * (8 if spread else 4)


def middle_kernel(n, ways, axes, shapes, order, heads, *refs):
    take = iter(refs)

    def some(count):
        return [next(take) for _ in range(count)]

    shift, g, gains, q_bias, h_bias = some(5)
    tables, segs = some(3), some(2)
    base_in, act_in, ar_in, w2_in, wd_in = some(5)
    some(4)
    out, full, d_ar, d_act = next(take), some(4), next(take), next(take)
    results = some(8)
    partial, right, left = some(3)
    line_sems, parts_sems = some(8), some(4)
    x_send, x_recv, weight, result, w_sem, r_sem = some(6)
    big, wd, act, ar, wq, packed, qr, kr, vr, dh, inv, base, load_sem, out_sem = some(14)
    p = lax.axis_index("pipe")
    tokens, width = partial.shape
    hidden, inner = d_act.shape[1], d_ar.shape[1]
    size = inner // heads
    w2 = big.at[pl.ds(0, hidden), pl.ds(0, width)]
    w1 = big.at[pl.ds(0, width), pl.ds(0, hidden)]

    t = lax.axis_index("tensor")
    rows = base.shape[0]
    own = base_in.at[pl.ds(pl.multiple_of(t * rows, rows), rows), :]
    loads = [
        pltpu.make_async_copy(source, target, load_sem.at[i])
        for i, (source, target) in enumerate(
            ((own, base), (ar_in, ar), (wd_in, wd), (act_in, act), (w2_in, w2))
        )
    ]
    for load in loads:
        load.start()

    def finished(line, s, total):
        mine = pl.ds(pl.multiple_of(s * line.sub, line.sub), line.sub)
        total = total + (base[mine, :].astype(f32) + shift[...])
        line.at(out, line.i, s)[...] = total.astype(bf16)

    line = LineSum(n, partial, right, left, line_sems, finished, out)
    parts = Spread(full, shapes, axes, ways, parts_sems)
    ring, part = parts.ring, parts.part
    across = {"pipe": 1 - p}
    greet([line.after, line.before, parts.core, across] + parts.ahead)
    count = len(parts.chunks)

    def x_copy(m, o):
        chunk = parts.at(m, 2 * o)
        return to(chunk, chunk, x_send.at[m, o - 1], x_recv.at[m, o - 1], across)

    for place, m in enumerate(order):
        parts.c_copy(m, 0, parts.at(m, 0)).start()

        @pl.when(p == place % 2)
        def _():
            for step in range(1, ring):
                parts.y_copy(m, step, parts.at(m, 0)).start()

    def from_ring(m):
        for step in range(1, ring):
            o = (ring - step) % ring
            parts.y_copy(m, step, parts.at(m, 0)).wait_recv()
            x_copy(m, o).start()
            parts.c_copy(m, o, parts.at(m, 2 * o)).start()

    def from_across(m):
        for o in range(1, ring):
            x_copy(m, o).wait_recv()
            parts.c_copy(m, o, parts.at(m, 2 * o)).start()

    groups = min(4, line.subs)
    height = line.rows // groups

    def last_matmul(group):
        def rows_of(ref):
            return jnp.concatenate(
                [ref[pl.ds(j * line.rows + group * height, height), :] for j in range(n)], axis=0
            )

        heads_rows, act_rows = rows_of(ar), rows_of(act)

        def column(step, _):
            cols = pl.ds(pl.multiple_of(step * part, part), part)
            value = dot(heads_rows, wd[:, cols]) + dot(act_rows, w2[:, cols])
            value = value.astype(bf16)
            for j in range(n):
                partial[pl.ds(j * line.rows + group * height, height), cols] = value[
                    j * height : (j + 1) * height
                ]
            return 0

        lax.fori_loop(0, ways, column, 0)

    for load in loads:
        load.wait()
    last_matmul(0)

    blocks = [("act", j) for j in range(hidden // part)] + [("ar", 0)]
    wd_rows = full[3].shape[0]

    def weight_load(i):
        kind, j = blocks[i]
        if kind == "act":
            source, target = full[2].at[pl.ds(j * part, part), :], weight.at[i % 2]
        else:
            source, target = full[3], weight.at[i % 2, pl.ds(0, wd_rows), :]
        return pltpu.make_async_copy(source, target, w_sem.at[i % 2])

    def store(i):
        kind, j = blocks[i]
        if kind == "act":
            at = pl.ds(j * part, part)
            return pltpu.make_async_copy(result.at[i % 2], d_act.at[:, at], r_sem.at[i % 2])
        return pltpu.make_async_copy(qr, d_ar, r_sem.at[2])

    def product(i):
        if i == 0:
            for m in (2, 3):
                parts.arrived(m)
            weight_load(0).start()
        weight_load(i).wait()
        if i + 1 < len(blocks):
            weight_load(i + 1).start()
        kind, _ = blocks[i]
        if kind == "act" and i >= 2:
            store(i - 2).wait()

        def body(step, _):
            at = pl.ds(pl.multiple_of(step * BAND, BAND), BAND)
            if kind == "act":
                result[i % 2, at, :] = dot(g[at, :], weight[i % 2], ((1,), (1,))).astype(bf16)
            else:
                value = dot(g[at, :], weight[i % 2, pl.ds(0, wd_rows), :], ((1,), (1,)))
                qr[at, :] = value.astype(bf16)
            return 0

        lax.fori_loop(0, g.shape[0] // BAND, body, 0)
        store(i).start()

    early = sum(parts.chunks[m][0] in (2, 3) for m in range(count))
    ready = 2 * (-(-early // 2) + 2)
    pairs = -(-count // 2)

    fetch_at = 2 * pairs + 4
    q_load = pltpu.make_async_copy(full[0], wq, load_sem.at[0])
    h_load = pltpu.make_async_copy(full[1], w1, load_sem.at[1])

    def turn_(half, _):
        line.turn(half)
        for pair in range(pairs):
            both = list(enumerate(order))[2 * pair : 2 * pair + 2]

            @pl.when(half == 2 * pair + 2)
            def _():
                for place, m in both:

                    @pl.when(p == place % 2)
                    def _():
                        from_ring(m)

            @pl.when(half == 2 * pair + 4)
            def _():
                for place, m in both:

                    @pl.when(p != place % 2)
                    def _():
                        from_across(m)

        for group in range(1, groups):

            @pl.when(half == line.subs // groups * group - 3)
            def _():
                last_matmul(group)

        for i in range(len(blocks)):

            @pl.when(half == ready + i)
            def _():
                product(i)

        @pl.when(half == fetch_at)
        def _():
            for m in (0, 1):
                parts.arrived(m)
            q_load.start()
            h_load.start()

        return 0

    total = max(line.turns, fetch_at + 1, ready + len(blocks))
    lax.fori_loop(0, total, turn_, 0)
    line.drain()
    store(len(blocks) - 1).wait()
    for i in range(max(len(blocks) - 3, 0), len(blocks) - 1):
        store(i).wait()

    xh, n1, n2 = partial, right, left
    given = []

    def give(at, ref):
        given.append(pltpu.make_async_copy(ref, results[at], out_sem.at[at]))
        given[-1].start()

    def grad_load(j):
        return pltpu.make_async_copy(
            d_act.at[:, pl.ds(j * part, part)], result.at[j % 2], r_sem.at[j % 2]
        )

    grad_load(0).start()
    g1, b1, g2, b2 = (gains[m : m + 1, :] for m in range(4))

    def norm(step, _):
        at = pl.ds(pl.multiple_of(step * 128, 128), 128)
        x = out[at, :].astype(f32)
        x = x - jnp.mean(x, axis=1, keepdims=True)
        inv_std = lax.rsqrt(jnp.mean(x * x, axis=1, keepdims=True) + norm_epsilon)
        x = x * inv_std
        inv[at, :] = inv_std
        xh[at, :] = x.astype(bf16)
        n1[at, :] = (x * g1 + b1).astype(bf16)
        n2[at, :] = (x * g2 + b2).astype(bf16)
        return 0

    lax.fori_loop(0, tokens // 128, norm, 0)
    give(0, xh)
    give(1, inv)
    q_load.wait()
    for h in range(heads):
        cols = pl.ds(h * 3 * size, 3 * size)

        def project(step, _):
            at = pl.ds(pl.multiple_of(step * BAND, BAND), BAND)
            packed[at, :] = dot(n1[at, :], wq[:, cols])
            return 0

        lax.fori_loop(0, tokens // BAND, project, 0)
        at = pl.ds(h * size, size)
        attend_kernel(
            1.0 / math.sqrt(size), packed, q_bias[:, h * 3 * size : (h + 1) * 3 * size],
            *tables, *segs, ar.at[:, at], qr.at[:, at], kr.at[:, at], vr.at[:, at],
        )
    for at, ref in enumerate((ar, qr, kr, vr)):
        give(2 + at, ref)
    h_load.wait()
    for j in range(hidden // part):
        cols = pl.ds(j * part, part)
        grad_load(j).wait()
        if j + 1 < hidden // part:
            grad_load(j + 1).start()

        def feed(step, _):
            at = pl.ds(pl.multiple_of(step * BAND, BAND), BAND)
            act[at, cols], slope = gelu_parts(dot(n2[at, :], w1[:, cols]) + h_bias[:, cols])
            grad = result[j % 2, at, :].astype(f32)
            dh[at, cols] = (slope.astype(f32) * grad).astype(bf16)
            return 0

        lax.fori_loop(0, tokens // BAND, feed, 0)
    give(6, act)
    give(7, dh)
    for place, m in enumerate(order):

        @pl.when(p == place % 2)
        def _():
            for step in range(1, ring):
                parts.y_copy(m, step, parts.at(m, 0)).wait_send()
                x_copy(m, step).wait_send()

        for o in range(ring):
            parts.c_copy(m, o, parts.at(m, 2 * o)).wait_send()
    for copy in given:
        copy.wait()


def middle(source, shift, g, gains, q_bias, h_bias, tables, seg, act, ar, w2, wd, full, shapes, axes,
           heads, n, ways):
    tokens, width = g.shape
    vmem = pl.BlockSpec(memory_space=pltpu.VMEM)
    hbm = pl.BlockSpec(memory_space=pl.ANY)
    shape, dma = jax.ShapeDtypeStruct, pltpu.SemaphoreType.DMA
    part = shapes[3][1]
    chunks = chunks_of(shapes, axes, part)
    pieces = len(chunks)
    order = sorted(range(pieces), key=lambda m: (2, 3, 0, 1)[chunks[m][0]])
    inner, hidden = shapes[3][0], shapes[2][0]
    large = max(hidden, width)
    results = [shape((tokens, width), bf16), shape((tokens, 1), f32)]
    results += [shape((tokens, inner), bf16)] * 4 + [shape((tokens, hidden), bf16)] * 2
    args = [shift, g, gains, q_bias, h_bias, *tables, seg.reshape(-1, 1), seg.reshape(1, -1)]
    args += [source, act, ar, w2, wd]
    out = pl.pallas_call(
        functools.partial(middle_kernel, n, ways, axes, shapes, order, heads),
        in_specs=[vmem] * 10 + [hbm] * 9,
        out_specs=[vmem] + [hbm] * 14,
        out_shape=[shape((tokens, width), bf16)]
        + [shape(w.shape, bf16) for w in full]
        + [shape((tokens, inner), bf16), shape((tokens, hidden), bf16)]
        + results,
        input_output_aliases={15 + m: 1 + m for m in range(4)},
        scratch_shapes=[pltpu.VMEM((tokens, width), bf16)]
        + LineSum.scratch(n, tokens, width, True)
        + Spread.semaphores(pieces, ways)
        + [dma((pieces, ways // 2 - 1))] * 2
        + [
            pltpu.VMEM((2, max(part, inner), width), bf16),
            pltpu.VMEM((2, tokens, part), bf16),
            dma((2,)),
            dma((3,)),
            pltpu.VMEM((large, large), bf16),
            pltpu.VMEM((inner, width), bf16),
            pltpu.VMEM((tokens, hidden), bf16),
            pltpu.VMEM((tokens, inner), bf16),
            pltpu.VMEM((width, 3 * inner), bf16),
            pltpu.VMEM((tokens, 3 * inner // heads), f32),
            *[pltpu.VMEM((tokens, inner), bf16)] * 3,
            pltpu.VMEM((tokens, hidden), bf16),
            pltpu.VMEM((tokens, 1), f32),
            pltpu.VMEM((tokens // n, width), bf16),
            dma((5,)),
            dma((8,)),
        ],
        compiler_params=pltpu.CompilerParams(
            collective_id=2, has_side_effects=True, vmem_limit_bytes=(63 << 20) + (256 << 10)
        ),
        cost_estimate=pl.CostEstimate(flops=0, bytes_accessed=600 << 20, transcendentals=0),
        name="middle",
    )(*args, *full)
    return out[0], out[1:5], out[5], out[7:]


class GradSum:
    def __init__(self, k, ways, xh, g, lefts, rights, outs, own, scales, vec_out, norms, refs):
        (
            self.from_core, self.from_ring, self.from_pipe,
            self.load, self.away, self.near, self.far, self.core_in, self.ring_in, self.pipe_in,
            self.done, self.weight, self.vec, self.v_held, self.v_round, self.v_across,
            self.load_sem, self.c_send, self.c_recv, self.y_send, self.y_recv,
            self.x_send, self.x_recv, self.out_sem, self.in_sem,
        ) = refs
        self.k, self.ring = k, ways // 2
        self.xh, self.g, self.lefts, self.rights, self.outs = xh, g, lefts, rights, outs
        self.own, self.scales, self.vec_out, self.norms = own, scales, vec_out, norms
        self.part = self.load.shape[2]
        self.counts = [side.shape[1] // self.part for side in (*lefts, *rights)]
        self.starts = [sum(self.counts[:m]) for m in range(4)]
        self.count = sum(self.counts)
        p, d = lax.axis_index("pipe"), lax.axis_index("dp")
        y, c = d // 2, d % 2
        self.p = p
        self.core = {"dp": y * 2 + (1 - c)}
        self.ahead = [{"dp": lax.rem(y + o, self.ring) * 2 + c} for o in range(1, self.ring)]
        self.other = {"pipe": 1 - p}

    def each(self, c, act, matrices=range(4)):
        for m in matrices:

            @pl.when((c >= self.starts[m]) & (c < self.starts[m] + self.counts[m]))
            def _():
                act(m, pl.multiple_of((c - self.starts[m]) * self.part, self.part))

    def fetch(self, c):
        def act(m, at):
            pltpu.make_async_copy(
                self.lefts[m].at[:, pl.ds(at, self.part)],
                self.load.at[lax.rem(c, 3)],
                self.load_sem.at[lax.rem(c, 3)],
            ).start()

        self.each(c, act, (0, 1))

    def fetched(self, c):
        slot = lax.rem(c, 3)
        pltpu.make_async_copy(
            self.lefts[0].at[:, pl.ds(0, self.part)], self.load.at[slot], self.load_sem.at[slot]
        ).wait()

    def piece(self, c, slot, use):
        cols = pl.ds(slot * self.part, self.part)

        @pl.when(c < self.starts[2])
        def _():
            use(dot(self.load[lax.rem(c, 3)], self.g[:, cols], ((0,), (0,))))

        def right(m, at):
            side = self.rights[m - 2][:, pl.ds(at, self.part)]
            use(dot(self.xh[:, cols], side, ((0,), (0,))))

        self.each(c, right, (2, 3))

    def c_copy(self, c, o):
        return to(
            self.away.at[lax.rem(c, 2), o], self.from_core.at[c, o],
            self.c_send.at[c, o], self.c_recv.at[c, o], self.core,
        )

    def y_copy(self, c, o):
        return to(
            self.far.at[lax.rem(c, 3), o - 1], self.from_ring.at[c, o - 1],
            self.y_send.at[c, o - 1], self.y_recv.at[c, o - 1], self.ahead[o - 1],
        )

    def x_copy(self, c):
        return to(
            self.near.at[lax.rem(c, 5)], self.from_pipe.at[c],
            self.x_send.at[c], self.x_recv.at[c], self.other,
        )

    def core_load(self, c, o):
        return pltpu.make_async_copy(
            self.from_core.at[c, o], self.core_in.at[o], self.in_sem.at[0, o]
        )

    def ring_load(self, c, o):
        return pltpu.make_async_copy(
            self.from_ring.at[c, o - 1], self.ring_in.at[o - 1], self.in_sem.at[1, o]
        )

    def pipe_load(self, c):
        return pltpu.make_async_copy(self.from_pipe.at[c], self.pipe_in, self.in_sem.at[1, 0])

    def weight_load(self, m, at):
        return pltpu.make_async_copy(
            self.own[m - 2].at[:, pl.ds(at, self.part)], self.weight, self.in_sem.at[2, 0]
        )

    def store(self, c, start):
        def act(m, at):
            out = self.outs[m]
            if m < 2:
                out = out.at[pl.ds(at, self.part), :]
            else:
                out = out.at[:, pl.ds(at, self.part)]
            copy = pltpu.make_async_copy(self.done, out, self.out_sem.at[0])
            copy.start() if start else copy.wait()

        self.each(c, act)

    @property
    def turns(self):
        return self.count + 5

    def begin(self):
        self.fetch(0)
        self.fetch(1)
        self.vec[...] = jnp.zeros(self.vec.shape, f32)

    def v_copy(self, stage, o=1):
        last = self.count
        if stage == 0:
            return to(
                self.vec, self.v_held, self.c_send.at[last, 0], self.c_recv.at[last, 0], self.core
            )
        if stage == 1:
            return to(
                self.v_held, self.v_round.at[o - 1],
                self.y_send.at[last, o - 1], self.y_recv.at[last, o - 1], self.ahead[o - 1],
            )
        return to(
            self.vec_out, self.v_across, self.x_send.at[last], self.x_recv.at[last], self.other
        )

    def turn(self, it, v_start):
        @pl.when((it >= 1) & (it < self.count + 1))
        def _():
            for o in range(self.ring):
                self.c_copy(it - 1, o).wait_recv()
                self.core_load(it - 1, o).start()

        @pl.when((it >= 3) & (it < self.count + 3))
        def _():
            for o in range(1, self.ring):
                self.y_copy(it - 3, o).wait_recv()
                self.ring_load(it - 3, o).start()

        at_end = (it >= 5) & (it < self.count + 5) & (self.p == self.k)

        @pl.when(at_end)
        def _():
            self.x_copy(it - 5).wait_recv()
            self.pipe_load(it - 5).start()
            self.each(it - 5, lambda m, at: self.weight_load(m, at).start(), (2, 3))

        @pl.when(it < self.count)
        def _():
            c = it

            @pl.when(c < self.starts[2])
            def _():
                self.fetched(c)

            for o in range(self.ring):

                @pl.when(c >= 2)
                def _():
                    self.c_copy(c - 2, o).wait_send()

                def use(value):
                    self.away[lax.rem(c, 2), o] = value.astype(bf16)

                self.piece(c, 2 * o + 1, use)
                self.c_copy(c, o).start()

        @pl.when((it >= 1) & (it < self.count + 1))
        def _():
            c = it - 1
            for o in range(self.ring - 1, -1, -1):
                self.core_load(c, o).wait()
                if o > 0:

                    @pl.when(c >= 3)
                    def _():
                        self.y_copy(c - 3, o).wait_send()

                    def use(value):
                        value = value + self.core_in[o].astype(f32)
                        self.far[lax.rem(c, 3), o - 1] = value.astype(bf16)

                    self.piece(c, 2 * o, use)
                    self.y_copy(c, o).start()
                else:

                    @pl.when((c >= 5) & (self.p != self.k))
                    def _():
                        self.x_copy(c - 5).wait_send()

                    def use(value):
                        value = value + self.core_in[o].astype(f32)
                        self.near[lax.rem(c, 5)] = value.astype(bf16)

                    self.piece(c, 0, use)
            self.fetch(c + 2)

        @pl.when((it >= 3) & (it < self.count + 3))
        def _():
            c = it - 3
            total = self.near[lax.rem(c, 5)].astype(f32)
            for o in range(1, self.ring):
                self.ring_load(c, o).wait()
                total = total + self.ring_in[o - 1].astype(f32)
            self.near[lax.rem(c, 5)] = total.astype(bf16)

            @pl.when(self.p != self.k)
            def _():
                self.x_copy(c).start()

        @pl.when(at_end)
        def _():
            c = it - 5

            @pl.when(c >= 1)
            def _():
                self.store(c - 1, False)

            self.pipe_load(c).wait()
            core = self.near[lax.rem(c, 5)].astype(f32) + self.pipe_in[...].astype(f32)

            @pl.when(c < self.starts[2])
            def _():
                self.done[...] = core

            def finish(m, at):
                gain, bias = self.scales[:, 2 * m - 4 : 2 * m - 3], self.scales[:, 2 * m - 3 : 2 * m - 2]
                row = self.vec_out[pl.ds(c - self.starts[2], 1), :]
                self.done[...] = gain * core + bias * row
                self.weight_load(m, at).wait()
                weight = self.weight[...].astype(f32)
                lane = lax.broadcasted_iota(jnp.int32, self.norms.shape, 1)
                gain_sum = jnp.sum(weight * core, axis=1, keepdims=True)
                bias_sum = jnp.sum(weight * row, axis=1, keepdims=True)
                both = jnp.where(lane == 2 * m - 4, gain_sum, 0.0)
                both = both + jnp.where(lane == 2 * m - 3, bias_sum, 0.0)
                self.norms[...] = self.norms[...] + both

            self.each(c, finish, (2, 3))
            self.store(c, True)

        @pl.when(it == v_start)
        def _():
            self.v_copy(0).start()

        @pl.when(it == v_start + 1)
        def _():
            self.v_copy(0).wait()
            self.v_held[...] = self.v_held[...] + self.vec[...]
            for o in range(1, self.ring):
                self.v_copy(1, o).start()

        @pl.when(it == v_start + 2)
        def _():
            total = self.v_held[...]
            for o in range(1, self.ring):
                self.v_copy(1, o).wait()
                total = total + self.v_round[o - 1]
            self.vec_out[...] = total

            @pl.when(self.p != self.k)
            def _():
                self.v_copy(2).start()

        @pl.when((it == v_start + 3) & (self.p == self.k))
        def _():
            self.v_copy(2).wait_recv()
            self.vec_out[...] = self.vec_out[...] + self.v_across[...]

    def drain(self):
        last = self.count
        for o in range(self.ring):
            for c in (last - 2, last - 1):
                self.c_copy(c, o).wait_send()
            for c in (last - 3, last - 2, last - 1):
                if o > 0:
                    self.y_copy(c, o).wait_send()

        @pl.when(self.p == self.k)
        def _():
            self.store(jnp.int32(last - 1), False)

        @pl.when(self.p != self.k)
        def _():
            self.v_copy(2).wait_send()
            for c in range(last - 5, last):
                self.x_copy(c).wait_send()

    @staticmethod
    def landing(ways, part, count):
        ring = ways // 2
        return [
            jax.ShapeDtypeStruct((count, *lead, part, part), bf16)
            for lead in ((ring,), (ring - 1,), ())
        ]

    @staticmethod
    def scratch(ways, part, tokens, count):
        ring = ways // 2
        dma = pltpu.SemaphoreType.DMA
        return [
            pltpu.VMEM((3, tokens, part), bf16),
            pltpu.VMEM((2, ring, part, part), bf16),
            pltpu.VMEM((5, part, part), bf16),
            pltpu.VMEM((3, ring - 1, part, part), bf16),
            pltpu.VMEM((ring, part, part), bf16),
            pltpu.VMEM((ring - 1, part, part), bf16),
            pltpu.VMEM((part, part), bf16),
            pltpu.VMEM((part, part), f32),
            pltpu.VMEM((part, part), bf16),
            pltpu.VMEM((16, part), f32),
            pltpu.VMEM((16, part), f32),
            pltpu.VMEM((ring - 1, 16, part), f32),
            pltpu.VMEM((16, part), f32),
            dma((3,)),
            dma((count + 1, ring)),
            dma((count + 1, ring)),
            dma((count + 1, ring - 1)),
            dma((count + 1, ring - 1)),
            dma((count + 1,)),
            dma((count + 1,)),
            dma((1,)),
            dma((3, max(ring, 2))),
        ]


class BackWork:
    def __init__(self, given, ways, heads, g, tables, segs, gains, hbm, dq, dh, u, vec, refs):
        self.given = given
        self.wq, self.w1, self.w2, self.wd, self.qr, self.kr, self.vr, self.slope = hbm
        (
            self.wa, self.wb, self.hq, self.hk, self.hv, self.sl, self.d_ar,
            self.q_sum, self.dk, self.dv, self.sem,
        ) = refs
        self.ways, self.heads, self.g, self.vec = ways, heads, g, vec
        self.tables, self.segs, self.gains = tables, segs, gains
        self.dq, self.dh, self.u_rows = dq, dh, u
        self.part = g.shape[1] // ways
        self.size = self.qr.shape[1] // heads
        pieces = [("head", h) for h in range(heads)]
        pieces += [("hidden", j) for j in range(dh.shape[1] // self.part)]
        pieces += [("rows", j) for j in range(ways)]
        self.pieces = pieces

    def loads(self, n):
        kind, j = self.pieces[n]
        slot, part, size = n % 2, self.part, self.size
        width, hidden, inner = self.g.shape[1], self.dh.shape[1], self.dq.shape[1]
        if kind == "head":
            cols = pl.ds(j * size, size)
            if self.given:
                pairs = [(self.wd.at[:, cols], self.d_ar.at[slot])]
            else:
                pairs = [(self.wd.at[cols, :], self.wa.at[slot, pl.ds(0, size), pl.ds(0, width)])]
            pairs += [
                (ref.at[:, cols], held.at[slot])
                for ref, held in ((self.qr, self.hq), (self.kr, self.hk), (self.vr, self.hv))
            ]
        elif kind == "hidden":
            at = pl.ds(j * part, part)
            pairs = [(self.slope.at[:, at], self.dh.at[:, at])] if self.given else [
                (self.w2.at[at, :], self.wa.at[slot, pl.ds(0, part), pl.ds(0, width)]),
                (self.slope.at[:, at], self.sl.at[slot]),
            ]
        else:
            at = pl.ds(j * part, part)
            pairs = [
                (self.w1.at[at, :], self.wa.at[slot, pl.ds(0, part), pl.ds(0, hidden)]),
                (self.wq.at[at, :], self.wb.at[slot, :, pl.ds(0, inner)]),
            ]
        return [
            pltpu.make_async_copy(source, target, self.sem.at[slot, i])
            for i, (source, target) in enumerate(pairs)
        ]

    def begin(self, n):
        if n < len(self.pieces):
            for load in self.loads(n):
                load.start()

    def run(self, n):
        for load in self.loads(n):
            load.wait()
        self.begin(n + 1)
        kind, j = self.pieces[n]
        getattr(self, kind)(j, n % 2)

    def blocks(self, act):
        def body(step, _):
            act(pl.ds(pl.multiple_of(step * BAND, BAND), BAND))
            return 0

        lax.fori_loop(0, self.g.shape[0] // BAND, body, 0)

    def head(self, h, slot):
        size, width = self.size, self.g.shape[1]
        weight = self.wa.at[slot, pl.ds(0, size), pl.ds(0, width)]

        def act(at):
            self.d_ar[0, at, :] = dot(self.g[at, :], weight[...], ((1,), (1,))).astype(bf16)

        if not self.given:
            self.blocks(act)
        attend_back_kernel(
            1.0 / math.sqrt(size), self.hq.at[slot], self.hk.at[slot], self.hv.at[slot],
            self.d_ar.at[slot if self.given else 0], *self.tables, *self.segs,
            self.dq.at[:, pl.ds(h * 3 * size, 3 * size)], self.q_sum.at[pl.ds(h, 1)],
            self.dk, self.dv,
        )
        if h == self.heads - 1:
            sums = jnp.concatenate([self.q_sum[i] for i in range(self.heads)], axis=1)
            for row in range(sums.shape[1] // self.part):
                self.vec[row : row + 1, :] = sums[:, row * self.part : (row + 1) * self.part]

    def hidden(self, j, slot):
        part, width = self.part, self.g.shape[1]
        weight = self.wa.at[slot, pl.ds(0, part), pl.ds(0, width)]
        cols = pl.ds(j * part, part)
        first = self.dq.shape[1] // part
        row = first + j
        self.vec[row : row + 1, :] = jnp.zeros((1, part), f32)

        def act(at):
            if self.given:
                value = self.dh[at, cols]
            else:
                value = dot(self.g[at, :], weight[...], ((1,), (1,)))
                value = (self.sl[slot, at, :].astype(f32) * value).astype(bf16)
                self.dh[at, cols] = value
            self.vec[row : row + 1, :] += jnp.sum(value.astype(f32), axis=0, keepdims=True)

        self.blocks(act)
        if j == 0:
            d = lax.axis_index("dp")
            ring = self.ways // 2
            for r in range(self.ways):
                place = lax.rem(d // 2 + r // 2, ring) * 2 + lax.rem(d + r % 2, 2)
                total = jnp.sum(self.g[:, pl.ds(r * part, part)].astype(f32), axis=0, keepdims=True)
                self.vec[pl.ds(first + self.dh.shape[1] // part + place, 1), :] = total

    def rows(self, j, slot):
        part, hidden, inner = self.part, self.dh.shape[1], self.dq.shape[1]
        weight_1 = self.wa.at[slot, pl.ds(0, part), pl.ds(0, hidden)]
        weight_q = self.wb.at[slot, :, pl.ds(0, inner)]
        cols = pl.ds(j * part, part)
        gain_1, gain_2 = (gain[:, cols] for gain in self.gains)

        def act(at):
            value = dot(self.dq[at, :], weight_q[...], ((1,), (1,))) * gain_1
            value = value + dot(self.dh[at, :], weight_1[...], ((1,), (1,))) * gain_2
            self.u_rows[at, cols] = value.astype(bf16)

        self.blocks(act)

    @staticmethod
    def scratch(given, ways, heads, tokens, width, hidden, size):
        part = width // ways
        return [
            pltpu.VMEM((2, max(part, size), max(width, hidden)), bf16),
            pltpu.VMEM((2, part, 3 * heads * size), bf16),
            *[pltpu.VMEM((2, tokens, size), bf16)] * 3,
            pltpu.VMEM((2, tokens, part), bf16),
            pltpu.VMEM((2 if given else 1, tokens, size), bf16),
            pltpu.VMEM((heads, 1, 3 * size), f32),
            *[pltpu.VMEM((BAND, size), f32)] * 2,
            pltpu.SemaphoreType.DMA((2, 4)),
        ]


def back_kernel(n, ways, heads, k, *refs):
    take = iter(refs)

    def some(count):
        return [next(take) for _ in range(count)]

    g, xh, scales = some(3)
    tables, segs, gains = some(3), some(2), some(2)
    inv_in = next(take)
    weights, attended, slope = some(4), some(3), next(take)
    lefts, own = some(2), some(2)
    outward = weights[2:]
    if k == 1:
        weights = weights[:2] + [None, next(take)]
    if k == 0:
        y_part, y_base, y_shift = some(3)
        norms_in = next(take)
        some(4)
    vec_out, norms, outs = next(take), next(take), some(4)
    if k == 0:
        norm_rows, rows_out, rows_away, y_rows, y_away, y_land = some(6)
    else:
        out, branch = some(2)
    landing = some(3)
    dq, dh, u, inv_std, inv_sem, right, left = some(7)
    line_sems = some(4 if k == 0 else 8)
    work_refs = some(11)
    grad_refs = landing + some(22)
    p, t = lax.axis_index("pipe"), lax.axis_index("tensor")
    other = {"pipe": 1 - p}
    if k == 0:
        stage, handed, d_send, d_recv, stage_sem = some(5)
        y_in, y_stage, y_line, y_handed, yz_send, yz_recv, yx_send, yx_recv, y_sem = some(9)
        n_land, n_send, n_recv = some(3)

    def d_copy(s, sub):
        mine = pl.ds(pl.multiple_of(s * sub, sub), sub)
        return to(handed.at[mine, :], rows_away.at[mine, :], d_send.at[s], d_recv.at[s], other)

    def d_store(s, sub):
        mine = pl.ds(pl.multiple_of(s * sub, sub), sub)
        slot = lax.rem(s, 2)
        return pltpu.make_async_copy(stage.at[slot], rows_out.at[mine, :], stage_sem.at[slot])

    def finished(line, s, total):
        mine = pl.ds(pl.multiple_of(s * line.sub, line.sub), line.sub)
        xr = line.at(xh, line.i, s)[...].astype(f32)
        mean = jnp.mean(total, axis=1, keepdims=True)
        proj = jnp.mean(total * xr, axis=1, keepdims=True)
        total = inv_std[mine, :] * (total - mean - xr * proj)
        total = line.at(g, line.i, s)[...].astype(f32) + total
        if k == 1:
            line.at(out, line.i, s)[...] = total.astype(bf16)
        else:

            @pl.when(s >= 2)
            def _():
                d_store(s - 2, line.sub).wait()

            stage[lax.rem(s, 2)] = total
            d_store(s, line.sub).start()
            handed[mine, :] = total.astype(bf16)

            @pl.when(p == 1)
            def _():
                d_copy(s, line.sub).start()

    line = LineSum(n, u, right, left, line_sems, finished, out if k else None)
    vec = grad_refs[12]
    work = BackWork(
        k == 1, ways, heads, g, tables, segs, gains, (*weights, *attended, slope), dq, dh, u, vec,
        work_refs,
    )
    grads = GradSum(k, ways, xh, g, lefts, (dq, dh), outs, own, scales, vec_out, norms, grad_refs)
    places = [line.after, line.before, grads.core, grads.other] + grads.ahead
    if k == 0:
        along = [{"tensor": lax.rem(t + step, n)} for step in range(1, n)]
        places = places[2:] + along
    rows = inv_std.shape[0]
    inv_load = pltpu.make_async_copy(
        inv_in.at[pl.ds(pl.multiple_of(t * rows, rows), rows), :], inv_std, inv_sem.at[0]
    )
    inv_load.start()
    greet(places)
    inv_load.wait()
    grads.begin()
    norms[...] = norms_in[...] if k == 0 else jnp.zeros(norms.shape, f32)
    work.begin(0)

    count = len(work.pieces)
    last_hidden = heads + dh.shape[1] // work.part
    middle = (last_hidden + count) // 2
    if k == 1:
        step = -(-(count - last_hidden) // 4)
        plan = {1: (0, 1), 3: (1, heads), 4: (heads, last_hidden)}
        plan |= {5 + i: (last_hidden + i * step, last_hidden + (i + 1) * step) for i in range(4)}
        begin, v_start = 9, 3
    else:
        mid_hidden = (heads + last_hidden) // 2
        plan = {
            3: (0, 1), 7: (1, heads), 9: (heads, mid_hidden), 11: (mid_hidden, last_hidden),
            13: (last_hidden, middle), 15: (middle, count),
        }
        begin, v_start = 16, 6

    if k == 0:
        block = rows // 4

        def yz_copy(step):
            owner = lax.rem(t + step, n)
            theirs = pl.ds(pl.multiple_of(owner * rows, rows), rows)
            return to(
                y_part.at[theirs, :], y_land.at[step - 1], yz_send.at[step - 1],
                yz_recv.at[step - 1], along[step - 1],
            )

        def yx_copy(q):
            mine = pl.ds(q * block, block)
            return to(y_handed.at[mine, :], y_away.at[mine, :], yx_send.at[q], yx_recv.at[q], other)

        def y_store(q):
            mine = pl.ds(q * block, block)
            return pltpu.make_async_copy(y_stage, y_rows.at[mine, :], y_sem.at[n + 1])

        def y_finish(q):
            mine = pl.ds(q * block, block)
            if q == 0:
                for step in range(1, n):
                    yz_copy(step).wait_recv()
            else:
                y_store(q - 1).wait()
            start = pl.multiple_of(t * rows + q * block, block)
            loads = [pltpu.make_async_copy(y_part.at[pl.ds(start, block), :], y_in.at[0], y_sem.at[0])]
            loads += [
                pltpu.make_async_copy(y_land.at[step - 1, mine, :], y_in.at[step], y_sem.at[step])
                for step in range(1, n)
            ]
            loads.append(
                pltpu.make_async_copy(y_base.at[pl.ds(start, block), :], y_in.at[n], y_sem.at[n])
            )
            shift = pltpu.make_async_copy(y_shift, y_line, y_sem.at[n + 2])
            shift.start()
            for load in loads:
                load.start()
            for load in loads:
                load.wait()
            shift.wait()
            total = y_in[n].astype(f32) + y_line[...]
            for step in range(n):
                total = total + y_in[step].astype(f32)
            y_stage[...] = total
            y_store(q).start()
            y_handed[mine, :] = total.astype(bf16)

            @pl.when(p == 0)
            def _():
                yx_copy(q).start()

        for step in range(1, n):
            yz_copy(step).start()

    b_start = grads.count + 1

    def b_loads(j):
        part = work.part
        cols = pl.ds(j * part, part)
        tokens, hidden = g.shape[0], dh.shape[1]
        half = min(tokens, hidden)
        pairs = [
            (outward[0].at[pl.ds(i * half, half), cols], grads.load.at[i, pl.ds(0, half), :])
            for i in range(hidden // half)
        ]
        rows = outward[1].shape[0]
        pairs.append((outward[1].at[:, cols], work.wb.at[j % 2, pl.ds(0, rows), pl.ds(0, part)]))
        if j == 0:
            pairs += [(lefts[0], dh), (lefts[1], dq.at[:, pl.ds(0, rows)])]
        return [
            pltpu.make_async_copy(source, target, work.sem.at[i // 4, i % 4])
            for i, (source, target) in enumerate(pairs)
        ]

    def b_store(j):
        part = work.part
        return pltpu.make_async_copy(
            work.sl.at[j % 2], branch.at[:, pl.ds(j * part, part)], grads.load_sem.at[j % 2]
        )

    def b_block(j):
        part, hidden = work.part, dh.shape[1]
        half = min(g.shape[0], hidden)
        rows = outward[1].shape[0]
        loads = b_loads(j)
        for load in loads:
            load.start()
        if j >= 2:
            b_store(j - 2).wait()
        for load in loads:
            load.wait()

        def act(at):
            value = dot(dq[at, pl.ds(0, rows)], work.wb[j % 2, pl.ds(0, rows), pl.ds(0, part)])
            for i in range(hidden // half):
                value = value + dot(
                    dh[at, pl.ds(i * half, half)], grads.load[i, pl.ds(0, half), :]
                )
            work.sl[j % 2, at, :] = value.astype(bf16)

        work.blocks(act)
        b_store(j).start()

    def turn_(half, _):
        @pl.when(half >= begin)
        def _():
            line.turn(half - begin)

        @pl.when(lax.rem(half, 2) == 0)
        def _():
            grads.turn(half // 2, v_start)

        for at, (low, high) in plan.items():

            @pl.when(half == at)
            def _():
                for piece in range(low, high):
                    work.run(piece)

        if k == 0:
            for q in range(4):

                @pl.when(half == 2 * q + 17)
                def _():
                    y_finish(q)

        else:
            for j in range(ways):

                @pl.when(half == 2 * b_start + 1 + j)
                def _():
                    b_block(j)

        return 0

    total = max(begin + line.turns, 2 * grads.turns)
    total = max(total, 2 * b_start + 1 + ways if k else 25)
    lax.fori_loop(0, total, turn_, 0)
    line.drain()
    grads.drain()
    if k == 1:
        b_store(ways - 2).wait()
        b_store(ways - 1).wait()
        return
    y_store(3).wait()
    share = norms.shape[0] // n

    def n_copy(step):
        owner = lax.rem(t + step, n)
        theirs = norms.at[pl.ds(pl.multiple_of(owner * share, share), share), :]
        return to(
            theirs, n_land.at[step - 1], n_send.at[step - 1], n_recv.at[step - 1], along[step - 1]
        )

    for step in range(1, n):
        n_copy(step).start()
    mine = norms[pl.ds(pl.multiple_of(t * share, share), share), :]
    for step in range(1, n):
        n_copy(step).wait()
        mine = mine + n_land[step - 1]
    norm_rows[...] = mine
    for step in range(1, n):
        yz_copy(step).wait_send()
    for s in range(max(line.subs - 2, 0), line.subs):
        d_store(s, line.sub).wait()

    @pl.when(p == 1)
    def _():
        for s in range(line.subs):
            d_copy(s, line.sub).wait_send()
        for q in range(4):
            yx_copy(q).wait_recv()

    @pl.when(p == 0)
    def _():
        for s in range(line.subs):
            d_copy(s, line.sub).wait_recv()
        for q in range(4):
            yx_copy(q).wait_send()


def back_section(
    k, g, xh, inv_std, scales, tables, seg, gains, weights, attended, slope, lefts, own, heads,
    n, ways, extra_in, held=None,
):
    tokens, width = g.shape
    part, rows = width // ways, tokens // n
    hidden, inner = slope.shape[1], 3 * attended[0].shape[1]
    size = inner // 3 // heads
    vmem, hbm = pl.BlockSpec(memory_space=pltpu.VMEM), pl.BlockSpec(memory_space=pl.ANY)
    shape, dma = jax.ShapeDtypeStruct, pltpu.SemaphoreType.DMA
    sides = (lefts[0].shape[1], lefts[1].shape[1], inner, hidden)
    count = sum(sides) // part
    out_shape = [shape((16, part), f32), shape((part, 128), f32)]
    out_specs = [vmem, vmem] + [hbm] * 4
    out_shape += [
        shape((side, part) if m < 2 else (part, side), f32) for m, side in enumerate(sides)
    ]
    if k == 0:
        out_shape += [shape((part // n, 128), f32)]
        out_shape += [shape((rows, width), f32), shape((rows, width), bf16)] * 2
        out_shape += [shape((n - 1, rows, width), bf16)]
        out_specs += [vmem] + [hbm] * 5
        block = rows // 4
        extra = [
            pltpu.VMEM((2, rows // subs_of(rows), width), f32),
            pltpu.VMEM((rows, width), bf16),
            dma((subs_of(rows),)),
            dma((subs_of(rows),)),
            dma((2,)),
            pltpu.VMEM((n + 1, block, width), bf16),
            pltpu.VMEM((block, width), f32),
            pltpu.VMEM((1, width), f32),
            pltpu.VMEM((rows, width), bf16),
            dma((n - 1,)),
            dma((n - 1,)),
            dma((4,)),
            dma((4,)),
            dma((n + 3,)),
            pltpu.VMEM((n - 1, part // n, 128), f32),
            dma((n - 1,)),
            dma((n - 1,)),
        ]
    else:
        out_shape += [shape((tokens, width), bf16)] * 2
        out_specs += [vmem, hbm]
        extra = []
    landing = GradSum.landing(ways, part, count)
    args = [
        g, xh, scales, *tables, seg.reshape(-1, 1), seg.reshape(1, -1), *gains, inv_std,
        *weights, *attended, slope, *lefts, *own, *(extra_in or ()),
    ]
    specs = [vmem] * 10 + [hbm] * (len(args) - 10)
    aliases = {}
    if k == 0:
        aliases = {len(args) + 1 + m: 2 + m for m in range(4)}
        args += held
        specs += [vmem] + [hbm] * 4
    line = LineSum.scratch(n, tokens, width, k == 1)
    return pl.pallas_call(
        functools.partial(back_kernel, n, ways, heads, k),
        in_specs=specs,
        out_specs=out_specs + [hbm] * 3,
        out_shape=out_shape + landing,
        input_output_aliases=aliases,
        scratch_shapes=[
            pltpu.VMEM((tokens, inner), bf16),
            pltpu.VMEM((tokens, hidden), bf16),
            pltpu.VMEM((tokens, width), bf16),
            pltpu.VMEM((rows, 1), f32),
            dma((1,)),
            *line,
            *BackWork.scratch(k == 1, ways, heads, tokens, width, hidden, size),
            *GradSum.scratch(ways, part, tokens, count),
            *extra,
        ],
        compiler_params=pltpu.CompilerParams(
            collective_id=3 + k, has_side_effects=True, vmem_limit_bytes=63 << 20
        ),
        cost_estimate=pl.CostEstimate(flops=0, bytes_accessed=600 << 20, transcendentals=0),
        name="back_section",
    )(*args)


def per_device(
    boundary,
    segments,
    ln1_gain,
    ln1_bias,
    ln2_gain,
    ln2_bias,
    qkv_weight,
    qkv_bias,
    dense_weight,
    dense_bias,
    fc1_weight,
    fc1_bias,
    fc2_weight,
    fc2_bias,
):
    pipe, d, t = lax.axis_index("pipe"), lax.axis_index("dp"), lax.axis_index("tensor")
    ways, ring = lax.axis_size("dp"), lax.axis_size("dp") // 2
    nt = lax.axis_size("tensor")
    first = pipe == 0
    seqs, length, width = boundary.shape[1] // 2, boundary.shape[2], boundary.shape[3]
    tokens, rows, part = seqs * length, length // nt, width // ways
    heads, size = qkv_weight.shape[2], qkv_weight.shape[3] // 3
    y, c = d // 2, d % 2

    def pipe_send(v, source):
        return lax.ppermute(v, "pipe", [(source, 1 - source)])

    def true_order(v):
        parts = []
        for j in range(ways):
            place = ((j // 2 - y) % ring) * 2 + (c ^ (j % 2))
            parts.append(lax.dynamic_slice_in_dim(v, place * part, part, v.ndim - 1))
        return jnp.concatenate(parts, axis=-1)

    def together(*values):
        return list(lax.optimization_barrier(values))

    seg = lax.dynamic_slice_in_dim(segments, pipe * seqs, seqs, 0)
    shards = (
        qkv_weight[0].reshape(part, heads * 3 * size),
        fc1_weight[0],
        fc2_weight[0],
        dense_weight[0],
    )
    axes = (0, 0, 1, 1)
    def in_place(v):
        whole = jnp.zeros((v.shape[0], v.shape[1] * ways), bf16)
        whole = lax.dynamic_update_slice_in_dim(whole, v, d * v.shape[1], 1)
        return whole.reshape(-1, part)

    small = [ln1_gain, ln1_bias, ln2_gain, ln2_bias, dense_bias, fc2_bias]
    small = jnp.concatenate(small + [in_place(qkv_bias[0]), in_place(fc1_bias)], axis=0)
    small = jnp.pad(small, ((0, 16 - small.shape[0]), (0, 0)))
    source, cotangent, small_all, weights_0, weights_1, found = enter_section(
        boundary[0], small, shards, seg, axes, ways, nt, heads
    )
    tables, (xh0, inv0, ar0, qr0, kr0, vr0, act0, slope0) = found[:3], found[3:]
    small_all = small_all.reshape(ways, 2, 16, part).astype(f32)
    cut = heads * 3 * size

    def vectors(k):
        rows_ = small_all[:, k]
        found = [rows_[:, m].reshape(1, width) for m in range(6)]
        in_place = jnp.sum(rows_[:, 6:], axis=0).reshape(1, -1)
        return found + [in_place[:, cut : cut + fc1_weight.shape[2]], in_place[:, :cut]]

    wq0, w10, w20, wd0 = weights_0
    v0, v1 = vectors(0), vectors(1)
    x1, weights_1, d_ar1, found = middle(
        source, v0[4] + v0[5], cotangent,
        jnp.concatenate(v1[:4], axis=0), v1[7], v1[6], tables, seg, act0, ar0, w20, wd0, weights_1,
        [shard.shape for shard in shards], axes, heads, nt, ways,
    )
    xh1, inv1, ar1, qr1, kr1, vr1, act1, d_hidden1 = found
    wq1, w11, w21, wd1 = weights_1

    g1, _, g2, _ = vectors(1)[:4]

    def column(v):
        return v[0].astype(f32)[:, None]

    scales = jnp.concatenate([column(v) for v in (ln1_gain, ln1_bias, ln2_gain, ln2_bias)], axis=1)
    sums_1, norms, fc2_grad, dense_grad, qkv_grad, fc1_grad, g0, branch, *_ = back_section(
        1, cotangent, xh1, inv1, scales, tables, seg, (g1, g2), (wq1, w11, w21, wd1),
        (qr1, kr1, vr1), d_hidden1, (act1, ar1), shards[:2], heads, nt, ways, (d_ar1,),
    )

    g1, _, g2, _ = vectors(0)[:4]
    found = back_section(
        0, g0, xh0, inv0, scales, tables, seg, (g1, g2), weights_0,
        (qr0, kr0, vr0), slope0, (act0, ar0), shards[:2], heads, nt, ways,
        (branch, x1, v1[4] + v1[5]), [norms, fc2_grad, dense_grad, qkv_grad, fc1_grad],
    )
    sums_0, norms, fc2_grad, dense_grad, qkv_grad, fc1_grad = found[:6]
    dx_rows, dx_away, y_rows, y_away = (v.reshape(seqs, rows, width) for v in found[7:11])
    dx_away, y_away = dx_away.astype(f32), y_away.astype(f32)

    boundary_out = true_order(
        jnp.where(
            first,
            jnp.concatenate([dx_rows, dx_away], axis=0),
            jnp.concatenate([y_away, y_rows], axis=0),
        )
    )[None]

    sums = jnp.where(first, sums_0, sums_1).reshape(-1)
    end = cut + shards[1].shape[1]
    qkv_sum, fc1_sum, g_sum = sums[:cut], sums[cut:end], sums[end : end + width]
    norms = found[6][:, :4].T

    qkv_grad = qkv_grad.reshape(part, heads, 3 * size)

    def own_part(v, axis):
        step = v.shape[axis] // ways
        return lax.dynamic_slice_in_dim(v, d * step, step, axis)

    bias_grad = own_part(g_sum, 0)[None]
    return (
        boundary_out,
        norms[0][None],
        norms[1][None],
        norms[2][None],
        norms[3][None],
        qkv_grad[None],
        own_part(qkv_sum.reshape(heads, 3 * size), 1)[None],
        dense_grad[None],
        bias_grad,
        fc1_grad[None],
        own_part(fc1_sum, 0)[None],
        fc2_grad[None],
        bias_grad,
    )


def solution(mesh):
    in_specs = (
        P("pipe", "dp", None, None),
        P("dp", None),
        P("pipe", "dp"),
        P("pipe", "dp"),
        P("pipe", "dp"),
        P("pipe", "dp"),
        P("pipe", "dp", "tensor", None),
        P("pipe", "tensor", "dp"),
        P("pipe", "tensor", "dp"),
        P("pipe", "dp"),
        P("pipe", "dp", "tensor"),
        P("pipe", ("tensor", "dp")),
        P("pipe", "tensor", "dp"),
        P("pipe", "dp"),
    )
    out_specs = (
        P("pipe", "dp", "tensor", None),
        P("pipe", ("dp", "tensor")),
        P("pipe", ("dp", "tensor")),
        P("pipe", ("dp", "tensor")),
        P("pipe", ("dp", "tensor")),
        P("pipe", "dp", "tensor", None),
        P("pipe", "tensor", "dp"),
        P("pipe", "tensor", "dp"),
        P("pipe", "dp"),
        P("pipe", "dp", "tensor"),
        P("pipe", ("tensor", "dp")),
        P("pipe", "tensor", "dp"),
        P("pipe", "dp"),
    )
    return jax.shard_map(
        per_device, mesh=mesh, in_specs=in_specs, out_specs=out_specs, check_vma=False
    )
```

```python
import functools
import math

import jax
import jax.numpy as jnp
from jax import lax
from jax.experimental import pallas as pl
from jax.experimental.pallas import tpu as pltpu
from jax.sharding import PartitionSpec as P

norm_epsilon = 1e-05
mask_fill = -1e30
BAND = 256
ROT = 128
f32, bf16 = jnp.float32, jnp.bfloat16


def dot(a, b, contract=((1,), (0,))):
    return lax.dot_general(a, b, (contract, ((), ())), preferred_element_type=f32)


def allowed(seg_col, seg_row, block):
    low = max(block - 1, 0) * BAND
    size = (block + 1) * BAND - low
    own = lax.broadcasted_iota(jnp.int32, (BAND, size), 0) + (block * BAND - low)
    key = lax.broadcasted_iota(jnp.int32, (BAND, size), 1)
    rows = pl.ds(block * BAND, BAND)
    return (own >= key) & (seg_col[rows, :] == seg_row[:, pl.ds(low, size)])


def turn(values, cos, forward, backward):
    head = values[:, :ROT]
    head = (
        head * cos
        + pltpu.roll(head, ROT - 32, 1) * forward
        + pltpu.roll(head, 32, 1) * backward
    )
    return jnp.concatenate([head, values[:, ROT:]], axis=1)


def attend_kernel(scale, qkv, bias, cos, sin_a, sin_b, seg_col, seg_row, out, qr, kr, vr):
    size = out.shape[1]
    for block in range(out.shape[0] // BAND):
        rows = pl.ds(block * BAND, BAND)
        c, a, b = cos[rows, :], sin_a[rows, :], sin_b[rows, :]
        q = turn(qkv[rows, :size] + bias[:, :size], c, a, b).astype(bf16)
        k = turn(qkv[rows, size : 2 * size] + bias[:, size : 2 * size], c, a, b).astype(bf16)
        qr[rows, :] = q
        kr[rows, :] = k
        vr[rows, :] = (qkv[rows, 2 * size :] + bias[:, 2 * size :]).astype(bf16)
        low = max(block - 1, 0) * BAND
        keys = pl.ds(low, (block + 1) * BAND - low)
        scores = dot(q, kr[keys, :], ((1,), (1,))) * scale
        scores = jnp.where(allowed(seg_col, seg_row, block), scores, mask_fill)
        weights = jnp.exp(scores - jnp.max(scores, axis=1, keepdims=True))
        weights = weights * (1.0 / jnp.sum(weights, axis=1, keepdims=True))
        out[rows, :] = dot(weights.astype(bf16), vr[keys, :]).astype(bf16)


def attend_back_kernel(
    scale, qr, kr, vr, grad, cos, sin_a, sin_b, seg_col, seg_row, out, out_sum, dk_acc, dv_acc
):
    size = grad.shape[1]
    blocks = grad.shape[0] // BAND
    sums = [jnp.zeros((1, size), f32)] * 3

    def emit(place, part, values):
        rows = pl.ds(place * BAND, BAND)
        if part < 2:
            values = turn(values, cos[rows, :], -sin_a[rows, :], -sin_b[rows, :])
        values = values.astype(bf16)
        out[rows, part * size : (part + 1) * size] = values
        sums[part] = sums[part] + jnp.sum(values.astype(f32), axis=0, keepdims=True)

    for block in range(blocks):
        rows = pl.ds(block * BAND, BAND)
        low = max(block - 1, 0) * BAND
        keys = pl.ds(low, (block + 1) * BAND - low)
        q, k, v, g = qr[rows, :], kr[keys, :], vr[keys, :], grad[rows, :]
        scores = dot(q, k, ((1,), (1,))) * scale
        scores = jnp.where(allowed(seg_col, seg_row, block), scores, mask_fill)
        weights = jnp.exp(scores - jnp.max(scores, axis=1, keepdims=True))
        weights = weights * (1.0 / jnp.sum(weights, axis=1, keepdims=True))
        grad_weights = dot(g, v, ((1,), (1,)))
        row_dot = jnp.sum(weights * grad_weights, axis=1, keepdims=True)
        grad_scores = (weights * (grad_weights - row_dot)).astype(bf16)
        emit(block, 0, dot(grad_scores, k) * scale)
        dk = dot(grad_scores, q, ((0,), (0,))) * scale
        dv = dot(weights.astype(bf16), g, ((0,), (0,)))
        if block > 0:
            emit(block - 1, 1, dk_acc[...] + dk[:BAND])
            emit(block - 1, 2, dv_acc[...] + dv[:BAND])
            dk, dv = dk[BAND:], dv[BAND:]
        if block == blocks - 1:
            emit(block, 1, dk)
            emit(block, 2, dv)
        else:
            dk_acc[...] = dk
            dv_acc[...] = dv
    out_sum[0] = jnp.concatenate(sums, axis=1)


def gelu_parts(h):
    t = 1.0 / (1.0 + (0.3275911 * math.sqrt(0.5)) * jnp.abs(h))
    poly = 1.061405429 * t - 1.453152027
    poly = poly * t + 1.421413741
    poly = poly * t - 0.284496736
    poly = poly * t + 0.254829592
    bell = jnp.exp(-0.5 * h * h)
    tail = 0.5 * poly * t * bell
    cdf = jnp.where(h >= 0.0, 1.0 - tail, tail)
    slope = cdf + h * bell * (1.0 / math.sqrt(2.0 * math.pi))
    return (h * cdf).astype(bf16), slope.astype(bf16)


def to(source, target, send, recv, place):
    return pltpu.make_async_remote_copy(
        src_ref=source,
        dst_ref=target,
        send_sem=send,
        recv_sem=recv,
        device_id=place,
        device_id_type=pl.DeviceIdType.MESH,
    )


def greet(places):
    barrier = pltpu.get_barrier_semaphore()
    for place in places:
        pl.semaphore_signal(
            barrier, inc=1, device_id=place, device_id_type=pl.DeviceIdType.MESH
        )
    pl.semaphore_wait(barrier, len(places))


def chunks_of(shapes, axes, part):
    return [
        (m, row, col)
        for m, (shape, axis) in enumerate(zip(shapes, axes))
        for row in range(0, shape[0], part)
        for col in range(0, shape[1], part)
    ]


def chunk_at(ref, axis, shape, chunk, slot, part):
    _, row, col = chunk
    row, col = (row + slot * shape[0], col) if axis == 0 else (row, col + slot * shape[1])
    return ref.at[pl.ds(row, part), pl.ds(col, part)]


class Spread:
    def __init__(self, full, shapes, axes, ways, sems):
        self.full, self.shapes, self.axes = full, shapes, axes
        self.ring = ways // 2
        self.y_send, self.y_recv, self.c_send, self.c_recv = sems
        self.part = shapes[3][1]
        self.chunks = chunks_of(shapes, axes, self.part)
        d = lax.axis_index("dp")
        y, c = d // 2, d % 2
        self.core = {"dp": y * 2 + (1 - c)}
        self.ahead = [{"dp": lax.rem(y + o, self.ring) * 2 + c} for o in range(1, self.ring)]

    def at(self, n, slot):
        m = self.chunks[n][0]
        return chunk_at(
            self.full[m], self.axes[m], self.shapes[m], self.chunks[n], slot, self.part
        )

    def y_copy(self, n, step, source):
        target = self.at(n, 2 * ((self.ring - step) % self.ring))
        return to(
            source, target, self.y_send.at[n, step - 1], self.y_recv.at[n, step - 1],
            self.ahead[step - 1],
        )

    def c_copy(self, n, o, source):
        target = self.at(n, 2 * o + 1)
        return to(source, target, self.c_send.at[n, o], self.c_recv.at[n, o], self.core)

    def begin(self, n, source):
        for step in range(1, self.ring):
            self.y_copy(n, step, source).start()
        self.c_copy(n, 0, source).start()

    def forward(self, n):
        for step in range(1, self.ring):
            o = (self.ring - step) % self.ring
            self.y_copy(n, step, self.at(n, 0)).wait_recv()
            self.c_copy(n, o, self.at(n, 2 * o)).start()

    def arrived(self, m):
        for n in range(len(self.chunks)):
            if self.chunks[n][0] == m:
                for o in range(self.ring):
                    self.c_copy(n, o, self.at(n, 2 * o)).wait_recv()

    def finish(self, waited=()):
        for n in range(len(self.chunks)):
            for step in range(1, self.ring):
                self.y_copy(n, step, self.at(n, 0)).wait_send()
            for o in range(self.ring):
                self.c_copy(n, o, self.at(n, 2 * o)).wait_send()
        for m in range(4):
            if m not in waited:
                self.arrived(m)

    @staticmethod
    def semaphores(pieces, ways):
        dma = pltpu.SemaphoreType.DMA
        return [dma((pieces, ways // 2 - 1))] * 2 + [dma((pieces, ways // 2))] * 2


def small_rows(sm, m, count, slots, part, scattered=False):
    def block(slot):
        return sm[pl.ds(slot * 32, 16), :].astype(f32)

    if not scattered:
        return jnp.concatenate([block(slot)[m : m + 1] for slot in range(slots)], axis=1)
    total = block(0)
    for slot in range(1, slots):
        total = total + block(slot)
    return jnp.concatenate([total[m + j : m + j + 1] for j in range(count)], axis=1)


def enter_kernel(
    ways, nt, axes, heads,
    boundary, small, s0, s1, s2, s3, seg_col, seg_row, frequency,
    source, cotangent, small_all, f0, f1, f2, f3, o0, o1, o2, o3,
    cos_out, sin_a_out, sin_b_out, xh_out, inv_out,
    ar_out, qr_out, kr_out, vr_out, act_out, slope_out,
    x_send, x_recv, y_send, y_recv, c_send, c_recv, z_send, z_recv,
    b0, b1, b2, b3, local, keep_sem, out_sem,
    xv, sm, n1, n2, wq, w1, packed, cos, sin_a, sin_b, xh, inv, ar, qr, kr, vr, act, slope,
):
    shards, bounce = (s0, s1, s2, s3), (b0, b1, b2, b3)
    shapes = [s.shape for s in shards]
    full, later = (f0, f1, f2, f3), (o0, o1, o2, o3)
    p, d, t = lax.axis_index("pipe"), lax.axis_index("dp"), lax.axis_index("tensor")
    sems = (y_send, y_recv, c_send, c_recv)
    now = Spread(full, shapes, axes, ways, sems)
    then = Spread(later, shapes, axes, ways, sems)
    ring, chunks, part = now.ring, now.chunks, now.part
    length = boundary.shape[1]
    rows = length // nt
    across = {"pipe": 1 - p}
    others = [{"tensor": lax.rem(t + step, nt)} for step in range(1, nt)]
    places = [
        (lax.rem(d // 2 + o, ring) * 2 + lax.rem(d + b, 2)) * part
        for o in range(ring)
        for b in range(2)
    ]
    mine = pl.ds(pl.multiple_of(t * rows, rows), rows)

    loads = [pltpu.make_async_copy(shards[m], bounce[m], local.at[m]) for m in range(4)]
    for load in loads:
        load.start()
    keeps = [
        pltpu.make_async_copy(
            boundary.at[p, :, pl.ds(pl.multiple_of(places[r], part), part)],
            xv.at[:, pl.ds(r * part, part)],
            keep_sem.at[r],
        )
        for r in range(ways)
    ]
    greet([across, now.core] + now.ahead + others)

    def in_shard(n):
        m, row, col = chunks[n]
        return shards[m].at[pl.ds(row, part), pl.ds(col, part)]

    def small_at(slot, count=32, row=0):
        return small_all.at[pl.ds(slot * 32 + row, count), :]

    def x_given(r, target):
        return to(
            boundary.at[1 - p, mine, pl.ds(pl.multiple_of(places[r], part), part)],
            target.at[mine, pl.ds(r * part, part)],
            x_send.at[r], x_recv.at[r], across,
        )

    def x_small():
        here = small_all.at[pl.ds(pl.multiple_of(p * 16, 16), 16), :]
        return to(small, here, x_send.at[ways], x_recv.at[ways], across)

    def x_copy(n, target):
        at = ways + 1 + n
        return to(in_shard(n), target, x_send.at[at], x_recv.at[at], across)

    def small_y(step):
        target = small_at(2 * ((ring - step) % ring))
        return to(
            small_at(0), target, y_send.at[last, step - 1], y_recv.at[last, step - 1],
            now.ahead[step - 1],
        )

    def small_c(o):
        target = small_at(2 * o + 1)
        return to(small_at(2 * o), target, c_send.at[last, o], c_recv.at[last, o], now.core)

    def stores(matrices):
        return [
            pltpu.make_async_copy(
                bounce[m],
                matrices[m].at[pl.ds(0, shapes[m][0]), :]
                if axes[m] == 0
                else matrices[m].at[:, pl.ds(0, shapes[m][1])],
                local.at[m],
            )
            for m in range(4)
        ]

    last = len(chunks)
    small_own = pltpu.make_async_copy(
        small, small_all.at[pl.ds(pl.multiple_of(p * 16, 16), 16), :], local.at[4]
    )
    small_own.start()
    x_small().start()

    @pl.when(p == 0)
    def _():
        for r in range(ways):
            x_given(r, source).start()

    @pl.when(p == 1)
    def _():
        for r in range(ways):
            x_given(r, cotangent).start()

    for keep in keeps:
        keep.start()
    for load in loads:
        load.wait()

    @pl.when(p == 0)
    def _():
        for store in stores(full):
            store.start()
        for n in range(last):
            x_copy(n, now.at(n, 0)).start()
            now.begin(n, in_shard(n))

    @pl.when(p == 1)
    def _():
        for store in stores(later):
            store.start()
        for n in range(last):
            x_copy(n, then.at(n, 0)).start()

    for keep in keeps:
        keep.wait()

    def kept_store(target):
        return pltpu.make_async_copy(xv, target, keep_sem.at[0])

    @pl.when(p == 0)
    def _():
        kept_store(source).start()

    @pl.when(p == 1)
    def _():
        kept_store(cotangent).start()

    small_own.wait()
    x_small().wait_recv()
    for step in range(1, ring):
        small_y(step).start()
    small_c(0).start()

    def table(block, _):
        at = pl.ds(pl.multiple_of(block * BAND, BAND), BAND)
        same = seg_col[at, :] == seg_row[...]
        key = lax.broadcasted_iota(jnp.int32, (BAND, length), 1)
        start = jnp.min(jnp.where(same, key, length), axis=1, keepdims=True)
        place = lax.broadcasted_iota(jnp.int32, (BAND, 1), 0) + block * BAND
        angle = (place - start).astype(f32) * frequency[...]
        lane = lax.broadcasted_iota(jnp.int32, (BAND, ROT), 1)
        sine = jnp.sin(angle)
        cos[at, :] = jnp.cos(angle)
        sin_a[at, :] = jnp.where(lane < 32, -sine, 0.0)
        sin_b[at, :] = jnp.where((lane >= 32) & (lane < 64), sine, 0.0)
        return 0

    lax.fori_loop(0, length // BAND, table, 0)
    outs = []

    def give(at, ref, target):
        outs.append(pltpu.make_async_copy(ref, target, out_sem.at[at]))
        outs[-1].start()

    give(0, cos, cos_out)
    give(1, sin_a, sin_a_out)
    give(2, sin_b, sin_b_out)

    kept_store(source).wait()
    for r in range(ways):
        x_given(r, source).wait_recv()

    def z_copy(step, ref):
        return to(
            ref.at[mine, :], ref.at[mine, :], z_send.at[step - 1], z_recv.at[step - 1],
            others[step - 1],
        )

    @pl.when(p == 0)
    def _():
        for step in range(1, nt):
            z_copy(step, cotangent).start()

    @pl.when(p == 1)
    def _():
        for step in range(1, nt):
            z_copy(step, source).start()

    for step in range(1, ring):
        small_y(step).wait_recv()
        small_c((ring - step) % ring).start()

    def norm():
        for step in range(1, nt):
            z_copy(step, source).wait_recv()
        for o in range(ring):
            small_c(o).wait()
        vectors = pltpu.make_async_copy(small_all, sm, keep_sem.at[1])
        vectors.start()

        @pl.when(p == 1)
        def _():
            whole = pltpu.make_async_copy(source, xv, keep_sem.at[0])
            whole.start()
            whole.wait()

        vectors.wait()
        g1, b1, g2, b2 = (small_rows(sm, m, 1, ways, part) for m in range(4))

        def block(step, _):
            at = pl.ds(pl.multiple_of(step * 128, 128), 128)
            x = xv[at, :].astype(f32)
            x = x - jnp.mean(x, axis=1, keepdims=True)
            inv_std = lax.rsqrt(jnp.mean(x * x, axis=1, keepdims=True) + norm_epsilon)
            x = x * inv_std
            inv[at, :] = inv_std
            xh[at, :] = x.astype(bf16)
            n1[at, :] = (x * g1 + b1).astype(bf16)
            n2[at, :] = (x * g2 + b2).astype(bf16)
            return 0

        lax.fori_loop(0, length // 128, block, 0)
        give(3, xh, xh_out)
        give(4, inv, inv_out)
        now.arrived(0)
        stores(full)[0].wait()
        pltpu.make_async_copy(full[0], wq, keep_sem.at[2]).start()

    size = wq.shape[1] // heads // 3

    def attention(h):
        if h == 0:
            pltpu.make_async_copy(full[0], wq, keep_sem.at[2]).wait()
            now.arrived(1)
            stores(full)[1].wait()
            pltpu.make_async_copy(full[1], w1, keep_sem.at[3]).start()
        cols = pl.ds(h * 3 * size, 3 * size)

        def block(step, _):
            at = pl.ds(pl.multiple_of(step * BAND, BAND), BAND)
            packed[at, :] = dot(n1[at, :], wq[:, cols])
            return 0

        lax.fori_loop(0, length // BAND, block, 0)
        bias = small_rows(sm, 6, heads * 3 * size // part, ways, part, True)
        bias = bias[:, h * 3 * size : (h + 1) * 3 * size]
        at = pl.ds(h * size, size)
        attend_kernel(
            1.0 / math.sqrt(size), packed, bias, cos, sin_a, sin_b, seg_col, seg_row,
            ar.at[:, at], qr.at[:, at], kr.at[:, at], vr.at[:, at],
        )
        if h == heads - 1:
            for n, (ref, target) in enumerate(
                ((ar, ar_out), (qr, qr_out), (kr, kr_out), (vr, vr_out))
            ):
                give(5 + n, ref, target)

    hidden = w1.shape[1] // part
    bias_row = 6 + heads * 3 * size // part

    def feed(j):
        if j == 0:
            pltpu.make_async_copy(full[1], w1, keep_sem.at[3]).wait()
        cols = pl.ds(j * part, part)
        bias = small_rows(sm, bias_row + j, 1, ways, part, True)

        def block(step, _):
            at = pl.ds(pl.multiple_of(step * BAND, BAND), BAND)
            act[at, cols], slope[at, cols] = gelu_parts(dot(n2[at, :], w1[:, cols]) + bias)
            return 0

        lax.fori_loop(0, length // BAND, block, 0)
        if j == hidden - 1:
            give(9, act, act_out)
            give(10, slope, slope_out)

    work = [[] for _ in range(last)]
    begin = min(7, last - 1)
    steps = [norm] + [functools.partial(attention, h) for h in range(heads)]
    for n, step in enumerate(steps):
        work[min(begin + n, last - 1)].append(step)
    for j in range(hidden):
        work[min(begin + len(steps) + j // 2, last - 1)].append(functools.partial(feed, j))

    for n in range(last):
        x_copy(n, now.at(n, 0)).wait_recv()

        @pl.when(p == 1)
        def _():
            now.begin(n, now.at(n, 0))

        if n > 0:
            now.forward(n - 1)
        for step in work[n]:
            step()
    now.forward(last - 1)

    now.finish((0, 1))
    for n in range(last):
        x_copy(n, now.at(n, 0)).wait_send()
    for step in range(1, ring):
        small_y(step).wait_send()
    x_small().wait_send()
    for r in range(ways):
        x_given(r, source).wait_send()
    for step in range(1, nt):
        z_copy(step, source).wait_send()
    for store in stores(full)[2:]:
        store.wait()
    for out in outs:
        out.wait()


def enter_section(boundary, small, shards, seg, axes, ways, nt, heads):
    hbm, vmem = pl.BlockSpec(memory_space=pl.ANY), pl.BlockSpec(memory_space=pltpu.VMEM)
    shape = jax.ShapeDtypeStruct
    part = shards[3].shape[1]
    length, width = boundary.shape[1:]
    pieces = len(chunks_of([s.shape for s in shards], axes, part))
    full = [
        shape((s.shape[0] * ways, s.shape[1]) if axis == 0 else (s.shape[0], s.shape[1] * ways), bf16)
        for s, axis in zip(shards, axes)
    ]
    dma = pltpu.SemaphoreType.DMA
    lane = jnp.arange(ROT, dtype=f32)
    frequency = jnp.exp(-math.log(10000.0) * 2.0 * (lane % 32) / 64)
    frequency = jnp.where(lane < 64, frequency, 0.0)[None]
    inner, columns = shards[0].shape[1], shards[1].shape[1]
    results = (
        [shape((length, ROT), f32)] * 3
        + [shape((length, width), bf16), shape((length, 1), f32)]
        + [shape((length, inner // 3), bf16)] * 4
        + [shape((length, columns), bf16)] * 2
    )
    out = pl.pallas_call(
        functools.partial(enter_kernel, ways, nt, axes, heads),
        in_specs=[hbm] * 6 + [vmem] * 3,
        out_specs=[hbm] * (11 + len(results)),
        out_shape=[
            shape((length, width), bf16),
            shape((length, width), bf16),
            shape((32 * ways, part), bf16),
            *full,
            *full,
            *results,
        ],
        scratch_shapes=[
            dma((ways + 1 + pieces,)),
            dma((ways + 1 + pieces,)),
            *Spread.semaphores(pieces + 1, ways),
            dma((nt - 1,)),
            dma((nt - 1,)),
            *[pltpu.VMEM(s.shape, bf16) for s in shards],
            dma((5,)),
            dma((max(ways, 4),)),
            dma((11,)),
            pltpu.VMEM((length, width), bf16),
            pltpu.VMEM((32 * ways, part), bf16),
            pltpu.VMEM((length, width), bf16),
            pltpu.VMEM((length, width), bf16),
            pltpu.VMEM(full[0].shape, bf16),
            pltpu.VMEM(full[1].shape, bf16),
            pltpu.VMEM((length, inner // heads), f32),
            *[pltpu.VMEM(r.shape, r.dtype) for r in results],
        ],
        compiler_params=pltpu.CompilerParams(
            collective_id=1, has_side_effects=True, vmem_limit_bytes=62 << 20
        ),
        cost_estimate=pl.CostEstimate(flops=0, bytes_accessed=600 << 20, transcendentals=0),
        name="enter_section",
    )(boundary, small, *shards, seg.reshape(-1, 1), seg.reshape(1, -1), frequency)
    return out[0], out[1], out[2], out[3:7], out[7:11], out[11:]


def subs_of(rows):
    return max(1, min(16, rows // 16))


class LineSum:
    def __init__(self, n, partial, right, left, sems, finished, out=None):
        self.n, self.partial, self.right, self.left = n, partial, right, left
        self.finished, self.out = finished, out
        self.r_send, self.r_recv, self.l_send, self.l_recv = sems[:4]
        self.spread = sems[4:]
        self.i = lax.axis_index("tensor")
        self.rows = partial.shape[0] // n
        self.subs = subs_of(self.rows)
        self.sub = self.rows // self.subs
        self.after = {"tensor": lax.rem(self.i + 1, n)}
        self.before = {"tensor": lax.rem(self.i + n - 1, n)}

    def at(self, ref, j, s):
        start = pl.multiple_of(j * self.rows + s * self.sub, self.sub)
        return ref.at[pl.ds(start, self.sub), :]

    def r_copy(self, j, s, source):
        target = self.at(self.right, j, s)
        return to(source, target, self.r_send.at[j, s], self.r_recv.at[j, s], self.after)

    def l_copy(self, j, s, source):
        target = self.at(self.left, j, s)
        return to(source, target, self.l_send.at[j, s], self.l_recv.at[j, s], self.before)

    def ar_copy(self, j, s):
        rows = self.at(self.out, j, s)
        return to(rows, rows, self.spread[0].at[j, s], self.spread[1].at[j, s], self.after)

    def al_copy(self, j, s):
        rows = self.at(self.out, j, s)
        return to(rows, rows, self.spread[2].at[j, s], self.spread[3].at[j, s], self.before)

    def add(self, ref, j, s):
        ref = self.at(ref, j, s)
        own = self.at(self.partial, j, s)[...].astype(f32)
        ref[...] = (ref[...].astype(f32) + own).astype(bf16)

    def reduce_right(self, s):
        for k in range(self.n - 1):
            j = self.n - 1 - k

            @pl.when(self.i == 0)
            def _():
                self.r_copy(j, s, self.at(self.partial, j, s)).start()

            @pl.when((self.i > 0) & (self.i < j))
            def _():
                self.r_copy(j, s, self.at(self.right, j, s)).wait_recv()
                self.add(self.right, j, s)
                self.r_copy(j, s, self.at(self.right, j, s)).start()

    def reduce_left(self, s):
        for k in range(self.n - 1):

            @pl.when(self.i == self.n - 1)
            def _():
                self.l_copy(k, s, self.at(self.partial, k, s)).start()

            @pl.when((self.i < self.n - 1) & (self.i > k))
            def _():
                self.l_copy(k, s, self.at(self.left, k, s)).wait_recv()
                self.add(self.left, k, s)
                self.l_copy(k, s, self.at(self.left, k, s)).start()

    def finish(self, s):
        i, n = self.i, self.n

        @pl.when(i > 0)
        def _():
            self.r_copy(i, s, self.at(self.right, i, s)).wait_recv()
            self.add(self.right, i, s)

        @pl.when(i == 0)
        def _():
            self.at(self.right, i, s)[...] = self.at(self.partial, i, s)[...]

        @pl.when(i < n - 1)
        def _():
            self.l_copy(i, s, self.at(self.left, i, s)).wait_recv()

        @pl.when(i == n - 1)
        def _():
            self.at(self.left, i, s)[...] = jnp.zeros((self.sub, self.left.shape[1]), bf16)

        total = self.at(self.right, i, s)[...].astype(f32)
        total = total + self.at(self.left, i, s)[...].astype(f32)
        self.finished(self, s, total)
        if self.out is not None:

            @pl.when(i < n - 1)
            def _():
                self.ar_copy(i, s).start()

            @pl.when(i > 0)
            def _():
                self.al_copy(i, s).start()

    def pass_on(self, step, s):
        i, n = self.i, self.n

        @pl.when(i >= step)
        def _():
            self.ar_copy(i - step, s).wait_recv()

            @pl.when(i < n - 1)
            def _():
                self.ar_copy(i - step, s).start()

        @pl.when(i + step < n)
        def _():
            self.al_copy(i + step, s).wait_recv()

            @pl.when(i > 0)
            def _():
                self.al_copy(i + step, s).start()

    @property
    def turns(self):
        return self.subs + (2 * self.n - 2 if self.out is not None else self.n - 1)

    def turn(self, it):
        def when_piece(s, act):
            @pl.when((s >= 0) & (s < self.subs))
            def _():
                act(s)

        when_piece(it - self.i, self.reduce_right)
        when_piece(it - (self.n - 1 - self.i), self.reduce_left)
        when_piece(it - (self.n - 1), self.finish)
        if self.out is not None:
            for step in range(1, self.n):
                when_piece(it - (self.n - 1) - step, functools.partial(self.pass_on, step))

    def drain(self):
        i, n = self.i, self.n

        def body(s, _):
            for j in range(n):

                @pl.when(i < j)
                def _():
                    self.r_copy(j, s, self.at(self.partial, j, s)).wait_send()

                @pl.when(i > j)
                def _():
                    self.l_copy(j, s, self.at(self.partial, j, s)).wait_send()

                if self.out is not None:

                    @pl.when((i >= j) & (i < n - 1))
                    def _():
                        self.ar_copy(j, s).wait_send()

                    @pl.when((i <= j) & (i > 0))
                    def _():
                        self.al_copy(j, s).wait_send()

            return 0

        lax.fori_loop(0, self.subs, body, 0)

    @staticmethod
    def scratch(n, tokens, width, spread):
        return [pltpu.VMEM((tokens, width), bf16)] * 2 + [
            pltpu.SemaphoreType.DMA((n, subs_of(tokens // n)))
        ] * (8 if spread else 4)


def middle_kernel(n, ways, axes, shapes, order, heads, *refs):
    take = iter(refs)

    def some(count):
        return [next(take) for _ in range(count)]

    shift, g, gains, q_bias, h_bias = some(5)
    tables, segs = some(3), some(2)
    base_in, act_in, ar_in, w2_in, wd_in = some(5)
    some(4)
    out, full, d_ar, d_act = next(take), some(4), next(take), next(take)
    results = some(8)
    partial, right, left = some(3)
    line_sems, parts_sems = some(8), some(4)
    x_send, x_recv, weight, result, w_sem, r_sem = some(6)
    big, wd, act, ar, wq, packed, qr, kr, vr, dh, inv, base, load_sem, out_sem = some(14)
    p = lax.axis_index("pipe")
    tokens, width = partial.shape
    hidden, inner = d_act.shape[1], d_ar.shape[1]
    size = inner // heads
    w2 = big.at[pl.ds(0, hidden), pl.ds(0, width)]
    w1 = big.at[pl.ds(0, width), pl.ds(0, hidden)]

    t = lax.axis_index("tensor")
    rows = base.shape[0]
    own = base_in.at[pl.ds(pl.multiple_of(t * rows, rows), rows), :]
    loads = [
        pltpu.make_async_copy(source, target, load_sem.at[i])
        for i, (source, target) in enumerate(
            ((own, base), (ar_in, ar), (wd_in, wd), (act_in, act), (w2_in, w2))
        )
    ]
    for load in loads:
        load.start()

    def finished(line, s, total):
        mine = pl.ds(pl.multiple_of(s * line.sub, line.sub), line.sub)
        total = total + (base[mine, :].astype(f32) + shift[...])
        line.at(out, line.i, s)[...] = total.astype(bf16)

    line = LineSum(n, partial, right, left, line_sems, finished, out)
    parts = Spread(full, shapes, axes, ways, parts_sems)
    ring, part = parts.ring, parts.part
    across = {"pipe": 1 - p}
    greet([line.after, line.before, parts.core, across] + parts.ahead)
    count = len(parts.chunks)

    def x_copy(m, o):
        chunk = parts.at(m, 2 * o)
        return to(chunk, chunk, x_send.at[m, o - 1], x_recv.at[m, o - 1], across)

    for place, m in enumerate(order):
        parts.c_copy(m, 0, parts.at(m, 0)).start()

        @pl.when(p == place % 2)
        def _():
            for step in range(1, ring):
                parts.y_copy(m, step, parts.at(m, 0)).start()

    def from_ring(m):
        for step in range(1, ring):
            o = (ring - step) % ring
            parts.y_copy(m, step, parts.at(m, 0)).wait_recv()
            x_copy(m, o).start()
            parts.c_copy(m, o, parts.at(m, 2 * o)).start()

    def from_across(m):
        for o in range(1, ring):
            x_copy(m, o).wait_recv()
            parts.c_copy(m, o, parts.at(m, 2 * o)).start()

    groups = min(4, line.subs)
    height = line.rows // groups

    def last_matmul(group):
        def rows_of(ref):
            return jnp.concatenate(
                [ref[pl.ds(j * line.rows + group * height, height), :] for j in range(n)], axis=0
            )

        heads_rows, act_rows = rows_of(ar), rows_of(act)

        def column(step, _):
            cols = pl.ds(pl.multiple_of(step * part, part), part)
            value = dot(heads_rows, wd[:, cols]) + dot(act_rows, w2[:, cols])
            value = value.astype(bf16)
            for j in range(n):
                partial[pl.ds(j * line.rows + group * height, height), cols] = value[
                    j * height : (j + 1) * height
                ]
            return 0

        lax.fori_loop(0, ways, column, 0)

    for load in loads:
        load.wait()
    last_matmul(0)

    blocks = [("act", j) for j in range(hidden // part)] + [("ar", 0)]
    wd_rows = full[3].shape[0]

    def weight_load(i):
        kind, j = blocks[i]
        if kind == "act":
            source, target = full[2].at[pl.ds(j * part, part), :], weight.at[i % 2]
        else:
            source, target = full[3], weight.at[i % 2, pl.ds(0, wd_rows), :]
        return pltpu.make_async_copy(source, target, w_sem.at[i % 2])

    def store(i):
        kind, j = blocks[i]
        if kind == "act":
            at = pl.ds(j * part, part)
            return pltpu.make_async_copy(result.at[i % 2], d_act.at[:, at], r_sem.at[i % 2])
        return pltpu.make_async_copy(qr, d_ar, r_sem.at[2])

    def product(i):
        if i == 0:
            for m in (2, 3):
                parts.arrived(m)
            weight_load(0).start()
        weight_load(i).wait()
        if i + 1 < len(blocks):
            weight_load(i + 1).start()
        kind, _ = blocks[i]
        if kind == "act" and i >= 2:
            store(i - 2).wait()

        def body(step, _):
            at = pl.ds(pl.multiple_of(step * BAND, BAND), BAND)
            if kind == "act":
                result[i % 2, at, :] = dot(g[at, :], weight[i % 2], ((1,), (1,))).astype(bf16)
            else:
                value = dot(g[at, :], weight[i % 2, pl.ds(0, wd_rows), :], ((1,), (1,)))
                qr[at, :] = value.astype(bf16)
            return 0

        lax.fori_loop(0, g.shape[0] // BAND, body, 0)
        store(i).start()

    early = sum(parts.chunks[m][0] in (2, 3) for m in range(count))
    ready = 2 * (-(-early // 2) + 2)
    pairs = -(-count // 2)

    fetch_at = 2 * pairs + 4
    q_load = pltpu.make_async_copy(full[0], wq, load_sem.at[0])
    h_load = pltpu.make_async_copy(full[1], w1, load_sem.at[1])

    def turn_(half, _):
        line.turn(half)
        for pair in range(pairs):
            both = list(enumerate(order))[2 * pair : 2 * pair + 2]

            @pl.when(half == 2 * pair + 2)
            def _():
                for place, m in both:

                    @pl.when(p == place % 2)
                    def _():
                        from_ring(m)

            @pl.when(half == 2 * pair + 4)
            def _():
                for place, m in both:

                    @pl.when(p != place % 2)
                    def _():
                        from_across(m)

        for group in range(1, groups):

            @pl.when(half == line.subs // groups * group - 3)
            def _():
                last_matmul(group)

        for i in range(len(blocks)):

            @pl.when(half == ready + i)
            def _():
                product(i)

        @pl.when(half == fetch_at)
        def _():
            for m in (0, 1):
                parts.arrived(m)
            q_load.start()
            h_load.start()

        return 0

    total = max(line.turns, fetch_at + 1, ready + len(blocks))
    lax.fori_loop(0, total, turn_, 0)
    line.drain()
    store(len(blocks) - 1).wait()
    for i in range(max(len(blocks) - 3, 0), len(blocks) - 1):
        store(i).wait()

    xh, n1, n2 = partial, right, left
    given = []

    def give(at, ref):
        given.append(pltpu.make_async_copy(ref, results[at], out_sem.at[at]))
        given[-1].start()

    def grad_load(j):
        return pltpu.make_async_copy(
            d_act.at[:, pl.ds(j * part, part)], result.at[j % 2], r_sem.at[j % 2]
        )

    grad_load(0).start()
    g1, b1, g2, b2 = (gains[m : m + 1, :] for m in range(4))

    def norm(step, _):
        at = pl.ds(pl.multiple_of(step * 128, 128), 128)
        x = out[at, :].astype(f32)
        x = x - jnp.mean(x, axis=1, keepdims=True)
        inv_std = lax.rsqrt(jnp.mean(x * x, axis=1, keepdims=True) + norm_epsilon)
        x = x * inv_std
        inv[at, :] = inv_std
        xh[at, :] = x.astype(bf16)
        n1[at, :] = (x * g1 + b1).astype(bf16)
        n2[at, :] = (x * g2 + b2).astype(bf16)
        return 0

    lax.fori_loop(0, tokens // 128, norm, 0)
    give(0, xh)
    give(1, inv)
    q_load.wait()
    for h in range(heads):
        cols = pl.ds(h * 3 * size, 3 * size)

        def project(step, _):
            at = pl.ds(pl.multiple_of(step * BAND, BAND), BAND)
            packed[at, :] = dot(n1[at, :], wq[:, cols])
            return 0

        lax.fori_loop(0, tokens // BAND, project, 0)
        at = pl.ds(h * size, size)
        attend_kernel(
            1.0 / math.sqrt(size), packed, q_bias[:, h * 3 * size : (h + 1) * 3 * size],
            *tables, *segs, ar.at[:, at], qr.at[:, at], kr.at[:, at], vr.at[:, at],
        )
    for at, ref in enumerate((ar, qr, kr, vr)):
        give(2 + at, ref)
    h_load.wait()
    for j in range(hidden // part):
        cols = pl.ds(j * part, part)
        grad_load(j).wait()
        if j + 1 < hidden // part:
            grad_load(j + 1).start()

        def feed(step, _):
            at = pl.ds(pl.multiple_of(step * BAND, BAND), BAND)
            act[at, cols], slope = gelu_parts(dot(n2[at, :], w1[:, cols]) + h_bias[:, cols])
            grad = result[j % 2, at, :].astype(f32)
            dh[at, cols] = (slope.astype(f32) * grad).astype(bf16)
            return 0

        lax.fori_loop(0, tokens // BAND, feed, 0)
    give(6, act)
    give(7, dh)
    for place, m in enumerate(order):

        @pl.when(p == place % 2)
        def _():
            for step in range(1, ring):
                parts.y_copy(m, step, parts.at(m, 0)).wait_send()
                x_copy(m, step).wait_send()

        for o in range(ring):
            parts.c_copy(m, o, parts.at(m, 2 * o)).wait_send()
    for copy in given:
        copy.wait()


def middle(source, shift, g, gains, q_bias, h_bias, tables, seg, act, ar, w2, wd, full, shapes, axes,
           heads, n, ways):
    tokens, width = g.shape
    vmem = pl.BlockSpec(memory_space=pltpu.VMEM)
    hbm = pl.BlockSpec(memory_space=pl.ANY)
    shape, dma = jax.ShapeDtypeStruct, pltpu.SemaphoreType.DMA
    part = shapes[3][1]
    chunks = chunks_of(shapes, axes, part)
    pieces = len(chunks)
    order = sorted(range(pieces), key=lambda m: (2, 3, 0, 1)[chunks[m][0]])
    inner, hidden = shapes[3][0], shapes[2][0]
    large = max(hidden, width)
    results = [shape((tokens, width), bf16), shape((tokens, 1), f32)]
    results += [shape((tokens, inner), bf16)] * 4 + [shape((tokens, hidden), bf16)] * 2
    args = [shift, g, gains, q_bias, h_bias, *tables, seg.reshape(-1, 1), seg.reshape(1, -1)]
    args += [source, act, ar, w2, wd]
    out = pl.pallas_call(
        functools.partial(middle_kernel, n, ways, axes, shapes, order, heads),
        in_specs=[vmem] * 10 + [hbm] * 9,
        out_specs=[vmem] + [hbm] * 14,
        out_shape=[shape((tokens, width), bf16)]
        + [shape(w.shape, bf16) for w in full]
        + [shape((tokens, inner), bf16), shape((tokens, hidden), bf16)]
        + results,
        input_output_aliases={15 + m: 1 + m for m in range(4)},
        scratch_shapes=[pltpu.VMEM((tokens, width), bf16)]
        + LineSum.scratch(n, tokens, width, True)
        + Spread.semaphores(pieces, ways)
        + [dma((pieces, ways // 2 - 1))] * 2
        + [
            pltpu.VMEM((2, max(part, inner), width), bf16),
            pltpu.VMEM((2, tokens, part), bf16),
            dma((2,)),
            dma((3,)),
            pltpu.VMEM((large, large), bf16),
            pltpu.VMEM((inner, width), bf16),
            pltpu.VMEM((tokens, hidden), bf16),
            pltpu.VMEM((tokens, inner), bf16),
            pltpu.VMEM((width, 3 * inner), bf16),
            pltpu.VMEM((tokens, 3 * inner // heads), f32),
            *[pltpu.VMEM((tokens, inner), bf16)] * 3,
            pltpu.VMEM((tokens, hidden), bf16),
            pltpu.VMEM((tokens, 1), f32),
            pltpu.VMEM((tokens // n, width), bf16),
            dma((5,)),
            dma((8,)),
        ],
        compiler_params=pltpu.CompilerParams(
            collective_id=2, has_side_effects=True, vmem_limit_bytes=(63 << 20) + (256 << 10)
        ),
        cost_estimate=pl.CostEstimate(flops=0, bytes_accessed=600 << 20, transcendentals=0),
        name="middle",
    )(*args, *full)
    return out[0], out[1:5], out[5], out[7:]


class GradSum:
    def __init__(self, k, ways, xh, g, lefts, rights, outs, own, scales, vec_out, norms, refs):
        (
            self.from_core, self.from_ring, self.from_pipe,
            self.load, self.away, self.near, self.far, self.core_in, self.ring_in, self.pipe_in,
            self.done, self.weight, self.vec, self.v_held, self.v_round, self.v_across,
            self.load_sem, self.c_send, self.c_recv, self.y_send, self.y_recv,
            self.x_send, self.x_recv, self.out_sem, self.in_sem,
        ) = refs
        self.k, self.ring = k, ways // 2
        self.xh, self.g, self.lefts, self.rights, self.outs = xh, g, lefts, rights, outs
        self.own, self.scales, self.vec_out, self.norms = own, scales, vec_out, norms
        self.part = self.load.shape[2]
        self.counts = [side.shape[1] // self.part for side in (*lefts, *rights)]
        self.starts = [sum(self.counts[:m]) for m in range(4)]
        self.count = sum(self.counts)
        p, d = lax.axis_index("pipe"), lax.axis_index("dp")
        y, c = d // 2, d % 2
        self.p = p
        self.core = {"dp": y * 2 + (1 - c)}
        self.ahead = [{"dp": lax.rem(y + o, self.ring) * 2 + c} for o in range(1, self.ring)]
        self.other = {"pipe": 1 - p}

    def each(self, c, act, matrices=range(4)):
        for m in matrices:

            @pl.when((c >= self.starts[m]) & (c < self.starts[m] + self.counts[m]))
            def _():
                act(m, pl.multiple_of((c - self.starts[m]) * self.part, self.part))

    def fetch(self, c):
        def act(m, at):
            pltpu.make_async_copy(
                self.lefts[m].at[:, pl.ds(at, self.part)],
                self.load.at[lax.rem(c, 3)],
                self.load_sem.at[lax.rem(c, 3)],
            ).start()

        self.each(c, act, (0, 1))

    def fetched(self, c):
        slot = lax.rem(c, 3)
        pltpu.make_async_copy(
            self.lefts[0].at[:, pl.ds(0, self.part)], self.load.at[slot], self.load_sem.at[slot]
        ).wait()

    def piece(self, c, slot, use):
        cols = pl.ds(slot * self.part, self.part)

        @pl.when(c < self.starts[2])
        def _():
            use(dot(self.load[lax.rem(c, 3)], self.g[:, cols], ((0,), (0,))))

        def right(m, at):
            side = self.rights[m - 2][:, pl.ds(at, self.part)]
            use(dot(self.xh[:, cols], side, ((0,), (0,))))

        self.each(c, right, (2, 3))

    def c_copy(self, c, o):
        return to(
            self.away.at[lax.rem(c, 2), o], self.from_core.at[c, o],
            self.c_send.at[c, o], self.c_recv.at[c, o], self.core,
        )

    def y_copy(self, c, o):
        return to(
            self.far.at[lax.rem(c, 3), o - 1], self.from_ring.at[c, o - 1],
            self.y_send.at[c, o - 1], self.y_recv.at[c, o - 1], self.ahead[o - 1],
        )

    def x_copy(self, c):
        return to(
            self.near.at[lax.rem(c, 5)], self.from_pipe.at[c],
            self.x_send.at[c], self.x_recv.at[c], self.other,
        )

    def core_load(self, c, o):
        return pltpu.make_async_copy(
            self.from_core.at[c, o], self.core_in.at[o], self.in_sem.at[0, o]
        )

    def ring_load(self, c, o):
        return pltpu.make_async_copy(
            self.from_ring.at[c, o - 1], self.ring_in.at[o - 1], self.in_sem.at[1, o]
        )

    def pipe_load(self, c):
        return pltpu.make_async_copy(self.from_pipe.at[c], self.pipe_in, self.in_sem.at[1, 0])

    def weight_load(self, m, at):
        return pltpu.make_async_copy(
            self.own[m - 2].at[:, pl.ds(at, self.part)], self.weight, self.in_sem.at[2, 0]
        )

    def store(self, c, start):
        def act(m, at):
            out = self.outs[m]
            if m < 2:
                out = out.at[pl.ds(at, self.part), :]
            else:
                out = out.at[:, pl.ds(at, self.part)]
            copy = pltpu.make_async_copy(self.done, out, self.out_sem.at[0])
            copy.start() if start else copy.wait()

        self.each(c, act)

    @property
    def turns(self):
        return self.count + 5

    def begin(self):
        self.fetch(0)
        self.fetch(1)
        self.vec[...] = jnp.zeros(self.vec.shape, f32)

    def v_copy(self, stage, o=1):
        last = self.count
        if stage == 0:
            return to(
                self.vec, self.v_held, self.c_send.at[last, 0], self.c_recv.at[last, 0], self.core
            )
        if stage == 1:
            return to(
                self.v_held, self.v_round.at[o - 1],
                self.y_send.at[last, o - 1], self.y_recv.at[last, o - 1], self.ahead[o - 1],
            )
        return to(
            self.vec_out, self.v_across, self.x_send.at[last], self.x_recv.at[last], self.other
        )

    def turn(self, it, v_start):
        @pl.when((it >= 1) & (it < self.count + 1))
        def _():
            for o in range(self.ring):
                self.c_copy(it - 1, o).wait_recv()
                self.core_load(it - 1, o).start()

        @pl.when((it >= 3) & (it < self.count + 3))
        def _():
            for o in range(1, self.ring):
                self.y_copy(it - 3, o).wait_recv()
                self.ring_load(it - 3, o).start()

        at_end = (it >= 5) & (it < self.count + 5) & (self.p == self.k)

        @pl.when(at_end)
        def _():
            self.x_copy(it - 5).wait_recv()
            self.pipe_load(it - 5).start()
            self.each(it - 5, lambda m, at: self.weight_load(m, at).start(), (2, 3))

        @pl.when(it < self.count)
        def _():
            c = it

            @pl.when(c < self.starts[2])
            def _():
                self.fetched(c)

            for o in range(self.ring):

                @pl.when(c >= 2)
                def _():
                    self.c_copy(c - 2, o).wait_send()

                def use(value):
                    self.away[lax.rem(c, 2), o] = value.astype(bf16)

                self.piece(c, 2 * o + 1, use)
                self.c_copy(c, o).start()

        @pl.when((it >= 1) & (it < self.count + 1))
        def _():
            c = it - 1
            for o in range(self.ring - 1, -1, -1):
                self.core_load(c, o).wait()
                if o > 0:

                    @pl.when(c >= 3)
                    def _():
                        self.y_copy(c - 3, o).wait_send()

                    def use(value):
                        value = value + self.core_in[o].astype(f32)
                        self.far[lax.rem(c, 3), o - 1] = value.astype(bf16)

                    self.piece(c, 2 * o, use)
                    self.y_copy(c, o).start()
                else:

                    @pl.when((c >= 5) & (self.p != self.k))
                    def _():
                        self.x_copy(c - 5).wait_send()

                    def use(value):
                        value = value + self.core_in[o].astype(f32)
                        self.near[lax.rem(c, 5)] = value.astype(bf16)

                    self.piece(c, 0, use)
            self.fetch(c + 2)

        @pl.when((it >= 3) & (it < self.count + 3))
        def _():
            c = it - 3
            total = self.near[lax.rem(c, 5)].astype(f32)
            for o in range(1, self.ring):
                self.ring_load(c, o).wait()
                total = total + self.ring_in[o - 1].astype(f32)
            self.near[lax.rem(c, 5)] = total.astype(bf16)

            @pl.when(self.p != self.k)
            def _():
                self.x_copy(c).start()

        @pl.when(at_end)
        def _():
            c = it - 5

            @pl.when(c >= 1)
            def _():
                self.store(c - 1, False)

            self.pipe_load(c).wait()
            core = self.near[lax.rem(c, 5)].astype(f32) + self.pipe_in[...].astype(f32)

            @pl.when(c < self.starts[2])
            def _():
                self.done[...] = core

            def finish(m, at):
                gain, bias = self.scales[:, 2 * m - 4 : 2 * m - 3], self.scales[:, 2 * m - 3 : 2 * m - 2]
                row = self.vec_out[pl.ds(c - self.starts[2], 1), :]
                self.done[...] = gain * core + bias * row
                self.weight_load(m, at).wait()
                weight = self.weight[...].astype(f32)
                lane = lax.broadcasted_iota(jnp.int32, self.norms.shape, 1)
                gain_sum = jnp.sum(weight * core, axis=1, keepdims=True)
                bias_sum = jnp.sum(weight * row, axis=1, keepdims=True)
                both = jnp.where(lane == 2 * m - 4, gain_sum, 0.0)
                both = both + jnp.where(lane == 2 * m - 3, bias_sum, 0.0)
                self.norms[...] = self.norms[...] + both

            self.each(c, finish, (2, 3))
            self.store(c, True)

        @pl.when(it == v_start)
        def _():
            self.v_copy(0).start()

        @pl.when(it == v_start + 1)
        def _():
            self.v_copy(0).wait()
            self.v_held[...] = self.v_held[...] + self.vec[...]
            for o in range(1, self.ring):
                self.v_copy(1, o).start()

        @pl.when(it == v_start + 2)
        def _():
            total = self.v_held[...]
            for o in range(1, self.ring):
                self.v_copy(1, o).wait()
                total = total + self.v_round[o - 1]
            self.vec_out[...] = total

            @pl.when(self.p != self.k)
            def _():
                self.v_copy(2).start()

        @pl.when((it == v_start + 3) & (self.p == self.k))
        def _():
            self.v_copy(2).wait_recv()
            self.vec_out[...] = self.vec_out[...] + self.v_across[...]

    def drain(self):
        last = self.count
        for o in range(self.ring):
            for c in (last - 2, last - 1):
                self.c_copy(c, o).wait_send()
            for c in (last - 3, last - 2, last - 1):
                if o > 0:
                    self.y_copy(c, o).wait_send()

        @pl.when(self.p == self.k)
        def _():
            self.store(jnp.int32(last - 1), False)

        @pl.when(self.p != self.k)
        def _():
            self.v_copy(2).wait_send()
            for c in range(last - 5, last):
                self.x_copy(c).wait_send()

    @staticmethod
    def landing(ways, part, count):
        ring = ways // 2
        return [
            jax.ShapeDtypeStruct((count, *lead, part, part), bf16)
            for lead in ((ring,), (ring - 1,), ())
        ]

    @staticmethod
    def scratch(ways, part, tokens, count):
        ring = ways // 2
        dma = pltpu.SemaphoreType.DMA
        return [
            pltpu.VMEM((3, tokens, part), bf16),
            pltpu.VMEM((2, ring, part, part), bf16),
            pltpu.VMEM((5, part, part), bf16),
            pltpu.VMEM((3, ring - 1, part, part), bf16),
            pltpu.VMEM((ring, part, part), bf16),
            pltpu.VMEM((ring - 1, part, part), bf16),
            pltpu.VMEM((part, part), bf16),
            pltpu.VMEM((part, part), f32),
            pltpu.VMEM((part, part), bf16),
            pltpu.VMEM((16, part), f32),
            pltpu.VMEM((16, part), f32),
            pltpu.VMEM((ring - 1, 16, part), f32),
            pltpu.VMEM((16, part), f32),
            dma((3,)),
            dma((count + 1, ring)),
            dma((count + 1, ring)),
            dma((count + 1, ring - 1)),
            dma((count + 1, ring - 1)),
            dma((count + 1,)),
            dma((count + 1,)),
            dma((1,)),
            dma((3, max(ring, 2))),
        ]


class BackWork:
    def __init__(self, given, ways, heads, g, tables, segs, gains, hbm, dq, dh, u, vec, refs):
        self.given = given
        self.wq, self.w1, self.w2, self.wd, self.qr, self.kr, self.vr, self.slope = hbm
        (
            self.wa, self.wb, self.hq, self.hk, self.hv, self.sl, self.d_ar,
            self.q_sum, self.dk, self.dv, self.sem,
        ) = refs
        self.ways, self.heads, self.g, self.vec = ways, heads, g, vec
        self.tables, self.segs, self.gains = tables, segs, gains
        self.dq, self.dh, self.u_rows = dq, dh, u
        self.part = g.shape[1] // ways
        self.size = self.qr.shape[1] // heads
        pieces = [("head", h) for h in range(heads)]
        pieces += [("hidden", j) for j in range(dh.shape[1] // self.part)]
        pieces += [("rows", j) for j in range(ways)]
        self.pieces = pieces

    def loads(self, n):
        kind, j = self.pieces[n]
        slot, part, size = n % 2, self.part, self.size
        width, hidden, inner = self.g.shape[1], self.dh.shape[1], self.dq.shape[1]
        if kind == "head":
            cols = pl.ds(j * size, size)
            if self.given:
                pairs = [(self.wd.at[:, cols], self.d_ar.at[slot])]
            else:
                pairs = [(self.wd.at[cols, :], self.wa.at[slot, pl.ds(0, size), pl.ds(0, width)])]
            pairs += [
                (ref.at[:, cols], held.at[slot])
                for ref, held in ((self.qr, self.hq), (self.kr, self.hk), (self.vr, self.hv))
            ]
        elif kind == "hidden":
            at = pl.ds(j * part, part)
            pairs = [(self.slope.at[:, at], self.dh.at[:, at])] if self.given else [
                (self.w2.at[at, :], self.wa.at[slot, pl.ds(0, part), pl.ds(0, width)]),
                (self.slope.at[:, at], self.sl.at[slot]),
            ]
        else:
            at = pl.ds(j * part, part)
            pairs = [
                (self.w1.at[at, :], self.wa.at[slot, pl.ds(0, part), pl.ds(0, hidden)]),
                (self.wq.at[at, :], self.wb.at[slot, :, pl.ds(0, inner)]),
            ]
        return [
            pltpu.make_async_copy(source, target, self.sem.at[slot, i])
            for i, (source, target) in enumerate(pairs)
        ]

    def begin(self, n):
        if n < len(self.pieces):
            for load in self.loads(n):
                load.start()

    def run(self, n):
        for load in self.loads(n):
            load.wait()
        self.begin(n + 1)
        kind, j = self.pieces[n]
        getattr(self, kind)(j, n % 2)

    def blocks(self, act):
        def body(step, _):
            act(pl.ds(pl.multiple_of(step * BAND, BAND), BAND))
            return 0

        lax.fori_loop(0, self.g.shape[0] // BAND, body, 0)

    def head(self, h, slot):
        size, width = self.size, self.g.shape[1]
        weight = self.wa.at[slot, pl.ds(0, size), pl.ds(0, width)]

        def act(at):
            self.d_ar[0, at, :] = dot(self.g[at, :], weight[...], ((1,), (1,))).astype(bf16)

        if not self.given:
            self.blocks(act)
        attend_back_kernel(
            1.0 / math.sqrt(size), self.hq.at[slot], self.hk.at[slot], self.hv.at[slot],
            self.d_ar.at[slot if self.given else 0], *self.tables, *self.segs,
            self.dq.at[:, pl.ds(h * 3 * size, 3 * size)], self.q_sum.at[pl.ds(h, 1)],
            self.dk, self.dv,
        )
        if h == self.heads - 1:
            sums = jnp.concatenate([self.q_sum[i] for i in range(self.heads)], axis=1)
            for row in range(sums.shape[1] // self.part):
                self.vec[row : row + 1, :] = sums[:, row * self.part : (row + 1) * self.part]

    def hidden(self, j, slot):
        part, width = self.part, self.g.shape[1]
        weight = self.wa.at[slot, pl.ds(0, part), pl.ds(0, width)]
        cols = pl.ds(j * part, part)
        first = self.dq.shape[1] // part
        row = first + j
        self.vec[row : row + 1, :] = jnp.zeros((1, part), f32)

        def act(at):
            if self.given:
                value = self.dh[at, cols]
            else:
                value = dot(self.g[at, :], weight[...], ((1,), (1,)))
                value = (self.sl[slot, at, :].astype(f32) * value).astype(bf16)
                self.dh[at, cols] = value
            self.vec[row : row + 1, :] += jnp.sum(value.astype(f32), axis=0, keepdims=True)

        self.blocks(act)
        if j == 0:
            d = lax.axis_index("dp")
            ring = self.ways // 2
            for r in range(self.ways):
                place = lax.rem(d // 2 + r // 2, ring) * 2 + lax.rem(d + r % 2, 2)
                total = jnp.sum(self.g[:, pl.ds(r * part, part)].astype(f32), axis=0, keepdims=True)
                self.vec[pl.ds(first + self.dh.shape[1] // part + place, 1), :] = total

    def rows(self, j, slot):
        part, hidden, inner = self.part, self.dh.shape[1], self.dq.shape[1]
        weight_1 = self.wa.at[slot, pl.ds(0, part), pl.ds(0, hidden)]
        weight_q = self.wb.at[slot, :, pl.ds(0, inner)]
        cols = pl.ds(j * part, part)
        gain_1, gain_2 = (gain[:, cols] for gain in self.gains)

        def act(at):
            value = dot(self.dq[at, :], weight_q[...], ((1,), (1,))) * gain_1
            value = value + dot(self.dh[at, :], weight_1[...], ((1,), (1,))) * gain_2
            self.u_rows[at, cols] = value.astype(bf16)

        self.blocks(act)

    @staticmethod
    def scratch(given, ways, heads, tokens, width, hidden, size):
        part = width // ways
        return [
            pltpu.VMEM((2, max(part, size), max(width, hidden)), bf16),
            pltpu.VMEM((2, part, 3 * heads * size), bf16),
            *[pltpu.VMEM((2, tokens, size), bf16)] * 3,
            pltpu.VMEM((2, tokens, part), bf16),
            pltpu.VMEM((2 if given else 1, tokens, size), bf16),
            pltpu.VMEM((heads, 1, 3 * size), f32),
            *[pltpu.VMEM((BAND, size), f32)] * 2,
            pltpu.SemaphoreType.DMA((2, 4)),
        ]


def back_kernel(n, ways, heads, k, *refs):
    take = iter(refs)

    def some(count):
        return [next(take) for _ in range(count)]

    g, xh, scales = some(3)
    tables, segs, gains = some(3), some(2), some(2)
    inv_in = next(take)
    weights, attended, slope = some(4), some(3), next(take)
    lefts, own = some(2), some(2)
    outward = weights[2:]
    if k == 1:
        weights = weights[:2] + [None, next(take)]
    if k == 0:
        y_part, y_base, y_shift = some(3)
        norms_in = next(take)
        some(4)
    vec_out, norms, outs = next(take), next(take), some(4)
    if k == 0:
        norm_rows, own_rows, away_rows, y_land = some(4)
    else:
        out, branch = some(2)
    landing = some(3)
    dq, dh, u, inv_std, inv_sem, right, left = some(7)
    line_sems = some(4 if k == 0 else 8)
    work_refs = some(11)
    grad_refs = landing + some(22)
    p, t = lax.axis_index("pipe"), lax.axis_index("tensor")
    other = {"pipe": 1 - p}
    if k == 0:
        stage, handed, d_send, d_recv, stage_sem = some(5)
        y_in, y_stage, y_line, y_handed, yz_send, yz_recv, yx_send, yx_recv, y_sem = some(9)
        n_land, n_send, n_recv = some(3)

    def d_copy(s, sub):
        mine = pl.ds(pl.multiple_of(s * sub, sub), sub)
        return to(handed.at[mine, :], away_rows.at[mine, :], d_send.at[s], d_recv.at[s], other)

    def d_store(s, sub):
        mine = pl.ds(pl.multiple_of(s * sub, sub), sub)
        slot = lax.rem(s, 2)
        return pltpu.make_async_copy(stage.at[slot], own_rows.at[mine, :], stage_sem.at[slot])

    def in_true_order(total):
        d, ring, part = lax.axis_index("dp"), ways // 2, total.shape[1] // ways
        for r in range(ways):
            place = lax.rem(d // 2 + r // 2, ring) * 2 + lax.rem(d + r % 2, 2)
            cols = pl.ds(pl.multiple_of(place * part, part), part)
            yield cols, total[:, r * part : (r + 1) * part]

    def finished(line, s, total):
        mine = pl.ds(pl.multiple_of(s * line.sub, line.sub), line.sub)
        xr = line.at(xh, line.i, s)[...].astype(f32)
        mean = jnp.mean(total, axis=1, keepdims=True)
        proj = jnp.mean(total * xr, axis=1, keepdims=True)
        total = inv_std[mine, :] * (total - mean - xr * proj)
        total = line.at(g, line.i, s)[...].astype(f32) + total
        if k == 1:
            line.at(out, line.i, s)[...] = total.astype(bf16)
        else:

            @pl.when(p == 0)
            def _():
                @pl.when(s >= 2)
                def _():
                    d_store(s - 2, line.sub).wait()

                for cols, value in in_true_order(total):
                    stage[lax.rem(s, 2), :, cols] = value
                d_store(s, line.sub).start()

            @pl.when(p == 1)
            def _():
                for cols, value in in_true_order(total):
                    handed[mine, cols] = value.astype(bf16)
                d_copy(s, line.sub).start()

    line = LineSum(n, u, right, left, line_sems, finished, out if k else None)
    vec = grad_refs[12]
    work = BackWork(
        k == 1, ways, heads, g, tables, segs, gains, (*weights, *attended, slope), dq, dh, u, vec,
        work_refs,
    )
    grads = GradSum(k, ways, xh, g, lefts, (dq, dh), outs, own, scales, vec_out, norms, grad_refs)
    places = [line.after, line.before, grads.core, grads.other] + grads.ahead
    if k == 0:
        along = [{"tensor": lax.rem(t + step, n)} for step in range(1, n)]
        places = places[2:] + along
    rows = inv_std.shape[0]
    inv_load = pltpu.make_async_copy(
        inv_in.at[pl.ds(pl.multiple_of(t * rows, rows), rows), :], inv_std, inv_sem.at[0]
    )
    inv_load.start()
    greet(places)
    inv_load.wait()
    grads.begin()
    norms[...] = norms_in[...] if k == 0 else jnp.zeros(norms.shape, f32)
    work.begin(0)

    count = len(work.pieces)
    last_hidden = heads + dh.shape[1] // work.part
    middle = (last_hidden + count) // 2
    if k == 1:
        step = -(-(count - last_hidden) // 4)
        plan = {1: (0, 1), 3: (1, heads), 4: (heads, last_hidden)}
        plan |= {5 + i: (last_hidden + i * step, last_hidden + (i + 1) * step) for i in range(4)}
        begin, v_start = 9, 3
    else:
        mid_hidden = (heads + last_hidden) // 2
        plan = {
            3: (0, 1), 7: (1, heads), 9: (heads, mid_hidden), 11: (mid_hidden, last_hidden),
            13: (last_hidden, middle), 15: (middle, count),
        }
        begin, v_start = 16, 6

    if k == 0:
        block = rows // 4

        def yz_copy(step):
            owner = lax.rem(t + step, n)
            theirs = pl.ds(pl.multiple_of(owner * rows, rows), rows)
            return to(
                y_part.at[theirs, :], y_land.at[step - 1], yz_send.at[step - 1],
                yz_recv.at[step - 1], along[step - 1],
            )

        def yx_copy(q):
            mine = pl.ds(q * block, block)
            return to(
                y_handed.at[mine, :], away_rows.at[mine, :], yx_send.at[q], yx_recv.at[q], other
            )

        def y_store(q):
            mine = pl.ds(q * block, block)
            return pltpu.make_async_copy(y_stage, own_rows.at[mine, :], y_sem.at[n + 1])

        def y_finish(q):
            mine = pl.ds(q * block, block)
            if q == 0:
                for step in range(1, n):
                    yz_copy(step).wait_recv()
            start = pl.multiple_of(t * rows + q * block, block)
            loads = [pltpu.make_async_copy(y_part.at[pl.ds(start, block), :], y_in.at[0], y_sem.at[0])]
            loads += [
                pltpu.make_async_copy(y_land.at[step - 1, mine, :], y_in.at[step], y_sem.at[step])
                for step in range(1, n)
            ]
            loads.append(
                pltpu.make_async_copy(y_base.at[pl.ds(start, block), :], y_in.at[n], y_sem.at[n])
            )
            shift = pltpu.make_async_copy(y_shift, y_line, y_sem.at[n + 2])
            shift.start()
            for load in loads:
                load.start()
            for load in loads:
                load.wait()
            shift.wait()
            total = y_in[n].astype(f32) + y_line[...]
            for step in range(n):
                total = total + y_in[step].astype(f32)

            @pl.when(p == 1)
            def _():
                if q > 0:
                    y_store(q - 1).wait()
                for cols, value in in_true_order(total):
                    y_stage[:, cols] = value
                y_store(q).start()

            @pl.when(p == 0)
            def _():
                for cols, value in in_true_order(total):
                    y_handed[mine, cols] = value.astype(bf16)
                yx_copy(q).start()

        for step in range(1, n):
            yz_copy(step).start()

    b_start = grads.count + 1

    def b_loads(j):
        part = work.part
        cols = pl.ds(j * part, part)
        tokens, hidden = g.shape[0], dh.shape[1]
        half = min(tokens, hidden)
        pairs = [
            (outward[0].at[pl.ds(i * half, half), cols], grads.load.at[i, pl.ds(0, half), :])
            for i in range(hidden // half)
        ]
        rows = outward[1].shape[0]
        pairs.append((outward[1].at[:, cols], work.wb.at[j % 2, pl.ds(0, rows), pl.ds(0, part)]))
        if j == 0:
            pairs += [(lefts[0], dh), (lefts[1], dq.at[:, pl.ds(0, rows)])]
        return [
            pltpu.make_async_copy(source, target, work.sem.at[i // 4, i % 4])
            for i, (source, target) in enumerate(pairs)
        ]

    def b_store(j):
        part = work.part
        return pltpu.make_async_copy(
            work.sl.at[j % 2], branch.at[:, pl.ds(j * part, part)], grads.load_sem.at[j % 2]
        )

    def b_block(j):
        part, hidden = work.part, dh.shape[1]
        half = min(g.shape[0], hidden)
        rows = outward[1].shape[0]
        loads = b_loads(j)
        for load in loads:
            load.start()
        if j >= 2:
            b_store(j - 2).wait()
        for load in loads:
            load.wait()

        def act(at):
            value = dot(dq[at, pl.ds(0, rows)], work.wb[j % 2, pl.ds(0, rows), pl.ds(0, part)])
            for i in range(hidden // half):
                value = value + dot(
                    dh[at, pl.ds(i * half, half)], grads.load[i, pl.ds(0, half), :]
                )
            work.sl[j % 2, at, :] = value.astype(bf16)

        work.blocks(act)
        b_store(j).start()

    def turn_(half, _):
        @pl.when(half >= begin)
        def _():
            line.turn(half - begin)

        @pl.when(lax.rem(half, 2) == 0)
        def _():
            grads.turn(half // 2, v_start)

        for at, (low, high) in plan.items():

            @pl.when(half == at)
            def _():
                for piece in range(low, high):
                    work.run(piece)

        if k == 0:
            for q in range(4):

                @pl.when(half == 2 * q + 17)
                def _():
                    y_finish(q)

        else:
            for j in range(ways):

                @pl.when(half == 2 * b_start + 1 + j)
                def _():
                    b_block(j)

        return 0

    total = max(begin + line.turns, 2 * grads.turns)
    total = max(total, 2 * b_start + 1 + ways if k else 25)
    lax.fori_loop(0, total, turn_, 0)
    line.drain()
    grads.drain()
    if k == 1:
        b_store(ways - 2).wait()
        b_store(ways - 1).wait()
        return
    share = norms.shape[0] // n

    def n_copy(step):
        owner = lax.rem(t + step, n)
        theirs = norms.at[pl.ds(pl.multiple_of(owner * share, share), share), :]
        return to(
            theirs, n_land.at[step - 1], n_send.at[step - 1], n_recv.at[step - 1], along[step - 1]
        )

    for step in range(1, n):
        n_copy(step).start()
    mine = norms[pl.ds(pl.multiple_of(t * share, share), share), :]
    for step in range(1, n):
        n_copy(step).wait()
        mine = mine + n_land[step - 1]
    norm_rows[...] = mine
    for step in range(1, n):
        yz_copy(step).wait_send()

    @pl.when(p == 1)
    def _():
        y_store(3).wait()
        for s in range(line.subs):
            d_copy(s, line.sub).wait_send()
        for q in range(4):
            yx_copy(q).wait_recv()

    @pl.when(p == 0)
    def _():
        for s in range(max(line.subs - 2, 0), line.subs):
            d_store(s, line.sub).wait()
        for s in range(line.subs):
            d_copy(s, line.sub).wait_recv()
        for q in range(4):
            yx_copy(q).wait_send()


def back_section(
    k, g, xh, inv_std, scales, tables, seg, gains, weights, attended, slope, lefts, own, heads,
    n, ways, extra_in, held=None,
):
    tokens, width = g.shape
    part, rows = width // ways, tokens // n
    hidden, inner = slope.shape[1], 3 * attended[0].shape[1]
    size = inner // 3 // heads
    vmem, hbm = pl.BlockSpec(memory_space=pltpu.VMEM), pl.BlockSpec(memory_space=pl.ANY)
    shape, dma = jax.ShapeDtypeStruct, pltpu.SemaphoreType.DMA
    sides = (lefts[0].shape[1], lefts[1].shape[1], inner, hidden)
    count = sum(sides) // part
    out_shape = [shape((16, part), f32), shape((part, 128), f32)]
    out_specs = [vmem, vmem] + [hbm] * 4
    out_shape += [
        shape((side, part) if m < 2 else (part, side), f32) for m, side in enumerate(sides)
    ]
    if k == 0:
        out_shape += [shape((part // n, 128), f32)]
        out_shape += [shape((rows, width), f32), shape((rows, width), bf16)]
        out_shape += [shape((n - 1, rows, width), bf16)]
        out_specs += [vmem] + [hbm] * 3
        block = rows // 4
        extra = [
            pltpu.VMEM((2, rows // subs_of(rows), width), f32),
            pltpu.VMEM((rows, width), bf16),
            dma((subs_of(rows),)),
            dma((subs_of(rows),)),
            dma((2,)),
            pltpu.VMEM((n + 1, block, width), bf16),
            pltpu.VMEM((block, width), f32),
            pltpu.VMEM((1, width), f32),
            pltpu.VMEM((rows, width), bf16),
            dma((n - 1,)),
            dma((n - 1,)),
            dma((4,)),
            dma((4,)),
            dma((n + 3,)),
            pltpu.VMEM((n - 1, part // n, 128), f32),
            dma((n - 1,)),
            dma((n - 1,)),
        ]
    else:
        out_shape += [shape((tokens, width), bf16)] * 2
        out_specs += [vmem, hbm]
        extra = []
    landing = GradSum.landing(ways, part, count)
    args = [
        g, xh, scales, *tables, seg.reshape(-1, 1), seg.reshape(1, -1), *gains, inv_std,
        *weights, *attended, slope, *lefts, *own, *(extra_in or ()),
    ]
    specs = [vmem] * 10 + [hbm] * (len(args) - 10)
    aliases = {}
    if k == 0:
        aliases = {len(args) + 1 + m: 2 + m for m in range(4)}
        args += held
        specs += [vmem] + [hbm] * 4
    line = LineSum.scratch(n, tokens, width, k == 1)
    return pl.pallas_call(
        functools.partial(back_kernel, n, ways, heads, k),
        in_specs=specs,
        out_specs=out_specs + [hbm] * 3,
        out_shape=out_shape + landing,
        input_output_aliases=aliases,
        scratch_shapes=[
            pltpu.VMEM((tokens, inner), bf16),
            pltpu.VMEM((tokens, hidden), bf16),
            pltpu.VMEM((tokens, width), bf16),
            pltpu.VMEM((rows, 1), f32),
            dma((1,)),
            *line,
            *BackWork.scratch(k == 1, ways, heads, tokens, width, hidden, size),
            *GradSum.scratch(ways, part, tokens, count),
            *extra,
        ],
        compiler_params=pltpu.CompilerParams(
            collective_id=3 + k, has_side_effects=True, vmem_limit_bytes=63 << 20
        ),
        cost_estimate=pl.CostEstimate(flops=0, bytes_accessed=600 << 20, transcendentals=0),
        name="back_section",
    )(*args)


def per_device(
    boundary,
    segments,
    ln1_gain,
    ln1_bias,
    ln2_gain,
    ln2_bias,
    qkv_weight,
    qkv_bias,
    dense_weight,
    dense_bias,
    fc1_weight,
    fc1_bias,
    fc2_weight,
    fc2_bias,
):
    pipe, d, t = lax.axis_index("pipe"), lax.axis_index("dp"), lax.axis_index("tensor")
    ways = lax.axis_size("dp")
    nt = lax.axis_size("tensor")
    first = pipe == 0
    seqs, length, width = boundary.shape[1] // 2, boundary.shape[2], boundary.shape[3]
    tokens, rows, part = seqs * length, length // nt, width // ways
    heads, size = qkv_weight.shape[2], qkv_weight.shape[3] // 3

    seg = lax.dynamic_slice_in_dim(segments, pipe * seqs, seqs, 0)
    shards = (
        qkv_weight[0].reshape(part, heads * 3 * size),
        fc1_weight[0],
        fc2_weight[0],
        dense_weight[0],
    )
    axes = (0, 0, 1, 1)
    def in_place(v):
        whole = jnp.zeros((v.shape[0], v.shape[1] * ways), bf16)
        whole = lax.dynamic_update_slice_in_dim(whole, v, d * v.shape[1], 1)
        return whole.reshape(-1, part)

    small = [ln1_gain, ln1_bias, ln2_gain, ln2_bias, dense_bias, fc2_bias]
    small = jnp.concatenate(small + [in_place(qkv_bias[0]), in_place(fc1_bias)], axis=0)
    small = jnp.pad(small, ((0, 16 - small.shape[0]), (0, 0)))
    source, cotangent, small_all, weights_0, weights_1, found = enter_section(
        boundary[0], small, shards, seg, axes, ways, nt, heads
    )
    tables, (xh0, inv0, ar0, qr0, kr0, vr0, act0, slope0) = found[:3], found[3:]
    small_all = small_all.reshape(ways, 2, 16, part).astype(f32)
    cut = heads * 3 * size

    def vectors(k):
        rows_ = small_all[:, k]
        found = [rows_[:, m].reshape(1, width) for m in range(6)]
        in_place = jnp.sum(rows_[:, 6:], axis=0).reshape(1, -1)
        return found + [in_place[:, cut : cut + fc1_weight.shape[2]], in_place[:, :cut]]

    wq0, w10, w20, wd0 = weights_0
    v0, v1 = vectors(0), vectors(1)
    x1, weights_1, d_ar1, found = middle(
        source, v0[4] + v0[5], cotangent,
        jnp.concatenate(v1[:4], axis=0), v1[7], v1[6], tables, seg, act0, ar0, w20, wd0, weights_1,
        [shard.shape for shard in shards], axes, heads, nt, ways,
    )
    xh1, inv1, ar1, qr1, kr1, vr1, act1, d_hidden1 = found
    wq1, w11, w21, wd1 = weights_1

    g1, _, g2, _ = vectors(1)[:4]

    def column(v):
        return v[0].astype(f32)[:, None]

    scales = jnp.concatenate([column(v) for v in (ln1_gain, ln1_bias, ln2_gain, ln2_bias)], axis=1)
    sums_1, norms, fc2_grad, dense_grad, qkv_grad, fc1_grad, g0, branch, *_ = back_section(
        1, cotangent, xh1, inv1, scales, tables, seg, (g1, g2), (wq1, w11, w21, wd1),
        (qr1, kr1, vr1), d_hidden1, (act1, ar1), shards[:2], heads, nt, ways, (d_ar1,),
    )

    g1, _, g2, _ = vectors(0)[:4]
    found = back_section(
        0, g0, xh0, inv0, scales, tables, seg, (g1, g2), weights_0,
        (qr0, kr0, vr0), slope0, (act0, ar0), shards[:2], heads, nt, ways,
        (branch, x1, v1[4] + v1[5]), [norms, fc2_grad, dense_grad, qkv_grad, fc1_grad],
    )
    sums_0, norms, fc2_grad, dense_grad, qkv_grad, fc1_grad = found[:6]
    own, away = (v.reshape(seqs, rows, width).astype(f32) for v in found[7:9])
    boundary_out = jnp.where(
        first, jnp.concatenate([own, away], axis=0), jnp.concatenate([away, own], axis=0)
    )[None]

    sums = jnp.where(first, sums_0, sums_1).reshape(-1)
    end = cut + shards[1].shape[1]
    qkv_sum, fc1_sum, g_sum = sums[:cut], sums[cut:end], sums[end : end + width]
    norms = found[6][:, :4].T

    qkv_grad = qkv_grad.reshape(part, heads, 3 * size)

    def own_part(v, axis):
        step = v.shape[axis] // ways
        return lax.dynamic_slice_in_dim(v, d * step, step, axis)

    bias_grad = own_part(g_sum, 0)[None]
    return (
        boundary_out,
        norms[0][None],
        norms[1][None],
        norms[2][None],
        norms[3][None],
        qkv_grad[None],
        own_part(qkv_sum.reshape(heads, 3 * size), 1)[None],
        dense_grad[None],
        bias_grad,
        fc1_grad[None],
        own_part(fc1_sum, 0)[None],
        fc2_grad[None],
        bias_grad,
    )


def solution(mesh):
    in_specs = (
        P("pipe", "dp", None, None),
        P("dp", None),
        P("pipe", "dp"),
        P("pipe", "dp"),
        P("pipe", "dp"),
        P("pipe", "dp"),
        P("pipe", "dp", "tensor", None),
        P("pipe", "tensor", "dp"),
        P("pipe", "tensor", "dp"),
        P("pipe", "dp"),
        P("pipe", "dp", "tensor"),
        P("pipe", ("tensor", "dp")),
        P("pipe", "tensor", "dp"),
        P("pipe", "dp"),
    )
    out_specs = (
        P("pipe", "dp", "tensor", None),
        P("pipe", ("dp", "tensor")),
        P("pipe", ("dp", "tensor")),
        P("pipe", ("dp", "tensor")),
        P("pipe", ("dp", "tensor")),
        P("pipe", "dp", "tensor", None),
        P("pipe", "tensor", "dp"),
        P("pipe", "tensor", "dp"),
        P("pipe", "dp"),
        P("pipe", "dp", "tensor"),
        P("pipe", ("tensor", "dp")),
        P("pipe", "tensor", "dp"),
        P("pipe", "dp"),
    )
    return jax.shard_map(
        per_device, mesh=mesh, in_specs=in_specs, out_specs=out_specs, check_vma=False
    )
```

```python
import functools
import math

import jax
import jax.numpy as jnp
from jax import lax
from jax.experimental import pallas as pl
from jax.experimental.pallas import tpu as pltpu
from jax.sharding import PartitionSpec as P

norm_epsilon = 1e-05
mask_fill = -1e30
BAND = 256
ROT = 128
f32, bf16 = jnp.float32, jnp.bfloat16


def dot(a, b, contract=((1,), (0,))):
    return lax.dot_general(a, b, (contract, ((), ())), preferred_element_type=f32)


def allowed(seg_col, seg_row, block):
    low = max(block - 1, 0) * BAND
    size = (block + 1) * BAND - low
    own = lax.broadcasted_iota(jnp.int32, (BAND, size), 0) + (block * BAND - low)
    key = lax.broadcasted_iota(jnp.int32, (BAND, size), 1)
    rows = pl.ds(block * BAND, BAND)
    return (own >= key) & (seg_col[rows, :] == seg_row[:, pl.ds(low, size)])


def turn(values, cos, forward, backward):
    head = values[:, :ROT]
    head = (
        head * cos
        + pltpu.roll(head, ROT - 32, 1) * forward
        + pltpu.roll(head, 32, 1) * backward
    )
    return jnp.concatenate([head, values[:, ROT:]], axis=1)


def attend_kernel(scale, qkv, bias, cos, sin_a, sin_b, seg_col, seg_row, out, qr, kr, vr):
    size = out.shape[1]
    for block in range(out.shape[0] // BAND):
        rows = pl.ds(block * BAND, BAND)
        c, a, b = cos[rows, :], sin_a[rows, :], sin_b[rows, :]
        q = turn(qkv[rows, :size] + bias[:, :size], c, a, b).astype(bf16)
        k = turn(qkv[rows, size : 2 * size] + bias[:, size : 2 * size], c, a, b).astype(bf16)
        qr[rows, :] = q
        kr[rows, :] = k
        vr[rows, :] = (qkv[rows, 2 * size :] + bias[:, 2 * size :]).astype(bf16)
        low = max(block - 1, 0) * BAND
        keys = pl.ds(low, (block + 1) * BAND - low)
        scores = dot(q, kr[keys, :], ((1,), (1,))) * scale
        scores = jnp.where(allowed(seg_col, seg_row, block), scores, mask_fill)
        weights = jnp.exp(scores - jnp.max(scores, axis=1, keepdims=True))
        weights = weights * (1.0 / jnp.sum(weights, axis=1, keepdims=True))
        out[rows, :] = dot(weights.astype(bf16), vr[keys, :]).astype(bf16)


def attend_back_kernel(
    scale, qr, kr, vr, grad, cos, sin_a, sin_b, seg_col, seg_row, out, out_sum, dk_acc, dv_acc
):
    size = grad.shape[1]
    blocks = grad.shape[0] // BAND
    sums = [jnp.zeros((1, size), f32)] * 3

    def emit(place, part, values):
        rows = pl.ds(place * BAND, BAND)
        if part < 2:
            values = turn(values, cos[rows, :], -sin_a[rows, :], -sin_b[rows, :])
        values = values.astype(bf16)
        out[rows, part * size : (part + 1) * size] = values
        sums[part] = sums[part] + jnp.sum(values.astype(f32), axis=0, keepdims=True)

    for block in range(blocks):
        rows = pl.ds(block * BAND, BAND)
        low = max(block - 1, 0) * BAND
        keys = pl.ds(low, (block + 1) * BAND - low)
        q, k, v, g = qr[rows, :], kr[keys, :], vr[keys, :], grad[rows, :]
        scores = dot(q, k, ((1,), (1,))) * scale
        scores = jnp.where(allowed(seg_col, seg_row, block), scores, mask_fill)
        weights = jnp.exp(scores - jnp.max(scores, axis=1, keepdims=True))
        weights = weights * (1.0 / jnp.sum(weights, axis=1, keepdims=True))
        grad_weights = dot(g, v, ((1,), (1,)))
        row_dot = jnp.sum(weights * grad_weights, axis=1, keepdims=True)
        grad_scores = (weights * (grad_weights - row_dot)).astype(bf16)
        emit(block, 0, dot(grad_scores, k) * scale)
        dk = dot(grad_scores, q, ((0,), (0,))) * scale
        dv = dot(weights.astype(bf16), g, ((0,), (0,)))
        if block > 0:
            emit(block - 1, 1, dk_acc[...] + dk[:BAND])
            emit(block - 1, 2, dv_acc[...] + dv[:BAND])
            dk, dv = dk[BAND:], dv[BAND:]
        if block == blocks - 1:
            emit(block, 1, dk)
            emit(block, 2, dv)
        else:
            dk_acc[...] = dk
            dv_acc[...] = dv
    out_sum[0] = jnp.concatenate(sums, axis=1)


def gelu_parts(h):
    t = 1.0 / (1.0 + (0.3275911 * math.sqrt(0.5)) * jnp.abs(h))
    poly = 1.061405429 * t - 1.453152027
    poly = poly * t + 1.421413741
    poly = poly * t - 0.284496736
    poly = poly * t + 0.254829592
    bell = jnp.exp(-0.5 * h * h)
    tail = 0.5 * poly * t * bell
    cdf = jnp.where(h >= 0.0, 1.0 - tail, tail)
    slope = cdf + h * bell * (1.0 / math.sqrt(2.0 * math.pi))
    return (h * cdf).astype(bf16), slope.astype(bf16)


def to(source, target, send, recv, place):
    return pltpu.make_async_remote_copy(
        src_ref=source,
        dst_ref=target,
        send_sem=send,
        recv_sem=recv,
        device_id=place,
        device_id_type=pl.DeviceIdType.MESH,
    )


def greet(places):
    barrier = pltpu.get_barrier_semaphore()
    for place in places:
        pl.semaphore_signal(
            barrier, inc=1, device_id=place, device_id_type=pl.DeviceIdType.MESH
        )
    pl.semaphore_wait(barrier, len(places))


def chunks_of(shapes, axes, part):
    return [
        (m, row, col)
        for m, (shape, axis) in enumerate(zip(shapes, axes))
        for row in range(0, shape[0], part)
        for col in range(0, shape[1], part)
    ]


def chunk_at(ref, axis, shape, chunk, slot, part):
    _, row, col = chunk
    row, col = (row + slot * shape[0], col) if axis == 0 else (row, col + slot * shape[1])
    return ref.at[pl.ds(row, part), pl.ds(col, part)]


class Spread:
    def __init__(self, full, shapes, axes, ways, sems):
        self.full, self.shapes, self.axes = full, shapes, axes
        self.ring = ways // 2
        self.y_send, self.y_recv, self.c_send, self.c_recv = sems
        self.part = shapes[3][1]
        self.chunks = chunks_of(shapes, axes, self.part)
        d = lax.axis_index("dp")
        y, c = d // 2, d % 2
        self.core = {"dp": y * 2 + (1 - c)}
        self.ahead = [{"dp": lax.rem(y + o, self.ring) * 2 + c} for o in range(1, self.ring)]

    def at(self, n, slot):
        m = self.chunks[n][0]
        return chunk_at(
            self.full[m], self.axes[m], self.shapes[m], self.chunks[n], slot, self.part
        )

    def y_copy(self, n, step, source):
        target = self.at(n, 2 * ((self.ring - step) % self.ring))
        return to(
            source, target, self.y_send.at[n, step - 1], self.y_recv.at[n, step - 1],
            self.ahead[step - 1],
        )

    def c_copy(self, n, o, source):
        target = self.at(n, 2 * o + 1)
        return to(source, target, self.c_send.at[n, o], self.c_recv.at[n, o], self.core)

    def begin(self, n, source):
        for step in range(1, self.ring):
            self.y_copy(n, step, source).start()
        self.c_copy(n, 0, source).start()

    def forward(self, n):
        for step in range(1, self.ring):
            o = (self.ring - step) % self.ring
            self.y_copy(n, step, self.at(n, 0)).wait_recv()
            self.c_copy(n, o, self.at(n, 2 * o)).start()

    def arrived(self, m):
        for n in range(len(self.chunks)):
            if self.chunks[n][0] == m:
                for o in range(self.ring):
                    self.c_copy(n, o, self.at(n, 2 * o)).wait_recv()

    def finish(self, waited=()):
        for n in range(len(self.chunks)):
            for step in range(1, self.ring):
                self.y_copy(n, step, self.at(n, 0)).wait_send()
            for o in range(self.ring):
                self.c_copy(n, o, self.at(n, 2 * o)).wait_send()
        for m in range(4):
            if m not in waited:
                self.arrived(m)

    @staticmethod
    def semaphores(pieces, ways):
        dma = pltpu.SemaphoreType.DMA
        return [dma((pieces, ways // 2 - 1))] * 2 + [dma((pieces, ways // 2))] * 2


def small_rows(sm, m, count, slots, part, scattered=False):
    def block(slot):
        return sm[pl.ds(slot * 32, 16), :].astype(f32)

    if not scattered:
        return jnp.concatenate([block(slot)[m : m + 1] for slot in range(slots)], axis=1)
    total = block(0)
    for slot in range(1, slots):
        total = total + block(slot)
    return jnp.concatenate([total[m + j : m + j + 1] for j in range(count)], axis=1)


def enter_kernel(
    ways, nt, axes, heads,
    boundary, small, s0, s1, s2, s3, seg_col, seg_row, frequency,
    source, cotangent, small_all, f0, f1, f2, f3, o0, o1, o2, o3,
    cos_out, sin_a_out, sin_b_out, xh_out, inv_out,
    ar_out, qr_out, kr_out, vr_out, act_out, slope_out,
    x_send, x_recv, y_send, y_recv, c_send, c_recv, z_send, z_recv,
    b0, b1, b2, b3, local, keep_sem, out_sem,
    xv, sm, n1, n2, wq, w1, packed, cos, sin_a, sin_b, xh, inv, ar, qr, kr, vr, act, slope,
):
    shards, bounce = (s0, s1, s2, s3), (b0, b1, b2, b3)
    shapes = [s.shape for s in shards]
    full, later = (f0, f1, f2, f3), (o0, o1, o2, o3)
    p, d, t = lax.axis_index("pipe"), lax.axis_index("dp"), lax.axis_index("tensor")
    sems = (y_send, y_recv, c_send, c_recv)
    now = Spread(full, shapes, axes, ways, sems)
    then = Spread(later, shapes, axes, ways, sems)
    ring, chunks, part = now.ring, now.chunks, now.part
    length = boundary.shape[1]
    rows = length // nt
    across = {"pipe": 1 - p}
    others = [{"tensor": lax.rem(t + step, nt)} for step in range(1, nt)]
    places = [
        (lax.rem(d // 2 + o, ring) * 2 + lax.rem(d + b, 2)) * part
        for o in range(ring)
        for b in range(2)
    ]
    mine = pl.ds(pl.multiple_of(t * rows, rows), rows)

    loads = [pltpu.make_async_copy(shards[m], bounce[m], local.at[m]) for m in range(4)]
    for load in loads:
        load.start()
    keeps = [
        pltpu.make_async_copy(
            boundary.at[p, :, pl.ds(pl.multiple_of(places[r], part), part)],
            xv.at[:, pl.ds(r * part, part)],
            keep_sem.at[r],
        )
        for r in range(ways)
    ]
    greet([across, now.core] + now.ahead + others)

    def in_shard(n):
        m, row, col = chunks[n]
        return shards[m].at[pl.ds(row, part), pl.ds(col, part)]

    def small_at(slot, count=32, row=0):
        return small_all.at[pl.ds(slot * 32 + row, count), :]

    def x_given(r, target):
        return to(
            boundary.at[1 - p, mine, pl.ds(pl.multiple_of(places[r], part), part)],
            target.at[mine, pl.ds(r * part, part)],
            x_send.at[r], x_recv.at[r], across,
        )

    def x_small():
        here = small_all.at[pl.ds(pl.multiple_of(p * 16, 16), 16), :]
        return to(small, here, x_send.at[ways], x_recv.at[ways], across)

    def x_copy(n, target):
        at = ways + 1 + n
        return to(in_shard(n), target, x_send.at[at], x_recv.at[at], across)

    def small_y(step):
        target = small_at(2 * ((ring - step) % ring))
        return to(
            small_at(0), target, y_send.at[last, step - 1], y_recv.at[last, step - 1],
            now.ahead[step - 1],
        )

    def small_c(o):
        target = small_at(2 * o + 1)
        return to(small_at(2 * o), target, c_send.at[last, o], c_recv.at[last, o], now.core)

    def stores(matrices):
        return [
            pltpu.make_async_copy(
                bounce[m],
                matrices[m].at[pl.ds(0, shapes[m][0]), :]
                if axes[m] == 0
                else matrices[m].at[:, pl.ds(0, shapes[m][1])],
                local.at[m],
            )
            for m in range(4)
        ]

    last = len(chunks)
    small_own = pltpu.make_async_copy(
        small, small_all.at[pl.ds(pl.multiple_of(p * 16, 16), 16), :], local.at[4]
    )
    small_own.start()
    x_small().start()

    @pl.when(p == 0)
    def _():
        for r in range(ways):
            x_given(r, source).start()

    @pl.when(p == 1)
    def _():
        for r in range(ways):
            x_given(r, cotangent).start()

    for keep in keeps:
        keep.start()
    for load in loads:
        load.wait()

    @pl.when(p == 0)
    def _():
        for store in stores(full):
            store.start()
        for n in range(last):
            x_copy(n, now.at(n, 0)).start()
            now.begin(n, in_shard(n))

    @pl.when(p == 1)
    def _():
        for store in stores(later):
            store.start()
        for n in range(last):
            x_copy(n, then.at(n, 0)).start()

    for keep in keeps:
        keep.wait()

    def kept_store(target):
        return pltpu.make_async_copy(xv, target, keep_sem.at[0])

    @pl.when(p == 0)
    def _():
        kept_store(source).start()

    @pl.when(p == 1)
    def _():
        kept_store(cotangent).start()

    small_own.wait()
    x_small().wait_recv()
    for step in range(1, ring):
        small_y(step).start()
    small_c(0).start()

    def table(block, _):
        at = pl.ds(pl.multiple_of(block * BAND, BAND), BAND)
        same = seg_col[at, :] == seg_row[...]
        key = lax.broadcasted_iota(jnp.int32, (BAND, length), 1)
        start = jnp.min(jnp.where(same, key, length), axis=1, keepdims=True)
        place = lax.broadcasted_iota(jnp.int32, (BAND, 1), 0) + block * BAND
        angle = (place - start).astype(f32) * frequency[...]
        lane = lax.broadcasted_iota(jnp.int32, (BAND, ROT), 1)
        sine = jnp.sin(angle)
        cos[at, :] = jnp.cos(angle)
        sin_a[at, :] = jnp.where(lane < 32, -sine, 0.0)
        sin_b[at, :] = jnp.where((lane >= 32) & (lane < 64), sine, 0.0)
        return 0

    lax.fori_loop(0, length // BAND, table, 0)
    outs = []

    def give(at, ref, target):
        outs.append(pltpu.make_async_copy(ref, target, out_sem.at[at]))
        outs[-1].start()

    give(0, cos, cos_out)
    give(1, sin_a, sin_a_out)
    give(2, sin_b, sin_b_out)

    kept_store(source).wait()
    for r in range(ways):
        x_given(r, source).wait_recv()

    def z_copy(step, ref):
        return to(
            ref.at[mine, :], ref.at[mine, :], z_send.at[step - 1], z_recv.at[step - 1],
            others[step - 1],
        )

    @pl.when(p == 0)
    def _():
        for step in range(1, nt):
            z_copy(step, cotangent).start()

    @pl.when(p == 1)
    def _():
        for step in range(1, nt):
            z_copy(step, source).start()

    for step in range(1, ring):
        small_y(step).wait_recv()
        small_c((ring - step) % ring).start()

    def norm():
        for step in range(1, nt):
            z_copy(step, source).wait_recv()
        for o in range(ring):
            small_c(o).wait()
        vectors = pltpu.make_async_copy(small_all, sm, keep_sem.at[1])
        vectors.start()

        @pl.when(p == 1)
        def _():
            whole = pltpu.make_async_copy(source, xv, keep_sem.at[0])
            whole.start()
            whole.wait()

        vectors.wait()
        g1, b1, g2, b2 = (small_rows(sm, m, 1, ways, part) for m in range(4))

        def block(step, _):
            at = pl.ds(pl.multiple_of(step * 128, 128), 128)
            x = xv[at, :].astype(f32)
            x = x - jnp.mean(x, axis=1, keepdims=True)
            inv_std = lax.rsqrt(jnp.mean(x * x, axis=1, keepdims=True) + norm_epsilon)
            x = x * inv_std
            inv[at, :] = inv_std
            xh[at, :] = x.astype(bf16)
            n1[at, :] = (x * g1 + b1).astype(bf16)
            n2[at, :] = (x * g2 + b2).astype(bf16)
            return 0

        lax.fori_loop(0, length // 128, block, 0)
        give(3, xh, xh_out)
        give(4, inv, inv_out)
        now.arrived(0)
        stores(full)[0].wait()
        pltpu.make_async_copy(full[0], wq, keep_sem.at[2]).start()

    size = wq.shape[1] // heads // 3

    def attention(h):
        if h == 0:
            pltpu.make_async_copy(full[0], wq, keep_sem.at[2]).wait()
            now.arrived(1)
            stores(full)[1].wait()
            pltpu.make_async_copy(full[1], w1, keep_sem.at[3]).start()
        cols = pl.ds(h * 3 * size, 3 * size)

        def block(step, _):
            at = pl.ds(pl.multiple_of(step * BAND, BAND), BAND)
            packed[at, :] = dot(n1[at, :], wq[:, cols])
            return 0

        lax.fori_loop(0, length // BAND, block, 0)
        bias = small_rows(sm, 6, heads * 3 * size // part, ways, part, True)
        bias = bias[:, h * 3 * size : (h + 1) * 3 * size]
        at = pl.ds(h * size, size)
        attend_kernel(
            1.0 / math.sqrt(size), packed, bias, cos, sin_a, sin_b, seg_col, seg_row,
            ar.at[:, at], qr.at[:, at], kr.at[:, at], vr.at[:, at],
        )
        if h == heads - 1:
            for n, (ref, target) in enumerate(
                ((ar, ar_out), (qr, qr_out), (kr, kr_out), (vr, vr_out))
            ):
                give(5 + n, ref, target)

    hidden = w1.shape[1] // part
    bias_row = 6 + heads * 3 * size // part

    def feed(j):
        if j == 0:
            pltpu.make_async_copy(full[1], w1, keep_sem.at[3]).wait()
        cols = pl.ds(j * part, part)
        bias = small_rows(sm, bias_row + j, 1, ways, part, True)

        def block(step, _):
            at = pl.ds(pl.multiple_of(step * BAND, BAND), BAND)
            act[at, cols], slope[at, cols] = gelu_parts(dot(n2[at, :], w1[:, cols]) + bias)
            return 0

        lax.fori_loop(0, length // BAND, block, 0)
        if j == hidden - 1:
            give(9, act, act_out)
            give(10, slope, slope_out)

    work = [[] for _ in range(last)]
    begin = min(7, last - 1)
    steps = [norm] + [functools.partial(attention, h) for h in range(heads)]
    for n, step in enumerate(steps):
        work[min(begin + n, last - 1)].append(step)
    for j in range(hidden):
        work[min(begin + len(steps) + j // 2, last - 1)].append(functools.partial(feed, j))

    for n in range(last):
        x_copy(n, now.at(n, 0)).wait_recv()

        @pl.when(p == 1)
        def _():
            now.begin(n, now.at(n, 0))

        if n > 0:
            now.forward(n - 1)
        for step in work[n]:
            step()
    now.forward(last - 1)

    now.finish((0, 1))
    for n in range(last):
        x_copy(n, now.at(n, 0)).wait_send()
    for step in range(1, ring):
        small_y(step).wait_send()
    x_small().wait_send()
    for r in range(ways):
        x_given(r, source).wait_send()
    for step in range(1, nt):
        z_copy(step, source).wait_send()
    for store in stores(full)[2:]:
        store.wait()
    for out in outs:
        out.wait()


def enter_section(boundary, small, shards, seg, axes, ways, nt, heads):
    hbm, vmem = pl.BlockSpec(memory_space=pl.ANY), pl.BlockSpec(memory_space=pltpu.VMEM)
    shape = jax.ShapeDtypeStruct
    part = shards[3].shape[1]
    length, width = boundary.shape[1:]
    pieces = len(chunks_of([s.shape for s in shards], axes, part))
    full = [
        shape((s.shape[0] * ways, s.shape[1]) if axis == 0 else (s.shape[0], s.shape[1] * ways), bf16)
        for s, axis in zip(shards, axes)
    ]
    dma = pltpu.SemaphoreType.DMA
    lane = jnp.arange(ROT, dtype=f32)
    frequency = jnp.exp(-math.log(10000.0) * 2.0 * (lane % 32) / 64)
    frequency = jnp.where(lane < 64, frequency, 0.0)[None]
    inner, columns = shards[0].shape[1], shards[1].shape[1]
    results = (
        [shape((length, ROT), f32)] * 3
        + [shape((length, width), bf16), shape((length, 1), f32)]
        + [shape((length, inner // 3), bf16)] * 4
        + [shape((length, columns), bf16)] * 2
    )
    out = pl.pallas_call(
        functools.partial(enter_kernel, ways, nt, axes, heads),
        in_specs=[hbm] * 6 + [vmem] * 3,
        out_specs=[hbm] * (11 + len(results)),
        out_shape=[
            shape((length, width), bf16),
            shape((length, width), bf16),
            shape((32 * ways, part), bf16),
            *full,
            *full,
            *results,
        ],
        scratch_shapes=[
            dma((ways + 1 + pieces,)),
            dma((ways + 1 + pieces,)),
            *Spread.semaphores(pieces + 1, ways),
            dma((nt - 1,)),
            dma((nt - 1,)),
            *[pltpu.VMEM(s.shape, bf16) for s in shards],
            dma((5,)),
            dma((max(ways, 4),)),
            dma((11,)),
            pltpu.VMEM((length, width), bf16),
            pltpu.VMEM((32 * ways, part), bf16),
            pltpu.VMEM((length, width), bf16),
            pltpu.VMEM((length, width), bf16),
            pltpu.VMEM(full[0].shape, bf16),
            pltpu.VMEM(full[1].shape, bf16),
            pltpu.VMEM((length, inner // heads), f32),
            *[pltpu.VMEM(r.shape, r.dtype) for r in results],
        ],
        compiler_params=pltpu.CompilerParams(
            collective_id=1, has_side_effects=True, vmem_limit_bytes=62 << 20
        ),
        cost_estimate=pl.CostEstimate(flops=0, bytes_accessed=600 << 20, transcendentals=0),
        name="enter_section",
    )(boundary, small, *shards, seg.reshape(-1, 1), seg.reshape(1, -1), frequency)
    return out[0], out[1], out[2], out[3:7], out[7:11], out[11:]


def subs_of(rows):
    return max(1, min(16, rows // 16))


class LineSum:
    def __init__(self, n, partial, right, left, sems, finished, out=None):
        self.n, self.partial, self.right, self.left = n, partial, right, left
        self.finished, self.out = finished, out
        self.r_send, self.r_recv, self.l_send, self.l_recv = sems[:4]
        self.spread = sems[4:]
        self.i = lax.axis_index("tensor")
        self.rows = partial.shape[0] // n
        self.subs = subs_of(self.rows)
        self.sub = self.rows // self.subs
        self.after = {"tensor": lax.rem(self.i + 1, n)}
        self.before = {"tensor": lax.rem(self.i + n - 1, n)}

    def at(self, ref, j, s):
        start = pl.multiple_of(j * self.rows + s * self.sub, self.sub)
        return ref.at[pl.ds(start, self.sub), :]

    def r_copy(self, j, s, source):
        target = self.at(self.right, j, s)
        return to(source, target, self.r_send.at[j, s], self.r_recv.at[j, s], self.after)

    def l_copy(self, j, s, source):
        target = self.at(self.left, j, s)
        return to(source, target, self.l_send.at[j, s], self.l_recv.at[j, s], self.before)

    def ar_copy(self, j, s):
        rows = self.at(self.out, j, s)
        return to(rows, rows, self.spread[0].at[j, s], self.spread[1].at[j, s], self.after)

    def al_copy(self, j, s):
        rows = self.at(self.out, j, s)
        return to(rows, rows, self.spread[2].at[j, s], self.spread[3].at[j, s], self.before)

    def add(self, ref, j, s):
        ref = self.at(ref, j, s)
        own = self.at(self.partial, j, s)[...].astype(f32)
        ref[...] = (ref[...].astype(f32) + own).astype(bf16)

    def reduce_right(self, s):
        for k in range(self.n - 1):
            j = self.n - 1 - k

            @pl.when(self.i == 0)
            def _():
                self.r_copy(j, s, self.at(self.partial, j, s)).start()

            @pl.when((self.i > 0) & (self.i < j))
            def _():
                self.r_copy(j, s, self.at(self.right, j, s)).wait_recv()
                self.add(self.right, j, s)
                self.r_copy(j, s, self.at(self.right, j, s)).start()

    def reduce_left(self, s):
        for k in range(self.n - 1):

            @pl.when(self.i == self.n - 1)
            def _():
                self.l_copy(k, s, self.at(self.partial, k, s)).start()

            @pl.when((self.i < self.n - 1) & (self.i > k))
            def _():
                self.l_copy(k, s, self.at(self.left, k, s)).wait_recv()
                self.add(self.left, k, s)
                self.l_copy(k, s, self.at(self.left, k, s)).start()

    def finish(self, s):
        i, n = self.i, self.n

        @pl.when(i > 0)
        def _():
            self.r_copy(i, s, self.at(self.right, i, s)).wait_recv()
            self.add(self.right, i, s)

        @pl.when(i == 0)
        def _():
            self.at(self.right, i, s)[...] = self.at(self.partial, i, s)[...]

        @pl.when(i < n - 1)
        def _():
            self.l_copy(i, s, self.at(self.left, i, s)).wait_recv()

        @pl.when(i == n - 1)
        def _():
            self.at(self.left, i, s)[...] = jnp.zeros((self.sub, self.left.shape[1]), bf16)

        total = self.at(self.right, i, s)[...].astype(f32)
        total = total + self.at(self.left, i, s)[...].astype(f32)
        self.finished(self, s, total)
        if self.out is not None:

            @pl.when(i < n - 1)
            def _():
                self.ar_copy(i, s).start()

            @pl.when(i > 0)
            def _():
                self.al_copy(i, s).start()

    def pass_on(self, step, s):
        i, n = self.i, self.n

        @pl.when(i >= step)
        def _():
            self.ar_copy(i - step, s).wait_recv()

            @pl.when(i < n - 1)
            def _():
                self.ar_copy(i - step, s).start()

        @pl.when(i + step < n)
        def _():
            self.al_copy(i + step, s).wait_recv()

            @pl.when(i > 0)
            def _():
                self.al_copy(i + step, s).start()

    @property
    def turns(self):
        return self.subs + (2 * self.n - 2 if self.out is not None else self.n - 1)

    def turn(self, it):
        def when_piece(s, act):
            @pl.when((s >= 0) & (s < self.subs))
            def _():
                act(s)

        when_piece(it - self.i, self.reduce_right)
        when_piece(it - (self.n - 1 - self.i), self.reduce_left)
        when_piece(it - (self.n - 1), self.finish)
        if self.out is not None:
            for step in range(1, self.n):
                when_piece(it - (self.n - 1) - step, functools.partial(self.pass_on, step))

    def drain(self):
        i, n = self.i, self.n

        def body(s, _):
            for j in range(n):

                @pl.when(i < j)
                def _():
                    self.r_copy(j, s, self.at(self.partial, j, s)).wait_send()

                @pl.when(i > j)
                def _():
                    self.l_copy(j, s, self.at(self.partial, j, s)).wait_send()

                if self.out is not None:

                    @pl.when((i >= j) & (i < n - 1))
                    def _():
                        self.ar_copy(j, s).wait_send()

                    @pl.when((i <= j) & (i > 0))
                    def _():
                        self.al_copy(j, s).wait_send()

            return 0

        lax.fori_loop(0, self.subs, body, 0)

    @staticmethod
    def scratch(n, tokens, width, spread):
        return [pltpu.VMEM((tokens, width), bf16)] * 2 + [
            pltpu.SemaphoreType.DMA((n, subs_of(tokens // n)))
        ] * (8 if spread else 4)


def middle_kernel(n, ways, axes, shapes, order, heads, *refs):
    take = iter(refs)

    def some(count):
        return [next(take) for _ in range(count)]

    shift, g, gains, q_bias, h_bias = some(5)
    tables, segs = some(3), some(2)
    base_in, act_in, ar_in, w2_in, wd_in = some(5)
    some(4)
    out, full, d_ar, d_act = next(take), some(4), next(take), next(take)
    results = some(8)
    partial, right, left = some(3)
    line_sems, parts_sems = some(8), some(4)
    x_send, x_recv, weight, result, w_sem, r_sem = some(6)
    big, wd, act, ar, wq, packed, qr, kr, vr, dh, inv, base, load_sem, out_sem = some(14)
    p = lax.axis_index("pipe")
    tokens, width = partial.shape
    hidden, inner = d_act.shape[1], d_ar.shape[1]
    size = inner // heads
    w2 = big.at[pl.ds(0, hidden), pl.ds(0, width)]
    w1 = big.at[pl.ds(0, width), pl.ds(0, hidden)]

    t = lax.axis_index("tensor")
    rows = base.shape[0]
    own = base_in.at[pl.ds(pl.multiple_of(t * rows, rows), rows), :]
    loads = [
        pltpu.make_async_copy(source, target, load_sem.at[i])
        for i, (source, target) in enumerate(
            ((own, base), (ar_in, ar), (wd_in, wd), (act_in, act), (w2_in, w2))
        )
    ]
    for load in loads:
        load.start()

    def finished(line, s, total):
        mine = pl.ds(pl.multiple_of(s * line.sub, line.sub), line.sub)
        total = total + (base[mine, :].astype(f32) + shift[...])
        line.at(out, line.i, s)[...] = total.astype(bf16)

    line = LineSum(n, partial, right, left, line_sems, finished, out)
    parts = Spread(full, shapes, axes, ways, parts_sems)
    ring, part = parts.ring, parts.part
    across = {"pipe": 1 - p}
    greet([line.after, line.before, parts.core, across] + parts.ahead)
    count = len(parts.chunks)

    def x_copy(m, o):
        chunk = parts.at(m, 2 * o)
        return to(chunk, chunk, x_send.at[m, o - 1], x_recv.at[m, o - 1], across)

    for place, m in enumerate(order):
        parts.c_copy(m, 0, parts.at(m, 0)).start()

        @pl.when(p == place % 2)
        def _():
            for step in range(1, ring):
                parts.y_copy(m, step, parts.at(m, 0)).start()

    def from_ring(m):
        for step in range(1, ring):
            o = (ring - step) % ring
            parts.y_copy(m, step, parts.at(m, 0)).wait_recv()
            x_copy(m, o).start()
            parts.c_copy(m, o, parts.at(m, 2 * o)).start()

    def from_across(m):
        for o in range(1, ring):
            x_copy(m, o).wait_recv()
            parts.c_copy(m, o, parts.at(m, 2 * o)).start()

    groups = min(4, line.subs)
    height = line.rows // groups

    def last_matmul(group):
        def rows_of(ref):
            return jnp.concatenate(
                [ref[pl.ds(j * line.rows + group * height, height), :] for j in range(n)], axis=0
            )

        heads_rows, act_rows = rows_of(ar), rows_of(act)

        def column(step, _):
            cols = pl.ds(pl.multiple_of(step * part, part), part)
            value = dot(heads_rows, wd[:, cols]) + dot(act_rows, w2[:, cols])
            value = value.astype(bf16)
            for j in range(n):
                partial[pl.ds(j * line.rows + group * height, height), cols] = value[
                    j * height : (j + 1) * height
                ]
            return 0

        lax.fori_loop(0, ways, column, 0)

    for load in loads:
        load.wait()
    last_matmul(0)

    blocks = [("act", j) for j in range(hidden // part)] + [("ar", 0)]
    wd_rows = full[3].shape[0]

    def weight_load(i):
        kind, j = blocks[i]
        if kind == "act":
            source, target = full[2].at[pl.ds(j * part, part), :], weight.at[i % 2]
        else:
            source, target = full[3], weight.at[i % 2, pl.ds(0, wd_rows), :]
        return pltpu.make_async_copy(source, target, w_sem.at[i % 2])

    def store(i):
        kind, j = blocks[i]
        if kind == "act":
            at = pl.ds(j * part, part)
            return pltpu.make_async_copy(result.at[i % 2], d_act.at[:, at], r_sem.at[i % 2])
        return pltpu.make_async_copy(qr, d_ar, r_sem.at[2])

    def product(i):
        if i == 0:
            for m in (2, 3):
                parts.arrived(m)
            weight_load(0).start()
        weight_load(i).wait()
        if i + 1 < len(blocks):
            weight_load(i + 1).start()
        kind, _ = blocks[i]
        if kind == "act" and i >= 2:
            store(i - 2).wait()

        def body(step, _):
            at = pl.ds(pl.multiple_of(step * BAND, BAND), BAND)
            if kind == "act":
                result[i % 2, at, :] = dot(g[at, :], weight[i % 2], ((1,), (1,))).astype(bf16)
            else:
                value = dot(g[at, :], weight[i % 2, pl.ds(0, wd_rows), :], ((1,), (1,)))
                qr[at, :] = value.astype(bf16)
            return 0

        lax.fori_loop(0, g.shape[0] // BAND, body, 0)
        store(i).start()

    early = sum(parts.chunks[m][0] in (2, 3) for m in range(count))
    ready = 2 * (-(-early // 2) + 2)
    pairs = -(-count // 2)

    fetch_at = 2 * pairs + 4
    q_load = pltpu.make_async_copy(full[0], wq, load_sem.at[0])
    h_load = pltpu.make_async_copy(full[1], w1, load_sem.at[1])

    def turn_(half, _):
        line.turn(half)
        for pair in range(pairs):
            both = list(enumerate(order))[2 * pair : 2 * pair + 2]

            @pl.when(half == 2 * pair + 2)
            def _():
                for place, m in both:

                    @pl.when(p == place % 2)
                    def _():
                        from_ring(m)

            @pl.when(half == 2 * pair + 4)
            def _():
                for place, m in both:

                    @pl.when(p != place % 2)
                    def _():
                        from_across(m)

        for group in range(1, groups):

            @pl.when(half == line.subs // groups * group - 3)
            def _():
                last_matmul(group)

        for i in range(len(blocks)):

            @pl.when(half == ready + i)
            def _():
                product(i)

        @pl.when(half == fetch_at)
        def _():
            for m in (0, 1):
                parts.arrived(m)
            q_load.start()
            h_load.start()

        return 0

    total = max(line.turns, fetch_at + 1, ready + len(blocks))
    lax.fori_loop(0, total, turn_, 0)
    line.drain()
    store(len(blocks) - 1).wait()
    for i in range(max(len(blocks) - 3, 0), len(blocks) - 1):
        store(i).wait()

    xh, n1, n2 = partial, right, left
    given = []

    def give(at, ref):
        given.append(pltpu.make_async_copy(ref, results[at], out_sem.at[at]))
        given[-1].start()

    def grad_load(j):
        return pltpu.make_async_copy(
            d_act.at[:, pl.ds(j * part, part)], result.at[j % 2], r_sem.at[j % 2]
        )

    grad_load(0).start()
    g1, b1, g2, b2 = (gains[m : m + 1, :] for m in range(4))

    def norm(step, _):
        at = pl.ds(pl.multiple_of(step * 128, 128), 128)
        x = out[at, :].astype(f32)
        x = x - jnp.mean(x, axis=1, keepdims=True)
        inv_std = lax.rsqrt(jnp.mean(x * x, axis=1, keepdims=True) + norm_epsilon)
        x = x * inv_std
        inv[at, :] = inv_std
        xh[at, :] = x.astype(bf16)
        n1[at, :] = (x * g1 + b1).astype(bf16)
        n2[at, :] = (x * g2 + b2).astype(bf16)
        return 0

    lax.fori_loop(0, tokens // 128, norm, 0)
    give(0, xh)
    give(1, inv)
    q_load.wait()
    for h in range(heads):
        cols = pl.ds(h * 3 * size, 3 * size)

        def project(step, _):
            at = pl.ds(pl.multiple_of(step * BAND, BAND), BAND)
            packed[at, :] = dot(n1[at, :], wq[:, cols])
            return 0

        lax.fori_loop(0, tokens // BAND, project, 0)
        at = pl.ds(h * size, size)
        attend_kernel(
            1.0 / math.sqrt(size), packed, q_bias[:, h * 3 * size : (h + 1) * 3 * size],
            *tables, *segs, ar.at[:, at], qr.at[:, at], kr.at[:, at], vr.at[:, at],
        )
    for at, ref in enumerate((ar, qr, kr, vr)):
        give(2 + at, ref)
    h_load.wait()
    for j in range(hidden // part):
        cols = pl.ds(j * part, part)
        grad_load(j).wait()
        if j + 1 < hidden // part:
            grad_load(j + 1).start()

        def feed(step, _):
            at = pl.ds(pl.multiple_of(step * BAND, BAND), BAND)
            act[at, cols], slope = gelu_parts(dot(n2[at, :], w1[:, cols]) + h_bias[:, cols])
            grad = result[j % 2, at, :].astype(f32)
            dh[at, cols] = (slope.astype(f32) * grad).astype(bf16)
            return 0

        lax.fori_loop(0, tokens // BAND, feed, 0)
    give(6, act)
    give(7, dh)
    for place, m in enumerate(order):

        @pl.when(p == place % 2)
        def _():
            for step in range(1, ring):
                parts.y_copy(m, step, parts.at(m, 0)).wait_send()
                x_copy(m, step).wait_send()

        for o in range(ring):
            parts.c_copy(m, o, parts.at(m, 2 * o)).wait_send()
    for copy in given:
        copy.wait()


def middle(source, shift, g, gains, q_bias, h_bias, tables, seg, act, ar, w2, wd, full, shapes, axes,
           heads, n, ways):
    tokens, width = g.shape
    vmem = pl.BlockSpec(memory_space=pltpu.VMEM)
    hbm = pl.BlockSpec(memory_space=pl.ANY)
    shape, dma = jax.ShapeDtypeStruct, pltpu.SemaphoreType.DMA
    part = shapes[3][1]
    chunks = chunks_of(shapes, axes, part)
    pieces = len(chunks)
    order = sorted(range(pieces), key=lambda m: (2, 3, 0, 1)[chunks[m][0]])
    inner, hidden = shapes[3][0], shapes[2][0]
    large = max(hidden, width)
    results = [shape((tokens, width), bf16), shape((tokens, 1), f32)]
    results += [shape((tokens, inner), bf16)] * 4 + [shape((tokens, hidden), bf16)] * 2
    args = [shift, g, gains, q_bias, h_bias, *tables, seg.reshape(-1, 1), seg.reshape(1, -1)]
    args += [source, act, ar, w2, wd]
    out = pl.pallas_call(
        functools.partial(middle_kernel, n, ways, axes, shapes, order, heads),
        in_specs=[vmem] * 10 + [hbm] * 9,
        out_specs=[vmem] + [hbm] * 14,
        out_shape=[shape((tokens, width), bf16)]
        + [shape(w.shape, bf16) for w in full]
        + [shape((tokens, inner), bf16), shape((tokens, hidden), bf16)]
        + results,
        input_output_aliases={15 + m: 1 + m for m in range(4)},
        scratch_shapes=[pltpu.VMEM((tokens, width), bf16)]
        + LineSum.scratch(n, tokens, width, True)
        + Spread.semaphores(pieces, ways)
        + [dma((pieces, ways // 2 - 1))] * 2
        + [
            pltpu.VMEM((2, max(part, inner), width), bf16),
            pltpu.VMEM((2, tokens, part), bf16),
            dma((2,)),
            dma((3,)),
            pltpu.VMEM((large, large), bf16),
            pltpu.VMEM((inner, width), bf16),
            pltpu.VMEM((tokens, hidden), bf16),
            pltpu.VMEM((tokens, inner), bf16),
            pltpu.VMEM((width, 3 * inner), bf16),
            pltpu.VMEM((tokens, 3 * inner // heads), f32),
            *[pltpu.VMEM((tokens, inner), bf16)] * 3,
            pltpu.VMEM((tokens, hidden), bf16),
            pltpu.VMEM((tokens, 1), f32),
            pltpu.VMEM((tokens // n, width), bf16),
            dma((5,)),
            dma((8,)),
        ],
        compiler_params=pltpu.CompilerParams(
            collective_id=2, has_side_effects=True, vmem_limit_bytes=(63 << 20) + (256 << 10)
        ),
        cost_estimate=pl.CostEstimate(flops=0, bytes_accessed=600 << 20, transcendentals=0),
        name="middle",
    )(*args, *full)
    return out[0], out[1:5], out[5], out[7:]


class GradSum:
    def __init__(self, k, ways, xh, g, lefts, rights, outs, own, scales, vec_out, norms, refs):
        (
            self.from_core, self.from_ring, self.from_pipe,
            self.load, self.away, self.near, self.far, self.core_in, self.ring_in, self.pipe_in,
            self.done, self.weight, self.vec, self.v_held, self.v_round, self.v_across,
            self.load_sem, self.c_send, self.c_recv, self.y_send, self.y_recv,
            self.x_send, self.x_recv, self.out_sem, self.in_sem,
        ) = refs
        self.k, self.ring = k, ways // 2
        self.xh, self.g, self.lefts, self.rights, self.outs = xh, g, lefts, rights, outs
        self.own, self.scales, self.vec_out, self.norms = own, scales, vec_out, norms
        self.part = self.load.shape[2]
        self.counts = [side.shape[1] // self.part for side in (*lefts, *rights)]
        self.starts = [sum(self.counts[:m]) for m in range(4)]
        self.count = sum(self.counts)
        p, d = lax.axis_index("pipe"), lax.axis_index("dp")
        y, c = d // 2, d % 2
        self.p = p
        self.core = {"dp": y * 2 + (1 - c)}
        self.ahead = [{"dp": lax.rem(y + o, self.ring) * 2 + c} for o in range(1, self.ring)]
        self.other = {"pipe": 1 - p}

    def each(self, c, act, matrices=range(4)):
        for m in matrices:

            @pl.when((c >= self.starts[m]) & (c < self.starts[m] + self.counts[m]))
            def _():
                act(m, pl.multiple_of((c - self.starts[m]) * self.part, self.part))

    def fetch(self, c):
        def act(m, at):
            pltpu.make_async_copy(
                self.lefts[m].at[:, pl.ds(at, self.part)],
                self.load.at[lax.rem(c, 3)],
                self.load_sem.at[lax.rem(c, 3)],
            ).start()

        self.each(c, act, (0, 1))

    def fetched(self, c):
        slot = lax.rem(c, 3)
        pltpu.make_async_copy(
            self.lefts[0].at[:, pl.ds(0, self.part)], self.load.at[slot], self.load_sem.at[slot]
        ).wait()

    def piece(self, c, slot, use):
        cols = pl.ds(slot * self.part, self.part)

        @pl.when(c < self.starts[2])
        def _():
            use(dot(self.load[lax.rem(c, 3)], self.g[:, cols], ((0,), (0,))))

        def right(m, at):
            side = self.rights[m - 2][:, pl.ds(at, self.part)]
            use(dot(self.xh[:, cols], side, ((0,), (0,))))

        self.each(c, right, (2, 3))

    def c_copy(self, c, o):
        return to(
            self.away.at[lax.rem(c, 2), o], self.from_core.at[c, o],
            self.c_send.at[c, o], self.c_recv.at[c, o], self.core,
        )

    def y_copy(self, c, o):
        return to(
            self.far.at[lax.rem(c, 3), o - 1], self.from_ring.at[c, o - 1],
            self.y_send.at[c, o - 1], self.y_recv.at[c, o - 1], self.ahead[o - 1],
        )

    def x_copy(self, c):
        return to(
            self.near.at[lax.rem(c, 5)], self.from_pipe.at[c],
            self.x_send.at[c], self.x_recv.at[c], self.other,
        )

    def core_load(self, c, o):
        return pltpu.make_async_copy(
            self.from_core.at[c, o], self.core_in.at[o], self.in_sem.at[0, o]
        )

    def ring_load(self, c, o):
        return pltpu.make_async_copy(
            self.from_ring.at[c, o - 1], self.ring_in.at[o - 1], self.in_sem.at[1, o]
        )

    def pipe_load(self, c):
        return pltpu.make_async_copy(self.from_pipe.at[c], self.pipe_in, self.in_sem.at[1, 0])

    def weight_load(self, m, at):
        return pltpu.make_async_copy(
            self.own[m - 2].at[:, pl.ds(at, self.part)], self.weight, self.in_sem.at[2, 0]
        )

    def store(self, c, start):
        def act(m, at):
            out = self.outs[m]
            if m < 2:
                out = out.at[pl.ds(at, self.part), :]
            else:
                out = out.at[:, pl.ds(at, self.part)]
            copy = pltpu.make_async_copy(self.done, out, self.out_sem.at[0])
            copy.start() if start else copy.wait()

        self.each(c, act)

    @property
    def turns(self):
        return self.count + 5

    def begin(self):
        self.fetch(0)
        self.fetch(1)
        self.vec[...] = jnp.zeros(self.vec.shape, f32)

    def v_copy(self, stage, o=1):
        last = self.count
        if stage == 0:
            return to(
                self.vec, self.v_held, self.c_send.at[last, 0], self.c_recv.at[last, 0], self.core
            )
        if stage == 1:
            return to(
                self.v_held, self.v_round.at[o - 1],
                self.y_send.at[last, o - 1], self.y_recv.at[last, o - 1], self.ahead[o - 1],
            )
        return to(
            self.vec_out, self.v_across, self.x_send.at[last], self.x_recv.at[last], self.other
        )

    def turn(self, it, v_start):
        @pl.when((it >= 1) & (it < self.count + 1))
        def _():
            for o in range(self.ring):
                self.c_copy(it - 1, o).wait_recv()
                self.core_load(it - 1, o).start()

        @pl.when((it >= 3) & (it < self.count + 3))
        def _():
            for o in range(1, self.ring):
                self.y_copy(it - 3, o).wait_recv()
                self.ring_load(it - 3, o).start()

        at_end = (it >= 5) & (it < self.count + 5) & (self.p == self.k)

        @pl.when(at_end)
        def _():
            self.x_copy(it - 5).wait_recv()
            self.pipe_load(it - 5).start()
            self.each(it - 5, lambda m, at: self.weight_load(m, at).start(), (2, 3))

        @pl.when(it < self.count)
        def _():
            c = it

            @pl.when(c < self.starts[2])
            def _():
                self.fetched(c)

            for o in range(self.ring):

                @pl.when(c >= 2)
                def _():
                    self.c_copy(c - 2, o).wait_send()

                def use(value):
                    self.away[lax.rem(c, 2), o] = value.astype(bf16)

                self.piece(c, 2 * o + 1, use)
                self.c_copy(c, o).start()

        @pl.when((it >= 1) & (it < self.count + 1))
        def _():
            c = it - 1
            for o in range(self.ring - 1, -1, -1):
                self.core_load(c, o).wait()
                if o > 0:

                    @pl.when(c >= 3)
                    def _():
                        self.y_copy(c - 3, o).wait_send()

                    def use(value):
                        value = value + self.core_in[o].astype(f32)
                        self.far[lax.rem(c, 3), o - 1] = value.astype(bf16)

                    self.piece(c, 2 * o, use)
                    self.y_copy(c, o).start()
                else:

                    @pl.when((c >= 5) & (self.p != self.k))
                    def _():
                        self.x_copy(c - 5).wait_send()

                    def use(value):
                        value = value + self.core_in[o].astype(f32)
                        self.near[lax.rem(c, 5)] = value.astype(bf16)

                    self.piece(c, 0, use)
            self.fetch(c + 2)

        @pl.when((it >= 3) & (it < self.count + 3))
        def _():
            c = it - 3
            total = self.near[lax.rem(c, 5)].astype(f32)
            for o in range(1, self.ring):
                self.ring_load(c, o).wait()
                total = total + self.ring_in[o - 1].astype(f32)
            self.near[lax.rem(c, 5)] = total.astype(bf16)

            @pl.when(self.p != self.k)
            def _():
                self.x_copy(c).start()

        @pl.when(at_end)
        def _():
            c = it - 5

            @pl.when(c >= 1)
            def _():
                self.store(c - 1, False)

            self.pipe_load(c).wait()
            core = self.near[lax.rem(c, 5)].astype(f32) + self.pipe_in[...].astype(f32)

            @pl.when(c < self.starts[2])
            def _():
                self.done[...] = core

            def finish(m, at):
                gain, bias = self.scales[:, 2 * m - 4 : 2 * m - 3], self.scales[:, 2 * m - 3 : 2 * m - 2]
                row = self.vec_out[pl.ds(c - self.starts[2], 1), :]
                self.done[...] = gain * core + bias * row
                self.weight_load(m, at).wait()
                weight = self.weight[...].astype(f32)
                lane = lax.broadcasted_iota(jnp.int32, self.norms.shape, 1)
                gain_sum = jnp.sum(weight * core, axis=1, keepdims=True)
                bias_sum = jnp.sum(weight * row, axis=1, keepdims=True)
                both = jnp.where(lane == 2 * m - 4, gain_sum, 0.0)
                both = both + jnp.where(lane == 2 * m - 3, bias_sum, 0.0)
                self.norms[...] = self.norms[...] + both

            self.each(c, finish, (2, 3))
            self.store(c, True)

        @pl.when(it == v_start)
        def _():
            self.v_copy(0).start()

        @pl.when(it == v_start + 1)
        def _():
            self.v_copy(0).wait()
            self.v_held[...] = self.v_held[...] + self.vec[...]
            for o in range(1, self.ring):
                self.v_copy(1, o).start()

        @pl.when(it == v_start + 2)
        def _():
            total = self.v_held[...]
            for o in range(1, self.ring):
                self.v_copy(1, o).wait()
                total = total + self.v_round[o - 1]
            self.vec_out[...] = total

            @pl.when(self.p != self.k)
            def _():
                self.v_copy(2).start()

        @pl.when((it == v_start + 3) & (self.p == self.k))
        def _():
            self.v_copy(2).wait_recv()
            self.vec_out[...] = self.vec_out[...] + self.v_across[...]

    def drain(self):
        last = self.count
        for o in range(self.ring):
            for c in (last - 2, last - 1):
                self.c_copy(c, o).wait_send()
            for c in (last - 3, last - 2, last - 1):
                if o > 0:
                    self.y_copy(c, o).wait_send()

        @pl.when(self.p == self.k)
        def _():
            self.store(jnp.int32(last - 1), False)

        @pl.when(self.p != self.k)
        def _():
            self.v_copy(2).wait_send()
            for c in range(last - 5, last):
                self.x_copy(c).wait_send()

    @staticmethod
    def landing(ways, part, count):
        ring = ways // 2
        return [
            jax.ShapeDtypeStruct((count, *lead, part, part), bf16)
            for lead in ((ring,), (ring - 1,), ())
        ]

    @staticmethod
    def scratch(ways, part, tokens, count):
        ring = ways // 2
        dma = pltpu.SemaphoreType.DMA
        return [
            pltpu.VMEM((3, tokens, part), bf16),
            pltpu.VMEM((2, ring, part, part), bf16),
            pltpu.VMEM((5, part, part), bf16),
            pltpu.VMEM((3, ring - 1, part, part), bf16),
            pltpu.VMEM((ring, part, part), bf16),
            pltpu.VMEM((ring - 1, part, part), bf16),
            pltpu.VMEM((part, part), bf16),
            pltpu.VMEM((part, part), f32),
            pltpu.VMEM((part, part), bf16),
            pltpu.VMEM((16, part), f32),
            pltpu.VMEM((16, part), f32),
            pltpu.VMEM((ring - 1, 16, part), f32),
            pltpu.VMEM((16, part), f32),
            dma((3,)),
            dma((count + 1, ring)),
            dma((count + 1, ring)),
            dma((count + 1, ring - 1)),
            dma((count + 1, ring - 1)),
            dma((count + 1,)),
            dma((count + 1,)),
            dma((1,)),
            dma((3, max(ring, 2))),
        ]


class BackWork:
    def __init__(self, given, ways, heads, g, tables, segs, gains, hbm, dq, dh, u, vec, refs):
        self.given = given
        self.wq, self.w1, self.w2, self.wd, self.qr, self.kr, self.vr, self.slope = hbm
        (
            self.wa, self.wb, self.hq, self.hk, self.hv, self.sl, self.d_ar,
            self.q_sum, self.dk, self.dv, self.sem,
        ) = refs
        self.ways, self.heads, self.g, self.vec = ways, heads, g, vec
        self.tables, self.segs, self.gains = tables, segs, gains
        self.dq, self.dh, self.u_rows = dq, dh, u
        self.part = g.shape[1] // ways
        self.size = self.qr.shape[1] // heads
        pieces = [("head", h) for h in range(heads)]
        pieces += [("hidden", j) for j in range(dh.shape[1] // self.part)]
        pieces += [("rows", j) for j in range(ways)]
        self.pieces = pieces

    def loads(self, n):
        kind, j = self.pieces[n]
        slot, part, size = n % 2, self.part, self.size
        width, hidden, inner = self.g.shape[1], self.dh.shape[1], self.dq.shape[1]
        if kind == "head":
            cols = pl.ds(j * size, size)
            if self.given:
                pairs = [(self.wd.at[:, cols], self.d_ar.at[slot])]
            else:
                pairs = [(self.wd.at[cols, :], self.wa.at[slot, pl.ds(0, size), pl.ds(0, width)])]
            pairs += [
                (ref.at[:, cols], held.at[slot])
                for ref, held in ((self.qr, self.hq), (self.kr, self.hk), (self.vr, self.hv))
            ]
        elif kind == "hidden":
            at = pl.ds(j * part, part)
            pairs = [(self.slope.at[:, at], self.dh.at[:, at])] if self.given else [
                (self.w2.at[at, :], self.wa.at[slot, pl.ds(0, part), pl.ds(0, width)]),
                (self.slope.at[:, at], self.sl.at[slot]),
            ]
        else:
            at = pl.ds(j * part, part)
            pairs = [
                (self.w1.at[at, :], self.wa.at[slot, pl.ds(0, part), pl.ds(0, hidden)]),
                (self.wq.at[at, :], self.wb.at[slot, :, pl.ds(0, inner)]),
            ]
        return [
            pltpu.make_async_copy(source, target, self.sem.at[slot, i])
            for i, (source, target) in enumerate(pairs)
        ]

    def begin(self, n):
        if n < len(self.pieces):
            for load in self.loads(n):
                load.start()

    def run(self, n):
        for load in self.loads(n):
            load.wait()
        self.begin(n + 1)
        kind, j = self.pieces[n]
        getattr(self, kind)(j, n % 2)

    def blocks(self, act):
        def body(step, _):
            act(pl.ds(pl.multiple_of(step * BAND, BAND), BAND))
            return 0

        lax.fori_loop(0, self.g.shape[0] // BAND, body, 0)

    def head(self, h, slot):
        size, width = self.size, self.g.shape[1]
        weight = self.wa.at[slot, pl.ds(0, size), pl.ds(0, width)]

        def act(at):
            self.d_ar[0, at, :] = dot(self.g[at, :], weight[...], ((1,), (1,))).astype(bf16)

        if not self.given:
            self.blocks(act)
        attend_back_kernel(
            1.0 / math.sqrt(size), self.hq.at[slot], self.hk.at[slot], self.hv.at[slot],
            self.d_ar.at[slot if self.given else 0], *self.tables, *self.segs,
            self.dq.at[:, pl.ds(h * 3 * size, 3 * size)], self.q_sum.at[pl.ds(h, 1)],
            self.dk, self.dv,
        )
        if h == self.heads - 1:
            sums = jnp.concatenate([self.q_sum[i] for i in range(self.heads)], axis=1)
            for row in range(sums.shape[1] // self.part):
                self.vec[row : row + 1, :] = sums[:, row * self.part : (row + 1) * self.part]

    def hidden(self, j, slot):
        part, width = self.part, self.g.shape[1]
        weight = self.wa.at[slot, pl.ds(0, part), pl.ds(0, width)]
        cols = pl.ds(j * part, part)
        first = self.dq.shape[1] // part
        row = first + j
        self.vec[row : row + 1, :] = jnp.zeros((1, part), f32)

        def act(at):
            if self.given:
                value = self.dh[at, cols]
            else:
                value = dot(self.g[at, :], weight[...], ((1,), (1,)))
                value = (self.sl[slot, at, :].astype(f32) * value).astype(bf16)
                self.dh[at, cols] = value
            self.vec[row : row + 1, :] += jnp.sum(value.astype(f32), axis=0, keepdims=True)

        self.blocks(act)
        if j == 0:
            d = lax.axis_index("dp")
            ring = self.ways // 2
            for r in range(self.ways):
                place = lax.rem(d // 2 + r // 2, ring) * 2 + lax.rem(d + r % 2, 2)
                total = jnp.sum(self.g[:, pl.ds(r * part, part)].astype(f32), axis=0, keepdims=True)
                self.vec[pl.ds(first + self.dh.shape[1] // part + place, 1), :] = total

    def rows(self, j, slot):
        part, hidden, inner = self.part, self.dh.shape[1], self.dq.shape[1]
        weight_1 = self.wa.at[slot, pl.ds(0, part), pl.ds(0, hidden)]
        weight_q = self.wb.at[slot, :, pl.ds(0, inner)]
        cols = pl.ds(j * part, part)
        gain_1, gain_2 = (gain[:, cols] for gain in self.gains)

        def act(at):
            value = dot(self.dq[at, :], weight_q[...], ((1,), (1,))) * gain_1
            value = value + dot(self.dh[at, :], weight_1[...], ((1,), (1,))) * gain_2
            self.u_rows[at, cols] = value.astype(bf16)

        self.blocks(act)

    @staticmethod
    def scratch(given, ways, heads, tokens, width, hidden, size):
        part = width // ways
        return [
            pltpu.VMEM((2, max(part, size), max(width, hidden)), bf16),
            pltpu.VMEM((2, part, 3 * heads * size), bf16),
            *[pltpu.VMEM((2, tokens, size), bf16)] * 3,
            pltpu.VMEM((2, tokens, part), bf16),
            pltpu.VMEM((2 if given else 1, tokens, size), bf16),
            pltpu.VMEM((heads, 1, 3 * size), f32),
            *[pltpu.VMEM((BAND, size), f32)] * 2,
            pltpu.SemaphoreType.DMA((2, 4)),
        ]


def back_kernel(n, ways, heads, k, *refs):
    take = iter(refs)

    def some(count):
        return [next(take) for _ in range(count)]

    g, xh, scales = some(3)
    tables, segs, gains = some(3), some(2), some(2)
    inv_in = next(take)
    weights, attended, slope = some(4), some(3), next(take)
    lefts, own = some(2), some(2)
    outward = weights[2:]
    if k == 1:
        weights = weights[:2] + [None, next(take)]
    if k == 0:
        y_part, y_base, y_shift = some(3)
        norms_in = next(take)
        some(4)
    vec_out, norms, outs = next(take), next(take), some(4)
    if k == 0:
        norm_rows, own_rows, away_rows, y_land = some(4)
    else:
        out, branch = some(2)
    landing = some(3)
    dq, dh, u, inv_std, inv_sem, right, left = some(7)
    line_sems = some(4 if k == 0 else 8)
    work_refs = some(11)
    grad_refs = landing + some(22)
    p, t = lax.axis_index("pipe"), lax.axis_index("tensor")
    other = {"pipe": 1 - p}
    if k == 0:
        stage, handed, d_send, d_recv, stage_sem = some(5)
        y_in, y_stage, y_line, y_handed, yz_send, yz_recv, yx_send, yx_recv, y_sem = some(9)
        n_land, n_send, n_recv = some(3)

    def d_copy(s, sub):
        mine = pl.ds(pl.multiple_of(s * sub, sub), sub)
        return to(handed.at[mine, :], away_rows.at[mine, :], d_send.at[s], d_recv.at[s], other)

    def d_store(s, sub):
        mine = pl.ds(pl.multiple_of(s * sub, sub), sub)
        slot = lax.rem(s, 2)
        return pltpu.make_async_copy(stage.at[slot], own_rows.at[mine, :], stage_sem.at[slot])

    def in_true_order(total):
        d, ring, part = lax.axis_index("dp"), ways // 2, total.shape[1] // ways
        for r in range(ways):
            place = lax.rem(d // 2 + r // 2, ring) * 2 + lax.rem(d + r % 2, 2)
            cols = pl.ds(pl.multiple_of(place * part, part), part)
            yield cols, total[:, r * part : (r + 1) * part]

    def finished(line, s, total):
        mine = pl.ds(pl.multiple_of(s * line.sub, line.sub), line.sub)
        xr = line.at(xh, line.i, s)[...].astype(f32)
        mean = jnp.mean(total, axis=1, keepdims=True)
        proj = jnp.mean(total * xr, axis=1, keepdims=True)
        total = inv_std[mine, :] * (total - mean - xr * proj)
        total = line.at(g, line.i, s)[...].astype(f32) + total
        if k == 1:
            line.at(out, line.i, s)[...] = total.astype(bf16)
        else:

            @pl.when(p == 0)
            def _():
                @pl.when(s >= 2)
                def _():
                    d_store(s - 2, line.sub).wait()

                for cols, value in in_true_order(total):
                    stage[lax.rem(s, 2), :, cols] = value
                d_store(s, line.sub).start()

            @pl.when(p == 1)
            def _():
                for cols, value in in_true_order(total):
                    handed[mine, cols] = value.astype(bf16)
                d_copy(s, line.sub).start()

    line = LineSum(n, u, right, left, line_sems, finished, out if k else None)
    vec = grad_refs[12]
    work = BackWork(
        k == 1, ways, heads, g, tables, segs, gains, (*weights, *attended, slope), dq, dh, u, vec,
        work_refs,
    )
    grads = GradSum(k, ways, xh, g, lefts, (dq, dh), outs, own, scales, vec_out, norms, grad_refs)
    places = [line.after, line.before, grads.core, grads.other] + grads.ahead
    if k == 0:
        along = [{"tensor": lax.rem(t + step, n)} for step in range(1, n)]
        places = places[2:] + along
    rows = inv_std.shape[0]
    inv_load = pltpu.make_async_copy(
        inv_in.at[pl.ds(pl.multiple_of(t * rows, rows), rows), :], inv_std, inv_sem.at[0]
    )
    inv_load.start()
    greet(places)
    inv_load.wait()
    grads.begin()
    norms[...] = norms_in[...] if k == 0 else jnp.zeros(norms.shape, f32)
    work.begin(0)

    count = len(work.pieces)
    last_hidden = heads + dh.shape[1] // work.part
    middle = (last_hidden + count) // 2
    if k == 1:
        step = -(-(count - last_hidden) // 4)
        plan = {1: (0, 1), 3: (1, heads), 4: (heads, last_hidden)}
        plan |= {5 + i: (last_hidden + i * step, last_hidden + (i + 1) * step) for i in range(4)}
        begin, v_start = 9, 3
    else:
        mid_hidden = (heads + last_hidden) // 2
        plan = {
            3: (0, 1), 7: (1, heads), 8: (heads, mid_hidden), 9: (mid_hidden, last_hidden),
            11: (last_hidden, middle), 13: (middle, count),
        }
        begin, v_start = 14, 5

    if k == 0:
        block = rows // 4

        def yz_copy(step):
            owner = lax.rem(t + step, n)
            theirs = pl.ds(pl.multiple_of(owner * rows, rows), rows)
            return to(
                y_part.at[theirs, :], y_land.at[step - 1], yz_send.at[step - 1],
                yz_recv.at[step - 1], along[step - 1],
            )

        def yx_copy(q):
            mine = pl.ds(q * block, block)
            return to(
                y_handed.at[mine, :], away_rows.at[mine, :], yx_send.at[q], yx_recv.at[q], other
            )

        def y_store(q):
            mine = pl.ds(q * block, block)
            return pltpu.make_async_copy(y_stage, own_rows.at[mine, :], y_sem.at[n + 1])

        def y_finish(q):
            mine = pl.ds(q * block, block)
            if q == 0:
                for step in range(1, n):
                    yz_copy(step).wait_recv()
            start = pl.multiple_of(t * rows + q * block, block)
            loads = [pltpu.make_async_copy(y_part.at[pl.ds(start, block), :], y_in.at[0], y_sem.at[0])]
            loads += [
                pltpu.make_async_copy(y_land.at[step - 1, mine, :], y_in.at[step], y_sem.at[step])
                for step in range(1, n)
            ]
            loads.append(
                pltpu.make_async_copy(y_base.at[pl.ds(start, block), :], y_in.at[n], y_sem.at[n])
            )
            shift = pltpu.make_async_copy(y_shift, y_line, y_sem.at[n + 2])
            shift.start()
            for load in loads:
                load.start()
            for load in loads:
                load.wait()
            shift.wait()
            total = y_in[n].astype(f32) + y_line[...]
            for step in range(n):
                total = total + y_in[step].astype(f32)

            @pl.when(p == 1)
            def _():
                if q > 0:
                    y_store(q - 1).wait()
                for cols, value in in_true_order(total):
                    y_stage[:, cols] = value
                y_store(q).start()

            @pl.when(p == 0)
            def _():
                for cols, value in in_true_order(total):
                    y_handed[mine, cols] = value.astype(bf16)
                yx_copy(q).start()

        for step in range(1, n):
            yz_copy(step).start()

    b_start = grads.count + 1

    def b_loads(j):
        part = work.part
        cols = pl.ds(j * part, part)
        tokens, hidden = g.shape[0], dh.shape[1]
        half = min(tokens, hidden)
        pairs = [
            (outward[0].at[pl.ds(i * half, half), cols], grads.load.at[i, pl.ds(0, half), :])
            for i in range(hidden // half)
        ]
        rows = outward[1].shape[0]
        pairs.append((outward[1].at[:, cols], work.wb.at[j % 2, pl.ds(0, rows), pl.ds(0, part)]))
        if j == 0:
            pairs += [(lefts[0], dh), (lefts[1], dq.at[:, pl.ds(0, rows)])]
        return [
            pltpu.make_async_copy(source, target, work.sem.at[i // 4, i % 4])
            for i, (source, target) in enumerate(pairs)
        ]

    def b_store(j):
        part = work.part
        return pltpu.make_async_copy(
            work.sl.at[j % 2], branch.at[:, pl.ds(j * part, part)], grads.load_sem.at[j % 2]
        )

    def b_block(j):
        part, hidden = work.part, dh.shape[1]
        half = min(g.shape[0], hidden)
        rows = outward[1].shape[0]
        loads = b_loads(j)
        for load in loads:
            load.start()
        if j >= 2:
            b_store(j - 2).wait()
        for load in loads:
            load.wait()

        def act(at):
            value = dot(dq[at, pl.ds(0, rows)], work.wb[j % 2, pl.ds(0, rows), pl.ds(0, part)])
            for i in range(hidden // half):
                value = value + dot(
                    dh[at, pl.ds(i * half, half)], grads.load[i, pl.ds(0, half), :]
                )
            work.sl[j % 2, at, :] = value.astype(bf16)

        work.blocks(act)
        b_store(j).start()

    def turn_(half, _):
        @pl.when(half >= begin)
        def _():
            line.turn(half - begin)

        @pl.when(lax.rem(half, 2) == 0)
        def _():
            grads.turn(half // 2, v_start)

        for at, (low, high) in plan.items():

            @pl.when(half == at)
            def _():
                for piece in range(low, high):
                    work.run(piece)

        if k == 0:
            for q in range(4):

                @pl.when(half == 2 * q + 17)
                def _():
                    y_finish(q)

        else:
            for j in range(ways):

                @pl.when(half == 2 * b_start + 1 + j)
                def _():
                    b_block(j)

        return 0

    total = max(begin + line.turns, 2 * grads.turns)
    total = max(total, 2 * b_start + 1 + ways if k else 25)
    lax.fori_loop(0, total, turn_, 0)
    line.drain()
    grads.drain()
    if k == 1:
        b_store(ways - 2).wait()
        b_store(ways - 1).wait()
        return
    share = norms.shape[0] // n

    def n_copy(step):
        owner = lax.rem(t + step, n)
        theirs = norms.at[pl.ds(pl.multiple_of(owner * share, share), share), :]
        return to(
            theirs, n_land.at[step - 1], n_send.at[step - 1], n_recv.at[step - 1], along[step - 1]
        )

    for step in range(1, n):
        n_copy(step).start()
    mine = norms[pl.ds(pl.multiple_of(t * share, share), share), :]
    for step in range(1, n):
        n_copy(step).wait()
        mine = mine + n_land[step - 1]
    norm_rows[...] = mine
    for step in range(1, n):
        yz_copy(step).wait_send()

    @pl.when(p == 1)
    def _():
        y_store(3).wait()
        for s in range(line.subs):
            d_copy(s, line.sub).wait_send()
        for q in range(4):
            yx_copy(q).wait_recv()

    @pl.when(p == 0)
    def _():
        for s in range(max(line.subs - 2, 0), line.subs):
            d_store(s, line.sub).wait()
        for s in range(line.subs):
            d_copy(s, line.sub).wait_recv()
        for q in range(4):
            yx_copy(q).wait_send()


def back_section(
    k, g, xh, inv_std, scales, tables, seg, gains, weights, attended, slope, lefts, own, heads,
    n, ways, extra_in, held=None,
):
    tokens, width = g.shape
    part, rows = width // ways, tokens // n
    hidden, inner = slope.shape[1], 3 * attended[0].shape[1]
    size = inner // 3 // heads
    vmem, hbm = pl.BlockSpec(memory_space=pltpu.VMEM), pl.BlockSpec(memory_space=pl.ANY)
    shape, dma = jax.ShapeDtypeStruct, pltpu.SemaphoreType.DMA
    sides = (lefts[0].shape[1], lefts[1].shape[1], inner, hidden)
    count = sum(sides) // part
    out_shape = [shape((16, part), f32), shape((part, 128), f32)]
    out_specs = [vmem, vmem] + [hbm] * 4
    out_shape += [
        shape((side, part) if m < 2 else (part, side), f32) for m, side in enumerate(sides)
    ]
    if k == 0:
        out_shape += [shape((part // n, 128), f32)]
        out_shape += [shape((rows, width), f32), shape((rows, width), bf16)]
        out_shape += [shape((n - 1, rows, width), bf16)]
        out_specs += [vmem] + [hbm] * 3
        block = rows // 4
        extra = [
            pltpu.VMEM((2, rows // subs_of(rows), width), f32),
            pltpu.VMEM((rows, width), bf16),
            dma((subs_of(rows),)),
            dma((subs_of(rows),)),
            dma((2,)),
            pltpu.VMEM((n + 1, block, width), bf16),
            pltpu.VMEM((block, width), f32),
            pltpu.VMEM((1, width), f32),
            pltpu.VMEM((rows, width), bf16),
            dma((n - 1,)),
            dma((n - 1,)),
            dma((4,)),
            dma((4,)),
            dma((n + 3,)),
            pltpu.VMEM((n - 1, part // n, 128), f32),
            dma((n - 1,)),
            dma((n - 1,)),
        ]
    else:
        out_shape += [shape((tokens, width), bf16)] * 2
        out_specs += [vmem, hbm]
        extra = []
    landing = GradSum.landing(ways, part, count)
    args = [
        g, xh, scales, *tables, seg.reshape(-1, 1), seg.reshape(1, -1), *gains, inv_std,
        *weights, *attended, slope, *lefts, *own, *(extra_in or ()),
    ]
    specs = [vmem] * 10 + [hbm] * (len(args) - 10)
    aliases = {}
    if k == 0:
        aliases = {len(args) + 1 + m: 2 + m for m in range(4)}
        args += held
        specs += [vmem] + [hbm] * 4
    line = LineSum.scratch(n, tokens, width, k == 1)
    return pl.pallas_call(
        functools.partial(back_kernel, n, ways, heads, k),
        in_specs=specs,
        out_specs=out_specs + [hbm] * 3,
        out_shape=out_shape + landing,
        input_output_aliases=aliases,
        scratch_shapes=[
            pltpu.VMEM((tokens, inner), bf16),
            pltpu.VMEM((tokens, hidden), bf16),
            pltpu.VMEM((tokens, width), bf16),
            pltpu.VMEM((rows, 1), f32),
            dma((1,)),
            *line,
            *BackWork.scratch(k == 1, ways, heads, tokens, width, hidden, size),
            *GradSum.scratch(ways, part, tokens, count),
            *extra,
        ],
        compiler_params=pltpu.CompilerParams(
            collective_id=3 + k, has_side_effects=True, vmem_limit_bytes=63 << 20
        ),
        cost_estimate=pl.CostEstimate(flops=0, bytes_accessed=600 << 20, transcendentals=0),
        name="back_section",
    )(*args)


def per_device(
    boundary,
    segments,
    ln1_gain,
    ln1_bias,
    ln2_gain,
    ln2_bias,
    qkv_weight,
    qkv_bias,
    dense_weight,
    dense_bias,
    fc1_weight,
    fc1_bias,
    fc2_weight,
    fc2_bias,
):
    pipe, d, t = lax.axis_index("pipe"), lax.axis_index("dp"), lax.axis_index("tensor")
    ways = lax.axis_size("dp")
    nt = lax.axis_size("tensor")
    first = pipe == 0
    seqs, length, width = boundary.shape[1] // 2, boundary.shape[2], boundary.shape[3]
    tokens, rows, part = seqs * length, length // nt, width // ways
    heads, size = qkv_weight.shape[2], qkv_weight.shape[3] // 3

    seg = lax.dynamic_slice_in_dim(segments, pipe * seqs, seqs, 0)
    shards = (
        qkv_weight[0].reshape(part, heads * 3 * size),
        fc1_weight[0],
        fc2_weight[0],
        dense_weight[0],
    )
    axes = (0, 0, 1, 1)
    def in_place(v):
        whole = jnp.zeros((v.shape[0], v.shape[1] * ways), bf16)
        whole = lax.dynamic_update_slice_in_dim(whole, v, d * v.shape[1], 1)
        return whole.reshape(-1, part)

    small = [ln1_gain, ln1_bias, ln2_gain, ln2_bias, dense_bias, fc2_bias]
    small = jnp.concatenate(small + [in_place(qkv_bias[0]), in_place(fc1_bias)], axis=0)
    small = jnp.pad(small, ((0, 16 - small.shape[0]), (0, 0)))
    source, cotangent, small_all, weights_0, weights_1, found = enter_section(
        boundary[0], small, shards, seg, axes, ways, nt, heads
    )
    tables, (xh0, inv0, ar0, qr0, kr0, vr0, act0, slope0) = found[:3], found[3:]
    small_all = small_all.reshape(ways, 2, 16, part).astype(f32)
    cut = heads * 3 * size

    def vectors(k):
        rows_ = small_all[:, k]
        found = [rows_[:, m].reshape(1, width) for m in range(6)]
        in_place = jnp.sum(rows_[:, 6:], axis=0).reshape(1, -1)
        return found + [in_place[:, cut : cut + fc1_weight.shape[2]], in_place[:, :cut]]

    wq0, w10, w20, wd0 = weights_0
    v0, v1 = vectors(0), vectors(1)
    x1, weights_1, d_ar1, found = middle(
        source, v0[4] + v0[5], cotangent,
        jnp.concatenate(v1[:4], axis=0), v1[7], v1[6], tables, seg, act0, ar0, w20, wd0, weights_1,
        [shard.shape for shard in shards], axes, heads, nt, ways,
    )
    xh1, inv1, ar1, qr1, kr1, vr1, act1, d_hidden1 = found
    wq1, w11, w21, wd1 = weights_1

    g1, _, g2, _ = vectors(1)[:4]

    def column(v):
        return v[0].astype(f32)[:, None]

    scales = jnp.concatenate([column(v) for v in (ln1_gain, ln1_bias, ln2_gain, ln2_bias)], axis=1)
    sums_1, norms, fc2_grad, dense_grad, qkv_grad, fc1_grad, g0, branch, *_ = back_section(
        1, cotangent, xh1, inv1, scales, tables, seg, (g1, g2), (wq1, w11, w21, wd1),
        (qr1, kr1, vr1), d_hidden1, (act1, ar1), shards[:2], heads, nt, ways, (d_ar1,),
    )

    g1, _, g2, _ = vectors(0)[:4]
    found = back_section(
        0, g0, xh0, inv0, scales, tables, seg, (g1, g2), weights_0,
        (qr0, kr0, vr0), slope0, (act0, ar0), shards[:2], heads, nt, ways,
        (branch, x1, v1[4] + v1[5]), [norms, fc2_grad, dense_grad, qkv_grad, fc1_grad],
    )
    sums_0, norms, fc2_grad, dense_grad, qkv_grad, fc1_grad = found[:6]
    own, away = (v.reshape(seqs, rows, width).astype(f32) for v in found[7:9])
    boundary_out = jnp.where(
        first, jnp.concatenate([own, away], axis=0), jnp.concatenate([away, own], axis=0)
    )[None]

    sums = jnp.where(first, sums_0, sums_1).reshape(-1)
    end = cut + shards[1].shape[1]
    qkv_sum, fc1_sum, g_sum = sums[:cut], sums[cut:end], sums[end : end + width]
    norms = found[6][:, :4].T

    qkv_grad = qkv_grad.reshape(part, heads, 3 * size)

    def own_part(v, axis):
        step = v.shape[axis] // ways
        return lax.dynamic_slice_in_dim(v, d * step, step, axis)

    bias_grad = own_part(g_sum, 0)[None]
    return (
        boundary_out,
        norms[0][None],
        norms[1][None],
        norms[2][None],
        norms[3][None],
        qkv_grad[None],
        own_part(qkv_sum.reshape(heads, 3 * size), 1)[None],
        dense_grad[None],
        bias_grad,
        fc1_grad[None],
        own_part(fc1_sum, 0)[None],
        fc2_grad[None],
        bias_grad,
    )


def solution(mesh):
    in_specs = (
        P("pipe", "dp", None, None),
        P("dp", None),
        P("pipe", "dp"),
        P("pipe", "dp"),
        P("pipe", "dp"),
        P("pipe", "dp"),
        P("pipe", "dp", "tensor", None),
        P("pipe", "tensor", "dp"),
        P("pipe", "tensor", "dp"),
        P("pipe", "dp"),
        P("pipe", "dp", "tensor"),
        P("pipe", ("tensor", "dp")),
        P("pipe", "tensor", "dp"),
        P("pipe", "dp"),
    )
    out_specs = (
        P("pipe", "dp", "tensor", None),
        P("pipe", ("dp", "tensor")),
        P("pipe", ("dp", "tensor")),
        P("pipe", ("dp", "tensor")),
        P("pipe", ("dp", "tensor")),
        P("pipe", "dp", "tensor", None),
        P("pipe", "tensor", "dp"),
        P("pipe", "tensor", "dp"),
        P("pipe", "dp"),
        P("pipe", "dp", "tensor"),
        P("pipe", ("tensor", "dp")),
        P("pipe", "tensor", "dp"),
        P("pipe", "dp"),
    )
    return jax.shard_map(
        per_device, mesh=mesh, in_specs=in_specs, out_specs=out_specs, check_vma=False
    )
```
